32 devices in a mesh: parts: 2 (over y), dp: 4 (over x, core), tensor: 4 (over z).
Axes of the slice: x: 2, y: 2, z: 4, core: 2. Of those that a mesh axis runs over, the one named last changes fastest.
Arguments:
- residual: bfloat16 [2048, 8192], P(('parts', 'dp'), 'tensor'), parts along dimension 0, may hold values from -6 to 6
- query: bfloat16 [2048, 32, 128], P(('parts', 'dp'), 'tensor'), parts along dimension 0, may hold values from -6 to 6
- cached_key_rows: bfloat16 [2048, 16, 8, 128], P(('parts', 'dp'), None, 'tensor'), parts along dimension 0, may hold values from -6 to 6
- cached_value_rows: bfloat16 [2048, 16, 8, 128], P(('parts', 'dp'), None, 'tensor'), parts along dimension 0, may hold values from -6 to 6
- new_token_key: bfloat16 [2048, 8, 128], P(('parts', 'dp'), 'tensor'), parts along dimension 0, may hold values from -6 to 6
- new_token_value: bfloat16 [2048, 8, 128], P(('parts', 'dp'), 'tensor'), parts along dimension 0, may hold values from -6 to 6
- lengths: int32 [2048], P(('parts', 'dp')), parts along dimension 0, may hold values from 2 to 16, as said below
- output_weight: bfloat16 [4096, 8192], P('tensor'), may hold values from -0.09375 to 0.09375
- slot_down_weight: bfloat16 [32, 64, 4096], P('dp', None, 'tensor'), may hold values from -0.09375 to 0.09375
- slot_up_weight: bfloat16 [32, 64, 8192], P('dp', None, 'tensor'), may hold values from -0.75 to 0.75
- placement: int32 [64], P('parts'), parts along dimension 0, may hold values from 0 to 31, as said below
- request_adapter: int32 [2048], P(('parts', 'dp')), parts along dimension 0, may hold values from 0 to 31, as said below
Outputs:
- hidden: bfloat16 [2048, 8192], P(('parts', 'dp'), 'tensor'), parts along dimension 0
The draws below stay inside these ranges and needn't reach their ends.
There are 2 independent parts, one for each index of `parts`. The reference program is written for one: setup_inputs(seed, part) draws one part's arguments, and reference() takes and returns one part's arrays. A program takes and returns all parts, laid end to end along the dimension named above; an argument that names none is the same for every part. Nothing has to cross between parts.
Inputs may be any that keep to these rules, and one draw needn't show every extreme that they name: `lengths`: at least 2 cached positions; some request holds 16. `placement`: each slot once; slot s is entry s % 8 of the adapter store on replica s // 8. `request_adapter`: of one replica's 256 requests at most 64 name adapters held by any one replica; in every part one replica, drawn afresh, is named by exactly 64 requests of every replica.
All inputs are finite; a program needn't handle non-finite values.
Results may differ from the reference program's by a relative error of at most 0.0095.
Values may be sent and summed in bfloat16 or wider, within the bound.
No kernel may reach another device: no remote copies, remote signals or barrier semaphores. Data moves between devices by JAX's collectives and lax.ppermute only.
A program may use at most 128 MiB of HBM per device.

```python
import math
import jax
import jax.numpy as jnp
from jax import lax

MODEL_WIDTH = 8192
QUERY_HEADS = 32
KEY_HEADS = 8
HEAD_SIZE = 128
ADAPTER_RANK = 64
REQ_DEV = 256
CACHE_LENGTH = 16
ADP_REP = 8
REQUEST_COUNT = 1024
CAP = 64
ADAPTER_TOTAL = 32
N_DP = 4
N_TENSOR = 4


def routing(key):
    slots = jax.random.permutation(jax.random.fold_in(key, 201), ADAPTER_TOTAL).astype(jnp.int32)
    hottest = jax.random.randint(jax.random.fold_in(key, 202), (), 0, N_DP)
    block_keys = jax.random.split(jax.random.fold_in(key, 203), N_DP)
    order = jax.vmap(lambda inner_product: jax.random.permutation(inner_product, REQ_DEV))(block_keys).astype(jnp.int32)
    offset = jax.random.randint(jax.random.fold_in(key, 204), (N_DP, 1), 0, N_DP - 1)
    spread = (offset + order - CAP) % (N_DP - 1)
    target = jnp.where(order < CAP, hottest, (hottest + 1 + spread) % N_DP)
    inside = jax.random.randint(jax.random.fold_in(key, 205), (N_DP, REQ_DEV), 0, ADP_REP)
    request_slot = (target * ADP_REP + inside).reshape(REQUEST_COUNT).astype(jnp.int32)
    holder = jnp.argsort(slots, stable=True).astype(jnp.int32)
    return (slots, holder[request_slot].astype(jnp.int32))


def draw_query(key, part):
    inner_product = jax.random.fold_in(key, 1)
    value_rows = jnp.clip(jax.random.normal(inner_product, (REQUEST_COUNT, QUERY_HEADS, HEAD_SIZE), jnp.float32), -4.0, 4.0)
    return value_rows.astype(jnp.bfloat16)


def draw_cached_key_rows(key, part):
    inner_product = jax.random.fold_in(key, 2)
    value_rows = jnp.clip(jax.random.normal(inner_product, (REQUEST_COUNT, CACHE_LENGTH, KEY_HEADS, HEAD_SIZE), jnp.float32), -4.0, 4.0)
    return value_rows.astype(jnp.bfloat16)


def draw_lengths(key, part):
    inner_product = jax.random.fold_in(key, 3)
    counts = jax.random.randint(jax.random.fold_in(inner_product, 1), (REQUEST_COUNT,), 2, CACHE_LENGTH + 1)
    fullest = jax.random.randint(jax.random.fold_in(inner_product, 2), (), 0, REQUEST_COUNT)
    counts = jnp.where(jnp.arange(REQUEST_COUNT) == fullest, CACHE_LENGTH, counts)
    return counts.astype(jnp.int32)


def draw_placement(key, part):
    slots, _ = routing(key)
    return slots


def draw_request_adapter(key, part):
    _, chosen_ids = routing(key)
    return chosen_ids


def block_levels(own_key, extent, cuts, low, largest):
    def one(axis_at, blocks):
        draws = jax.random.uniform(jax.random.fold_in(jax.random.fold_in(own_key, 6), axis_at), (blocks,), jnp.float32, low / len(cuts), largest / len(cuts))
        return jnp.repeat(jnp.exp(draws), extent[axis_at] // blocks).reshape((-1,) + (1,) * (len(extent) - axis_at - 1))

    gain = one(*cuts[0])
    for cut in cuts[1:]:
        gain = gain * one(*cut)
    return gain


def normal_values(key, extent, scale, limit, cuts=(), held_as=jnp.bfloat16):
    values = scale * jax.random.normal(key, extent, jnp.float32)
    if cuts:
        values = values * block_levels(key, extent, cuts, -0.22, 0.18)
    return jnp.clip(values, -limit, limit).astype(held_as)


def setup_inputs(seed: int = 0, part: int = 0) -> dict:
    streams_of = jax.random.split(jax.random.key(seed), 13)
    part_splits = jax.random.split(jax.random.fold_in(streams_of[12], part), 13)
    return {
        "residual": normal_values(part_splits[0], (REQUEST_COUNT, MODEL_WIDTH), 1.0, 6.0, ((0, 4), (1, 4))),
        "query": draw_query(jax.random.fold_in(jax.random.fold_in(streams_of[12], part), 71), part),
        "cached_key_rows": draw_cached_key_rows(jax.random.fold_in(jax.random.fold_in(streams_of[12], part), 71), part),
        "cached_value_rows": normal_values(part_splits[3], (REQUEST_COUNT, CACHE_LENGTH, KEY_HEADS, HEAD_SIZE), 1.0, 6.0, ((0, 4), (2, 4))),
        "new_token_key": normal_values(part_splits[4], (REQUEST_COUNT, KEY_HEADS, HEAD_SIZE), 1.0, 6.0, ((0, 4), (1, 4))),
        "new_token_value": normal_values(part_splits[5], (REQUEST_COUNT, KEY_HEADS, HEAD_SIZE), 1.0, 6.0, ((0, 4), (1, 4))),
        "lengths": draw_lengths(jax.random.fold_in(jax.random.fold_in(streams_of[12], part), 71), part),
        "output_weight": normal_values(streams_of[7], (QUERY_HEADS * HEAD_SIZE, MODEL_WIDTH), (QUERY_HEADS * HEAD_SIZE) ** -0.5, 0.09375, ((0, 4),)),
        "slot_down_weight": normal_values(streams_of[8], (ADAPTER_TOTAL, ADAPTER_RANK, QUERY_HEADS * HEAD_SIZE), (QUERY_HEADS * HEAD_SIZE) ** -0.5, 0.09375, ((0, 4), (2, 4))),
        "slot_up_weight": normal_values(streams_of[9], (ADAPTER_TOTAL, ADAPTER_RANK, MODEL_WIDTH), ADAPTER_RANK ** -0.5, 0.75, ((0, 4), (2, 4))),
        "placement": draw_placement(jax.random.fold_in(jax.random.fold_in(streams_of[12], part), 71), part),
        "request_adapter": draw_request_adapter(jax.random.fold_in(jax.random.fold_in(streams_of[12], part), 71), part),
    }


def attend(query, cached_key_rows, cached_value_rows, new_token_key, new_token_value, lengths):
    request_rows = query.shape[0]
    query_group_size = QUERY_HEADS // KEY_HEADS
    attention_scale = 1.0 / math.sqrt(HEAD_SIZE)
    grouped_queries = query.reshape(request_rows, KEY_HEADS, query_group_size, HEAD_SIZE).astype(jnp.float32)
    cached = jnp.einsum('bkgd,blkd->bkgl', grouped_queries, cached_key_rows.astype(jnp.float32)) * attention_scale
    fresh_scores = jnp.einsum('cfwt,cft->cfw', grouped_queries, new_token_key.astype(jnp.float32)) * attention_scale
    valid = jnp.arange(CACHE_LENGTH, dtype=jnp.int32)[None, :] < lengths[:, None]
    cached = jnp.where(valid[:, None, None, :], cached, -jnp.inf)
    top = jnp.maximum(lax.optimization_barrier(jnp.max(cached, axis=-1)), fresh_scores)
    cached_exp = jnp.exp(cached - top[..., None])
    fresh_exp = jnp.exp(fresh_scores - top)
    total_output = lax.optimization_barrier(jnp.sum(cached_exp, axis=-1)) + fresh_exp
    cached_weight = (cached_exp / total_output[..., None]).astype(jnp.bfloat16)
    fresh_weight = (fresh_exp / total_output).astype(jnp.bfloat16)
    mixed = jnp.einsum('bkgl,blkd->bkgd', cached_weight.astype(jnp.float32), cached_value_rows.astype(jnp.float32))
    mixed = mixed + fresh_weight.astype(jnp.float32)[..., None] * new_token_value.astype(jnp.float32)[:, :, None, :]
    return mixed.astype(jnp.bfloat16).reshape(request_rows, QUERY_HEADS * HEAD_SIZE)

def project(attended_output, output_weight):
    block_width = QUERY_HEADS * HEAD_SIZE // N_TENSOR
    pieces = jnp.moveaxis(attended_output.reshape(REQUEST_COUNT, N_TENSOR, block_width), 1, 0)
    blocks = output_weight.reshape(N_TENSOR, block_width, MODEL_WIDTH)

    def add_block(total_output, inputs):
        partial_piece, weight_block = inputs
        term = jnp.dot(partial_piece, weight_block, preferred_element_type=jnp.float32).astype(jnp.bfloat16)
        term = lax.optimization_barrier(term)
        return (total_output + term.astype(jnp.float32), None)
    total_output, _ = lax.scan(add_block, jnp.zeros((REQUEST_COUNT, MODEL_WIDTH), jnp.float32), (pieces, blocks))
    return total_output

def apply_adapter(attended_output, request_slot, slot_down_weight, slot_up_weight):
    block_rows = math.gcd(REQUEST_COUNT, 32)

    def one_block(inputs):
        rows_in, slot_inputs = inputs
        down_weights = slot_down_weight[slot_inputs].astype(jnp.float32)
        rank_mid = jnp.einsum('bf,brf->br', rows_in.astype(jnp.float32), down_weights).astype(jnp.bfloat16)
        up_weights = slot_up_weight[slot_inputs].astype(jnp.float32)
        return jnp.einsum('br,brc->bc', rank_mid.astype(jnp.float32), up_weights).astype(jnp.bfloat16)
    result = lax.map(one_block, (attended_output.reshape(REQUEST_COUNT // block_rows, block_rows, QUERY_HEADS * HEAD_SIZE), request_slot.reshape(REQUEST_COUNT // block_rows, block_rows)))
    return result.reshape(REQUEST_COUNT, MODEL_WIDTH)

def reference(residual, query, cached_key_rows, cached_value_rows, new_token_key, new_token_value, lengths, output_weight, slot_down_weight, slot_up_weight, placement, request_adapter):
    attended_output = attend(query, cached_key_rows, cached_value_rows, new_token_key, new_token_value, lengths)
    base_output = project(attended_output, output_weight)
    request_slot = placement[request_adapter].astype(jnp.int32)
    adapter_delta = apply_adapter(attended_output, request_slot, slot_down_weight, slot_up_weight)
    total_output = residual.astype(jnp.float32) + base_output + adapter_delta.astype(jnp.float32)
    return total_output.astype(jnp.bfloat16)
```

```python
import functools
import math

import jax
import jax.numpy as jnp
from jax import lax
from jax.experimental import pallas as pl
from jax.experimental.pallas import tpu as pltpu
from jax.sharding import PartitionSpec as P

GROUP = 8
PAIR = 2
MASKED = -1e30
VMEM_LIMIT = 48 * 1024 * 1024
CHAINS = 2


def _dot(a, b, dims):
    return lax.dot_general(a, b, (dims, ((), ())), preferred_element_type=jnp.float32)


def _iota(shape, axis):
    return lax.broadcasted_iota(jnp.int32, shape, axis)


def attend_kernel(heads, kv, cache, q_ref, k_ref, v_ref, nk_ref, nv_ref, len_ref, out_ref, held):
    group_rows = GROUP * heads
    group_cols = GROUP * cache * kv
    fresh_cols = GROUP * kv
    per_kv = heads // kv
    requests = len_ref.shape[1]
    groups = requests // GROUP
    step_groups = out_ref.shape[0] // GROUP
    scale = 1.0 / math.sqrt(q_ref.shape[1])

    row = _iota((group_rows, group_cols), 0)
    col = _iota((group_rows, group_cols), 1)
    same = (row // heads == col // (cache * kv)) & ((row % heads) // per_kv == col % kv)
    own_bias = jnp.where(same, 0.0, MASKED)
    row = _iota((group_rows, fresh_cols), 0)
    col = _iota((group_rows, fresh_cols), 1)
    same = (row // heads == col // kv) & ((row % heads) // per_kv == col % kv)
    fresh_bias = jnp.where(same, 0.0, MASKED)

    first = pl.program_id(0) * step_groups
    counts = len_ref[...].astype(jnp.float32)
    group_of = _iota((step_groups, requests), 1) // GROUP == _iota((step_groups, requests), 0) + first
    counts = jnp.where(group_of, counts, 0.0).astype(jnp.bfloat16)
    spread = _iota((requests, group_cols), 0) % GROUP == _iota((requests, group_cols), 1) // (cache * kv)
    counts = _dot(counts, spread.astype(jnp.bfloat16), ((1,), (0,)))
    position = (_iota((step_groups, group_cols), 1) // kv) % cache
    length_bias = jnp.where(position.astype(jnp.float32) < counts, 0.0, MASKED)

    for pair in range(step_groups // PAIR):
        for side in range(PAIR):
            g = pair * PAIR + side
            q = q_ref[pl.ds(g * group_rows, group_rows), :]
            k = k_ref[pl.ds(g * group_cols, group_cols), :]
            v = v_ref[pl.ds(g * group_cols, group_cols), :]
            nk = nk_ref[pl.ds(g * fresh_cols, fresh_cols), :]
            nv = nv_ref[pl.ds(g * fresh_cols, fresh_cols), :]
            scores = _dot(q, k, ((1,), (1,))) * scale + (own_bias + length_bias[g : g + 1, :])
            fresh = _dot(q, nk, ((1,), (1,))) * scale + fresh_bias
            top = jnp.maximum(
                jnp.max(scores, axis=1, keepdims=True), jnp.max(fresh, axis=1, keepdims=True)
            )
            scores = jnp.exp(scores - top)
            fresh = jnp.exp(fresh - top)
            total = jnp.sum(scores, axis=1, keepdims=True) + jnp.sum(fresh, axis=1, keepdims=True)
            inverse = 1.0 / total
            mixed = _dot((scores * inverse).astype(jnp.bfloat16), v, ((1,), (0,)))
            mixed = mixed + _dot((fresh * inverse).astype(jnp.bfloat16), nv, ((1,), (0,)))
            held[pair % 2, pl.ds(side * group_rows, group_rows), :] = mixed
        width = q_ref.shape[1]
        for h in range(heads):
            part = held[pair % 2, pl.ds(h, PAIR * GROUP, stride=heads), :]
            out_ref[pl.ds(pair * PAIR * GROUP, PAIR * GROUP), pl.ds(h * width, width)] = part.astype(
                jnp.bfloat16
            )


def attend(query, keys, values, new_key, new_value, lengths):
    requests, heads, width = query.shape
    cache, kv = keys.shape[1], keys.shape[2]
    steps = 4
    per = requests // steps

    def rows(count):
        return pl.BlockSpec((per * count, width), lambda i: (i, 0))

    return pl.pallas_call(
        functools.partial(attend_kernel, heads, kv, cache),
        grid=(steps,),
        in_specs=[
            rows(heads),
            rows(cache * kv),
            rows(cache * kv),
            rows(kv),
            rows(kv),
            pl.BlockSpec((1, requests), lambda i: (0, 0)),
        ],
        out_specs=pl.BlockSpec((per, heads * width), lambda i: (i, 0)),
        out_shape=jax.ShapeDtypeStruct((requests, heads * width), jnp.bfloat16),
        scratch_shapes=[pltpu.VMEM((2, PAIR * GROUP * heads, width), jnp.float32)],
        compiler_params=pltpu.CompilerParams(vmem_limit_bytes=VMEM_LIMIT),
        name="attend",
    )(
        query.reshape(requests * heads, width),
        keys.reshape(requests * cache * kv, width),
        values.reshape(requests * cache * kv, width),
        new_key.reshape(requests * kv, width),
        new_value.reshape(requests * kv, width),
        lengths.reshape(1, requests),
    )


def project_kernel(blocks_ref, a_ref, w_ref, out_ref):
    out_ref[...] = _dot(a_ref[...], w_ref[...], ((1,), (0,))).astype(jnp.bfloat16)


def project(attended, weight, blocks, block_width):
    rows, depth = attended.shape
    count = blocks.shape[0]
    return pl.pallas_call(
        project_kernel,
        grid_spec=pltpu.PrefetchScalarGridSpec(
            num_scalar_prefetch=1,
            grid=(count,),
            in_specs=[
                pl.BlockSpec((rows, depth), lambda i, b: (0, 0)),
                pl.BlockSpec((depth, block_width), lambda i, b: (0, b[i])),
            ],
            out_specs=pl.BlockSpec((rows, block_width), lambda i, b: (0, i)),
        ),
        out_shape=jax.ShapeDtypeStruct((rows, count * block_width), jnp.bfloat16),
        compiler_params=pltpu.CompilerParams(vmem_limit_bytes=VMEM_LIMIT),
        name="project",
    )(blocks, attended, weight)


def ring_order(count):
    return list(range(0, count, 2)) + list(range(1, count, 2))[::-1]


def gather_by_exchange(blocks, count):
    held = [blocks]
    reach = count // 2
    place = [0]
    while reach:
        perm = [(i, i ^ reach) for i in range(count)]
        held = held + [lax.ppermute(h, "dp", perm) for h in held]
        place = place + [p ^ reach for p in place]
        reach //= 2
    return held, place


def per_device(
    residual,
    query,
    cached_key_rows,
    cached_value_rows,
    new_token_key,
    new_token_value,
    lengths,
    output_weight,
    slot_down_weight,
    slot_up_weight,
    placement,
    request_adapter,
):
    tensor_count = lax.axis_size("tensor")
    dp_count = lax.axis_size("dp")
    order = ring_order(tensor_count)
    spot = {device: p for p, device in enumerate(order)}
    ring = [(order[p], order[(p + 1) % tensor_count]) for p in range(tensor_count)]
    table = [
        [order[(spot[t] - 1 - s) % tensor_count] for s in range(tensor_count)]
        for t in range(tensor_count)
    ]
    here = lax.axis_index("tensor")
    owners = jnp.asarray(table, jnp.int32)[here]

    downs, places = gather_by_exchange(slot_down_weight, dp_count)
    ups, _ = gather_by_exchange(slot_up_weight, dp_count)

    attended = attend(
        query, cached_key_rows, cached_value_rows, new_token_key, new_token_value, lengths
    )
    rows = attended.shape[0]
    out_width = residual.shape[1]
    chain_width = out_width // CHAINS
    block_width = min(512, chain_width)
    per_chain = chain_width // block_width
    blocks = owners[:, None, None] * (CHAINS * per_chain) + jnp.arange(
        CHAINS * per_chain, dtype=jnp.int32
    ).reshape(1, CHAINS, per_chain)

    first = [project(attended, output_weight, blocks[0, c], block_width) for c in range(CHAINS)]
    rest = project(attended, output_weight, blocks[1:].reshape(-1), block_width)

    table_size = placement.shape[0]
    matches = request_adapter[:, None] == jnp.arange(table_size, dtype=jnp.int32)[None, :]
    request_slot = jnp.sum(jnp.where(matches, placement[None, :], 0), axis=1)
    slots, rank = slot_down_weight.shape[0], slot_down_weight.shape[1]
    holder = (request_slot // slots) ^ lax.axis_index("dp")
    inside = request_slot % slots

    mid = jnp.zeros((rows, rank), jnp.float32)
    chosen = []
    for down, place in zip(downs, places):
        pick = (holder == place)[:, None] & (
            inside[:, None] == jnp.arange(slots, dtype=jnp.int32)[None, :]
        )
        chosen.append(pick)
        projected = jnp.einsum("nf,arf->nar", attended, down, preferred_element_type=jnp.float32)
        mid = mid + jnp.sum(jnp.where(pick[:, :, None], projected, 0.0), axis=1)
    mid = mid.astype(jnp.bfloat16)
    mids = [mid]
    for step in range(1, tensor_count):
        perm = [(i, (i + step) % tensor_count) for i in range(tensor_count)]
        mids.append(lax.ppermute(mid, "tensor", perm))
    rank_mid = sum(m.astype(jnp.float32) for m in mids).astype(jnp.bfloat16)

    delta = jnp.zeros((rows, out_width), jnp.float32)
    for up, pick in zip(ups, chosen):
        masked = pick.astype(jnp.bfloat16)[:, :, None] * rank_mid[:, None, :]
        delta = delta + jnp.einsum("nar,arc->nc", masked, up, preferred_element_type=jnp.float32)
    delta = delta.astype(jnp.bfloat16)

    outs = []
    travelling = list(first)
    for step in range(1, tensor_count):
        for c in range(CHAINS):
            arrived = lax.ppermute(travelling[c], "tensor", ring)
            at = ((step - 1) * CHAINS + c) * chain_width
            own = lax.slice_in_dim(rest, at, at + chain_width, axis=1)
            total = arrived.astype(jnp.float32) + own.astype(jnp.float32)
            if step < tensor_count - 1:
                travelling[c] = total.astype(jnp.bfloat16)
            else:
                cols = slice(c * chain_width, (c + 1) * chain_width)
                total = (
                    residual[:, cols].astype(jnp.float32)
                    + total
                    + delta[:, cols].astype(jnp.float32)
                )
                outs.append(total.astype(jnp.bfloat16))
    return jnp.concatenate(outs, axis=1)


def solution(mesh):
    placed = (
        P(("parts", "dp"), "tensor"),
        P(("parts", "dp"), "tensor", None),
        P(("parts", "dp"), None, "tensor", None),
        P(("parts", "dp"), None, "tensor", None),
        P(("parts", "dp"), "tensor", None),
        P(("parts", "dp"), "tensor", None),
        P(("parts", "dp")),
        P("tensor", None),
        P("dp", None, "tensor"),
        P("dp", None, "tensor"),
        P("parts"),
        P(("parts", "dp")),
    )
    return jax.shard_map(
        per_device,
        mesh=mesh,
        in_specs=placed,
        out_specs=P(("parts", "dp"), "tensor"),
        check_vma=False,
    )
```

```python
import functools
import math

import jax
import jax.numpy as jnp
from jax import lax
from jax.experimental import pallas as pl
from jax.experimental.pallas import tpu as pltpu
from jax.sharding import PartitionSpec as P

GROUP = 8
CAP = 64
LANES = 128
MASKED = -1e30
VMEM_LIMIT = 60 * 1024 * 1024
CHAINS = 2
PIECE = 512
SPLIT = 2

VMEM = pl.BlockSpec(memory_space=pltpu.VMEM)
ANY = pl.BlockSpec(memory_space=pl.ANY)
PARAMS = pltpu.CompilerParams(vmem_limit_bytes=VMEM_LIMIT)


def _dot(a, b, left=1, right=0):
    return lax.dot_general(
        a, b, (((left,), (right,)), ((), ())), preferred_element_type=jnp.float32
    )


def _iota(shape, axis):
    return lax.broadcasted_iota(jnp.int32, shape, axis)


def ring_order(count):
    return list(range(0, count, 2)) + list(range(1, count, 2))[::-1]


def column_owner(step):
    count = lax.axis_size("tensor")
    here = lax.axis_index("tensor")
    half = here // 2
    spot = jnp.where(here % 2 == 0, half, count - 1 - half)
    spot = lax.rem(spot - 1 - step + 2 * count, count)
    return jnp.where(2 * spot < count, 2 * spot, 2 * (count - spot) - 1)


class Weights:
    def __init__(self, w_ref, held, sems, first, width):
        depth = w_ref.shape[0] // SPLIT
        self.piece = min(PIECE, width)
        self.held = held
        self.copies = []
        for p in range(width // self.piece):
            at = pl.multiple_of(first + p * self.piece, self.piece)
            self.copies.append(
                [
                    pltpu.make_async_copy(
                        w_ref.at[pl.ds(s * depth, depth), pl.ds(at, self.piece)],
                        held.at[p, pl.ds(s * depth, depth), :],
                        sems.at[p, s],
                    )
                    for s in range(SPLIT)
                ]
            )

    def start(self):
        for piece in self.copies:
            for copy in piece:
                copy.start()

    def products(self, a):
        for p, piece in enumerate(self.copies):
            for copy in piece:
                copy.wait()
            yield pl.ds(p * self.piece, self.piece), _dot(a, self.held[p])

    @staticmethod
    def scratch(depth, width):
        piece = min(PIECE, width)
        count = width // piece
        return [
            pltpu.VMEM((count, depth, piece), jnp.bfloat16),
            pltpu.SemaphoreType.DMA((count, SPLIT)),
        ]


def attend_kernel(
    heads, kv, cache, steps,
    len_ref, q_hbm, k_hbm, v_hbm, nk_hbm, nv_hbm, w_hbm,
    a_ref, out_ref,
    q_ref, k_ref, v_ref, nk_ref, nv_ref, scores_ref, mixed_ref, sems, fresh_sems, w_held, w_sems,
):
    requests = len_ref.shape[1]
    width = q_hbm.shape[1]
    per = requests // steps
    groups = per // GROUP
    group_rows = GROUP * heads
    group_cols = GROUP * cache * kv
    per_kv = heads // kv
    scale = 1.0 / math.sqrt(width)

    def part(kind, step):
        source, target, count = (
            (q_hbm, q_ref, heads),
            (k_hbm, k_ref, cache * kv),
            (v_hbm, v_ref, cache * kv),
        )[kind]
        rows = pl.ds(step * per * count, per * count)
        return pltpu.make_async_copy(source.at[rows, :], target.at[rows, :], sems.at[kind, step])

    fresh = [
        pltpu.make_async_copy(source, target, fresh_sems.at[i])
        for i, (source, target) in enumerate(((nk_hbm, nk_ref), (nv_hbm, nv_ref)))
    ]
    chunk = out_ref.shape[1]
    first = column_owner(0) * (CHAINS * chunk)
    weights = Weights(w_hbm, w_held, w_sems, first, chunk)
    part(0, 0).start()
    part(1, 0).start()
    fresh[0].start()
    part(2, 0).start()
    fresh[1].start()
    for step in range(1, steps):
        for kind in range(3):
            part(kind, step).start()
    weights.start()

    row = _iota((group_rows, group_cols), 0)
    col = _iota((group_rows, group_cols), 1)
    same = (row // heads == col // (cache * kv)) & ((row % heads) // per_kv == col % kv)
    own_bias = jnp.where(same, 0.0, MASKED)
    row = _iota((group_rows, per * kv), 0)
    col = _iota((group_rows, per * kv), 1)
    fresh_kv = (row % heads) // per_kv == col % kv
    fresh_distance = col // kv - row // heads

    counts = len_ref[...].astype(jnp.float32)
    all_groups = requests // GROUP
    of_group = _iota((all_groups, requests), 1) // GROUP == _iota((all_groups, requests), 0)
    counts = jnp.where(of_group, counts, 0.0).astype(jnp.bfloat16)
    spread = _iota((requests, group_cols), 0) % GROUP == _iota((requests, group_cols), 1) // (cache * kv)
    counts = _dot(counts, spread.astype(jnp.bfloat16))
    position = (_iota((all_groups, group_cols), 1) // kv) % cache
    length_bias = jnp.where(position.astype(jnp.float32) < counts, 0.0, MASKED)

    for step in range(steps):
        side = step % 2
        part(0, step).wait()
        part(1, step).wait()
        if step == 0:
            fresh[0].wait()
        q_at = step * per * heads
        k_at = step * per * cache * kv
        f_at = step * per * kv
        for g in range(groups):
            rows = pl.ds(g * group_rows, group_rows)
            scores_ref[side, rows, pl.ds(0, group_cols)] = _dot(
                q_ref[pl.ds(q_at + g * group_rows, group_rows), :],
                k_ref[pl.ds(k_at + g * group_cols, group_cols), :],
                1,
                1,
            )
        scores_ref[side, :, pl.ds(group_cols, per * kv)] = _dot(
            q_ref[pl.ds(q_at, per * heads), :], nk_ref[pl.ds(f_at, per * kv), :], 1, 1
        )
        part(2, step).wait()
        if step == 0:
            fresh[1].wait()
        inverses = []
        weights_cached = []
        weights_fresh = []
        for g in range(groups):
            rows = pl.ds(g * group_rows, group_rows)
            bias = own_bias + length_bias[step * groups + g : step * groups + g + 1, :]
            cached = scores_ref[side, rows, pl.ds(0, group_cols)] * scale + bias
            new = scores_ref[side, rows, pl.ds(group_cols, per * kv)] * scale
            new = jnp.where(fresh_kv & (fresh_distance == g * GROUP), new, MASKED)
            top = jnp.maximum(
                jnp.max(cached, axis=1, keepdims=True), jnp.max(new, axis=1, keepdims=True)
            )
            cached = jnp.exp(cached - top)
            new = jnp.exp(new - top)
            total = jnp.sum(cached, axis=1, keepdims=True) + jnp.sum(new, axis=1, keepdims=True)
            inverse = 1.0 / total
            weights_cached.append((cached * inverse).astype(jnp.bfloat16))
            weights_fresh.append((new * inverse).astype(jnp.bfloat16))
        new = _dot(jnp.concatenate(weights_fresh, axis=0), nv_ref[pl.ds(f_at, per * kv), :])
        for g in range(groups):
            rows = slice(g * group_rows, (g + 1) * group_rows)
            mixed_ref[side, rows, :] = new[rows, :] + _dot(
                weights_cached[g], v_ref[pl.ds(k_at + g * group_cols, group_cols), :]
            )
        for h in range(heads):
            a_ref[pl.ds(step * per, per), pl.ds(h * width, width)] = mixed_ref[
                side, pl.ds(h, per, stride=heads), :
            ].astype(jnp.bfloat16)

    for columns, product in weights.products(a_ref[...]):
        out_ref[:, columns] = product.astype(jnp.bfloat16)


def attend(query, keys, values, new_key, new_value, lengths, weight, chunk):
    requests, heads, width = query.shape
    cache, kv = keys.shape[1], keys.shape[2]
    steps = 4
    per = requests // steps
    columns = GROUP * cache * kv + per * kv
    return pl.pallas_call(
        functools.partial(attend_kernel, heads, kv, cache, steps),
        in_specs=[VMEM] + [ANY] * 6,
        out_specs=[VMEM, VMEM],
        out_shape=[
            jax.ShapeDtypeStruct((requests, heads * width), jnp.bfloat16),
            jax.ShapeDtypeStruct((requests, chunk), jnp.bfloat16),
        ],
        scratch_shapes=[
            pltpu.VMEM((requests * heads, width), jnp.bfloat16),
            pltpu.VMEM((requests * cache * kv, width), jnp.bfloat16),
            pltpu.VMEM((requests * cache * kv, width), jnp.bfloat16),
            pltpu.VMEM((requests * kv, width), jnp.bfloat16),
            pltpu.VMEM((requests * kv, width), jnp.bfloat16),
            pltpu.VMEM((2, per * heads, columns), jnp.float32),
            pltpu.VMEM((2, per * heads, width), jnp.float32),
            pltpu.SemaphoreType.DMA((3, steps)),
            pltpu.SemaphoreType.DMA((2,)),
        ]
        + Weights.scratch(weight.shape[0], chunk),
        compiler_params=PARAMS,
        name="attend",
    )(
        lengths.reshape(1, requests),
        query.reshape(requests * heads, width),
        keys.reshape(requests * cache * kv, width),
        values.reshape(requests * cache * kv, width),
        new_key.reshape(requests * kv, width),
        new_value.reshape(requests * kv, width),
        weight,
    )


def hop_kernel(step, chain, arriving, after, *refs):
    if arriving:
        arrived_ref, *refs = refs
    a_ref, w_hbm, *refs = refs
    out_ref, held, sems = refs[after:]
    chunk = out_ref.shape[1]
    first = column_owner(step) * (CHAINS * chunk) + chain * chunk
    weights = Weights(w_hbm, held, sems, first, chunk)
    weights.start()
    for columns, product in weights.products(a_ref[...]):
        if arriving:
            product = product + arrived_ref[:, columns].astype(jnp.float32)
        out_ref[:, columns] = product.astype(jnp.bfloat16)


def hop(step, chain, arrived, attended, weight, chunk, after=()):
    arriving = arrived is not None
    operands = ([arrived] if arriving else []) + [attended, weight, *after]
    return pl.pallas_call(
        functools.partial(hop_kernel, step, chain, arriving, len(after)),
        in_specs=[VMEM] * (1 + arriving) + [ANY] * (1 + len(after)),
        out_specs=VMEM,
        out_shape=jax.ShapeDtypeStruct((attended.shape[0], chunk), jnp.bfloat16),
        scratch_shapes=Weights.scratch(weight.shape[0], chunk),
        compiler_params=PARAMS,
        name="hop",
    )(*operands)


def route_kernel(replicas, slots, after, *refs):
    a_ref, adapter_ref, placement_ref, *refs = refs
    chosen_ref, *sent_refs = refs[after:]
    requests = adapter_ref.shape[1]
    table = placement_ref.shape[1]
    matches = _iota((table, requests), 0) == adapter_ref[...]
    placed = jnp.broadcast_to(placement_ref[...].astype(jnp.float32), (8, table))
    slot = _dot(placed.astype(jnp.bfloat16), matches.astype(jnp.bfloat16)).astype(jnp.int32)
    slot = slot[0:1, :]
    holder = (slot // slots) ^ lax.axis_index("dp")
    inside = slot % slots
    of_holder = _iota((max(replicas, 8), requests), 0) == holder
    earlier = _iota((requests, requests), 0) < _iota((requests, requests), 1)
    before = _dot(of_holder.astype(jnp.bfloat16), earlier.astype(jnp.bfloat16))
    before = jnp.sum(jnp.where(of_holder, before, 0.0), axis=0, keepdims=True).astype(jnp.int32)
    target = holder * CAP + before
    here = _iota((replicas * CAP, requests), 0) == target
    chosen = here.astype(jnp.bfloat16)
    chosen_ref[...] = chosen
    rows = _dot(chosen, a_ref[...]).astype(jnp.bfloat16)
    inner = jnp.sum(jnp.where(here, inside.astype(jnp.float32), 0.0), axis=1, keepdims=True)
    inner = jnp.broadcast_to(inner, (replicas * CAP, LANES)).astype(jnp.bfloat16)
    width = a_ref.shape[1]
    for r, sent_ref in enumerate(sent_refs):
        sent_ref[:, pl.ds(0, width)] = rows[r * CAP : (r + 1) * CAP, :]
        sent_ref[:, pl.ds(width, LANES)] = inner[r * CAP : (r + 1) * CAP, :]


def route(attended, request_adapter, placement, replicas, slots, after=()):
    requests, width = attended.shape
    return pl.pallas_call(
        functools.partial(route_kernel, replicas, slots, len(after)),
        in_specs=[VMEM] * 3 + [ANY] * len(after),
        out_specs=[VMEM] * (1 + replicas),
        out_shape=[jax.ShapeDtypeStruct((replicas * CAP, requests), jnp.bfloat16)]
        + [jax.ShapeDtypeStruct((CAP, width + LANES), jnp.bfloat16)] * replicas,
        compiler_params=PARAMS,
        name="route",
    )(attended, request_adapter.reshape(1, -1), placement.reshape(1, -1), *after)


def down_kernel(replicas, after, *refs):
    received = refs[:replicas]
    down_ref = refs[replicas]
    mid_ref, inside_ref = refs[replicas + 1 + after :]
    slots, rank, width = down_ref.shape
    rows = jnp.concatenate([r[:, pl.ds(0, width)] for r in received], axis=0)
    inside = jnp.concatenate([r[:, pl.ds(width, LANES)] for r in received], axis=0)
    inside_ref[...] = inside
    projected = _dot(rows, down_ref[...].reshape(slots * rank, width), 1, 1)
    lane_slot = _iota(projected.shape, 1) // rank
    mine = lane_slot == inside[:, 0:1].astype(jnp.int32)
    projected = jnp.where(mine, projected, 0.0).astype(jnp.bfloat16)
    fold = _iota((slots * rank, LANES), 0) % rank == _iota((slots * rank, LANES), 1)
    mid_ref[...] = _dot(projected, fold.astype(jnp.bfloat16)).astype(jnp.bfloat16)


def down(received, slot_down_weight, after=()):
    replicas = len(received)
    rows = replicas * CAP
    return pl.pallas_call(
        functools.partial(down_kernel, replicas, len(after)),
        in_specs=[VMEM] * (replicas + 1) + [ANY] * len(after),
        out_specs=[VMEM, VMEM],
        out_shape=[jax.ShapeDtypeStruct((rows, LANES), jnp.bfloat16)] * 2,
        compiler_params=PARAMS,
        name="down",
    )(*received, slot_down_weight, *after)


def up_kernel(parts, after, *refs):
    mids = refs[:parts]
    inside_ref, up_ref = refs[parts : parts + 2]
    out_refs = refs[parts + 2 + after :]
    slots, rank, width = up_ref.shape
    mid = mids[0][...].astype(jnp.float32)
    for m in mids[1:]:
        mid = mid + m[...].astype(jnp.float32)
    spread = _iota((LANES, slots * rank), 1) % rank == _iota((LANES, slots * rank), 0)
    wide = _dot(mid.astype(jnp.bfloat16), spread.astype(jnp.bfloat16))
    mine = _iota(wide.shape, 1) // rank == inside_ref[:, 0:1].astype(jnp.int32)
    wide = jnp.where(mine, wide, 0.0).astype(jnp.bfloat16)
    delta = _dot(wide, up_ref[...].reshape(slots * rank, width)).astype(jnp.bfloat16)
    for r, out_ref in enumerate(out_refs):
        out_ref[...] = delta[r * CAP : (r + 1) * CAP, :]


def up(mids, inside, slot_up_weight, after=()):
    rows = inside.shape[0]
    replicas = rows // CAP
    width = slot_up_weight.shape[2]
    return pl.pallas_call(
        functools.partial(up_kernel, len(mids), len(after)),
        in_specs=[VMEM] * (len(mids) + 2) + [ANY] * len(after),
        out_specs=[VMEM] * replicas,
        out_shape=[jax.ShapeDtypeStruct((CAP, width), jnp.bfloat16)] * replicas,
        compiler_params=PARAMS,
        name="up",
    )(*mids, inside, slot_up_weight, *after)


def settle_kernel(step, replicas, after, *refs):
    returned = refs[:replicas]
    chosen_ref, a_ref, residual_ref, w_hbm = refs[replicas : replicas + 4]
    out_ref, held, sems = refs[replicas + 4 + after :]
    width = out_ref.shape[1]
    weights = Weights(w_hbm, held, sems, column_owner(step) * width, width)
    weights.start()
    rows = jnp.concatenate([r[...] for r in returned], axis=0)
    delta = _dot(chosen_ref[...], rows, 0, 0)
    for columns, product in weights.products(a_ref[...]):
        own = residual_ref[:, columns].astype(jnp.float32) + product
        out_ref[:, columns] = own + delta[:, columns.start : columns.start + columns.size]


def settle(step, returned, chosen, attended, residual, weight, after=()):
    replicas = len(returned)
    return pl.pallas_call(
        functools.partial(settle_kernel, step, replicas, len(after)),
        in_specs=[VMEM] * (replicas + 3) + [ANY] * (1 + len(after)),
        out_specs=VMEM,
        out_shape=jax.ShapeDtypeStruct(residual.shape, jnp.float32),
        scratch_shapes=Weights.scratch(weight.shape[0], residual.shape[1]),
        compiler_params=PARAMS,
        name="settle",
    )(*returned, chosen, attended, residual, weight, *after)


def finish_kernel(arrived_ref, settled_ref, *refs):
    refs[-1][...] = (settled_ref[...] + arrived_ref[...].astype(jnp.float32)).astype(jnp.bfloat16)


def finish(chain, arrived, settled, earlier):
    rows, chunk = arrived.shape
    piece = min(PIECE, chunk)
    count = chunk // piece
    operands = [arrived, settled] + ([earlier] if earlier is not None else [])
    return pl.pallas_call(
        finish_kernel,
        grid=(count,),
        in_specs=[
            pl.BlockSpec((rows, piece), lambda i: (0, i)),
            pl.BlockSpec((rows, piece), lambda i: (0, chain * count + i)),
        ]
        + ([ANY] if earlier is not None else []),
        out_specs=pl.BlockSpec((rows, piece), lambda i: (0, chain * count + i)),
        out_shape=jax.ShapeDtypeStruct(settled.shape, jnp.bfloat16),
        input_output_aliases={2: 0} if earlier is not None else {},
        compiler_params=PARAMS,
        name="finish",
    )(*operands)


def per_device(
    residual,
    query,
    cached_key_rows,
    cached_value_rows,
    new_token_key,
    new_token_value,
    lengths,
    output_weight,
    slot_down_weight,
    slot_up_weight,
    placement,
    request_adapter,
):
    count = lax.axis_size("tensor")
    replicas = lax.axis_size("dp")
    chunk = residual.shape[1] // CHAINS
    order = ring_order(count)
    ring = [(order[p], order[(p + 1) % count]) for p in range(count)]

    def forward(x):
        return lax.ppermute(x, "tensor", ring)

    def exchange(blocks):
        moved = [
            lax.ppermute(blocks[r], "dp", [(i, i ^ r) for i in range(replicas)])
            for r in range(1, replicas)
        ]
        return [blocks[0]] + moved

    attended, first = attend(
        query, cached_key_rows, cached_value_rows, new_token_key, new_token_value, lengths,
        output_weight, chunk,
    )
    travelling = [first] + [
        hop(0, c, None, attended, output_weight, chunk) for c in range(1, CHAINS)
    ]
    chosen, *leaving = route(
        attended, request_adapter, placement, replicas, slot_down_weight.shape[0],
        after=travelling[1:],
    )
    rows_here = exchange(leaving)

    latest = chosen
    stage = 0
    for step in range(1, count - 1):
        for c in range(CHAINS):
            arrived = forward(travelling[c])
            travelling[c] = hop(step, c, arrived, attended, output_weight, chunk, after=[latest])
            latest = travelling[c]
            if stage == 1:
                mid, inside = down(rows_here, slot_down_weight, after=[latest])
                latest = mid
            if stage == 2:
                mids = [mid] + [
                    lax.ppermute(mid, "tensor", [(i, (i + k) % count) for i in range(count)])
                    for k in range(1, count)
                ]
                deltas = up(mids, inside, slot_up_weight, after=[latest])
                latest = deltas[0]
            stage += 1
    returned = exchange(deltas)
    settled = settle(
        count - 1, returned, chosen, attended, residual, output_weight, after=[latest]
    )
    out = None
    for c in range(CHAINS):
        out = finish(c, forward(travelling[c]), settled, out)
    return out


def solution(mesh):
    placed = (
        P(("parts", "dp"), "tensor"),
        P(("parts", "dp"), "tensor", None),
        P(("parts", "dp"), None, "tensor", None),
        P(("parts", "dp"), None, "tensor", None),
        P(("parts", "dp"), "tensor", None),
        P(("parts", "dp"), "tensor", None),
        P(("parts", "dp")),
        P("tensor", None),
        P("dp", None, "tensor"),
        P("dp", None, "tensor"),
        P("parts"),
        P(("parts", "dp")),
    )
    return jax.shard_map(
        per_device,
        mesh=mesh,
        in_specs=placed,
        out_specs=P(("parts", "dp"), "tensor"),
        check_vma=False,
    )
```

```python
import functools
import math

import jax
import jax.numpy as jnp
from jax import lax
from jax.experimental import pallas as pl
from jax.experimental.pallas import tpu as pltpu
from jax.sharding import PartitionSpec as P

GROUP = 8
CAP = 64
LANES = 128
MASKED = -1e30
VMEM_LIMIT = 50 * 1024 * 1024
FULL_VMEM = 61 * 1024 * 1024
CHAINS = 2
PIECE = 512
SPLIT = 2

VMEM = pl.BlockSpec(memory_space=pltpu.VMEM)
ANY = pl.BlockSpec(memory_space=pl.ANY)
BRIEF = pl.CostEstimate(flops=1, transcendentals=0, bytes_accessed=1)
PARAMS = pltpu.CompilerParams(vmem_limit_bytes=VMEM_LIMIT)


def _dot(a, b, left=1, right=0):
    return lax.dot_general(
        a, b, (((left,), (right,)), ((), ())), preferred_element_type=jnp.float32
    )


def _iota(shape, axis):
    return lax.broadcasted_iota(jnp.int32, shape, axis)


def ring_order(count):
    return list(range(0, count, 2)) + list(range(1, count, 2))[::-1]


def column_owner(step):
    count = lax.axis_size("tensor")
    here = lax.axis_index("tensor")
    half = here // 2
    spot = jnp.where(here % 2 == 0, half, count - 1 - half)
    spot = lax.rem(spot - 1 - step + 2 * count, count)
    return jnp.where(2 * spot < count, 2 * spot, 2 * (count - spot) - 1)


class Weights:
    def __init__(self, w_ref, held, sems, first, width):
        depth = w_ref.shape[0] // SPLIT
        self.piece = min(PIECE, width)
        self.held = held
        self.copies = []
        for p in range(width // self.piece):
            at = pl.multiple_of(first + p * self.piece, self.piece)
            self.copies.append(
                [
                    pltpu.make_async_copy(
                        w_ref.at[pl.ds(s * depth, depth), pl.ds(at, self.piece)],
                        held.at[p, pl.ds(s * depth, depth), :],
                        sems.at[p, s],
                    )
                    for s in range(SPLIT)
                ]
            )

    def start(self):
        for piece in self.copies:
            for copy in piece:
                copy.start()

    def products(self, a):
        for p, piece in enumerate(self.copies):
            for copy in piece:
                copy.wait()
            yield pl.ds(p * self.piece, self.piece), _dot(a, self.held[p])

    @staticmethod
    def scratch(depth, width):
        piece = min(PIECE, width)
        count = width // piece
        return [
            pltpu.VMEM((count, depth, piece), jnp.bfloat16),
            pltpu.SemaphoreType.DMA((count, SPLIT)),
        ]


def attend_kernel(
    heads, kv, cache, steps,
    len_ref, q_hbm, k_hbm, v_hbm, nk_hbm, nv_hbm, w_hbm,
    a_ref, out_ref,
    q_ref, k_ref, v_ref, nk_ref, nv_ref, scores_ref, mixed_ref, sems, fresh_sems, w_held, w_sems,
):
    requests = len_ref.shape[1]
    width = q_hbm.shape[1]
    per = requests // steps
    groups = per // GROUP
    group_rows = GROUP * heads
    group_cols = GROUP * cache * kv
    per_kv = heads // kv
    scale = 1.0 / math.sqrt(width)

    def part(kind, step):
        source, target, count = (
            (q_hbm, q_ref, heads),
            (k_hbm, k_ref, cache * kv),
            (v_hbm, v_ref, cache * kv),
        )[kind]
        rows = pl.ds(step * per * count, per * count)
        return pltpu.make_async_copy(source.at[rows, :], target.at[rows, :], sems.at[kind, step])

    fresh = [
        pltpu.make_async_copy(source, target, fresh_sems.at[i])
        for i, (source, target) in enumerate(((nk_hbm, nk_ref), (nv_hbm, nv_ref)))
    ]
    chunk = out_ref.shape[1]
    first = column_owner(0) * (CHAINS * chunk)
    weights = Weights(w_hbm, w_held, w_sems, first, chunk)
    part(0, 0).start()
    part(1, 0).start()
    fresh[0].start()
    part(2, 0).start()
    fresh[1].start()
    for step in range(1, steps):
        for kind in range(3):
            part(kind, step).start()
    weights.start()

    row = _iota((group_rows, group_cols), 0)
    col = _iota((group_rows, group_cols), 1)
    same = (row // heads == col // (cache * kv)) & ((row % heads) // per_kv == col % kv)
    own_bias = jnp.where(same, 0.0, MASKED)
    row = _iota((group_rows, per * kv), 0)
    col = _iota((group_rows, per * kv), 1)
    fresh_kv = (row % heads) // per_kv == col % kv
    fresh_distance = col // kv - row // heads

    counts = len_ref[...].astype(jnp.float32)
    all_groups = requests // GROUP
    of_group = _iota((all_groups, requests), 1) // GROUP == _iota((all_groups, requests), 0)
    counts = jnp.where(of_group, counts, 0.0).astype(jnp.bfloat16)
    spread = _iota((requests, group_cols), 0) % GROUP == _iota((requests, group_cols), 1) // (cache * kv)
    counts = _dot(counts, spread.astype(jnp.bfloat16))
    position = (_iota((all_groups, group_cols), 1) // kv) % cache
    length_bias = jnp.where(position.astype(jnp.float32) < counts, 0.0, MASKED)

    for step in range(steps):
        side = step % 2
        part(0, step).wait()
        part(1, step).wait()
        if step == 0:
            fresh[0].wait()
        q_at = step * per * heads
        k_at = step * per * cache * kv
        f_at = step * per * kv
        for g in range(groups):
            rows = pl.ds(g * group_rows, group_rows)
            scores_ref[side, rows, pl.ds(0, group_cols)] = _dot(
                q_ref[pl.ds(q_at + g * group_rows, group_rows), :],
                k_ref[pl.ds(k_at + g * group_cols, group_cols), :],
                1,
                1,
            )
        scores_ref[side, :, pl.ds(group_cols, per * kv)] = _dot(
            q_ref[pl.ds(q_at, per * heads), :], nk_ref[pl.ds(f_at, per * kv), :], 1, 1
        )
        part(2, step).wait()
        if step == 0:
            fresh[1].wait()
        inverses = []
        weights_cached = []
        weights_fresh = []
        for g in range(groups):
            rows = pl.ds(g * group_rows, group_rows)
            bias = own_bias + length_bias[step * groups + g : step * groups + g + 1, :]
            cached = scores_ref[side, rows, pl.ds(0, group_cols)] * scale + bias
            new = scores_ref[side, rows, pl.ds(group_cols, per * kv)] * scale
            new = jnp.where(fresh_kv & (fresh_distance == g * GROUP), new, MASKED)
            top = jnp.maximum(
                jnp.max(cached, axis=1, keepdims=True), jnp.max(new, axis=1, keepdims=True)
            )
            cached = jnp.exp(cached - top)
            new = jnp.exp(new - top)
            total = jnp.sum(cached, axis=1, keepdims=True) + jnp.sum(new, axis=1, keepdims=True)
            inverse = 1.0 / total
            weights_cached.append((cached * inverse).astype(jnp.bfloat16))
            weights_fresh.append((new * inverse).astype(jnp.bfloat16))
        new = _dot(jnp.concatenate(weights_fresh, axis=0), nv_ref[pl.ds(f_at, per * kv), :])
        for g in range(groups):
            rows = slice(g * group_rows, (g + 1) * group_rows)
            mixed_ref[side, rows, :] = new[rows, :] + _dot(
                weights_cached[g], v_ref[pl.ds(k_at + g * group_cols, group_cols), :]
            )
        for h in range(heads):
            a_ref[pl.ds(step * per, per), pl.ds(h * width, width)] = mixed_ref[
                side, pl.ds(h, per, stride=heads), :
            ].astype(jnp.bfloat16)

    for columns, product in weights.products(a_ref[...]):
        out_ref[:, columns] = product.astype(jnp.bfloat16)


def attend(query, keys, values, new_key, new_value, lengths, weight, chunk):
    requests, heads, width = query.shape
    cache, kv = keys.shape[1], keys.shape[2]
    steps = 4
    per = requests // steps
    columns = GROUP * cache * kv + per * kv
    return pl.pallas_call(
        functools.partial(attend_kernel, heads, kv, cache, steps),
        in_specs=[VMEM] + [ANY] * 6,
        out_specs=[VMEM, VMEM],
        out_shape=[
            jax.ShapeDtypeStruct((requests, heads * width), jnp.bfloat16),
            jax.ShapeDtypeStruct((requests, chunk), jnp.bfloat16),
        ],
        scratch_shapes=[
            pltpu.VMEM((requests * heads, width), jnp.bfloat16),
            pltpu.VMEM((requests * cache * kv, width), jnp.bfloat16),
            pltpu.VMEM((requests * cache * kv, width), jnp.bfloat16),
            pltpu.VMEM((requests * kv, width), jnp.bfloat16),
            pltpu.VMEM((requests * kv, width), jnp.bfloat16),
            pltpu.VMEM((2, per * heads, columns), jnp.float32),
            pltpu.VMEM((2, per * heads, width), jnp.float32),
            pltpu.SemaphoreType.DMA((3, steps)),
            pltpu.SemaphoreType.DMA((2,)),
        ]
        + Weights.scratch(weight.shape[0], chunk),
        compiler_params=pltpu.CompilerParams(vmem_limit_bytes=FULL_VMEM),
        name="attend",
    )(
        lengths.reshape(1, requests),
        query.reshape(requests * heads, width),
        keys.reshape(requests * cache * kv, width),
        values.reshape(requests * cache * kv, width),
        new_key.reshape(requests * kv, width),
        new_value.reshape(requests * kv, width),
        weight,
    )


def hop_kernel(step, chain, arriving, after, *refs):
    if arriving:
        arrived_ref, *refs = refs
    a_ref, w_hbm, *refs = refs
    out_ref, held, sems = refs[after:]
    chunk = out_ref.shape[1]
    first = column_owner(step) * (CHAINS * chunk) + chain * chunk
    weights = Weights(w_hbm, held, sems, first, chunk)
    weights.start()
    for columns, product in weights.products(a_ref[...]):
        if arriving:
            product = product + arrived_ref[:, columns].astype(jnp.float32)
        out_ref[:, columns] = product.astype(jnp.bfloat16)


def hop(step, chain, arrived, attended, weight, chunk, after=()):
    arriving = arrived is not None
    operands = ([arrived] if arriving else []) + [attended, weight, *after]
    return pl.pallas_call(
        functools.partial(hop_kernel, step, chain, arriving, len(after)),
        in_specs=[VMEM] * (1 + arriving) + [ANY] + [ANY] * len(after),
        out_specs=VMEM,
        out_shape=jax.ShapeDtypeStruct((attended.shape[0], chunk), jnp.bfloat16),
        scratch_shapes=Weights.scratch(weight.shape[0], chunk),
        compiler_params=PARAMS,
        cost_estimate=BRIEF,
        name="hop",
    )(*operands)


def route_kernel(replicas, slots, after, *refs):
    a_ref, adapter_ref, placement_ref, *refs = refs
    chosen_ref, *sent_refs = refs[after:]
    requests = adapter_ref.shape[1]
    table = placement_ref.shape[1]
    matches = _iota((table, requests), 0) == adapter_ref[...]
    placed = jnp.broadcast_to(placement_ref[...].astype(jnp.float32), (8, table))
    slot = _dot(placed.astype(jnp.bfloat16), matches.astype(jnp.bfloat16)).astype(jnp.int32)
    slot = slot[0:1, :]
    holder = (slot // slots) ^ lax.axis_index("dp")
    inside = slot % slots
    of_holder = _iota((max(replicas, 8), requests), 0) == holder
    earlier = _iota((requests, requests), 0) < _iota((requests, requests), 1)
    before = _dot(of_holder.astype(jnp.bfloat16), earlier.astype(jnp.bfloat16))
    before = jnp.sum(jnp.where(of_holder, before, 0.0), axis=0, keepdims=True).astype(jnp.int32)
    target = holder * CAP + before
    here = _iota((replicas * CAP, requests), 0) == target
    chosen = here.astype(jnp.bfloat16)
    chosen_ref[...] = chosen
    rows = _dot(chosen, a_ref[...]).astype(jnp.bfloat16)
    inner = jnp.sum(jnp.where(here, inside.astype(jnp.float32), 0.0), axis=1, keepdims=True)
    inner = jnp.broadcast_to(inner, (replicas * CAP, LANES)).astype(jnp.bfloat16)
    width = a_ref.shape[1]
    for r, sent_ref in enumerate(sent_refs):
        sent_ref[:, pl.ds(0, width)] = rows[r * CAP : (r + 1) * CAP, :]
        sent_ref[:, pl.ds(width, LANES)] = inner[r * CAP : (r + 1) * CAP, :]


def route(attended, request_adapter, placement, replicas, slots, after=()):
    requests, width = attended.shape
    return pl.pallas_call(
        functools.partial(route_kernel, replicas, slots, len(after)),
        in_specs=[VMEM] * 3 + [ANY] * len(after),
        out_specs=[VMEM] * (1 + replicas),
        out_shape=[jax.ShapeDtypeStruct((replicas * CAP, requests), jnp.bfloat16)]
        + [jax.ShapeDtypeStruct((CAP, width + LANES), jnp.bfloat16)] * replicas,
        compiler_params=PARAMS,
        cost_estimate=BRIEF,
        name="route",
    )(attended, request_adapter.reshape(1, -1), placement.reshape(1, -1), *after)


def down_kernel(replicas, after, *refs):
    received = refs[:replicas]
    down_ref = refs[replicas]
    mid_ref, inside_ref = refs[replicas + 1 + after :]
    slots, rank, width = down_ref.shape
    rows = jnp.concatenate([r[:, pl.ds(0, width)] for r in received], axis=0)
    inside = jnp.concatenate([r[:, pl.ds(width, LANES)] for r in received], axis=0)
    inside_ref[...] = inside
    projected = _dot(rows, down_ref[...].reshape(slots * rank, width), 1, 1)
    lane_slot = _iota(projected.shape, 1) // rank
    mine = lane_slot == inside[:, 0:1].astype(jnp.int32)
    projected = jnp.where(mine, projected, 0.0).astype(jnp.bfloat16)
    fold = _iota((slots * rank, LANES), 0) % rank == _iota((slots * rank, LANES), 1)
    mid_ref[...] = _dot(projected, fold.astype(jnp.bfloat16)).astype(jnp.bfloat16)


def down(received, slot_down_weight, after=()):
    replicas = len(received)
    rows = replicas * CAP
    return pl.pallas_call(
        functools.partial(down_kernel, replicas, len(after)),
        in_specs=[VMEM] * (replicas + 1) + [ANY] * len(after),
        out_specs=[VMEM, VMEM],
        out_shape=[jax.ShapeDtypeStruct((rows, LANES), jnp.bfloat16)] * 2,
        compiler_params=PARAMS,
        cost_estimate=BRIEF,
        name="down",
    )(*received, slot_down_weight, *after)


def up_kernel(parts, after, *refs):
    mids = refs[:parts]
    inside_ref, up_ref = refs[parts : parts + 2]
    out_refs = refs[parts + 2 + after :]
    slots, rank, width = up_ref.shape
    mid = mids[0][...].astype(jnp.float32)
    for m in mids[1:]:
        mid = mid + m[...].astype(jnp.float32)
    spread = _iota((LANES, slots * rank), 1) % rank == _iota((LANES, slots * rank), 0)
    wide = _dot(mid.astype(jnp.bfloat16), spread.astype(jnp.bfloat16))
    mine = _iota(wide.shape, 1) // rank == inside_ref[:, 0:1].astype(jnp.int32)
    wide = jnp.where(mine, wide, 0.0).astype(jnp.bfloat16)
    delta = _dot(wide, up_ref[...].reshape(slots * rank, width)).astype(jnp.bfloat16)
    for r, out_ref in enumerate(out_refs):
        out_ref[...] = delta[r * CAP : (r + 1) * CAP, :]


def up(mids, inside, slot_up_weight, after=()):
    rows = inside.shape[0]
    replicas = rows // CAP
    width = slot_up_weight.shape[2]
    return pl.pallas_call(
        functools.partial(up_kernel, len(mids), len(after)),
        in_specs=[VMEM] * (len(mids) + 2) + [ANY] * len(after),
        out_specs=[VMEM] * replicas,
        out_shape=[jax.ShapeDtypeStruct((CAP, width), jnp.bfloat16)] * replicas,
        compiler_params=PARAMS,
        cost_estimate=BRIEF,
        name="up",
    )(*mids, inside, slot_up_weight, *after)


def settle_kernel(step, replicas, after, *refs):
    returned = refs[:replicas]
    chosen_ref, a_ref, residual_ref, w_hbm = refs[replicas : replicas + 4]
    out_ref, held, sems = refs[replicas + 4 + after :]
    width = out_ref.shape[1]
    weights = Weights(w_hbm, held, sems, column_owner(step) * width, width)
    weights.start()
    rows = jnp.concatenate([r[...] for r in returned], axis=0)
    delta = _dot(chosen_ref[...], rows, 0, 0)
    for columns, product in weights.products(a_ref[...]):
        own = residual_ref[:, columns].astype(jnp.float32) + product
        out_ref[:, columns] = own + delta[:, columns.start : columns.start + columns.size]


def settle(step, returned, chosen, attended, residual, weight, after=()):
    replicas = len(returned)
    return pl.pallas_call(
        functools.partial(settle_kernel, step, replicas, len(after)),
        in_specs=[VMEM] * (replicas + 3) + [ANY] + [ANY] * len(after),
        out_specs=VMEM,
        out_shape=jax.ShapeDtypeStruct(residual.shape, jnp.float32),
        scratch_shapes=Weights.scratch(weight.shape[0], residual.shape[1]),
        compiler_params=PARAMS,
        cost_estimate=BRIEF,
        name="settle",
    )(*returned, chosen, attended, residual, weight, *after)


def finish_kernel(arrived_ref, settled_ref, *refs):
    refs[-1][...] = (settled_ref[...] + arrived_ref[...].astype(jnp.float32)).astype(jnp.bfloat16)


def finish(chain, arrived, settled, earlier):
    rows, chunk = arrived.shape
    piece = min(PIECE, chunk)
    count = chunk // piece
    operands = [arrived, settled] + ([earlier] if earlier is not None else [])
    return pl.pallas_call(
        finish_kernel,
        grid=(count,),
        in_specs=[
            pl.BlockSpec((rows, piece), lambda i: (0, i)),
            pl.BlockSpec((rows, piece), lambda i: (0, chain * count + i)),
        ]
        + ([ANY] if earlier is not None else []),
        out_specs=pl.BlockSpec((rows, piece), lambda i: (0, chain * count + i)),
        out_shape=jax.ShapeDtypeStruct(settled.shape, jnp.bfloat16),
        input_output_aliases={2: 0} if earlier is not None else {},
        compiler_params=PARAMS,
        cost_estimate=BRIEF,
        name="finish",
    )(*operands)


def per_device(
    residual,
    query,
    cached_key_rows,
    cached_value_rows,
    new_token_key,
    new_token_value,
    lengths,
    output_weight,
    slot_down_weight,
    slot_up_weight,
    placement,
    request_adapter,
):
    count = lax.axis_size("tensor")
    replicas = lax.axis_size("dp")
    chunk = residual.shape[1] // CHAINS
    order = ring_order(count)
    ring = [(order[p], order[(p + 1) % count]) for p in range(count)]

    def forward(x):
        return lax.ppermute(x, "tensor", ring)

    def exchange(blocks):
        moved = [
            lax.ppermute(blocks[r], "dp", [(i, i ^ r) for i in range(replicas)])
            for r in range(1, replicas)
        ]
        return [blocks[0]] + moved

    attended, first = attend(
        query, cached_key_rows, cached_value_rows, new_token_key, new_token_value, lengths,
        output_weight, chunk,
    )
    travelling = [first] + [
        hop(0, c, None, attended, output_weight, chunk) for c in range(1, CHAINS)
    ]
    chosen, *leaving = route(
        attended, request_adapter, placement, replicas, slot_down_weight.shape[0],
        after=travelling[1:],
    )
    rows_here = exchange(leaving)

    def take_hop(step, c, after):
        arrived = forward(travelling[c])
        travelling[c] = hop(step, c, arrived, attended, output_weight, chunk, after=after)

    rank_sums = deltas = returned = None
    for step in range(1, count - 1):
        for c in range(CHAINS):
            if step == 1 and c == 0:
                take_hop(step, c, rows_here)
                mid, inside = down(rows_here, slot_down_weight, after=[travelling[c]])
                rank_sums = [mid] + [
                    lax.ppermute(mid, "tensor", [(i, (i + k) % count) for i in range(count)])
                    for k in range(1, count)
                ]
            elif step == 1 and c == 1:
                take_hop(step, c, rank_sums)
                deltas = up(rank_sums, inside, slot_up_weight, after=[travelling[c]])
                returned = exchange(deltas)
            elif step == count - 2 and c == CHAINS - 1:
                take_hop(step, c, returned)
            else:
                take_hop(step, c, [deltas[0]])
    settled = settle(
        count - 1, returned, chosen, attended, residual, output_weight, after=[travelling[-1]]
    )
    out = None
    for c in range(CHAINS):
        out = finish(c, forward(travelling[c]), settled, out)
    return out


def solution(mesh):
    placed = (
        P(("parts", "dp"), "tensor"),
        P(("parts", "dp"), "tensor", None),
        P(("parts", "dp"), None, "tensor", None),
        P(("parts", "dp"), None, "tensor", None),
        P(("parts", "dp"), "tensor", None),
        P(("parts", "dp"), "tensor", None),
        P(("parts", "dp")),
        P("tensor", None),
        P("dp", None, "tensor"),
        P("dp", None, "tensor"),
        P("parts"),
        P(("parts", "dp")),
    )
    return jax.shard_map(
        per_device,
        mesh=mesh,
        in_specs=placed,
        out_specs=P(("parts", "dp"), "tensor"),
        check_vma=False,
    )
```

```python
import functools
import math

import jax
import jax.numpy as jnp
from jax import lax
from jax.experimental import pallas as pl
from jax.experimental.pallas import tpu as pltpu
from jax.sharding import PartitionSpec as P

GROUP = 8
CAP = 64
LANES = 128
MASKED = -1e30
VMEM_LIMIT = 50 * 1024 * 1024
FULL_VMEM = 61 * 1024 * 1024
CHAINS = 2
PIECE = 512
SPLIT = 2

VMEM = pl.BlockSpec(memory_space=pltpu.VMEM)
ANY = pl.BlockSpec(memory_space=pl.ANY)
BRIEF = pl.CostEstimate(flops=1, transcendentals=0, bytes_accessed=1)
PARAMS = pltpu.CompilerParams(vmem_limit_bytes=VMEM_LIMIT)


def _dot(a, b, left=1, right=0):
    return lax.dot_general(
        a, b, (((left,), (right,)), ((), ())), preferred_element_type=jnp.float32
    )


def _iota(shape, axis):
    return lax.broadcasted_iota(jnp.int32, shape, axis)


def ring_order(count):
    return list(range(0, count, 2)) + list(range(1, count, 2))[::-1]


def column_owner(step):
    count = lax.axis_size("tensor")
    here = lax.axis_index("tensor")
    half = here // 2
    spot = jnp.where(here % 2 == 0, half, count - 1 - half)
    spot = lax.rem(spot - 1 - step + 2 * count, count)
    return jnp.where(2 * spot < count, 2 * spot, 2 * (count - spot) - 1)


class Weights:
    def __init__(self, w_ref, held, sems, first, width):
        depth = w_ref.shape[0] // SPLIT
        self.piece = min(PIECE, width)
        self.held = held
        self.copies = []
        for p in range(width // self.piece):
            at = pl.multiple_of(first + p * self.piece, self.piece)
            self.copies.append(
                [
                    pltpu.make_async_copy(
                        w_ref.at[pl.ds(s * depth, depth), pl.ds(at, self.piece)],
                        held.at[p, pl.ds(s * depth, depth), :],
                        sems.at[p, s],
                    )
                    for s in range(SPLIT)
                ]
            )

    def start(self):
        for piece in self.copies:
            for copy in piece:
                copy.start()

    def products(self, a):
        for p, piece in enumerate(self.copies):
            for copy in piece:
                copy.wait()
            yield pl.ds(p * self.piece, self.piece), _dot(a, self.held[p])

    @staticmethod
    def scratch(depth, width):
        piece = min(PIECE, width)
        count = width // piece
        return [
            pltpu.VMEM((count, depth, piece), jnp.bfloat16),
            pltpu.SemaphoreType.DMA((count, SPLIT)),
        ]


def attend_kernel(
    heads, kv, cache, steps,
    len_ref, q_hbm, k_hbm, v_hbm, nk_hbm, nv_hbm, w_hbm,
    a_ref, out_ref,
    q_ref, k_ref, v_ref, nk_ref, nv_ref, scores_ref, mixed_ref, sems, fresh_sems, w_held, w_sems,
):
    requests = len_ref.shape[1]
    width = q_hbm.shape[1]
    per = requests // steps
    groups = per // GROUP
    group_rows = GROUP * heads
    group_cols = GROUP * cache * kv
    per_kv = heads // kv
    scale = 1.0 / math.sqrt(width)

    def part(kind, step):
        source, target, count = (
            (q_hbm, q_ref, heads),
            (k_hbm, k_ref, cache * kv),
            (v_hbm, v_ref, cache * kv),
        )[kind]
        rows = pl.ds(step * per * count, per * count)
        return pltpu.make_async_copy(source.at[rows, :], target.at[rows, :], sems.at[kind, step])

    fresh = [
        pltpu.make_async_copy(source, target, fresh_sems.at[i])
        for i, (source, target) in enumerate(((nk_hbm, nk_ref), (nv_hbm, nv_ref)))
    ]
    chunk = out_ref.shape[1]
    first = column_owner(0) * (CHAINS * chunk)
    weights = Weights(w_hbm, w_held, w_sems, first, chunk)
    part(0, 0).start()
    part(1, 0).start()
    fresh[0].start()
    part(2, 0).start()
    fresh[1].start()
    for step in range(1, steps):
        for kind in range(3):
            part(kind, step).start()
    weights.start()

    row = _iota((group_rows, group_cols), 0)
    col = _iota((group_rows, group_cols), 1)
    same = (row // heads == col // (cache * kv)) & ((row % heads) // per_kv == col % kv)
    own_bias = jnp.where(same, 0.0, MASKED)
    row = _iota((group_rows, per * kv), 0)
    col = _iota((group_rows, per * kv), 1)
    fresh_kv = (row % heads) // per_kv == col % kv
    fresh_distance = col // kv - row // heads

    counts = len_ref[...].astype(jnp.float32)
    all_groups = requests // GROUP
    of_group = _iota((all_groups, requests), 1) // GROUP == _iota((all_groups, requests), 0)
    counts = jnp.where(of_group, counts, 0.0).astype(jnp.bfloat16)
    spread = _iota((requests, group_cols), 0) % GROUP == _iota((requests, group_cols), 1) // (cache * kv)
    counts = _dot(counts, spread.astype(jnp.bfloat16))
    position = (_iota((all_groups, group_cols), 1) // kv) % cache
    length_bias = jnp.where(position.astype(jnp.float32) < counts, 0.0, MASKED)

    for step in range(steps):
        side = step % 2
        part(0, step).wait()
        part(1, step).wait()
        if step == 0:
            fresh[0].wait()
        q_at = step * per * heads
        k_at = step * per * cache * kv
        f_at = step * per * kv
        for g in range(groups):
            rows = pl.ds(g * group_rows, group_rows)
            scores_ref[side, rows, pl.ds(0, group_cols)] = _dot(
                q_ref[pl.ds(q_at + g * group_rows, group_rows), :],
                k_ref[pl.ds(k_at + g * group_cols, group_cols), :],
                1,
                1,
            )
        scores_ref[side, :, pl.ds(group_cols, per * kv)] = _dot(
            q_ref[pl.ds(q_at, per * heads), :], nk_ref[pl.ds(f_at, per * kv), :], 1, 1
        )
        part(2, step).wait()
        if step == 0:
            fresh[1].wait()
        inverses = []
        weights_cached = []
        weights_fresh = []
        for g in range(groups):
            rows = pl.ds(g * group_rows, group_rows)
            bias = own_bias + length_bias[step * groups + g : step * groups + g + 1, :]
            cached = scores_ref[side, rows, pl.ds(0, group_cols)] * scale + bias
            new = scores_ref[side, rows, pl.ds(group_cols, per * kv)] * scale
            new = jnp.where(fresh_kv & (fresh_distance == g * GROUP), new, MASKED)
            top = jnp.maximum(
                jnp.max(cached, axis=1, keepdims=True), jnp.max(new, axis=1, keepdims=True)
            )
            cached = jnp.exp(cached - top)
            new = jnp.exp(new - top)
            total = jnp.sum(cached, axis=1, keepdims=True) + jnp.sum(new, axis=1, keepdims=True)
            inverse = 1.0 / total
            weights_cached.append((cached * inverse).astype(jnp.bfloat16))
            weights_fresh.append((new * inverse).astype(jnp.bfloat16))
        new = _dot(jnp.concatenate(weights_fresh, axis=0), nv_ref[pl.ds(f_at, per * kv), :])
        for g in range(groups):
            rows = slice(g * group_rows, (g + 1) * group_rows)
            mixed_ref[side, rows, :] = new[rows, :] + _dot(
                weights_cached[g], v_ref[pl.ds(k_at + g * group_cols, group_cols), :]
            )
        for h in range(heads):
            a_ref[pl.ds(step * per, per), pl.ds(h * width, width)] = mixed_ref[
                side, pl.ds(h, per, stride=heads), :
            ].astype(jnp.bfloat16)

    for columns, product in weights.products(a_ref[...]):
        out_ref[:, columns] = product.astype(jnp.bfloat16)


def attend(query, keys, values, new_key, new_value, lengths, weight, chunk):
    requests, heads, width = query.shape
    cache, kv = keys.shape[1], keys.shape[2]
    steps = 4
    per = requests // steps
    columns = GROUP * cache * kv + per * kv
    return pl.pallas_call(
        functools.partial(attend_kernel, heads, kv, cache, steps),
        in_specs=[VMEM] + [ANY] * 6,
        out_specs=[VMEM, VMEM],
        out_shape=[
            jax.ShapeDtypeStruct((requests, heads * width), jnp.bfloat16),
            jax.ShapeDtypeStruct((requests, chunk), jnp.bfloat16),
        ],
        scratch_shapes=[
            pltpu.VMEM((requests * heads, width), jnp.bfloat16),
            pltpu.VMEM((requests * cache * kv, width), jnp.bfloat16),
            pltpu.VMEM((requests * cache * kv, width), jnp.bfloat16),
            pltpu.VMEM((requests * kv, width), jnp.bfloat16),
            pltpu.VMEM((requests * kv, width), jnp.bfloat16),
            pltpu.VMEM((2, per * heads, columns), jnp.float32),
            pltpu.VMEM((2, per * heads, width), jnp.float32),
            pltpu.SemaphoreType.DMA((3, steps)),
            pltpu.SemaphoreType.DMA((2,)),
        ]
        + Weights.scratch(weight.shape[0], chunk),
        compiler_params=pltpu.CompilerParams(vmem_limit_bytes=FULL_VMEM),
        name="attend",
    )(
        lengths.reshape(1, requests),
        query.reshape(requests * heads, width),
        keys.reshape(requests * cache * kv, width),
        values.reshape(requests * cache * kv, width),
        new_key.reshape(requests * kv, width),
        new_value.reshape(requests * kv, width),
        weight,
    )


def hop_kernel(step, chain, arriving, after, *refs):
    if arriving:
        arrived_ref, *refs = refs
    a_ref, w_hbm, *refs = refs
    out_ref, held, sems = refs[after:]
    chunk = out_ref.shape[1]
    first = column_owner(step) * (CHAINS * chunk) + chain * chunk
    weights = Weights(w_hbm, held, sems, first, chunk)
    weights.start()
    for columns, product in weights.products(a_ref[...]):
        if arriving:
            product = product + arrived_ref[:, columns].astype(jnp.float32)
        out_ref[:, columns] = product.astype(jnp.bfloat16)


def hop(step, chain, arrived, attended, weight, chunk, after=()):
    arriving = arrived is not None
    operands = ([arrived] if arriving else []) + [attended, weight, *after]
    return pl.pallas_call(
        functools.partial(hop_kernel, step, chain, arriving, len(after)),
        in_specs=[VMEM] * (1 + arriving) + [ANY] + [ANY] * len(after),
        out_specs=VMEM,
        out_shape=jax.ShapeDtypeStruct((attended.shape[0], chunk), jnp.bfloat16),
        scratch_shapes=Weights.scratch(weight.shape[0], chunk),
        compiler_params=PARAMS,
        cost_estimate=BRIEF,
        name="hop",
    )(*operands)


def route_kernel(replicas, slots, after, *refs):
    a_ref, adapter_ref, placement_ref, *refs = refs
    chosen_ref, *sent_refs = refs[after:]
    requests = adapter_ref.shape[1]
    table = placement_ref.shape[1]
    matches = _iota((table, requests), 0) == adapter_ref[...]
    placed = jnp.broadcast_to(placement_ref[...].astype(jnp.float32), (8, table))
    slot = _dot(placed.astype(jnp.bfloat16), matches.astype(jnp.bfloat16)).astype(jnp.int32)
    slot = slot[0:1, :]
    holder = (slot // slots) ^ lax.axis_index("dp")
    inside = slot % slots
    of_holder = _iota((max(replicas, 8), requests), 0) == holder
    earlier = _iota((requests, requests), 0) < _iota((requests, requests), 1)
    before = _dot(of_holder.astype(jnp.bfloat16), earlier.astype(jnp.bfloat16))
    before = jnp.sum(jnp.where(of_holder, before, 0.0), axis=0, keepdims=True).astype(jnp.int32)
    target = holder * CAP + before
    here = _iota((replicas * CAP, requests), 0) == target
    chosen = here.astype(jnp.bfloat16)
    chosen_ref[...] = chosen
    rows = _dot(chosen, a_ref[...]).astype(jnp.bfloat16)
    inner = jnp.sum(jnp.where(here, inside.astype(jnp.float32), 0.0), axis=1, keepdims=True)
    inner = jnp.broadcast_to(inner, (replicas * CAP, LANES)).astype(jnp.bfloat16)
    width = a_ref.shape[1]
    for r, sent_ref in enumerate(sent_refs):
        sent_ref[:, pl.ds(0, width)] = rows[r * CAP : (r + 1) * CAP, :]
        sent_ref[:, pl.ds(width, LANES)] = inner[r * CAP : (r + 1) * CAP, :]


def route(attended, request_adapter, placement, replicas, slots, after=()):
    requests, width = attended.shape
    return pl.pallas_call(
        functools.partial(route_kernel, replicas, slots, len(after)),
        in_specs=[VMEM] * 3 + [ANY] * len(after),
        out_specs=[VMEM] * (1 + replicas),
        out_shape=[jax.ShapeDtypeStruct((replicas * CAP, requests), jnp.bfloat16)]
        + [jax.ShapeDtypeStruct((CAP, width + LANES), jnp.bfloat16)] * replicas,
        compiler_params=PARAMS,
        cost_estimate=BRIEF,
        name="route",
    )(attended, request_adapter.reshape(1, -1), placement.reshape(1, -1), *after)


def down_kernel(replicas, after, *refs):
    received = refs[:replicas]
    down_ref = refs[replicas]
    mid_ref, inside_ref = refs[replicas + 1 + after :]
    slots, rank, width = down_ref.shape
    rows = jnp.concatenate([r[:, pl.ds(0, width)] for r in received], axis=0)
    inside = jnp.concatenate([r[:, pl.ds(width, LANES)] for r in received], axis=0)
    inside_ref[...] = inside
    projected = _dot(rows, down_ref[...].reshape(slots * rank, width), 1, 1)
    lane_slot = _iota(projected.shape, 1) // rank
    mine = lane_slot == inside[:, 0:1].astype(jnp.int32)
    projected = jnp.where(mine, projected, 0.0).astype(jnp.bfloat16)
    beside = LANES // rank
    some = projected.shape[0] // beside
    packed = 0.0
    for b in range(beside):
        lane = _iota((slots * rank, LANES), 1) - b * rank
        fold = _iota((slots * rank, LANES), 0) % rank == lane
        packed = packed + _dot(projected[b * some : (b + 1) * some, :], fold.astype(jnp.bfloat16))
    mid_ref[...] = packed.astype(jnp.bfloat16)


def down(received, slot_down_weight, after=()):
    replicas = len(received)
    rows = replicas * CAP
    return pl.pallas_call(
        functools.partial(down_kernel, replicas, len(after)),
        in_specs=[VMEM] * (replicas + 1) + [ANY] * len(after),
        out_specs=[VMEM, VMEM],
        out_shape=[
            jax.ShapeDtypeStruct((rows * slot_down_weight.shape[1] // LANES, LANES), jnp.bfloat16),
            jax.ShapeDtypeStruct((rows, LANES), jnp.bfloat16),
        ],
        compiler_params=PARAMS,
        cost_estimate=BRIEF,
        name="down",
    )(*received, slot_down_weight, *after)


def up_kernel(parts, after, *refs):
    mids = refs[:parts]
    inside_ref, up_ref = refs[parts : parts + 2]
    out_refs = refs[parts + 2 + after :]
    slots, rank, width = up_ref.shape
    mid = mids[0][...].astype(jnp.float32)
    for m in mids[1:]:
        mid = mid + m[...].astype(jnp.float32)
    mid = mid.astype(jnp.bfloat16)
    wide = []
    for b in range(LANES // rank):
        lane = _iota((LANES, slots * rank), 0) - b * rank
        spread = _iota((LANES, slots * rank), 1) % rank == lane
        wide.append(_dot(mid, spread.astype(jnp.bfloat16)))
    wide = jnp.concatenate(wide, axis=0)
    mine = _iota(wide.shape, 1) // rank == inside_ref[:, 0:1].astype(jnp.int32)
    wide = jnp.where(mine, wide, 0.0).astype(jnp.bfloat16)
    delta = _dot(wide, up_ref[...].reshape(slots * rank, width)).astype(jnp.bfloat16)
    for r, out_ref in enumerate(out_refs):
        out_ref[...] = delta[r * CAP : (r + 1) * CAP, :]


def up(mids, inside, slot_up_weight, after=()):
    rows = inside.shape[0]
    replicas = rows // CAP
    width = slot_up_weight.shape[2]
    return pl.pallas_call(
        functools.partial(up_kernel, len(mids), len(after)),
        in_specs=[VMEM] * (len(mids) + 2) + [ANY] * len(after),
        out_specs=[VMEM] * replicas,
        out_shape=[jax.ShapeDtypeStruct((CAP, width), jnp.bfloat16)] * replicas,
        compiler_params=PARAMS,
        cost_estimate=BRIEF,
        name="up",
    )(*mids, inside, slot_up_weight, *after)


def settle_kernel(step, replicas, after, *refs):
    returned = refs[:replicas]
    chosen_ref, a_ref, residual_ref, w_hbm = refs[replicas : replicas + 4]
    out_ref, held, sems = refs[replicas + 4 + after :]
    width = out_ref.shape[1]
    weights = Weights(w_hbm, held, sems, column_owner(step) * width, width)
    weights.start()
    rows = jnp.concatenate([r[...] for r in returned], axis=0)
    delta = _dot(chosen_ref[...], rows, 0, 0)
    for columns, product in weights.products(a_ref[...]):
        own = residual_ref[:, columns].astype(jnp.float32) + product
        out_ref[:, columns] = own + delta[:, columns.start : columns.start + columns.size]


def settle(step, returned, chosen, attended, residual, weight, after=()):
    replicas = len(returned)
    return pl.pallas_call(
        functools.partial(settle_kernel, step, replicas, len(after)),
        in_specs=[VMEM] * (replicas + 3) + [ANY] + [ANY] * len(after),
        out_specs=VMEM,
        out_shape=jax.ShapeDtypeStruct(residual.shape, jnp.float32),
        scratch_shapes=Weights.scratch(weight.shape[0], residual.shape[1]),
        compiler_params=PARAMS,
        cost_estimate=BRIEF,
        name="settle",
    )(*returned, chosen, attended, residual, weight, *after)


def finish_kernel(arrived_ref, settled_ref, *refs):
    refs[-1][...] = (settled_ref[...] + arrived_ref[...].astype(jnp.float32)).astype(jnp.bfloat16)


def finish(chain, arrived, settled, earlier):
    rows, chunk = arrived.shape
    piece = min(PIECE, chunk)
    count = chunk // piece
    operands = [arrived, settled] + ([earlier] if earlier is not None else [])
    return pl.pallas_call(
        finish_kernel,
        grid=(count,),
        in_specs=[
            pl.BlockSpec((rows, piece), lambda i: (0, i)),
            pl.BlockSpec((rows, piece), lambda i: (0, chain * count + i)),
        ]
        + ([ANY] if earlier is not None else []),
        out_specs=pl.BlockSpec((rows, piece), lambda i: (0, chain * count + i)),
        out_shape=jax.ShapeDtypeStruct(settled.shape, jnp.bfloat16),
        input_output_aliases={2: 0} if earlier is not None else {},
        compiler_params=PARAMS,
        cost_estimate=BRIEF,
        name="finish",
    )(*operands)


def per_device(
    residual,
    query,
    cached_key_rows,
    cached_value_rows,
    new_token_key,
    new_token_value,
    lengths,
    output_weight,
    slot_down_weight,
    slot_up_weight,
    placement,
    request_adapter,
):
    count = lax.axis_size("tensor")
    replicas = lax.axis_size("dp")
    chunk = residual.shape[1] // CHAINS
    order = ring_order(count)
    ring = [(order[p], order[(p + 1) % count]) for p in range(count)]

    def forward(x):
        return lax.ppermute(x, "tensor", ring)

    def exchange(blocks):
        moved = [
            lax.ppermute(blocks[r], "dp", [(i, i ^ r) for i in range(replicas)])
            for r in range(1, replicas)
        ]
        return [blocks[0]] + moved

    attended, first = attend(
        query, cached_key_rows, cached_value_rows, new_token_key, new_token_value, lengths,
        output_weight, chunk,
    )
    travelling = [first] + [
        hop(0, c, None, attended, output_weight, chunk) for c in range(1, CHAINS)
    ]
    chosen, *leaving = route(
        attended, request_adapter, placement, replicas, slot_down_weight.shape[0],
        after=travelling[1:],
    )
    rows_here = exchange(leaving)

    def take_hop(step, c, after):
        arrived = forward(travelling[c])
        travelling[c] = hop(step, c, arrived, attended, output_weight, chunk, after=after)

    rank_sums = deltas = returned = None
    for step in range(1, count - 1):
        for c in range(CHAINS):
            if step == 1 and c == 0:
                take_hop(step, c, rows_here)
                mid, inside = down(rows_here, slot_down_weight, after=[travelling[c]])
                rank_sums = [mid] + [
                    lax.ppermute(mid, "tensor", [(i, (i + k) % count) for i in range(count)])
                    for k in range(1, count)
                ]
            elif step == 1:
                take_hop(step, c, [mid])
            elif step == 2 and c == 0:
                take_hop(step, c, [])
                deltas = up(rank_sums, inside, slot_up_weight, after=[travelling[c]])
                returned = exchange(deltas)
            else:
                take_hop(step, c, [deltas[0]])
    settled = settle(
        count - 1, returned, chosen, attended, residual, output_weight, after=[travelling[-1]]
    )
    out = None
    for c in range(CHAINS):
        out = finish(c, forward(travelling[c]), settled, out)
    return out


def solution(mesh):
    placed = (
        P(("parts", "dp"), "tensor"),
        P(("parts", "dp"), "tensor", None),
        P(("parts", "dp"), None, "tensor", None),
        P(("parts", "dp"), None, "tensor", None),
        P(("parts", "dp"), "tensor", None),
        P(("parts", "dp"), "tensor", None),
        P(("parts", "dp")),
        P("tensor", None),
        P("dp", None, "tensor"),
        P("dp", None, "tensor"),
        P("parts"),
        P(("parts", "dp")),
    )
    return jax.shard_map(
        per_device,
        mesh=mesh,
        in_specs=placed,
        out_specs=P(("parts", "dp"), "tensor"),
        check_vma=False,
    )
```

```python
import functools
import math

import jax
import jax.numpy as jnp
from jax import lax
from jax.experimental import pallas as pl
from jax.experimental.pallas import tpu as pltpu
from jax.sharding import PartitionSpec as P

GROUP = 8
CAP = 64
LANES = 128
MASKED = -1e30
VMEM_LIMIT = 50 * 1024 * 1024
FULL_VMEM = 61 * 1024 * 1024
SHARES = (5, 3)
PIECE = 256
SPLIT = 2

VMEM = pl.BlockSpec(memory_space=pltpu.VMEM)
ANY = pl.BlockSpec(memory_space=pl.ANY)
BRIEF = pl.CostEstimate(flops=1, transcendentals=0, bytes_accessed=1)
PARAMS = pltpu.CompilerParams(vmem_limit_bytes=VMEM_LIMIT)


def _dot(a, b, left=1, right=0):
    return lax.dot_general(
        a, b, (((left,), (right,)), ((), ())), preferred_element_type=jnp.float32
    )


def _iota(shape, axis):
    return lax.broadcasted_iota(jnp.int32, shape, axis)


def ring_order(count):
    return list(range(0, count, 2)) + list(range(1, count, 2))[::-1]


def column_owner(step):
    count = lax.axis_size("tensor")
    here = lax.axis_index("tensor")
    half = here // 2
    spot = jnp.where(here % 2 == 0, half, count - 1 - half)
    spot = lax.rem(spot - 1 - step + 2 * count, count)
    return jnp.where(2 * spot < count, 2 * spot, 2 * (count - spot) - 1)


def chain_columns(width):
    unit = width // sum(SHARES)
    return [(sum(SHARES[:c]) * unit, SHARES[c] * unit) for c in range(len(SHARES))]


def piece_of(width):
    return math.gcd(width, PIECE)


class Weights:
    def __init__(self, w_ref, held, sems, first, width):
        depth = w_ref.shape[0] // SPLIT
        self.piece = piece_of(width)
        self.held = held
        self.copies = []
        for p in range(width // self.piece):
            at = pl.multiple_of(first + p * self.piece, self.piece)
            self.copies.append(
                [
                    pltpu.make_async_copy(
                        w_ref.at[pl.ds(s * depth, depth), pl.ds(at, self.piece)],
                        held.at[p, pl.ds(s * depth, depth), :],
                        sems.at[p, s],
                    )
                    for s in range(SPLIT)
                ]
            )

    def start(self):
        for piece in self.copies:
            for copy in piece:
                copy.start()

    def products(self, a):
        for p, piece in enumerate(self.copies):
            for copy in piece:
                copy.wait()
            yield pl.ds(p * self.piece, self.piece), _dot(a, self.held[p])

    @staticmethod
    def scratch(depth, width):
        piece = piece_of(width)
        count = width // piece
        return [
            pltpu.VMEM((count, depth, piece), jnp.bfloat16),
            pltpu.SemaphoreType.DMA((count, SPLIT)),
        ]


def attend_kernel(
    heads, kv, cache, steps, block,
    len_ref, q_hbm, k_hbm, v_hbm, nk_hbm, nv_hbm, w_hbm,
    a_ref, out_ref,
    q_ref, k_ref, v_ref, nk_ref, nv_ref, scores_ref, mixed_ref, sems, fresh_sems, w_held, w_sems,
):
    requests = len_ref.shape[1]
    width = q_hbm.shape[1]
    per = requests // steps
    groups = per // GROUP
    group_rows = GROUP * heads
    group_cols = GROUP * cache * kv
    per_kv = heads // kv
    scale = 1.0 / math.sqrt(width)

    def part(kind, step):
        source, target, count = (
            (q_hbm, q_ref, heads),
            (k_hbm, k_ref, cache * kv),
            (v_hbm, v_ref, cache * kv),
        )[kind]
        rows = pl.ds(step * per * count, per * count)
        return pltpu.make_async_copy(source.at[rows, :], target.at[rows, :], sems.at[kind, step])

    fresh = [
        pltpu.make_async_copy(source, target, fresh_sems.at[i])
        for i, (source, target) in enumerate(((nk_hbm, nk_ref), (nv_hbm, nv_ref)))
    ]
    chunk = out_ref.shape[1]
    first = column_owner(0) * block
    weights = Weights(w_hbm, w_held, w_sems, first, chunk)
    part(0, 0).start()
    part(1, 0).start()
    fresh[0].start()
    part(2, 0).start()
    fresh[1].start()
    for step in range(1, steps):
        for kind in range(3):
            part(kind, step).start()
    weights.start()

    row = _iota((group_rows, group_cols), 0)
    col = _iota((group_rows, group_cols), 1)
    same = (row // heads == col // (cache * kv)) & ((row % heads) // per_kv == col % kv)
    own_bias = jnp.where(same, 0.0, MASKED)
    row = _iota((group_rows, per * kv), 0)
    col = _iota((group_rows, per * kv), 1)
    fresh_kv = (row % heads) // per_kv == col % kv
    fresh_distance = col // kv - row // heads

    counts = len_ref[...].astype(jnp.float32)
    all_groups = requests // GROUP
    of_group = _iota((all_groups, requests), 1) // GROUP == _iota((all_groups, requests), 0)
    counts = jnp.where(of_group, counts, 0.0).astype(jnp.bfloat16)
    spread = _iota((requests, group_cols), 0) % GROUP == _iota((requests, group_cols), 1) // (cache * kv)
    counts = _dot(counts, spread.astype(jnp.bfloat16))
    position = (_iota((all_groups, group_cols), 1) // kv) % cache
    length_bias = jnp.where(position.astype(jnp.float32) < counts, 0.0, MASKED)

    for step in range(steps):
        side = step % 2
        part(0, step).wait()
        part(1, step).wait()
        if step == 0:
            fresh[0].wait()
        q_at = step * per * heads
        k_at = step * per * cache * kv
        f_at = step * per * kv
        for g in range(groups):
            rows = pl.ds(g * group_rows, group_rows)
            scores_ref[side, rows, pl.ds(0, group_cols)] = _dot(
                q_ref[pl.ds(q_at + g * group_rows, group_rows), :],
                k_ref[pl.ds(k_at + g * group_cols, group_cols), :],
                1,
                1,
            )
        scores_ref[side, :, pl.ds(group_cols, per * kv)] = _dot(
            q_ref[pl.ds(q_at, per * heads), :], nk_ref[pl.ds(f_at, per * kv), :], 1, 1
        )
        part(2, step).wait()
        if step == 0:
            fresh[1].wait()
        inverses = []
        weights_cached = []
        weights_fresh = []
        for g in range(groups):
            rows = pl.ds(g * group_rows, group_rows)
            bias = own_bias + length_bias[step * groups + g : step * groups + g + 1, :]
            cached = scores_ref[side, rows, pl.ds(0, group_cols)] * scale + bias
            new = scores_ref[side, rows, pl.ds(group_cols, per * kv)] * scale
            new = jnp.where(fresh_kv & (fresh_distance == g * GROUP), new, MASKED)
            top = jnp.maximum(
                jnp.max(cached, axis=1, keepdims=True), jnp.max(new, axis=1, keepdims=True)
            )
            cached = jnp.exp(cached - top)
            new = jnp.exp(new - top)
            total = jnp.sum(cached, axis=1, keepdims=True) + jnp.sum(new, axis=1, keepdims=True)
            inverse = 1.0 / total
            weights_cached.append((cached * inverse).astype(jnp.bfloat16))
            weights_fresh.append((new * inverse).astype(jnp.bfloat16))
        new = _dot(jnp.concatenate(weights_fresh, axis=0), nv_ref[pl.ds(f_at, per * kv), :])
        for g in range(groups):
            rows = slice(g * group_rows, (g + 1) * group_rows)
            mixed_ref[side, rows, :] = new[rows, :] + _dot(
                weights_cached[g], v_ref[pl.ds(k_at + g * group_cols, group_cols), :]
            )
        for h in range(heads):
            a_ref[pl.ds(step * per, per), pl.ds(h * width, width)] = mixed_ref[
                side, pl.ds(h, per, stride=heads), :
            ].astype(jnp.bfloat16)

    for columns, product in weights.products(a_ref[...]):
        out_ref[:, columns] = product.astype(jnp.bfloat16)


def attend(query, keys, values, new_key, new_value, lengths, weight, block):
    requests, heads, width = query.shape
    cache, kv = keys.shape[1], keys.shape[2]
    steps = 4
    per = requests // steps
    columns = GROUP * cache * kv + per * kv
    chunk = chain_columns(block)[0][1]
    return pl.pallas_call(
        functools.partial(attend_kernel, heads, kv, cache, steps, block),
        in_specs=[VMEM] + [ANY] * 6,
        out_specs=[VMEM, VMEM],
        out_shape=[
            jax.ShapeDtypeStruct((requests, heads * width), jnp.bfloat16),
            jax.ShapeDtypeStruct((requests, chunk), jnp.bfloat16),
        ],
        scratch_shapes=[
            pltpu.VMEM((requests * heads, width), jnp.bfloat16),
            pltpu.VMEM((requests * cache * kv, width), jnp.bfloat16),
            pltpu.VMEM((requests * cache * kv, width), jnp.bfloat16),
            pltpu.VMEM((requests * kv, width), jnp.bfloat16),
            pltpu.VMEM((requests * kv, width), jnp.bfloat16),
            pltpu.VMEM((2, per * heads, columns), jnp.float32),
            pltpu.VMEM((2, per * heads, width), jnp.float32),
            pltpu.SemaphoreType.DMA((3, steps)),
            pltpu.SemaphoreType.DMA((2,)),
        ]
        + Weights.scratch(weight.shape[0], chunk),
        compiler_params=pltpu.CompilerParams(vmem_limit_bytes=FULL_VMEM),
        name="attend",
    )(
        lengths.reshape(1, requests),
        query.reshape(requests * heads, width),
        keys.reshape(requests * cache * kv, width),
        values.reshape(requests * cache * kv, width),
        new_key.reshape(requests * kv, width),
        new_value.reshape(requests * kv, width),
        weight,
    )


def hop_kernel(step, block, start, arriving, after, *refs):
    if arriving:
        arrived_ref, *refs = refs
    a_ref, w_hbm, *refs = refs
    out_ref, held, sems = refs[after:]
    chunk = out_ref.shape[1]
    first = column_owner(step) * block + start
    weights = Weights(w_hbm, held, sems, first, chunk)
    weights.start()
    for columns, product in weights.products(a_ref[...]):
        if arriving:
            product = product + arrived_ref[:, columns].astype(jnp.float32)
        out_ref[:, columns] = product.astype(jnp.bfloat16)


def hop(step, chain, arrived, attended, weight, block, after=()):
    arriving = arrived is not None
    start, chunk = chain_columns(block)[chain]
    operands = ([arrived] if arriving else []) + [attended, weight, *after]
    return pl.pallas_call(
        functools.partial(hop_kernel, step, block, start, arriving, len(after)),
        in_specs=[VMEM] * (1 + arriving) + [ANY] + [ANY] * len(after),
        out_specs=VMEM,
        out_shape=jax.ShapeDtypeStruct((attended.shape[0], chunk), jnp.bfloat16),
        scratch_shapes=Weights.scratch(weight.shape[0], chunk),
        compiler_params=PARAMS,
        cost_estimate=BRIEF,
        name="hop",
    )(*operands)


def route_kernel(replicas, slots, after, *refs):
    a_ref, adapter_ref, placement_ref, *refs = refs
    chosen_ref, *sent_refs = refs[after:]
    requests = adapter_ref.shape[1]
    table = placement_ref.shape[1]
    matches = _iota((table, requests), 0) == adapter_ref[...]
    placed = jnp.broadcast_to(placement_ref[...].astype(jnp.float32), (8, table))
    slot = _dot(placed.astype(jnp.bfloat16), matches.astype(jnp.bfloat16)).astype(jnp.int32)
    slot = slot[0:1, :]
    holder = (slot // slots) ^ lax.axis_index("dp")
    inside = slot % slots
    of_holder = _iota((max(replicas, 8), requests), 0) == holder
    earlier = _iota((requests, requests), 0) < _iota((requests, requests), 1)
    before = _dot(of_holder.astype(jnp.bfloat16), earlier.astype(jnp.bfloat16))
    before = jnp.sum(jnp.where(of_holder, before, 0.0), axis=0, keepdims=True).astype(jnp.int32)
    target = holder * CAP + before
    here = _iota((replicas * CAP, requests), 0) == target
    chosen = here.astype(jnp.bfloat16)
    chosen_ref[...] = chosen
    rows = _dot(chosen, a_ref[...]).astype(jnp.bfloat16)
    inner = jnp.sum(jnp.where(here, inside.astype(jnp.float32), 0.0), axis=1, keepdims=True)
    inner = jnp.broadcast_to(inner, (replicas * CAP, LANES)).astype(jnp.bfloat16)
    width = a_ref.shape[1]
    for r, sent_ref in enumerate(sent_refs):
        sent_ref[:, pl.ds(0, width)] = rows[r * CAP : (r + 1) * CAP, :]
        sent_ref[:, pl.ds(width, LANES)] = inner[r * CAP : (r + 1) * CAP, :]


def route(attended, request_adapter, placement, replicas, slots, after=()):
    requests, width = attended.shape
    return pl.pallas_call(
        functools.partial(route_kernel, replicas, slots, len(after)),
        in_specs=[VMEM] * 3 + [ANY] * len(after),
        out_specs=[VMEM] * (1 + replicas),
        out_shape=[jax.ShapeDtypeStruct((replicas * CAP, requests), jnp.bfloat16)]
        + [jax.ShapeDtypeStruct((CAP, width + LANES), jnp.bfloat16)] * replicas,
        compiler_params=PARAMS,
        cost_estimate=BRIEF,
        name="route",
    )(attended, request_adapter.reshape(1, -1), placement.reshape(1, -1), *after)


def down_kernel(replicas, after, *refs):
    received = refs[:replicas]
    down_ref = refs[replicas]
    mid_ref, inside_ref = refs[replicas + 1 + after :]
    slots, rank, width = down_ref.shape
    rows = jnp.concatenate([r[:, pl.ds(0, width)] for r in received], axis=0)
    inside = jnp.concatenate([r[:, pl.ds(width, LANES)] for r in received], axis=0)
    inside_ref[...] = inside
    projected = _dot(rows, down_ref[...].reshape(slots * rank, width), 1, 1)
    lane_slot = _iota(projected.shape, 1) // rank
    mine = lane_slot == inside[:, 0:1].astype(jnp.int32)
    projected = jnp.where(mine, projected, 0.0).astype(jnp.bfloat16)
    beside = LANES // rank
    some = projected.shape[0] // beside
    packed = 0.0
    for b in range(beside):
        lane = _iota((slots * rank, LANES), 1) - b * rank
        fold = _iota((slots * rank, LANES), 0) % rank == lane
        packed = packed + _dot(projected[b * some : (b + 1) * some, :], fold.astype(jnp.bfloat16))
    mid_ref[...] = packed.astype(jnp.bfloat16)


def down(received, slot_down_weight, after=()):
    replicas = len(received)
    rows = replicas * CAP
    return pl.pallas_call(
        functools.partial(down_kernel, replicas, len(after)),
        in_specs=[VMEM] * (replicas + 1) + [ANY] * len(after),
        out_specs=[VMEM, VMEM],
        out_shape=[
            jax.ShapeDtypeStruct((rows * slot_down_weight.shape[1] // LANES, LANES), jnp.bfloat16),
            jax.ShapeDtypeStruct((rows, LANES), jnp.bfloat16),
        ],
        compiler_params=PARAMS,
        cost_estimate=BRIEF,
        name="down",
    )(*received, slot_down_weight, *after)


def up_kernel(parts, after, *refs):
    mids = refs[:parts]
    inside_ref, up_ref = refs[parts : parts + 2]
    out_refs = refs[parts + 2 + after :]
    slots, rank, width = up_ref.shape
    mid = mids[0][...].astype(jnp.float32)
    for m in mids[1:]:
        mid = mid + m[...].astype(jnp.float32)
    mid = mid.astype(jnp.bfloat16)
    wide = []
    for b in range(LANES // rank):
        lane = _iota((LANES, slots * rank), 0) - b * rank
        spread = _iota((LANES, slots * rank), 1) % rank == lane
        wide.append(_dot(mid, spread.astype(jnp.bfloat16)))
    wide = jnp.concatenate(wide, axis=0)
    mine = _iota(wide.shape, 1) // rank == inside_ref[:, 0:1].astype(jnp.int32)
    wide = jnp.where(mine, wide, 0.0).astype(jnp.bfloat16)
    delta = _dot(wide, up_ref[...].reshape(slots * rank, width)).astype(jnp.bfloat16)
    for r, out_ref in enumerate(out_refs):
        out_ref[...] = delta[r * CAP : (r + 1) * CAP, :]


def up(mids, inside, slot_up_weight, after=()):
    rows = inside.shape[0]
    replicas = rows // CAP
    width = slot_up_weight.shape[2]
    return pl.pallas_call(
        functools.partial(up_kernel, len(mids), len(after)),
        in_specs=[VMEM] * (len(mids) + 2) + [ANY] * len(after),
        out_specs=[VMEM] * replicas,
        out_shape=[jax.ShapeDtypeStruct((CAP, width), jnp.bfloat16)] * replicas,
        compiler_params=PARAMS,
        cost_estimate=BRIEF,
        name="up",
    )(*mids, inside, slot_up_weight, *after)


def settle_kernel(step, replicas, after, *refs):
    returned = refs[:replicas]
    chosen_ref, a_ref, residual_ref, w_hbm = refs[replicas : replicas + 4]
    out_ref, held, sems = refs[replicas + 4 + after :]
    width = out_ref.shape[1]
    weights = Weights(w_hbm, held, sems, column_owner(step) * width, width)
    weights.start()
    rows = jnp.concatenate([r[...] for r in returned], axis=0)
    delta = _dot(chosen_ref[...], rows, 0, 0)
    for columns, product in weights.products(a_ref[...]):
        own = residual_ref[:, columns].astype(jnp.float32) + product
        out_ref[:, columns] = own + delta[:, columns.start : columns.start + columns.size]


def settle(step, returned, chosen, attended, residual, weight, after=()):
    replicas = len(returned)
    return pl.pallas_call(
        functools.partial(settle_kernel, step, replicas, len(after)),
        in_specs=[VMEM] * (replicas + 3) + [ANY] + [ANY] * len(after),
        out_specs=VMEM,
        out_shape=jax.ShapeDtypeStruct(residual.shape, jnp.float32),
        scratch_shapes=Weights.scratch(weight.shape[0], residual.shape[1]),
        compiler_params=PARAMS,
        cost_estimate=BRIEF,
        name="settle",
    )(*returned, chosen, attended, residual, weight, *after)


def finish_kernel(arrived_ref, settled_ref, *refs):
    refs[-1][...] = (settled_ref[...] + arrived_ref[...].astype(jnp.float32)).astype(jnp.bfloat16)


def finish(chain, arrived, settled, earlier):
    rows = arrived.shape[0]
    start, chunk = chain_columns(settled.shape[1])[chain]
    piece = math.gcd(start, chunk)
    first, count = start // piece, chunk // piece
    operands = [arrived, settled] + ([earlier] if earlier is not None else [])
    return pl.pallas_call(
        finish_kernel,
        grid=(count,),
        in_specs=[
            pl.BlockSpec((rows, piece), lambda i: (0, i)),
            pl.BlockSpec((rows, piece), lambda i: (0, first + i)),
        ]
        + ([ANY] if earlier is not None else []),
        out_specs=pl.BlockSpec((rows, piece), lambda i: (0, first + i)),
        out_shape=jax.ShapeDtypeStruct(settled.shape, jnp.bfloat16),
        input_output_aliases={2: 0} if earlier is not None else {},
        compiler_params=PARAMS,
        cost_estimate=BRIEF,
        name="finish",
    )(*operands)


def per_device(
    residual,
    query,
    cached_key_rows,
    cached_value_rows,
    new_token_key,
    new_token_value,
    lengths,
    output_weight,
    slot_down_weight,
    slot_up_weight,
    placement,
    request_adapter,
):
    count = lax.axis_size("tensor")
    replicas = lax.axis_size("dp")
    block = residual.shape[1]
    order = ring_order(count)
    ring = [(order[p], order[(p + 1) % count]) for p in range(count)]

    def exchange(blocks):
        moved = [
            lax.ppermute(blocks[r], "dp", [(i, i ^ r) for i in range(replicas)])
            for r in range(1, replicas)
        ]
        return [blocks[0]] + moved

    def next_hop(step, chain, after):
        arrived = lax.ppermute(travelling[chain], "tensor", ring)
        travelling[chain] = hop(step, chain, arrived, attended, output_weight, block, after)

    attended, first = attend(
        query, cached_key_rows, cached_value_rows, new_token_key, new_token_value, lengths,
        output_weight, block,
    )
    chosen, *leaving = route(
        attended, request_adapter, placement, replicas, slot_down_weight.shape[0]
    )
    rows_here = exchange(leaving)
    mid, inside = down(rows_here, slot_down_weight)
    rank_sums = [mid] + [
        lax.ppermute(mid, "tensor", [(i, (i + k) % count) for i in range(count)])
        for k in range(1, count)
    ]

    travelling = [first, hop(0, 1, None, attended, output_weight, block, after=[mid])]
    next_hop(1, 0, after=rank_sums + travelling[1:])
    next_hop(1, 1, after=())
    deltas = up(rank_sums, inside, slot_up_weight, after=[travelling[1]])
    returned = exchange(deltas)
    for step in range(2, count - 1):
        for chain in range(2):
            next_hop(step, chain, after=returned if (step, chain) == (2, 0) else ())
    settled = settle(
        count - 1, returned, chosen, attended, residual, output_weight, after=[travelling[1]]
    )
    out = None
    for chain in range(2):
        arrived = lax.ppermute(travelling[chain], "tensor", ring)
        out = finish(chain, arrived, settled, out)
    return out


def solution(mesh):
    placed = (
        P(("parts", "dp"), "tensor"),
        P(("parts", "dp"), "tensor", None),
        P(("parts", "dp"), None, "tensor", None),
        P(("parts", "dp"), None, "tensor", None),
        P(("parts", "dp"), "tensor", None),
        P(("parts", "dp"), "tensor", None),
        P(("parts", "dp")),
        P("tensor", None),
        P("dp", None, "tensor"),
        P("dp", None, "tensor"),
        P("parts"),
        P(("parts", "dp")),
    )
    return jax.shard_map(
        per_device,
        mesh=mesh,
        in_specs=placed,
        out_specs=P(("parts", "dp"), "tensor"),
        check_vma=False,
    )
```

```python
import functools
import math

import jax
import jax.numpy as jnp
from jax import lax
from jax.experimental import pallas as pl
from jax.experimental.pallas import tpu as pltpu
from jax.sharding import PartitionSpec as P

GROUP = 8
CAP = 64
LANES = 128
MASKED = -1e30
VMEM_LIMIT = 50 * 1024 * 1024
FULL_VMEM = 61 * 1024 * 1024
SHARES = ((5, 3),)
PIECE = 512
SPLIT = 4

VMEM = pl.BlockSpec(memory_space=pltpu.VMEM)
ANY = pl.BlockSpec(memory_space=pl.ANY)
PARAMS = pltpu.CompilerParams(vmem_limit_bytes=VMEM_LIMIT)


def _dot(a, b, left=1, right=0):
    return lax.dot_general(
        a, b, (((left,), (right,)), ((), ())), preferred_element_type=jnp.float32
    )


def _iota(shape, axis):
    return lax.broadcasted_iota(jnp.int32, shape, axis)


def ring_order(count):
    return list(range(0, count, 2)) + list(range(1, count, 2))[::-1]


def column_owner(step):
    count = lax.axis_size("tensor")
    here = lax.axis_index("tensor")
    half = here // 2
    spot = jnp.where(here % 2 == 0, half, count - 1 - half)
    spot = lax.rem(spot - 1 - step + 2 * count, count)
    return jnp.where(2 * spot < count, 2 * spot, 2 * (count - spot) - 1)


def chain_columns(width):
    shares = next(s for s in SHARES if width % (sum(s) * LANES) == 0)
    unit = width // sum(shares)
    return [(sum(shares[:c]) * unit, shares[c] * unit) for c in range(len(shares))]


class Weights:
    def __init__(self, w_ref, held, sems, first, width):
        depth = w_ref.shape[0] // SPLIT
        first = pl.multiple_of(first, LANES)
        self.held = held
        self.copies = [
            pltpu.make_async_copy(
                w_ref.at[pl.ds(s * depth, depth), pl.ds(first, width)],
                held.at[pl.ds(s * depth, depth), :],
                sems.at[s],
            )
            for s in range(SPLIT)
        ]

    def start(self):
        for copy in self.copies:
            copy.start()

    def products(self, a):
        for copy in self.copies:
            copy.wait()
        width = self.held.shape[1]
        for at in range(0, width, PIECE):
            columns = pl.ds(at, min(PIECE, width - at))
            yield columns, _dot(a, self.held[:, columns])

    @staticmethod
    def scratch(depth, width):
        return [
            pltpu.VMEM((depth, width), jnp.bfloat16),
            pltpu.SemaphoreType.DMA((SPLIT,)),
        ]


def row_max(arrays):
    full = None
    tops = []
    for x in arrays:
        width = x.shape[1]
        if width % LANES:
            tops.append(jnp.max(x, axis=1, keepdims=True))
            continue
        for at in range(0, width, LANES):
            tile = x[:, at : at + LANES]
            full = tile if full is None else jnp.maximum(full, tile)
    if full is not None:
        tops.append(jnp.max(full, axis=1, keepdims=True))
    return functools.reduce(jnp.maximum, tops)


def attend_kernel(
    heads, kv, cache, steps, block, replicas, slots,
    len_hbm, adapter_hbm, placement_hbm, q_hbm, k_hbm, v_hbm, nk_hbm, nv_hbm, w_hbm,
    *refs,
):
    a_ref, out_ref, chosen_ref, *sent_refs = refs[: 3 + replicas]
    (
        len_ref, adapter_ref, placement_ref, q_ref, k_ref, v_ref, nk_ref, nv_ref,
        scores_ref, mixed_ref, sems, small_sems, w_held, w_sems,
    ) = refs[3 + replicas :]
    requests = len_ref.shape[1]
    width = q_hbm.shape[1]
    per = requests // steps
    groups = per // GROUP
    group_rows = GROUP * heads
    group_cols = GROUP * cache * kv
    per_kv = heads // kv
    scale = math.log2(math.e) / math.sqrt(width)

    def part(kind, step):
        source, target, count = (
            (q_hbm, q_ref, heads),
            (k_hbm, k_ref, cache * kv),
            (v_hbm, v_ref, cache * kv),
        )[kind]
        rows = pl.ds(step * per * count, per * count)
        return pltpu.make_async_copy(source.at[rows, :], target.at[rows, :], sems.at[kind, step])

    small = [
        pltpu.make_async_copy(source, target, small_sems.at[i])
        for i, (source, target) in enumerate(
            (
                (nk_hbm, nk_ref),
                (len_hbm, len_ref),
                (nv_hbm, nv_ref),
                (adapter_hbm, adapter_ref),
                (placement_hbm, placement_ref),
            )
        )
    ]
    chunk = out_ref.shape[1]
    weights = Weights(w_hbm, w_held, w_sems, column_owner(0) * block, chunk)
    part(0, 0).start()
    part(1, 0).start()
    for copy in small[:2]:
        copy.start()
    part(0, 1).start()
    part(1, 1).start()
    part(2, 0).start()
    for copy in small[2:]:
        copy.start()
    part(2, 1).start()
    for step in range(2, steps):
        for kind in range(3):
            part(kind, step).start()
    weights.start()

    row = _iota((group_rows, group_cols), 0)
    col = _iota((group_rows, group_cols), 1)
    same = (row // heads == col // (cache * kv)) & ((row % heads) // per_kv == col % kv)
    own_bias = jnp.where(same, 0.0, MASKED)
    row = _iota((group_rows, per * kv), 0)
    col = _iota((group_rows, per * kv), 1)
    fresh_kv = (row % heads) // per_kv == col % kv
    fresh_distance = col // kv - row // heads
    ones = jnp.ones((max(group_cols, per * kv), LANES), jnp.bfloat16)

    def scores(step):
        side = step % 2
        part(0, step).wait()
        part(1, step).wait()
        q_at = step * per * heads
        k_at = step * per * cache * kv
        for g in range(groups):
            scores_ref[side, pl.ds(g * group_rows, group_rows), pl.ds(0, group_cols)] = _dot(
                q_ref[pl.ds(q_at + g * group_rows, group_rows), :],
                k_ref[pl.ds(k_at + g * group_cols, group_cols), :],
                1,
                1,
            )
        if step == 0:
            small[0].wait()
        scores_ref[side, :, pl.ds(group_cols, per * kv)] = _dot(
            q_ref[pl.ds(q_at, per * heads), :], nk_ref[pl.ds(step * per * kv, per * kv), :], 1, 1
        )

    scores(0)
    small[1].wait()
    counts = len_ref[...].astype(jnp.float32)
    all_groups = requests // GROUP
    of_group = _iota((all_groups, requests), 1) // GROUP == _iota((all_groups, requests), 0)
    counts = jnp.where(of_group, counts, 0.0).astype(jnp.bfloat16)
    spread = _iota((requests, group_cols), 0) % GROUP == _iota((requests, group_cols), 1) // (cache * kv)
    counts = _dot(counts, spread.astype(jnp.bfloat16))
    position = (_iota((all_groups, group_cols), 1) // kv) % cache
    length_bias = jnp.where(position.astype(jnp.float32) < counts, 0.0, MASKED)

    for step in range(steps):
        side = step % 2
        if step + 1 < steps:
            scores(step + 1)
        k_at = step * per * cache * kv
        f_at = step * per * kv
        part(2, step).wait()
        if step == 0:
            small[2].wait()
        held = []
        fresh = []
        for g in range(groups):
            rows = pl.ds(g * group_rows, group_rows)
            bias = own_bias + length_bias[step * groups + g : step * groups + g + 1, :]
            cached = scores_ref[side, rows, pl.ds(0, group_cols)] + bias
            new = scores_ref[side, rows, pl.ds(group_cols, per * kv)]
            new = jnp.where(fresh_kv & (fresh_distance == g * GROUP), new, MASKED)
            top = row_max([cached, new])
            held.append(jnp.exp2((cached - top) * scale).astype(jnp.bfloat16))
            fresh.append(jnp.exp2((new - top) * scale).astype(jnp.bfloat16))
        values = jnp.concatenate([nv_ref[pl.ds(f_at, per * kv), :], ones[: per * kv]], axis=1)
        fresh = _dot(jnp.concatenate(fresh, axis=0), values)
        for g in range(groups):
            rows = slice(g * group_rows, (g + 1) * group_rows)
            values = v_ref[pl.ds(k_at + g * group_cols, group_cols), :]
            values = jnp.concatenate([values, ones[:group_cols]], axis=1)
            mixed = fresh[rows, :] + _dot(held[g], values)
            mixed_ref[side, rows, :] = mixed[:, :width] / mixed[:, width : width + 1]
        for h in range(heads):
            a_ref[pl.ds(step * per, per), pl.ds(h * width, width)] = mixed_ref[
                side, pl.ds(h, per, stride=heads), :
            ].astype(jnp.bfloat16)

    for copy in small[3:]:
        copy.wait()
    route(slots, a_ref, adapter_ref, placement_ref, chosen_ref, sent_refs)
    for columns, product in weights.products(a_ref[...]):
        out_ref[:, columns] = product.astype(jnp.bfloat16)


def route(slots, a_ref, adapter_ref, placement_ref, chosen_ref, sent_refs):
    replicas = len(sent_refs)
    requests = adapter_ref.shape[1]
    table = placement_ref.shape[1]
    matches = _iota((table, requests), 0) == adapter_ref[...]
    placed = jnp.broadcast_to(placement_ref[...].astype(jnp.float32), (8, table))
    slot = _dot(placed.astype(jnp.bfloat16), matches.astype(jnp.bfloat16)).astype(jnp.int32)
    slot = slot[0:1, :]
    holder = (slot // slots) ^ lax.axis_index("dp")
    inside = slot % slots
    of_holder = _iota((max(replicas, 8), requests), 0) == holder
    earlier = _iota((requests, requests), 0) < _iota((requests, requests), 1)
    before = _dot(of_holder.astype(jnp.bfloat16), earlier.astype(jnp.bfloat16))
    before = jnp.sum(jnp.where(of_holder, before, 0.0), axis=0, keepdims=True).astype(jnp.int32)
    target = holder * CAP + before
    here = _iota((replicas * CAP, requests), 0) == target
    chosen = here.astype(jnp.bfloat16)
    chosen_ref[...] = chosen
    rows = _dot(chosen, a_ref[...]).astype(jnp.bfloat16)
    inner = jnp.sum(jnp.where(here, inside.astype(jnp.float32), 0.0), axis=1, keepdims=True)
    inner = jnp.broadcast_to(inner, (replicas * CAP, LANES)).astype(jnp.bfloat16)
    width = a_ref.shape[1]
    for r, sent_ref in enumerate(sent_refs):
        sent_ref[:, pl.ds(0, width)] = rows[r * CAP : (r + 1) * CAP, :]
        sent_ref[:, pl.ds(width, LANES)] = inner[r * CAP : (r + 1) * CAP, :]


def attend(
    query, keys, values, new_key, new_value, lengths, weight, request_adapter, placement,
    block, replicas, slots,
):
    requests, heads, width = query.shape
    cache, kv = keys.shape[1], keys.shape[2]
    steps = 4
    per = requests // steps
    columns = GROUP * cache * kv + per * kv
    features = heads * width
    chunk = chain_columns(block)[0][1]
    small = [lengths.reshape(1, -1), request_adapter.reshape(1, -1), placement.reshape(1, -1)]
    operands = [
        query.reshape(requests * heads, width),
        keys.reshape(requests * cache * kv, width),
        values.reshape(requests * cache * kv, width),
        new_key.reshape(requests * kv, width),
        new_value.reshape(requests * kv, width),
    ]
    return pl.pallas_call(
        functools.partial(attend_kernel, heads, kv, cache, steps, block, replicas, slots),
        in_specs=[ANY] * 9,
        out_specs=[VMEM] * (3 + replicas),
        out_shape=[
            jax.ShapeDtypeStruct((requests, features), jnp.bfloat16),
            jax.ShapeDtypeStruct((requests, chunk), jnp.bfloat16),
            jax.ShapeDtypeStruct((replicas * CAP, requests), jnp.bfloat16),
        ]
        + [jax.ShapeDtypeStruct((CAP, features + LANES), jnp.bfloat16)] * replicas,
        scratch_shapes=[pltpu.VMEM(x.shape, x.dtype) for x in small + operands]
        + [
            pltpu.VMEM((2, per * heads, columns), jnp.float32),
            pltpu.VMEM((2, per * heads, width), jnp.float32),
            pltpu.SemaphoreType.DMA((3, steps)),
            pltpu.SemaphoreType.DMA((5,)),
        ]
        + Weights.scratch(weight.shape[0], chunk),
        compiler_params=pltpu.CompilerParams(vmem_limit_bytes=FULL_VMEM),
        name="attend",
    )(*small, *operands, weight)


def hop_kernel(step, block, start, arriving, after, *refs):
    if arriving:
        arrived_ref, *refs = refs
    a_ref, w_hbm, *refs = refs
    out_ref, held, sems = refs[after:]
    chunk = out_ref.shape[1]
    first = column_owner(step) * block + start
    weights = Weights(w_hbm, held, sems, first, chunk)
    weights.start()
    for columns, product in weights.products(a_ref[...]):
        if arriving:
            product = product + arrived_ref[:, columns].astype(jnp.float32)
        out_ref[:, columns] = product.astype(jnp.bfloat16)


def hop(step, chain, arrived, attended, weight, block, after=()):
    arriving = arrived is not None
    start, chunk = chain_columns(block)[chain]
    operands = ([arrived] if arriving else []) + [attended, weight, *after]
    return pl.pallas_call(
        functools.partial(hop_kernel, step, block, start, arriving, len(after)),
        in_specs=[VMEM] * (1 + arriving) + [ANY] + [ANY] * len(after),
        out_specs=VMEM,
        out_shape=jax.ShapeDtypeStruct((attended.shape[0], chunk), jnp.bfloat16),
        scratch_shapes=Weights.scratch(weight.shape[0], chunk),
        compiler_params=PARAMS,
        name="hop",
    )(*operands)


def down_kernel(replicas, after, *refs):
    received = refs[:replicas]
    down_ref = refs[replicas]
    mid_ref, inside_ref = refs[replicas + 1 + after :]
    slots, rank, width = down_ref.shape
    rows = jnp.concatenate([r[:, pl.ds(0, width)] for r in received], axis=0)
    inside = jnp.concatenate([r[:, pl.ds(width, LANES)] for r in received], axis=0)
    inside_ref[...] = inside
    projected = _dot(rows, down_ref[...].reshape(slots * rank, width), 1, 1)
    lane_slot = _iota(projected.shape, 1) // rank
    mine = lane_slot == inside[:, 0:1].astype(jnp.int32)
    projected = jnp.where(mine, projected, 0.0).astype(jnp.bfloat16)
    beside = LANES // rank
    some = projected.shape[0] // beside
    packed = 0.0
    for b in range(beside):
        lane = _iota((slots * rank, LANES), 1) - b * rank
        fold = _iota((slots * rank, LANES), 0) % rank == lane
        packed = packed + _dot(projected[b * some : (b + 1) * some, :], fold.astype(jnp.bfloat16))
    mid_ref[...] = packed.astype(jnp.bfloat16)


def down(received, slot_down_weight, after=()):
    replicas = len(received)
    rows = replicas * CAP
    return pl.pallas_call(
        functools.partial(down_kernel, replicas, len(after)),
        in_specs=[VMEM] * (replicas + 1) + [ANY] * len(after),
        out_specs=[VMEM, VMEM],
        out_shape=[
            jax.ShapeDtypeStruct((rows * slot_down_weight.shape[1] // LANES, LANES), jnp.bfloat16),
            jax.ShapeDtypeStruct((rows, LANES), jnp.bfloat16),
        ],
        compiler_params=PARAMS,
        name="down",
    )(*received, slot_down_weight, *after)


def up_kernel(parts, after, *refs):
    mids = refs[:parts]
    inside_ref, up_ref = refs[parts : parts + 2]
    out_refs = refs[parts + 2 + after :]
    slots, rank, width = up_ref.shape
    mid = mids[0][...].astype(jnp.float32)
    for m in mids[1:]:
        mid = mid + m[...].astype(jnp.float32)
    mid = mid.astype(jnp.bfloat16)
    wide = []
    for b in range(LANES // rank):
        lane = _iota((LANES, slots * rank), 0) - b * rank
        spread = _iota((LANES, slots * rank), 1) % rank == lane
        wide.append(_dot(mid, spread.astype(jnp.bfloat16)))
    wide = jnp.concatenate(wide, axis=0)
    mine = _iota(wide.shape, 1) // rank == inside_ref[:, 0:1].astype(jnp.int32)
    wide = jnp.where(mine, wide, 0.0).astype(jnp.bfloat16)
    delta = _dot(wide, up_ref[...].reshape(slots * rank, width)).astype(jnp.bfloat16)
    for r, out_ref in enumerate(out_refs):
        out_ref[...] = delta[r * CAP : (r + 1) * CAP, :]


def up(mids, inside, slot_up_weight, after=()):
    rows = inside.shape[0]
    replicas = rows // CAP
    width = slot_up_weight.shape[2]
    return pl.pallas_call(
        functools.partial(up_kernel, len(mids), len(after)),
        in_specs=[VMEM] * (len(mids) + 2) + [ANY] * len(after),
        out_specs=[VMEM] * replicas,
        out_shape=[jax.ShapeDtypeStruct((CAP, width), jnp.bfloat16)] * replicas,
        compiler_params=PARAMS,
        name="up",
    )(*mids, inside, slot_up_weight, *after)


def settle_kernel(step, replicas, after, *refs):
    returned = refs[:replicas]
    chosen_ref, a_ref, residual_ref, w_hbm = refs[replicas : replicas + 4]
    *out_refs, held, sems = refs[replicas + 4 + after :]
    width = residual_ref.shape[1]
    weights = Weights(w_hbm, held, sems, column_owner(step) * width, width)
    weights.start()
    rows = jnp.concatenate([r[...] for r in returned], axis=0)
    delta = _dot(chosen_ref[...], rows, 0, 0)
    total = residual_ref[...].astype(jnp.float32) + delta
    total = total + jnp.concatenate([p for _, p in weights.products(a_ref[...])], axis=1)
    for (start, chunk), out_ref in zip(chain_columns(width), out_refs):
        out_ref[...] = total[:, start : start + chunk]


def settle(step, returned, chosen, attended, residual, weight, after=()):
    replicas = len(returned)
    rows, width = residual.shape
    chains = chain_columns(width)
    return pl.pallas_call(
        functools.partial(settle_kernel, step, replicas, len(after)),
        in_specs=[VMEM] * (replicas + 3) + [ANY] * (1 + len(after)),
        out_specs=[VMEM] * len(chains),
        out_shape=[jax.ShapeDtypeStruct((rows, chunk), jnp.float32) for _, chunk in chains],
        scratch_shapes=Weights.scratch(weight.shape[0], width),
        compiler_params=PARAMS,
        name="settle",
    )(*returned, chosen, attended, residual, weight, *after)


def finish_kernel(start, arrived_ref, settled_ref, *refs):
    out_hbm, held, sems = refs[-3:]
    rows, chunk = arrived_ref.shape
    half = rows // 2
    copies = []
    for i in range(2):
        part = pl.ds(i * half, half)
        total = settled_ref[part, :] + arrived_ref[part, :].astype(jnp.float32)
        held[part, :] = total.astype(jnp.bfloat16)
        target = out_hbm.at[part, pl.ds(start, chunk)]
        copies.append(pltpu.make_async_copy(held.at[part, :], target, sems.at[i]))
        copies[-1].start()
    for copy in copies:
        copy.wait()


def finish(chain, arrived, settled, earlier, width):
    rows = arrived.shape[0]
    start, chunk = chain_columns(width)[chain]
    operands = [arrived, settled] + ([earlier] if earlier is not None else [])
    return pl.pallas_call(
        functools.partial(finish_kernel, start),
        in_specs=[VMEM, VMEM] + ([ANY] if earlier is not None else []),
        out_specs=ANY,
        out_shape=jax.ShapeDtypeStruct((rows, width), jnp.bfloat16),
        input_output_aliases={2: 0} if earlier is not None else {},
        scratch_shapes=[
            pltpu.VMEM((rows, chunk), jnp.bfloat16),
            pltpu.SemaphoreType.DMA((2,)),
        ],
        compiler_params=PARAMS,
        name="finish",
    )(*operands)


def hold_kernel(*refs):
    pass


def hold(x, after):
    return pl.pallas_call(
        hold_kernel,
        in_specs=[ANY] * (1 + len(after)),
        out_specs=ANY,
        out_shape=jax.ShapeDtypeStruct(x.shape, x.dtype),
        input_output_aliases={0: 0},
        compiler_params=PARAMS,
        name="hold",
    )(x, *after)


def per_device(
    residual,
    query,
    cached_key_rows,
    cached_value_rows,
    new_token_key,
    new_token_value,
    lengths,
    output_weight,
    slot_down_weight,
    slot_up_weight,
    placement,
    request_adapter,
):
    count = lax.axis_size("tensor")
    replicas = lax.axis_size("dp")
    block = residual.shape[1]
    order = ring_order(count)
    ring = [(order[p], order[(p + 1) % count]) for p in range(count)]

    def exchange(blocks):
        moved = [
            lax.ppermute(blocks[r], "dp", [(i, i ^ r) for i in range(replicas)])
            for r in range(1, replicas)
        ]
        return [blocks[0]] + moved

    def next_hop(step, chain, after):
        arrived = lax.ppermute(travelling[chain], "tensor", ring)
        travelling[chain] = hop(step, chain, arrived, attended, output_weight, block, after)

    attended, first, chosen, *leaving = attend(
        query, cached_key_rows, cached_value_rows, new_token_key, new_token_value, lengths,
        output_weight, request_adapter, placement, block, replicas, slot_down_weight.shape[0],
    )
    second = hop(0, 1, None, attended, output_weight, block)
    rows_here = exchange(leaving)
    mid, inside = down(rows_here, slot_down_weight, after=[second])
    rank_sums = [mid] + [
        lax.ppermute(mid, "tensor", [(i, (i + k) % count) for i in range(count)])
        for k in range(1, count)
    ]

    travelling = [first, hold(second, after=[mid])]
    next_hop(1, 0, after=rank_sums + travelling[1:])
    next_hop(1, 1, after=())
    deltas = up(rank_sums, inside, slot_up_weight, after=[travelling[1]])
    returned = exchange(deltas)
    for step in range(2, count - 1):
        for chain in range(2):
            next_hop(step, chain, after=returned if (step, chain) == (2, 0) else ())
    settled = settle(
        count - 1, returned, chosen, attended, residual, output_weight, after=[travelling[1]]
    )
    out = None
    for chain in range(2):
        arrived = lax.ppermute(travelling[chain], "tensor", ring)
        out = finish(chain, arrived, settled[chain], out, block)
    return out


def solution(mesh):
    placed = (
        P(("parts", "dp"), "tensor"),
        P(("parts", "dp"), "tensor", None),
        P(("parts", "dp"), None, "tensor", None),
        P(("parts", "dp"), None, "tensor", None),
        P(("parts", "dp"), "tensor", None),
        P(("parts", "dp"), "tensor", None),
        P(("parts", "dp")),
        P("tensor", None),
        P("dp", None, "tensor"),
        P("dp", None, "tensor"),
        P("parts"),
        P(("parts", "dp")),
    )
    return jax.shard_map(
        per_device,
        mesh=mesh,
        in_specs=placed,
        out_specs=P(("parts", "dp"), "tensor"),
        check_vma=False,
    )
```

```python
import functools
import math

import jax
import jax.numpy as jnp
from jax import lax
from jax.experimental import pallas as pl
from jax.experimental.pallas import tpu as pltpu
from jax.sharding import PartitionSpec as P

GROUP = 8
CAP = 64
LANES = 128
MASKED = -1e30
VMEM_LIMIT = 50 * 1024 * 1024
FULL_VMEM = 61 * 1024 * 1024
SHARES = ((5, 3),)
PIECE = 512
SPLIT = 4

VMEM = pl.BlockSpec(memory_space=pltpu.VMEM)
ANY = pl.BlockSpec(memory_space=pl.ANY)
PARAMS = pltpu.CompilerParams(vmem_limit_bytes=VMEM_LIMIT)


def _dot(a, b, left=1, right=0):
    return lax.dot_general(
        a, b, (((left,), (right,)), ((), ())), preferred_element_type=jnp.float32
    )


def _iota(shape, axis):
    return lax.broadcasted_iota(jnp.int32, shape, axis)


def ring_order(count):
    return list(range(0, count, 2)) + list(range(1, count, 2))[::-1]


def column_owner(step):
    count = lax.axis_size("tensor")
    here = lax.axis_index("tensor")
    half = here // 2
    spot = jnp.where(here % 2 == 0, half, count - 1 - half)
    spot = lax.rem(spot - 1 - step + 2 * count, count)
    return jnp.where(2 * spot < count, 2 * spot, 2 * (count - spot) - 1)


def chain_columns(width):
    shares = next(s for s in SHARES if width % (sum(s) * LANES) == 0)
    unit = width // sum(shares)
    return [(sum(shares[:c]) * unit, shares[c] * unit) for c in range(len(shares))]


class Weights:
    def __init__(self, w_ref, held, sems, first, width):
        depth = w_ref.shape[0] // SPLIT
        first = pl.multiple_of(first, LANES)
        self.held = held
        self.copies = [
            pltpu.make_async_copy(
                w_ref.at[pl.ds(s * depth, depth), pl.ds(first, width)],
                held.at[pl.ds(s * depth, depth), :],
                sems.at[s],
            )
            for s in range(SPLIT)
        ]

    def start(self):
        for copy in self.copies:
            copy.start()

    def products(self, a):
        for copy in self.copies:
            copy.wait()
        width = self.held.shape[1]
        for at in range(0, width, PIECE):
            columns = pl.ds(at, min(PIECE, width - at))
            yield columns, _dot(a, self.held[:, columns])

    @staticmethod
    def scratch(depth, width):
        return [
            pltpu.VMEM((depth, width), jnp.bfloat16),
            pltpu.SemaphoreType.DMA((SPLIT,)),
        ]


def row_max(arrays):
    full = None
    tops = []
    for x in arrays:
        width = x.shape[1]
        if width % LANES:
            tops.append(jnp.max(x, axis=1, keepdims=True))
            continue
        for at in range(0, width, LANES):
            tile = x[:, at : at + LANES]
            full = tile if full is None else jnp.maximum(full, tile)
    if full is not None:
        tops.append(jnp.max(full, axis=1, keepdims=True))
    return functools.reduce(jnp.maximum, tops)


def attend_kernel(
    heads, kv, cache, steps, block, slots,
    len_hbm, adapter_hbm, placement_hbm, q_hbm, k_hbm, v_hbm, nk_hbm, nv_hbm, w_hbm,
    *refs,
):
    a_ref, out_ref, chosen_ref, sent_ref = refs[:4]
    (
        len_ref, adapter_ref, placement_ref, q_ref, k_ref, v_ref, nk_ref, nv_ref,
        scores_ref, mixed_ref, sems, small_sems, w_held, w_sems,
    ) = refs[4:]
    requests = len_ref.shape[1]
    width = q_hbm.shape[1]
    per = requests // steps
    groups = per // GROUP
    group_rows = GROUP * heads
    group_cols = GROUP * cache * kv
    per_kv = heads // kv
    scale = math.log2(math.e) / math.sqrt(width)

    def part(kind, step):
        source, target, count = (
            (q_hbm, q_ref, heads),
            (k_hbm, k_ref, cache * kv),
            (v_hbm, v_ref, cache * kv),
        )[kind]
        rows = pl.ds(step * per * count, per * count)
        return pltpu.make_async_copy(source.at[rows, :], target.at[rows, :], sems.at[kind, step])

    small = [
        pltpu.make_async_copy(source, target, small_sems.at[i])
        for i, (source, target) in enumerate(
            (
                (nk_hbm, nk_ref),
                (len_hbm, len_ref),
                (nv_hbm, nv_ref),
                (adapter_hbm, adapter_ref),
                (placement_hbm, placement_ref),
            )
        )
    ]
    chunk = out_ref.shape[1]
    weights = Weights(w_hbm, w_held, w_sems, column_owner(0) * block, chunk)
    part(0, 0).start()
    part(1, 0).start()
    for copy in small[:2]:
        copy.start()
    part(0, 1).start()
    part(1, 1).start()
    part(2, 0).start()
    for copy in small[2:]:
        copy.start()
    part(2, 1).start()
    for step in range(2, steps):
        for kind in range(3):
            part(kind, step).start()
    weights.start()

    row = _iota((group_rows, group_cols), 0)
    col = _iota((group_rows, group_cols), 1)
    same = (row // heads == col // (cache * kv)) & ((row % heads) // per_kv == col % kv)
    own_bias = jnp.where(same, 0.0, MASKED)
    row = _iota((group_rows, per * kv), 0)
    col = _iota((group_rows, per * kv), 1)
    fresh_kv = (row % heads) // per_kv == col % kv
    fresh_distance = col // kv - row // heads
    ones = jnp.ones((max(group_cols, per * kv), LANES), jnp.bfloat16)

    def scores(step):
        side = step % 2
        part(0, step).wait()
        part(1, step).wait()
        q_at = step * per * heads
        k_at = step * per * cache * kv
        for g in range(groups):
            scores_ref[side, pl.ds(g * group_rows, group_rows), pl.ds(0, group_cols)] = _dot(
                q_ref[pl.ds(q_at + g * group_rows, group_rows), :],
                k_ref[pl.ds(k_at + g * group_cols, group_cols), :],
                1,
                1,
            )
        if step == 0:
            small[0].wait()
        scores_ref[side, :, pl.ds(group_cols, per * kv)] = _dot(
            q_ref[pl.ds(q_at, per * heads), :], nk_ref[pl.ds(step * per * kv, per * kv), :], 1, 1
        )

    scores(0)
    small[1].wait()
    counts = len_ref[...].astype(jnp.float32)
    all_groups = requests // GROUP
    of_group = _iota((all_groups, requests), 1) // GROUP == _iota((all_groups, requests), 0)
    counts = jnp.where(of_group, counts, 0.0).astype(jnp.bfloat16)
    spread = _iota((requests, group_cols), 0) % GROUP == _iota((requests, group_cols), 1) // (cache * kv)
    counts = _dot(counts, spread.astype(jnp.bfloat16))
    position = (_iota((all_groups, group_cols), 1) // kv) % cache
    length_bias = jnp.where(position.astype(jnp.float32) < counts, 0.0, MASKED)

    for step in range(steps):
        side = step % 2
        if step + 1 < steps:
            scores(step + 1)
        k_at = step * per * cache * kv
        f_at = step * per * kv
        part(2, step).wait()
        if step == 0:
            small[2].wait()
        held = []
        fresh = []
        for g in range(groups):
            rows = pl.ds(g * group_rows, group_rows)
            bias = own_bias + length_bias[step * groups + g : step * groups + g + 1, :]
            cached = scores_ref[side, rows, pl.ds(0, group_cols)] + bias
            new = scores_ref[side, rows, pl.ds(group_cols, per * kv)]
            new = jnp.where(fresh_kv & (fresh_distance == g * GROUP), new, MASKED)
            top = row_max([cached, new])
            held.append(jnp.exp2((cached - top) * scale).astype(jnp.bfloat16))
            fresh.append(jnp.exp2((new - top) * scale).astype(jnp.bfloat16))
        values = jnp.concatenate([nv_ref[pl.ds(f_at, per * kv), :], ones[: per * kv]], axis=1)
        fresh = _dot(jnp.concatenate(fresh, axis=0), values)
        for g in range(groups):
            rows = slice(g * group_rows, (g + 1) * group_rows)
            values = v_ref[pl.ds(k_at + g * group_cols, group_cols), :]
            values = jnp.concatenate([values, ones[:group_cols]], axis=1)
            mixed = fresh[rows, :] + _dot(held[g], values)
            mixed_ref[side, rows, :] = mixed[:, :width] / mixed[:, width : width + 1]
        for h in range(heads):
            a_ref[pl.ds(step * per, per), pl.ds(h * width, width)] = mixed_ref[
                side, pl.ds(h, per, stride=heads), :
            ].astype(jnp.bfloat16)

    for copy in small[3:]:
        copy.wait()
    route(slots, a_ref, adapter_ref, placement_ref, chosen_ref, sent_ref)
    for columns, product in weights.products(a_ref[...]):
        out_ref[:, columns] = product.astype(jnp.bfloat16)


def route(slots, a_ref, adapter_ref, placement_ref, chosen_ref, sent_ref):
    replicas = sent_ref.shape[0] // CAP
    requests = adapter_ref.shape[1]
    table = placement_ref.shape[1]
    matches = _iota((table, requests), 0) == adapter_ref[...]
    placed = jnp.broadcast_to(placement_ref[...].astype(jnp.float32), (8, table))
    slot = _dot(placed.astype(jnp.bfloat16), matches.astype(jnp.bfloat16)).astype(jnp.int32)
    slot = slot[0:1, :]
    holder = slot // slots
    inside = slot % slots
    of_holder = _iota((max(replicas, 8), requests), 0) == holder
    earlier = _iota((requests, requests), 0) < _iota((requests, requests), 1)
    before = _dot(of_holder.astype(jnp.bfloat16), earlier.astype(jnp.bfloat16))
    before = jnp.sum(jnp.where(of_holder, before, 0.0), axis=0, keepdims=True).astype(jnp.int32)
    target = holder * CAP + before
    here = _iota((replicas * CAP, requests), 0) == target
    chosen = here.astype(jnp.bfloat16)
    chosen_ref[...] = chosen
    rows = _dot(chosen, a_ref[...]).astype(jnp.bfloat16)
    inner = jnp.sum(jnp.where(here, inside.astype(jnp.float32), 0.0), axis=1, keepdims=True)
    inner = jnp.broadcast_to(inner, (replicas * CAP, LANES)).astype(jnp.bfloat16)
    width = a_ref.shape[1]
    sent_ref[:, pl.ds(0, width)] = rows
    sent_ref[:, pl.ds(width, LANES)] = inner


def attend(
    query, keys, values, new_key, new_value, lengths, weight, request_adapter, placement,
    block, replicas, slots,
):
    requests, heads, width = query.shape
    cache, kv = keys.shape[1], keys.shape[2]
    steps = 4
    per = requests // steps
    columns = GROUP * cache * kv + per * kv
    features = heads * width
    chunk = chain_columns(block)[0][1]
    small = [lengths.reshape(1, -1), request_adapter.reshape(1, -1), placement.reshape(1, -1)]
    operands = [
        query.reshape(requests * heads, width),
        keys.reshape(requests * cache * kv, width),
        values.reshape(requests * cache * kv, width),
        new_key.reshape(requests * kv, width),
        new_value.reshape(requests * kv, width),
    ]
    return pl.pallas_call(
        functools.partial(attend_kernel, heads, kv, cache, steps, block, slots),
        in_specs=[ANY] * 9,
        out_specs=[VMEM] * 4,
        out_shape=[
            jax.ShapeDtypeStruct((requests, features), jnp.bfloat16),
            jax.ShapeDtypeStruct((requests, chunk), jnp.bfloat16),
            jax.ShapeDtypeStruct((replicas * CAP, requests), jnp.bfloat16),
            jax.ShapeDtypeStruct((replicas * CAP, features + LANES), jnp.bfloat16),
        ],
        scratch_shapes=[pltpu.VMEM(x.shape, x.dtype) for x in small + operands]
        + [
            pltpu.VMEM((2, per * heads, columns), jnp.float32),
            pltpu.VMEM((2, per * heads, width), jnp.float32),
            pltpu.SemaphoreType.DMA((3, steps)),
            pltpu.SemaphoreType.DMA((5,)),
        ]
        + Weights.scratch(weight.shape[0], chunk),
        compiler_params=pltpu.CompilerParams(vmem_limit_bytes=FULL_VMEM),
        name="attend",
    )(*small, *operands, weight)


def hop_kernel(step, block, start, arriving, after, *refs):
    if arriving:
        arrived_ref, *refs = refs
    a_ref, w_hbm, *refs = refs
    out_ref, held, sems = refs[after:]
    chunk = out_ref.shape[1]
    first = column_owner(step) * block + start
    weights = Weights(w_hbm, held, sems, first, chunk)
    weights.start()
    for columns, product in weights.products(a_ref[...]):
        if arriving:
            product = product + arrived_ref[:, columns].astype(jnp.float32)
        out_ref[:, columns] = product.astype(jnp.bfloat16)


def hop(step, chain, arrived, attended, weight, block, after=()):
    arriving = arrived is not None
    start, chunk = chain_columns(block)[chain]
    operands = ([arrived] if arriving else []) + [attended, weight, *after]
    return pl.pallas_call(
        functools.partial(hop_kernel, step, block, start, arriving, len(after)),
        in_specs=[VMEM] * (1 + arriving) + [ANY] + [ANY] * len(after),
        out_specs=VMEM,
        out_shape=jax.ShapeDtypeStruct((attended.shape[0], chunk), jnp.bfloat16),
        scratch_shapes=Weights.scratch(weight.shape[0], chunk),
        compiler_params=PARAMS,
        name="hop",
    )(*operands)


def down_kernel(count, after, *refs):
    received_ref, down_ref = refs[:2]
    mid_ref = refs[2 + after]
    slots, rank, width = down_ref.shape
    projected = _dot(
        received_ref[:, pl.ds(0, width)], down_ref[...].reshape(slots * rank, width), 1, 1
    )
    lane_slot = _iota(projected.shape, 1) // rank
    mine = lane_slot == received_ref[:, pl.ds(width, LANES)][:, 0:1].astype(jnp.int32)
    projected = jnp.where(mine, projected, 0.0).astype(jnp.bfloat16)
    beside = LANES // rank
    some = projected.shape[0] // beside
    packed = 0.0
    for b in range(beside):
        lane = _iota((slots * rank, LANES), 1) - b * rank
        fold = _iota((slots * rank, LANES), 0) % rank == lane
        packed = packed + _dot(projected[b * some : (b + 1) * some, :], fold.astype(jnp.bfloat16))
    packed = packed.astype(jnp.bfloat16)
    for t in range(count):
        mid_ref[pl.ds(t * some, some), :] = packed


def down(received, slot_down_weight, count, after=()):
    rows = received.shape[0] * slot_down_weight.shape[1] // LANES
    return pl.pallas_call(
        functools.partial(down_kernel, count, len(after)),
        in_specs=[VMEM] * 2 + [ANY] * len(after),
        out_specs=VMEM,
        out_shape=jax.ShapeDtypeStruct((count * rows, LANES), jnp.bfloat16),
        compiler_params=PARAMS,
        name="down",
    )(received, slot_down_weight, *after)


def up_kernel(count, after, *refs):
    mid_ref, received_ref, up_ref = refs[:3]
    out_ref = refs[3 + after]
    slots, rank, width = up_ref.shape
    some = mid_ref.shape[0] // count
    mid = 0.0
    for t in range(count):
        mid = mid + mid_ref[pl.ds(t * some, some), :].astype(jnp.float32)
    mid = mid.astype(jnp.bfloat16)
    wide = []
    for b in range(LANES // rank):
        lane = _iota((LANES, slots * rank), 0) - b * rank
        spread = _iota((LANES, slots * rank), 1) % rank == lane
        wide.append(_dot(mid, spread.astype(jnp.bfloat16)))
    wide = jnp.concatenate(wide, axis=0)
    inside = received_ref[:, pl.ds(received_ref.shape[1] - LANES, LANES)][:, 0:1]
    mine = _iota(wide.shape, 1) // rank == inside.astype(jnp.int32)
    wide = jnp.where(mine, wide, 0.0).astype(jnp.bfloat16)
    out_ref[...] = _dot(wide, up_ref[...].reshape(slots * rank, width)).astype(jnp.bfloat16)


def up(mids, count, received, slot_up_weight, after=()):
    return pl.pallas_call(
        functools.partial(up_kernel, count, len(after)),
        in_specs=[VMEM] * 3 + [ANY] * len(after),
        out_specs=VMEM,
        out_shape=jax.ShapeDtypeStruct(
            (received.shape[0], slot_up_weight.shape[2]), jnp.bfloat16
        ),
        compiler_params=PARAMS,
        name="up",
    )(mids, received, slot_up_weight, *after)


def settle_kernel(step, after, *refs):
    returned_ref, chosen_ref, a_ref, residual_ref, w_hbm = refs[:5]
    *out_refs, held, sems = refs[5 + after :]
    width = residual_ref.shape[1]
    weights = Weights(w_hbm, held, sems, column_owner(step) * width, width)
    weights.start()
    delta = _dot(chosen_ref[...], returned_ref[...], 0, 0)
    total = residual_ref[...].astype(jnp.float32) + delta
    total = total + jnp.concatenate([p for _, p in weights.products(a_ref[...])], axis=1)
    for (start, chunk), out_ref in zip(chain_columns(width), out_refs):
        out_ref[...] = total[:, start : start + chunk]


def settle(step, returned, chosen, attended, residual, weight, after=()):
    rows, width = residual.shape
    chains = chain_columns(width)
    return pl.pallas_call(
        functools.partial(settle_kernel, step, len(after)),
        in_specs=[VMEM] * 4 + [ANY] * (1 + len(after)),
        out_specs=[VMEM] * len(chains),
        out_shape=[jax.ShapeDtypeStruct((rows, chunk), jnp.float32) for _, chunk in chains],
        scratch_shapes=Weights.scratch(weight.shape[0], width),
        compiler_params=PARAMS,
        name="settle",
    )(returned, chosen, attended, residual, weight, *after)


def finish_kernel(start, arrived_ref, settled_ref, *refs):
    out_hbm, held, sems = refs[-3:]
    rows, chunk = arrived_ref.shape
    half = rows // 2
    copies = []
    for i in range(2):
        part = pl.ds(i * half, half)
        total = settled_ref[part, :] + arrived_ref[part, :].astype(jnp.float32)
        held[part, :] = total.astype(jnp.bfloat16)
        target = out_hbm.at[part, pl.ds(start, chunk)]
        copies.append(pltpu.make_async_copy(held.at[part, :], target, sems.at[i]))
        copies[-1].start()
    for copy in copies:
        copy.wait()


def finish(chain, arrived, settled, earlier, width):
    rows = arrived.shape[0]
    start, chunk = chain_columns(width)[chain]
    operands = [arrived, settled] + ([earlier] if earlier is not None else [])
    return pl.pallas_call(
        functools.partial(finish_kernel, start),
        in_specs=[VMEM, VMEM] + ([ANY] if earlier is not None else []),
        out_specs=ANY,
        out_shape=jax.ShapeDtypeStruct((rows, width), jnp.bfloat16),
        input_output_aliases={2: 0} if earlier is not None else {},
        scratch_shapes=[
            pltpu.VMEM((rows, chunk), jnp.bfloat16),
            pltpu.SemaphoreType.DMA((2,)),
        ],
        compiler_params=PARAMS,
        name="finish",
    )(*operands)


def hold_kernel(*refs):
    pass


def hold(x, after):
    return pl.pallas_call(
        hold_kernel,
        in_specs=[ANY] * (1 + len(after)),
        out_specs=ANY,
        out_shape=jax.ShapeDtypeStruct(x.shape, x.dtype),
        input_output_aliases={0: 0},
        compiler_params=PARAMS,
        name="hold",
    )(x, *after)


def per_device(
    residual,
    query,
    cached_key_rows,
    cached_value_rows,
    new_token_key,
    new_token_value,
    lengths,
    output_weight,
    slot_down_weight,
    slot_up_weight,
    placement,
    request_adapter,
):
    count = lax.axis_size("tensor")
    replicas = lax.axis_size("dp")
    block = residual.shape[1]
    order = ring_order(count)
    ring = [(order[p], order[(p + 1) % count]) for p in range(count)]

    def exchange(x, axis):
        return lax.all_to_all(x, axis, split_axis=0, concat_axis=0, tiled=True)

    def next_hop(step, chain, after):
        arrived = lax.ppermute(travelling[chain], "tensor", ring)
        travelling[chain] = hop(step, chain, arrived, attended, output_weight, block, after)

    attended, first, chosen, leaving = attend(
        query, cached_key_rows, cached_value_rows, new_token_key, new_token_value, lengths,
        output_weight, request_adapter, placement, block, replicas, slot_down_weight.shape[0],
    )
    second = hop(0, 1, None, attended, output_weight, block)
    rows_here = exchange(leaving, "dp")
    rank_terms = down(rows_here, slot_down_weight, count, after=[second])
    rank_sums = exchange(rank_terms, "tensor")

    travelling = [first, hold(second, after=[rank_sums])]
    next_hop(1, 0, after=travelling[1:])
    deltas = up(rank_sums, count, rows_here, slot_up_weight, after=travelling[:1])
    returned = exchange(deltas, "dp")
    next_hop(1, 1, after=[returned])
    for step in range(2, count - 1):
        for chain in range(2):
            next_hop(step, chain, after=[travelling[1 - chain]])
    settled = settle(
        count - 1, returned, chosen, attended, residual, output_weight, after=[travelling[1]]
    )
    out = None
    for chain in range(2):
        arrived = lax.ppermute(travelling[chain], "tensor", ring)
        out = finish(chain, arrived, settled[chain], out, block)
    return out


def solution(mesh):
    placed = (
        P(("parts", "dp"), "tensor"),
        P(("parts", "dp"), "tensor", None),
        P(("parts", "dp"), None, "tensor", None),
        P(("parts", "dp"), None, "tensor", None),
        P(("parts", "dp"), "tensor", None),
        P(("parts", "dp"), "tensor", None),
        P(("parts", "dp")),
        P("tensor", None),
        P("dp", None, "tensor"),
        P("dp", None, "tensor"),
        P("parts"),
        P(("parts", "dp")),
    )
    return jax.shard_map(
        per_device,
        mesh=mesh,
        in_specs=placed,
        out_specs=P(("parts", "dp"), "tensor"),
        check_vma=False,
    )
```

```python
import functools
import math

import jax
import jax.numpy as jnp
from jax import lax
from jax.experimental import pallas as pl
from jax.experimental.pallas import tpu as pltpu
from jax.sharding import PartitionSpec as P

GROUP = 4
CAP = 64
LANES = 128
MASKED = -1e30
VMEM_LIMIT = 50 * 1024 * 1024
FULL_VMEM = 61 * 1024 * 1024
SHARES = ((5, 3),)
PIECE = 512
SPLIT = 4

VMEM = pl.BlockSpec(memory_space=pltpu.VMEM)
ANY = pl.BlockSpec(memory_space=pl.ANY)
PARAMS = pltpu.CompilerParams(vmem_limit_bytes=VMEM_LIMIT)


def _dot(a, b, left=1, right=0):
    return lax.dot_general(
        a, b, (((left,), (right,)), ((), ())), preferred_element_type=jnp.float32
    )


def _iota(shape, axis):
    return lax.broadcasted_iota(jnp.int32, shape, axis)


def ring_order(count):
    return list(range(0, count, 2)) + list(range(1, count, 2))[::-1]


def column_owner(step):
    count = lax.axis_size("tensor")
    here = lax.axis_index("tensor")
    half = here // 2
    spot = jnp.where(here % 2 == 0, half, count - 1 - half)
    spot = lax.rem(spot - 1 - step + 2 * count, count)
    return jnp.where(2 * spot < count, 2 * spot, 2 * (count - spot) - 1)


def chain_columns(width):
    shares = next(s for s in SHARES if width % (sum(s) * LANES) == 0)
    unit = width // sum(shares)
    return [(sum(shares[:c]) * unit, shares[c] * unit) for c in range(len(shares))]


class Weights:
    def __init__(self, w_ref, held, sems, first, width):
        depth = w_ref.shape[0] // SPLIT
        first = pl.multiple_of(first, LANES)
        self.held = held
        self.copies = [
            pltpu.make_async_copy(
                w_ref.at[pl.ds(s * depth, depth), pl.ds(first, width)],
                held.at[pl.ds(s * depth, depth), :],
                sems.at[s],
            )
            for s in range(SPLIT)
        ]

    def start(self):
        for copy in self.copies:
            copy.start()

    def wait(self):
        for copy in self.copies:
            copy.wait()

    def products(self, a):
        width = self.held.shape[1]
        for at in range(0, width, PIECE):
            columns = pl.ds(at, min(PIECE, width - at))
            yield columns, _dot(a, self.held[:, columns])

    @staticmethod
    def scratch(depth, width):
        return [
            pltpu.VMEM((depth, width), jnp.bfloat16),
            pltpu.SemaphoreType.DMA((SPLIT,)),
        ]


def row_max(arrays):
    full = None
    tops = []
    for x in arrays:
        width = x.shape[1]
        if width % LANES:
            tops.append(jnp.max(x, axis=1, keepdims=True))
            continue
        for at in range(0, width, LANES):
            tile = x[:, at : at + LANES]
            full = tile if full is None else jnp.maximum(full, tile)
    if full is not None:
        tops.append(jnp.max(full, axis=1, keepdims=True))
    return functools.reduce(jnp.maximum, tops)


def attend_kernel(
    heads, kv, cache, steps, block, replicas, slots,
    len_hbm, adapter_hbm, placement_hbm, q_hbm, k_hbm, v_hbm, nk_hbm, nv_hbm, w_hbm,
    *refs,
):
    a_ref, out_ref, chosen_ref, *sent_refs = refs[: 3 + replicas]
    (
        len_ref, adapter_ref, placement_ref, q_ref, k_ref, v_ref, nk_ref, nv_ref,
        scores_ref, mixed_ref, sems, small_sems, w_held, w_sems,
    ) = refs[3 + replicas :]
    requests = len_ref.shape[1]
    width = q_hbm.shape[1]
    per = requests // steps
    groups = per // GROUP
    group_rows = GROUP * heads
    group_cols = GROUP * cache * kv
    per_kv = heads // kv
    scale = math.log2(math.e) / math.sqrt(width)

    def part(kind, step):
        source, target, count = (
            (q_hbm, q_ref, heads),
            (k_hbm, k_ref, cache * kv),
            (v_hbm, v_ref, cache * kv),
        )[kind]
        rows = pl.ds(step * per * count, per * count)
        return pltpu.make_async_copy(source.at[rows, :], target.at[rows, :], sems.at[kind, step])

    small = [
        pltpu.make_async_copy(source, target, small_sems.at[i])
        for i, (source, target) in enumerate(
            (
                (nk_hbm, nk_ref),
                (len_hbm, len_ref),
                (nv_hbm, nv_ref),
                (adapter_hbm, adapter_ref),
                (placement_hbm, placement_ref),
            )
        )
    ]
    chunk = out_ref.shape[1]
    weights = Weights(w_hbm, w_held, w_sems, column_owner(0) * block, chunk)
    part(0, 0).start()
    part(1, 0).start()
    for copy in small[:2]:
        copy.start()
    part(0, 1).start()
    part(1, 1).start()
    part(2, 0).start()
    for copy in small[2:]:
        copy.start()
    part(2, 1).start()
    for step in range(2, steps):
        for kind in range(3):
            part(kind, step).start()
    weights.start()

    row = _iota((group_rows, group_cols), 0)
    col = _iota((group_rows, group_cols), 1)
    same = (row // heads == col // (cache * kv)) & ((row % heads) // per_kv == col % kv)
    own_bias = jnp.where(same, 0.0, MASKED)
    row = _iota((group_rows, per * kv), 0)
    col = _iota((group_rows, per * kv), 1)
    fresh_kv = (row % heads) // per_kv == col % kv
    fresh_distance = col // kv - row // heads
    ones = jnp.ones((max(group_cols, per * kv), LANES), jnp.bfloat16)

    def arrive(step):
        part(0, step).wait()
        part(1, step).wait()

    def scores(step):
        side = step % 2
        q_at = step * per * heads
        k_at = step * per * cache * kv
        for g in range(groups):
            scores_ref[side, pl.ds(g * group_rows, group_rows), pl.ds(0, group_cols)] = _dot(
                q_ref[pl.ds(q_at + g * group_rows, group_rows), :],
                k_ref[pl.ds(k_at + g * group_cols, group_cols), :],
                1,
                1,
            )
        scores_ref[side, :, pl.ds(group_cols, per * kv)] = _dot(
            q_ref[pl.ds(q_at, per * heads), :], nk_ref[pl.ds(step * per * kv, per * kv), :], 1, 1
        )

    for copy in small:
        copy.wait()
    plan_routes(slots, adapter_ref, placement_ref, chosen_ref, sent_refs)
    counts = len_ref[...].astype(jnp.float32)
    all_groups = requests // GROUP
    of_group = _iota((all_groups, requests), 1) // GROUP == _iota((all_groups, requests), 0)
    counts = jnp.where(of_group, counts, 0.0).astype(jnp.bfloat16)
    spread = _iota((requests, group_cols), 0) % GROUP == _iota((requests, group_cols), 1) // (cache * kv)
    counts = _dot(counts, spread.astype(jnp.bfloat16))
    position = (_iota((all_groups, group_cols), 1) // kv) % cache
    length_bias = jnp.where(position.astype(jnp.float32) < counts, 0.0, MASKED)

    arrive(0)
    scores(0)
    for step in range(steps):
        side = step % 2
        k_at = step * per * cache * kv
        f_at = step * per * kv
        part(2, step).wait()
        if step + 1 < steps:
            arrive(step + 1)
            scores(step + 1)
        held = []
        fresh = []
        for g in range(groups):
            rows = pl.ds(g * group_rows, group_rows)
            bias = own_bias + length_bias[step * groups + g : step * groups + g + 1, :]
            cached = scores_ref[side, rows, pl.ds(0, group_cols)] + bias
            new = scores_ref[side, rows, pl.ds(group_cols, per * kv)]
            new = jnp.where(fresh_kv & (fresh_distance == g * GROUP), new, MASKED)
            top = row_max([cached, new])
            cached = jnp.exp2((cached - top) * scale).astype(jnp.bfloat16)
            fresh.append(jnp.exp2((new - top) * scale).astype(jnp.bfloat16))
            values = v_ref[pl.ds(k_at + g * group_cols, group_cols), :]
            held.append(_dot(cached, jnp.concatenate([values, ones[:group_cols]], axis=1)))
        values = jnp.concatenate([nv_ref[pl.ds(f_at, per * kv), :], ones[: per * kv]], axis=1)
        fresh = _dot(jnp.concatenate(fresh, axis=0), values)
        for g in range(groups):
            rows = slice(g * group_rows, (g + 1) * group_rows)
            mixed = fresh[rows, :] + held[g]
            mixed_ref[side, rows, :] = mixed[:, :width] / mixed[:, width:]
        for h in range(heads):
            a_ref[pl.ds(step * per, per), pl.ds(h * width, width)] = mixed_ref[
                side, pl.ds(h, per, stride=heads), :
            ].astype(jnp.bfloat16)

    weights.wait()
    for columns, product in weights.products(a_ref[...]):
        out_ref[:, columns] = product.astype(jnp.bfloat16)
    rows = _dot(chosen_ref[...], a_ref[...]).astype(jnp.bfloat16)
    for r, sent_ref in enumerate(sent_refs):
        sent_ref[:, pl.ds(0, heads * width)] = rows[r * CAP : (r + 1) * CAP, :]


def plan_routes(slots, adapter_ref, placement_ref, chosen_ref, sent_refs):
    replicas = len(sent_refs)
    requests = adapter_ref.shape[1]
    table = placement_ref.shape[1]
    matches = _iota((table, requests), 0) == adapter_ref[...]
    placed = jnp.broadcast_to(placement_ref[...].astype(jnp.float32), (8, table))
    slot = _dot(placed.astype(jnp.bfloat16), matches.astype(jnp.bfloat16)).astype(jnp.int32)
    slot = slot[0:1, :]
    holder = (slot // slots) ^ lax.axis_index("dp")
    inside = slot % slots
    of_holder = _iota((max(replicas, 8), requests), 0) == holder
    earlier = _iota((requests, requests), 0) < _iota((requests, requests), 1)
    before = _dot(of_holder.astype(jnp.bfloat16), earlier.astype(jnp.bfloat16))
    before = jnp.sum(jnp.where(of_holder, before, 0.0), axis=0, keepdims=True).astype(jnp.int32)
    target = holder * CAP + before
    here = _iota((replicas * CAP, requests), 0) == target
    chosen_ref[...] = here.astype(jnp.bfloat16)
    inner = jnp.sum(jnp.where(here, inside.astype(jnp.float32), 0.0), axis=1, keepdims=True)
    inner = jnp.broadcast_to(inner, (replicas * CAP, LANES)).astype(jnp.bfloat16)
    width = sent_refs[0].shape[1] - LANES
    for r, sent_ref in enumerate(sent_refs):
        sent_ref[:, pl.ds(width, LANES)] = inner[r * CAP : (r + 1) * CAP, :]


def attend(
    query, keys, values, new_key, new_value, lengths, weight, request_adapter, placement,
    block, replicas, slots,
):
    requests, heads, width = query.shape
    cache, kv = keys.shape[1], keys.shape[2]
    steps = 4
    per = requests // steps
    columns = GROUP * cache * kv + per * kv
    features = heads * width
    chunk = chain_columns(block)[0][1]
    small = [lengths.reshape(1, -1), request_adapter.reshape(1, -1), placement.reshape(1, -1)]
    operands = [
        query.reshape(requests * heads, width),
        keys.reshape(requests * cache * kv, width),
        values.reshape(requests * cache * kv, width),
        new_key.reshape(requests * kv, width),
        new_value.reshape(requests * kv, width),
    ]
    return pl.pallas_call(
        functools.partial(attend_kernel, heads, kv, cache, steps, block, replicas, slots),
        in_specs=[ANY] * 9,
        out_specs=[VMEM] * (3 + replicas),
        out_shape=[
            jax.ShapeDtypeStruct((requests, features), jnp.bfloat16),
            jax.ShapeDtypeStruct((requests, chunk), jnp.bfloat16),
            jax.ShapeDtypeStruct((replicas * CAP, requests), jnp.bfloat16),
        ]
        + [jax.ShapeDtypeStruct((CAP, features + LANES), jnp.bfloat16)] * replicas,
        scratch_shapes=[pltpu.VMEM(x.shape, x.dtype) for x in small + operands]
        + [
            pltpu.VMEM((2, per * heads, columns), jnp.float32),
            pltpu.VMEM((2, per * heads, width), jnp.float32),
            pltpu.SemaphoreType.DMA((3, steps)),
            pltpu.SemaphoreType.DMA((5,)),
        ]
        + Weights.scratch(weight.shape[0], chunk),
        compiler_params=pltpu.CompilerParams(vmem_limit_bytes=FULL_VMEM),
        name="attend",
    )(*small, *operands, weight)


def hop_kernel(step, block, start, arriving, after, *refs):
    if arriving:
        arrived_ref, *refs = refs
    a_ref, w_hbm, *refs = refs
    out_ref, held, sems = refs[after:]
    chunk = out_ref.shape[1]
    first = column_owner(step) * block + start
    weights = Weights(w_hbm, held, sems, first, chunk)
    weights.start()
    weights.wait()
    for columns, product in weights.products(a_ref[...]):
        if arriving:
            product = product + arrived_ref[:, columns].astype(jnp.float32)
        out_ref[:, columns] = product.astype(jnp.bfloat16)


def hop(step, chain, arrived, attended, weight, block, after=()):
    arriving = arrived is not None
    start, chunk = chain_columns(block)[chain]
    operands = ([arrived] if arriving else []) + [attended, weight, *after]
    return pl.pallas_call(
        functools.partial(hop_kernel, step, block, start, arriving, len(after)),
        in_specs=[VMEM] * (1 + arriving) + [ANY] + [ANY] * len(after),
        out_specs=VMEM,
        out_shape=jax.ShapeDtypeStruct((attended.shape[0], chunk), jnp.bfloat16),
        scratch_shapes=Weights.scratch(weight.shape[0], chunk),
        compiler_params=PARAMS,
        name="hop",
    )(*operands)


def down_kernel(replicas, after, *refs):
    received = refs[:replicas]
    down_ref = refs[replicas]
    mid_ref, inside_ref = refs[replicas + 1 + after :]
    slots, rank, width = down_ref.shape
    rows = jnp.concatenate([r[:, pl.ds(0, width)] for r in received], axis=0)
    inside = jnp.concatenate([r[:, pl.ds(width, LANES)] for r in received], axis=0)
    inside_ref[...] = inside
    projected = _dot(rows, down_ref[...].reshape(slots * rank, width), 1, 1)
    lane_slot = _iota(projected.shape, 1) // rank
    mine = lane_slot == inside[:, 0:1].astype(jnp.int32)
    projected = jnp.where(mine, projected, 0.0).astype(jnp.bfloat16)
    beside = LANES // rank
    some = projected.shape[0] // beside
    packed = 0.0
    for b in range(beside):
        lane = _iota((slots * rank, LANES), 1) - b * rank
        fold = _iota((slots * rank, LANES), 0) % rank == lane
        packed = packed + _dot(projected[b * some : (b + 1) * some, :], fold.astype(jnp.bfloat16))
    mid_ref[...] = packed.astype(jnp.bfloat16)


def down(received, slot_down_weight, after=()):
    replicas = len(received)
    rows = replicas * CAP
    return pl.pallas_call(
        functools.partial(down_kernel, replicas, len(after)),
        in_specs=[VMEM] * (replicas + 1) + [ANY] * len(after),
        out_specs=[VMEM, VMEM],
        out_shape=[
            jax.ShapeDtypeStruct((rows * slot_down_weight.shape[1] // LANES, LANES), jnp.bfloat16),
            jax.ShapeDtypeStruct((rows, LANES), jnp.bfloat16),
        ],
        compiler_params=PARAMS,
        name="down",
    )(*received, slot_down_weight, *after)


def up_kernel(parts, after, *refs):
    mids = refs[:parts]
    inside_ref, up_ref = refs[parts : parts + 2]
    out_refs = refs[parts + 2 + after :]
    slots, rank, width = up_ref.shape
    mid = mids[0][...].astype(jnp.float32)
    for m in mids[1:]:
        mid = mid + m[...].astype(jnp.float32)
    mid = mid.astype(jnp.bfloat16)
    wide = []
    for b in range(LANES // rank):
        lane = _iota((LANES, slots * rank), 0) - b * rank
        spread = _iota((LANES, slots * rank), 1) % rank == lane
        wide.append(_dot(mid, spread.astype(jnp.bfloat16)))
    wide = jnp.concatenate(wide, axis=0)
    mine = _iota(wide.shape, 1) // rank == inside_ref[:, 0:1].astype(jnp.int32)
    wide = jnp.where(mine, wide, 0.0).astype(jnp.bfloat16)
    delta = _dot(wide, up_ref[...].reshape(slots * rank, width)).astype(jnp.bfloat16)
    for r, out_ref in enumerate(out_refs):
        out_ref[...] = delta[r * CAP : (r + 1) * CAP, :]


def up(mids, inside, slot_up_weight, after=()):
    rows = inside.shape[0]
    replicas = rows // CAP
    width = slot_up_weight.shape[2]
    return pl.pallas_call(
        functools.partial(up_kernel, len(mids), len(after)),
        in_specs=[VMEM] * (len(mids) + 2) + [ANY] * len(after),
        out_specs=[VMEM] * replicas,
        out_shape=[jax.ShapeDtypeStruct((CAP, width), jnp.bfloat16)] * replicas,
        compiler_params=PARAMS,
        name="up",
    )(*mids, inside, slot_up_weight, *after)


def settle_kernel(step, replicas, after, *refs):
    returned = refs[:replicas]
    chosen_ref, a_ref, residual_ref, w_hbm = refs[replicas : replicas + 4]
    *out_refs, held, sems = refs[replicas + 4 + after :]
    width = residual_ref.shape[1]
    weights = Weights(w_hbm, held, sems, column_owner(step) * width, width)
    weights.start()
    rows = jnp.concatenate([r[...] for r in returned], axis=0)
    delta = _dot(chosen_ref[...], rows, 0, 0)
    total = residual_ref[...].astype(jnp.float32) + delta
    weights.wait()
    total = total + jnp.concatenate([p for _, p in weights.products(a_ref[...])], axis=1)
    for (start, chunk), out_ref in zip(chain_columns(width), out_refs):
        out_ref[...] = total[:, start : start + chunk]


def settle(step, returned, chosen, attended, residual, weight, after=()):
    replicas = len(returned)
    rows, width = residual.shape
    chains = chain_columns(width)
    return pl.pallas_call(
        functools.partial(settle_kernel, step, replicas, len(after)),
        in_specs=[VMEM] * (replicas + 3) + [ANY] * (1 + len(after)),
        out_specs=[VMEM] * len(chains),
        out_shape=[jax.ShapeDtypeStruct((rows, chunk), jnp.float32) for _, chunk in chains],
        scratch_shapes=Weights.scratch(weight.shape[0], width),
        compiler_params=PARAMS,
        name="settle",
    )(*returned, chosen, attended, residual, weight, *after)


def finish_kernel(start, arrived_ref, settled_ref, *refs):
    out_hbm, held, sems = refs[-3:]
    rows, chunk = arrived_ref.shape
    half = rows // 2
    copies = []
    for i in range(2):
        part = pl.ds(i * half, half)
        total = settled_ref[part, :] + arrived_ref[part, :].astype(jnp.float32)
        held[part, :] = total.astype(jnp.bfloat16)
        target = out_hbm.at[part, pl.ds(start, chunk)]
        copies.append(pltpu.make_async_copy(held.at[part, :], target, sems.at[i]))
        copies[-1].start()
    for copy in copies:
        copy.wait()


def finish(chain, arrived, settled, earlier, width):
    rows = arrived.shape[0]
    start, chunk = chain_columns(width)[chain]
    operands = [arrived, settled] + ([earlier] if earlier is not None else [])
    return pl.pallas_call(
        functools.partial(finish_kernel, start),
        in_specs=[VMEM, VMEM] + ([ANY] if earlier is not None else []),
        out_specs=ANY,
        out_shape=jax.ShapeDtypeStruct((rows, width), jnp.bfloat16),
        input_output_aliases={2: 0} if earlier is not None else {},
        scratch_shapes=[
            pltpu.VMEM((rows, chunk), jnp.bfloat16),
            pltpu.SemaphoreType.DMA((2,)),
        ],
        compiler_params=PARAMS,
        name="finish",
    )(*operands)


def hold_kernel(*refs):
    pass


def hold(x, after):
    return pl.pallas_call(
        hold_kernel,
        in_specs=[ANY] * (1 + len(after)),
        out_specs=ANY,
        out_shape=jax.ShapeDtypeStruct(x.shape, x.dtype),
        input_output_aliases={0: 0},
        compiler_params=PARAMS,
        name="hold",
    )(x, *after)


def per_device(
    residual,
    query,
    cached_key_rows,
    cached_value_rows,
    new_token_key,
    new_token_value,
    lengths,
    output_weight,
    slot_down_weight,
    slot_up_weight,
    placement,
    request_adapter,
):
    count = lax.axis_size("tensor")
    replicas = lax.axis_size("dp")
    block = residual.shape[1]
    order = ring_order(count)
    ring = [(order[p], order[(p + 1) % count]) for p in range(count)]

    def exchange(blocks):
        moved = [
            lax.ppermute(blocks[r], "dp", [(i, i ^ r) for i in range(replicas)])
            for r in range(1, replicas)
        ]
        return [blocks[0]] + moved

    def forward(x):
        return lax.ppermute(x, "tensor", ring)

    def next_hop(step, chain, after):
        arrived = forward(travelling[chain])
        travelling[chain] = hop(step, chain, arrived, attended, output_weight, block, after)

    attended, first, chosen, *leaving = attend(
        query, cached_key_rows, cached_value_rows, new_token_key, new_token_value, lengths,
        output_weight, request_adapter, placement, block, replicas, slot_down_weight.shape[0],
    )
    second = hop(0, 1, None, attended, output_weight, block)
    rows_here = exchange(leaving)
    mid, inside = down(rows_here, slot_down_weight, after=[second])
    rank_sums = [mid] + [
        lax.ppermute(mid, "tensor", [(i, (i + k) % count) for i in range(count)])
        for k in range(1, count)
    ]

    arrived = forward(first)
    second = hold(second, after=[mid, arrived])
    travelling = [
        hop(1, 0, arrived, attended, output_weight, block, after=rank_sums + [second]),
        second,
    ]
    next_hop(1, 1, after=())
    deltas = up(rank_sums, inside, slot_up_weight, after=[travelling[1]])
    returned = exchange(deltas)
    for step in range(2, count - 1):
        for chain in range(2):
            next_hop(step, chain, after=returned if (step, chain) == (2, 0) else ())
    settled = settle(
        count - 1, returned, chosen, attended, residual, output_weight, after=[travelling[1]]
    )
    out = None
    for chain in range(2):
        arrived = forward(travelling[chain])
        out = finish(chain, arrived, settled[chain], out, block)
    return out


def solution(mesh):
    placed = (
        P(("parts", "dp"), "tensor"),
        P(("parts", "dp"), "tensor", None),
        P(("parts", "dp"), None, "tensor", None),
        P(("parts", "dp"), None, "tensor", None),
        P(("parts", "dp"), "tensor", None),
        P(("parts", "dp"), "tensor", None),
        P(("parts", "dp")),
        P("tensor", None),
        P("dp", None, "tensor"),
        P("dp", None, "tensor"),
        P("parts"),
        P(("parts", "dp")),
    )
    return jax.shard_map(
        per_device,
        mesh=mesh,
        in_specs=placed,
        out_specs=P(("parts", "dp"), "tensor"),
        check_vma=False,
    )
```

```python
import functools
import math

import jax
import jax.numpy as jnp
from jax import lax
from jax.experimental import pallas as pl
from jax.experimental.pallas import tpu as pltpu
from jax.sharding import PartitionSpec as P

GROUP = 4
CAP = 64
LANES = 128
MASKED = -1e30
VMEM_LIMIT = 50 * 1024 * 1024
FULL_VMEM = 61 * 1024 * 1024
SHARES = ((5, 3),)
PIECE = 512
SPLIT = 4

VMEM = pl.BlockSpec(memory_space=pltpu.VMEM)
ANY = pl.BlockSpec(memory_space=pl.ANY)
PARAMS = pltpu.CompilerParams(vmem_limit_bytes=VMEM_LIMIT)


def _dot(a, b, left=1, right=0):
    return lax.dot_general(
        a, b, (((left,), (right,)), ((), ())), preferred_element_type=jnp.float32
    )


def _iota(shape, axis):
    return lax.broadcasted_iota(jnp.int32, shape, axis)


def ring_order(count):
    return list(range(0, count, 2)) + list(range(1, count, 2))[::-1]


def column_owner(step):
    count = lax.axis_size("tensor")
    here = lax.axis_index("tensor")
    half = here // 2
    spot = jnp.where(here % 2 == 0, half, count - 1 - half)
    spot = lax.rem(spot - 1 - step + 2 * count, count)
    return jnp.where(2 * spot < count, 2 * spot, 2 * (count - spot) - 1)


def chain_columns(width):
    shares = next(s for s in SHARES if width % (sum(s) * LANES) == 0)
    unit = width // sum(shares)
    return [(sum(shares[:c]) * unit, shares[c] * unit) for c in range(len(shares))]


class Weights:
    def __init__(self, w_ref, held, sems, first, width):
        depth = w_ref.shape[0] // SPLIT
        first = pl.multiple_of(first, LANES)
        self.held = held
        self.copies = [
            pltpu.make_async_copy(
                w_ref.at[pl.ds(s * depth, depth), pl.ds(first, width)],
                held.at[pl.ds(s * depth, depth), :],
                sems.at[s],
            )
            for s in range(SPLIT)
        ]

    def start(self):
        for copy in self.copies:
            copy.start()

    def wait(self):
        for copy in self.copies:
            copy.wait()

    def products(self, a):
        width = self.held.shape[1]
        for at in range(0, width, PIECE):
            columns = pl.ds(at, min(PIECE, width - at))
            yield columns, _dot(a, self.held[:, columns])

    @staticmethod
    def scratch(depth, width):
        return [
            pltpu.VMEM((depth, width), jnp.bfloat16),
            pltpu.SemaphoreType.DMA((SPLIT,)),
        ]


def row_max(arrays):
    full = None
    tops = []
    for x in arrays:
        width = x.shape[1]
        if width % LANES:
            tops.append(jnp.max(x, axis=1, keepdims=True))
            continue
        for at in range(0, width, LANES):
            tile = x[:, at : at + LANES]
            full = tile if full is None else jnp.maximum(full, tile)
    if full is not None:
        tops.append(jnp.max(full, axis=1, keepdims=True))
    return functools.reduce(jnp.maximum, tops)


def attend_kernel(
    heads, kv, cache, steps, block, replicas, slots,
    len_hbm, adapter_hbm, placement_hbm, q_hbm, k_hbm, v_hbm, nk_hbm, nv_hbm, w_hbm,
    *refs,
):
    a_hbm, out_hbm, chosen_hbm, *sent_hbm = refs[: 3 + replicas]
    (
        a_ref, out_ref, chosen_ref, sent_ref, out_sems,
        len_ref, adapter_ref, placement_ref, q_ref, k_ref, v_ref, nk_ref, nv_ref,
        scores_ref, mixed_ref, sems, small_sems, w_held, w_sems,
    ) = refs[3 + replicas :]
    requests = len_ref.shape[1]
    width = q_hbm.shape[1]
    per = requests // steps
    groups = per // GROUP
    group_rows = GROUP * heads
    group_cols = GROUP * cache * kv
    per_kv = heads // kv
    scale = math.log2(math.e) / math.sqrt(width)

    def part(kind, step):
        source, target, count = (
            (q_hbm, q_ref, heads),
            (k_hbm, k_ref, cache * kv),
            (v_hbm, v_ref, cache * kv),
        )[kind]
        rows = pl.ds(step * per * count, per * count)
        return pltpu.make_async_copy(source.at[rows, :], target.at[rows, :], sems.at[kind, step])

    small = [
        pltpu.make_async_copy(source, target, small_sems.at[i])
        for i, (source, target) in enumerate(
            (
                (nk_hbm, nk_ref),
                (len_hbm, len_ref),
                (nv_hbm, nv_ref),
                (adapter_hbm, adapter_ref),
                (placement_hbm, placement_ref),
            )
        )
    ]
    leaving = []

    def leave(source, target):
        copy = pltpu.make_async_copy(source, target, out_sems.at[len(leaving)])
        copy.start()
        leaving.append(copy)

    chunk = out_ref.shape[1]
    weights = Weights(w_hbm, w_held, w_sems, column_owner(0) * block, chunk)
    part(0, 0).start()
    part(1, 0).start()
    for copy in small[:2]:
        copy.start()
    part(0, 1).start()
    part(1, 1).start()
    part(2, 0).start()
    for copy in small[2:]:
        copy.start()
    part(2, 1).start()
    for step in range(2, steps):
        for kind in range(3):
            part(kind, step).start()
    weights.start()

    row = _iota((group_rows, group_cols), 0)
    col = _iota((group_rows, group_cols), 1)
    same = (row // heads == col // (cache * kv)) & ((row % heads) // per_kv == col % kv)
    own_bias = jnp.where(same, 0.0, MASKED)
    row = _iota((group_rows, per * kv), 0)
    col = _iota((group_rows, per * kv), 1)
    fresh_kv = (row % heads) // per_kv == col % kv
    fresh_distance = col // kv - row // heads
    ones = jnp.ones((max(group_cols, per * kv), LANES), jnp.bfloat16)

    def arrive(step):
        part(0, step).wait()
        part(1, step).wait()

    def scores(step):
        side = step % 2
        q_at = step * per * heads
        k_at = step * per * cache * kv
        for g in range(groups):
            scores_ref[side, pl.ds(g * group_rows, group_rows), pl.ds(0, group_cols)] = _dot(
                q_ref[pl.ds(q_at + g * group_rows, group_rows), :],
                k_ref[pl.ds(k_at + g * group_cols, group_cols), :],
                1,
                1,
            )
        scores_ref[side, :, pl.ds(group_cols, per * kv)] = _dot(
            q_ref[pl.ds(q_at, per * heads), :], nk_ref[pl.ds(step * per * kv, per * kv), :], 1, 1
        )

    for copy in small:
        copy.wait()
    plan_routes(slots, adapter_ref, placement_ref, chosen_ref, sent_ref)
    leave(chosen_ref, chosen_hbm)
    counts = len_ref[...].astype(jnp.float32)
    all_groups = requests // GROUP
    of_group = _iota((all_groups, requests), 1) // GROUP == _iota((all_groups, requests), 0)
    counts = jnp.where(of_group, counts, 0.0).astype(jnp.bfloat16)
    spread = _iota((requests, group_cols), 0) % GROUP == _iota((requests, group_cols), 1) // (cache * kv)
    counts = _dot(counts, spread.astype(jnp.bfloat16))
    position = (_iota((all_groups, group_cols), 1) // kv) % cache
    length_bias = jnp.where(position.astype(jnp.float32) < counts, 0.0, MASKED)

    arrive(0)
    scores(0)
    for step in range(steps):
        side = step % 2
        k_at = step * per * cache * kv
        f_at = step * per * kv
        part(2, step).wait()
        if step + 1 < steps:
            arrive(step + 1)
            scores(step + 1)
        held = []
        fresh = []
        for g in range(groups):
            rows = pl.ds(g * group_rows, group_rows)
            bias = own_bias + length_bias[step * groups + g : step * groups + g + 1, :]
            cached = scores_ref[side, rows, pl.ds(0, group_cols)] + bias
            new = scores_ref[side, rows, pl.ds(group_cols, per * kv)]
            new = jnp.where(fresh_kv & (fresh_distance == g * GROUP), new, MASKED)
            top = row_max([cached, new])
            cached = jnp.exp2((cached - top) * scale).astype(jnp.bfloat16)
            fresh.append(jnp.exp2((new - top) * scale).astype(jnp.bfloat16))
            values = v_ref[pl.ds(k_at + g * group_cols, group_cols), :]
            held.append(_dot(cached, jnp.concatenate([values, ones[:group_cols]], axis=1)))
        values = jnp.concatenate([nv_ref[pl.ds(f_at, per * kv), :], ones[: per * kv]], axis=1)
        fresh = _dot(jnp.concatenate(fresh, axis=0), values)
        for g in range(groups):
            rows = slice(g * group_rows, (g + 1) * group_rows)
            mixed = fresh[rows, :] + held[g]
            mixed_ref[side, rows, :] = mixed[:, :width] / mixed[:, width:]
        for h in range(heads):
            a_ref[pl.ds(step * per, per), pl.ds(h * width, width)] = mixed_ref[
                side, pl.ds(h, per, stride=heads), :
            ].astype(jnp.bfloat16)
        rows = pl.ds(step * per, per)
        leave(a_ref.at[rows, :], a_hbm.at[rows, :])

    weights.wait()
    for columns, product in weights.products(a_ref[...]):
        out_ref[:, columns] = product.astype(jnp.bfloat16)
        leave(out_ref.at[:, columns], out_hbm.at[:, columns])
    sent_ref[:, pl.ds(0, heads * width)] = _dot(chosen_ref[...], a_ref[...]).astype(jnp.bfloat16)
    for r in range(replicas):
        leave(sent_ref.at[pl.ds(r * CAP, CAP), :], sent_hbm[r])
    for copy in leaving:
        copy.wait()


def plan_routes(slots, adapter_ref, placement_ref, chosen_ref, sent_ref):
    replicas = sent_ref.shape[0] // CAP
    requests = adapter_ref.shape[1]
    table = placement_ref.shape[1]
    matches = _iota((table, requests), 0) == adapter_ref[...]
    placed = jnp.broadcast_to(placement_ref[...].astype(jnp.float32), (8, table))
    slot = _dot(placed.astype(jnp.bfloat16), matches.astype(jnp.bfloat16)).astype(jnp.int32)
    slot = slot[0:1, :]
    holder = (slot // slots) ^ lax.axis_index("dp")
    inside = slot % slots
    of_holder = _iota((max(replicas, 8), requests), 0) == holder
    earlier = _iota((requests, requests), 0) < _iota((requests, requests), 1)
    before = _dot(of_holder.astype(jnp.bfloat16), earlier.astype(jnp.bfloat16))
    before = jnp.sum(jnp.where(of_holder, before, 0.0), axis=0, keepdims=True).astype(jnp.int32)
    target = holder * CAP + before
    here = _iota((replicas * CAP, requests), 0) == target
    chosen_ref[...] = here.astype(jnp.bfloat16)
    inner = jnp.sum(jnp.where(here, inside.astype(jnp.float32), 0.0), axis=1, keepdims=True)
    inner = jnp.broadcast_to(inner, (replicas * CAP, LANES)).astype(jnp.bfloat16)
    sent_ref[:, pl.ds(sent_ref.shape[1] - LANES, LANES)] = inner


def attend(
    query, keys, values, new_key, new_value, lengths, weight, request_adapter, placement,
    block, replicas, slots,
):
    requests, heads, width = query.shape
    cache, kv = keys.shape[1], keys.shape[2]
    steps = 4
    per = requests // steps
    columns = GROUP * cache * kv + per * kv
    features = heads * width
    chunk = chain_columns(block)[0][1]
    small = [lengths.reshape(1, -1), request_adapter.reshape(1, -1), placement.reshape(1, -1)]
    operands = [
        query.reshape(requests * heads, width),
        keys.reshape(requests * cache * kv, width),
        values.reshape(requests * cache * kv, width),
        new_key.reshape(requests * kv, width),
        new_value.reshape(requests * kv, width),
    ]
    return pl.pallas_call(
        functools.partial(attend_kernel, heads, kv, cache, steps, block, replicas, slots),
        in_specs=[ANY] * 9,
        out_specs=[ANY] * (3 + replicas),
        out_shape=[
            jax.ShapeDtypeStruct((requests, features), jnp.bfloat16),
            jax.ShapeDtypeStruct((requests, chunk), jnp.bfloat16),
            jax.ShapeDtypeStruct((replicas * CAP, requests), jnp.bfloat16),
        ]
        + [jax.ShapeDtypeStruct((CAP, features + LANES), jnp.bfloat16)] * replicas,
        scratch_shapes=[
            pltpu.VMEM((requests, features), jnp.bfloat16),
            pltpu.VMEM((requests, chunk), jnp.bfloat16),
            pltpu.VMEM((replicas * CAP, requests), jnp.bfloat16),
            pltpu.VMEM((replicas * CAP, features + LANES), jnp.bfloat16),
            pltpu.SemaphoreType.DMA((1 + steps + pl.cdiv(chunk, PIECE) + replicas,)),
        ]
        + [pltpu.VMEM(x.shape, x.dtype) for x in small + operands]
        + [
            pltpu.VMEM((2, per * heads, columns), jnp.float32),
            pltpu.VMEM((2, per * heads, width), jnp.float32),
            pltpu.SemaphoreType.DMA((3, steps)),
            pltpu.SemaphoreType.DMA((5,)),
        ]
        + Weights.scratch(weight.shape[0], chunk),
        compiler_params=pltpu.CompilerParams(vmem_limit_bytes=FULL_VMEM),
        name="attend",
    )(*small, *operands, weight)


def hop_kernel(step, block, start, arriving, after, *refs):
    if arriving:
        arrived_ref, *refs = refs
    a_ref, w_hbm, *refs = refs
    out_ref, held, sems = refs[after:]
    chunk = out_ref.shape[1]
    first = column_owner(step) * block + start
    weights = Weights(w_hbm, held, sems, first, chunk)
    weights.start()
    weights.wait()
    for columns, product in weights.products(a_ref[...]):
        if arriving:
            product = product + arrived_ref[:, columns].astype(jnp.float32)
        out_ref[:, columns] = product.astype(jnp.bfloat16)


def hop(step, chain, arrived, attended, weight, block, after=()):
    arriving = arrived is not None
    start, chunk = chain_columns(block)[chain]
    operands = ([arrived] if arriving else []) + [attended, weight, *after]
    return pl.pallas_call(
        functools.partial(hop_kernel, step, block, start, arriving, len(after)),
        in_specs=[VMEM] * (1 + arriving) + [ANY] + [ANY] * len(after),
        out_specs=VMEM,
        out_shape=jax.ShapeDtypeStruct((attended.shape[0], chunk), jnp.bfloat16),
        scratch_shapes=Weights.scratch(weight.shape[0], chunk),
        compiler_params=PARAMS,
        name="hop",
    )(*operands)


def down_kernel(replicas, after, *refs):
    received = refs[:replicas]
    down_ref = refs[replicas]
    mid_ref, inside_ref = refs[replicas + 1 + after :]
    slots, rank, width = down_ref.shape
    rows = jnp.concatenate([r[:, pl.ds(0, width)] for r in received], axis=0)
    inside = jnp.concatenate([r[:, pl.ds(width, LANES)] for r in received], axis=0)
    inside_ref[...] = inside
    projected = _dot(rows, down_ref[...].reshape(slots * rank, width), 1, 1)
    lane_slot = _iota(projected.shape, 1) // rank
    mine = lane_slot == inside[:, 0:1].astype(jnp.int32)
    projected = jnp.where(mine, projected, 0.0).astype(jnp.bfloat16)
    beside = LANES // rank
    some = projected.shape[0] // beside
    packed = 0.0
    for b in range(beside):
        lane = _iota((slots * rank, LANES), 1) - b * rank
        fold = _iota((slots * rank, LANES), 0) % rank == lane
        packed = packed + _dot(projected[b * some : (b + 1) * some, :], fold.astype(jnp.bfloat16))
    mid_ref[...] = packed.astype(jnp.bfloat16)


def down(received, slot_down_weight, after=()):
    replicas = len(received)
    rows = replicas * CAP
    return pl.pallas_call(
        functools.partial(down_kernel, replicas, len(after)),
        in_specs=[VMEM] * (replicas + 1) + [ANY] * len(after),
        out_specs=[VMEM, VMEM],
        out_shape=[
            jax.ShapeDtypeStruct((rows * slot_down_weight.shape[1] // LANES, LANES), jnp.bfloat16),
            jax.ShapeDtypeStruct((rows, LANES), jnp.bfloat16),
        ],
        compiler_params=PARAMS,
        name="down",
    )(*received, slot_down_weight, *after)


def up_kernel(parts, after, *refs):
    mids = refs[:parts]
    inside_ref, up_ref = refs[parts : parts + 2]
    out_refs = refs[parts + 2 + after :]
    slots, rank, width = up_ref.shape
    mid = mids[0][...].astype(jnp.float32)
    for m in mids[1:]:
        mid = mid + m[...].astype(jnp.float32)
    mid = mid.astype(jnp.bfloat16)
    wide = []
    for b in range(LANES // rank):
        lane = _iota((LANES, slots * rank), 0) - b * rank
        spread = _iota((LANES, slots * rank), 1) % rank == lane
        wide.append(_dot(mid, spread.astype(jnp.bfloat16)))
    wide = jnp.concatenate(wide, axis=0)
    mine = _iota(wide.shape, 1) // rank == inside_ref[:, 0:1].astype(jnp.int32)
    wide = jnp.where(mine, wide, 0.0).astype(jnp.bfloat16)
    delta = _dot(wide, up_ref[...].reshape(slots * rank, width)).astype(jnp.bfloat16)
    for r, out_ref in enumerate(out_refs):
        out_ref[...] = delta[r * CAP : (r + 1) * CAP, :]


def up(mids, inside, slot_up_weight, after=()):
    rows = inside.shape[0]
    replicas = rows // CAP
    width = slot_up_weight.shape[2]
    return pl.pallas_call(
        functools.partial(up_kernel, len(mids), len(after)),
        in_specs=[VMEM] * (len(mids) + 2) + [ANY] * len(after),
        out_specs=[VMEM] * replicas,
        out_shape=[jax.ShapeDtypeStruct((CAP, width), jnp.bfloat16)] * replicas,
        compiler_params=PARAMS,
        name="up",
    )(*mids, inside, slot_up_weight, *after)


def settle_kernel(step, replicas, after, *refs):
    returned = refs[:replicas]
    chosen_ref, a_ref, residual_ref, w_hbm = refs[replicas : replicas + 4]
    *out_refs, held, sems = refs[replicas + 4 + after :]
    width = residual_ref.shape[1]
    weights = Weights(w_hbm, held, sems, column_owner(step) * width, width)
    weights.start()
    rows = jnp.concatenate([r[...] for r in returned], axis=0)
    delta = _dot(chosen_ref[...], rows, 0, 0)
    total = residual_ref[...].astype(jnp.float32) + delta
    weights.wait()
    total = total + jnp.concatenate([p for _, p in weights.products(a_ref[...])], axis=1)
    for (start, chunk), out_ref in zip(chain_columns(width), out_refs):
        out_ref[...] = total[:, start : start + chunk]


def settle(step, returned, chosen, attended, residual, weight, after=()):
    replicas = len(returned)
    rows, width = residual.shape
    chains = chain_columns(width)
    return pl.pallas_call(
        functools.partial(settle_kernel, step, replicas, len(after)),
        in_specs=[VMEM] * (replicas + 3) + [ANY] * (1 + len(after)),
        out_specs=[VMEM] * len(chains),
        out_shape=[jax.ShapeDtypeStruct((rows, chunk), jnp.float32) for _, chunk in chains],
        scratch_shapes=Weights.scratch(weight.shape[0], width),
        compiler_params=PARAMS,
        name="settle",
    )(*returned, chosen, attended, residual, weight, *after)


def finish_kernel(start, arrived_ref, settled_ref, *refs):
    out_hbm, held, sems = refs[-3:]
    rows, chunk = arrived_ref.shape
    half = rows // 2
    copies = []
    for i in range(2):
        part = pl.ds(i * half, half)
        total = settled_ref[part, :] + arrived_ref[part, :].astype(jnp.float32)
        held[part, :] = total.astype(jnp.bfloat16)
        target = out_hbm.at[part, pl.ds(start, chunk)]
        copies.append(pltpu.make_async_copy(held.at[part, :], target, sems.at[i]))
        copies[-1].start()
    for copy in copies:
        copy.wait()


def finish(chain, arrived, settled, earlier, width):
    rows = arrived.shape[0]
    start, chunk = chain_columns(width)[chain]
    operands = [arrived, settled] + ([earlier] if earlier is not None else [])
    return pl.pallas_call(
        functools.partial(finish_kernel, start),
        in_specs=[VMEM, VMEM] + ([ANY] if earlier is not None else []),
        out_specs=ANY,
        out_shape=jax.ShapeDtypeStruct((rows, width), jnp.bfloat16),
        input_output_aliases={2: 0} if earlier is not None else {},
        scratch_shapes=[
            pltpu.VMEM((rows, chunk), jnp.bfloat16),
            pltpu.SemaphoreType.DMA((2,)),
        ],
        compiler_params=PARAMS,
        name="finish",
    )(*operands)


def per_device(
    residual,
    query,
    cached_key_rows,
    cached_value_rows,
    new_token_key,
    new_token_value,
    lengths,
    output_weight,
    slot_down_weight,
    slot_up_weight,
    placement,
    request_adapter,
):
    count = lax.axis_size("tensor")
    replicas = lax.axis_size("dp")
    block = residual.shape[1]
    order = ring_order(count)
    ring = [(order[p], order[(p + 1) % count]) for p in range(count)]

    def exchange(blocks):
        moved = [
            lax.ppermute(blocks[r], "dp", [(i, i ^ r) for i in range(replicas)])
            for r in range(1, replicas)
        ]
        return [blocks[0]] + moved

    def forward(x):
        return lax.ppermute(x, "tensor", ring)

    def next_hop(step, chain, after):
        arrived = forward(travelling[chain])
        travelling[chain] = hop(step, chain, arrived, attended, output_weight, block, after)

    attended, first, chosen, *leaving = attend(
        query, cached_key_rows, cached_value_rows, new_token_key, new_token_value, lengths,
        output_weight, request_adapter, placement, block, replicas, slot_down_weight.shape[0],
    )
    rows_here = exchange(leaving)
    mid, inside = down(rows_here, slot_down_weight)
    rank_sums = [mid] + [
        lax.ppermute(mid, "tensor", [(i, (i + k) % count) for i in range(count)])
        for k in range(1, count)
    ]

    arrived = forward(first)
    second = hop(0, 1, None, attended, output_weight, block, after=[mid])
    travelling = [
        hop(1, 0, arrived, attended, output_weight, block, after=rank_sums + [second]),
        second,
    ]
    next_hop(1, 1, after=())
    deltas = up(rank_sums, inside, slot_up_weight, after=[travelling[1]])
    returned = exchange(deltas)
    for step in range(2, count - 1):
        for chain in range(2):
            next_hop(step, chain, after=returned if (step, chain) == (2, 0) else ())
    settled = settle(
        count - 1, returned, chosen, attended, residual, output_weight, after=[travelling[1]]
    )
    out = None
    for chain in range(2):
        arrived = forward(travelling[chain])
        out = finish(chain, arrived, settled[chain], out, block)
    return out


def solution(mesh):
    placed = (
        P(("parts", "dp"), "tensor"),
        P(("parts", "dp"), "tensor", None),
        P(("parts", "dp"), None, "tensor", None),
        P(("parts", "dp"), None, "tensor", None),
        P(("parts", "dp"), "tensor", None),
        P(("parts", "dp"), "tensor", None),
        P(("parts", "dp")),
        P("tensor", None),
        P("dp", None, "tensor"),
        P("dp", None, "tensor"),
        P("parts"),
        P(("parts", "dp")),
    )
    return jax.shard_map(
        per_device,
        mesh=mesh,
        in_specs=placed,
        out_specs=P(("parts", "dp"), "tensor"),
        check_vma=False,
    )
```

```python
import functools
import math

import jax
import jax.numpy as jnp
from jax import lax
from jax.experimental import pallas as pl
from jax.experimental.pallas import tpu as pltpu
from jax.sharding import PartitionSpec as P

GROUP = 4
CAP = 64
LANES = 128
MASKED = -1e30
VMEM_LIMIT = 50 * 1024 * 1024
FULL_VMEM = 61 * 1024 * 1024
SHARES = ((1, 1),)
PIECE = 512
SPLIT = 4

VMEM = pl.BlockSpec(memory_space=pltpu.VMEM)
ANY = pl.BlockSpec(memory_space=pl.ANY)
PARAMS = pltpu.CompilerParams(vmem_limit_bytes=VMEM_LIMIT)


def _dot(a, b, left=1, right=0):
    return lax.dot_general(
        a, b, (((left,), (right,)), ((), ())), preferred_element_type=jnp.float32
    )


def _iota(shape, axis):
    return lax.broadcasted_iota(jnp.int32, shape, axis)


def ring_order(count):
    return list(range(0, count, 2)) + list(range(1, count, 2))[::-1]


def column_owner(step):
    count = lax.axis_size("tensor")
    here = lax.axis_index("tensor")
    half = here // 2
    spot = jnp.where(here % 2 == 0, half, count - 1 - half)
    spot = lax.rem(spot - 1 - step + 2 * count, count)
    return jnp.where(2 * spot < count, 2 * spot, 2 * (count - spot) - 1)


def chain_columns(width):
    shares = next(s for s in SHARES if width % (sum(s) * LANES) == 0)
    unit = width // sum(shares)
    return [(sum(shares[:c]) * unit, shares[c] * unit) for c in range(len(shares))]


class Weights:
    def __init__(self, w_ref, held, sems, first, width):
        depth = w_ref.shape[0] // SPLIT
        first = pl.multiple_of(first, LANES)
        self.held = held
        self.copies = [
            pltpu.make_async_copy(
                w_ref.at[pl.ds(s * depth, depth), pl.ds(first, width)],
                held.at[pl.ds(s * depth, depth), :],
                sems.at[s],
            )
            for s in range(SPLIT)
        ]

    def start(self):
        for copy in self.copies:
            copy.start()

    def wait(self):
        for copy in self.copies:
            copy.wait()

    def products(self, a):
        width = self.held.shape[1]
        for at in range(0, width, PIECE):
            columns = pl.ds(at, min(PIECE, width - at))
            yield columns, _dot(a, self.held[:, columns])

    @staticmethod
    def scratch(depth, width):
        return [
            pltpu.VMEM((depth, width), jnp.bfloat16),
            pltpu.SemaphoreType.DMA((SPLIT,)),
        ]


def row_max(arrays):
    full = None
    tops = []
    for x in arrays:
        width = x.shape[1]
        if width % LANES:
            tops.append(jnp.max(x, axis=1, keepdims=True))
            continue
        for at in range(0, width, LANES):
            tile = x[:, at : at + LANES]
            full = tile if full is None else jnp.maximum(full, tile)
    if full is not None:
        tops.append(jnp.max(full, axis=1, keepdims=True))
    return functools.reduce(jnp.maximum, tops)


def attend_kernel(
    heads, kv, cache, steps, block, replicas, slots,
    len_hbm, adapter_hbm, placement_hbm, q_hbm, k_hbm, v_hbm, nk_hbm, nv_hbm, w_hbm,
    *refs,
):
    a_hbm, out_hbm, chosen_hbm, *sent_hbm = refs[: 3 + replicas]
    (
        a_ref, out_ref, chosen_ref, sent_ref, out_sems,
        len_ref, adapter_ref, placement_ref, q_ref, k_ref, v_ref, nk_ref, nv_ref,
        scores_ref, mixed_ref, sems, small_sems, w_held, w_sems,
    ) = refs[3 + replicas :]
    requests = len_ref.shape[1]
    width = q_hbm.shape[1]
    per = requests // steps
    groups = per // GROUP
    group_rows = GROUP * heads
    group_cols = GROUP * cache * kv
    per_kv = heads // kv
    scale = math.log2(math.e) / math.sqrt(width)

    def part(kind, step):
        source, target, count = (
            (q_hbm, q_ref, heads),
            (k_hbm, k_ref, cache * kv),
            (v_hbm, v_ref, cache * kv),
        )[kind]
        rows = pl.ds(step * per * count, per * count)
        return pltpu.make_async_copy(source.at[rows, :], target.at[rows, :], sems.at[kind, step])

    small = [
        pltpu.make_async_copy(source, target, small_sems.at[i])
        for i, (source, target) in enumerate(
            (
                (nk_hbm, nk_ref),
                (len_hbm, len_ref),
                (nv_hbm, nv_ref),
                (adapter_hbm, adapter_ref),
                (placement_hbm, placement_ref),
            )
        )
    ]
    leaving = []

    def leave(source, target):
        copy = pltpu.make_async_copy(source, target, out_sems.at[len(leaving)])
        copy.start()
        leaving.append(copy)

    chunk = out_ref.shape[1]
    weights = Weights(w_hbm, w_held, w_sems, column_owner(0) * block, chunk)
    part(0, 0).start()
    part(1, 0).start()
    for copy in small[:2]:
        copy.start()
    part(0, 1).start()
    part(1, 1).start()
    part(2, 0).start()
    for copy in small[2:]:
        copy.start()
    part(2, 1).start()
    for step in range(2, steps):
        for kind in range(3):
            part(kind, step).start()
    weights.start()

    row = _iota((group_rows, group_cols), 0)
    col = _iota((group_rows, group_cols), 1)
    same = (row // heads == col // (cache * kv)) & ((row % heads) // per_kv == col % kv)
    own_bias = jnp.where(same, 0.0, MASKED)
    row = _iota((group_rows, per * kv), 0)
    col = _iota((group_rows, per * kv), 1)
    fresh_kv = (row % heads) // per_kv == col % kv
    fresh_distance = col // kv - row // heads
    ones = jnp.ones((max(group_cols, per * kv), LANES), jnp.bfloat16)

    def arrive(step):
        part(0, step).wait()
        part(1, step).wait()

    def scores(step):
        side = step % 2
        q_at = step * per * heads
        k_at = step * per * cache * kv
        for g in range(groups):
            scores_ref[side, pl.ds(g * group_rows, group_rows), pl.ds(0, group_cols)] = _dot(
                q_ref[pl.ds(q_at + g * group_rows, group_rows), :],
                k_ref[pl.ds(k_at + g * group_cols, group_cols), :],
                1,
                1,
            )
        scores_ref[side, :, pl.ds(group_cols, per * kv)] = _dot(
            q_ref[pl.ds(q_at, per * heads), :], nk_ref[pl.ds(step * per * kv, per * kv), :], 1, 1
        )

    for copy in small:
        copy.wait()
    plan_routes(slots, adapter_ref, placement_ref, chosen_ref, sent_ref)
    leave(chosen_ref, chosen_hbm)
    counts = len_ref[...].astype(jnp.float32)
    all_groups = requests // GROUP
    of_group = _iota((all_groups, requests), 1) // GROUP == _iota((all_groups, requests), 0)
    counts = jnp.where(of_group, counts, 0.0).astype(jnp.bfloat16)
    spread = _iota((requests, group_cols), 0) % GROUP == _iota((requests, group_cols), 1) // (cache * kv)
    counts = _dot(counts, spread.astype(jnp.bfloat16))
    position = (_iota((all_groups, group_cols), 1) // kv) % cache
    length_bias = jnp.where(position.astype(jnp.float32) < counts, 0.0, MASKED)

    arrive(0)
    scores(0)
    for step in range(steps):
        side = step % 2
        k_at = step * per * cache * kv
        f_at = step * per * kv
        part(2, step).wait()
        if step + 1 < steps:
            arrive(step + 1)
            scores(step + 1)
        held = []
        fresh = []
        for g in range(groups):
            rows = pl.ds(g * group_rows, group_rows)
            bias = own_bias + length_bias[step * groups + g : step * groups + g + 1, :]
            cached = scores_ref[side, rows, pl.ds(0, group_cols)] + bias
            new = scores_ref[side, rows, pl.ds(group_cols, per * kv)]
            new = jnp.where(fresh_kv & (fresh_distance == g * GROUP), new, MASKED)
            top = row_max([cached, new])
            cached = jnp.exp2((cached - top) * scale).astype(jnp.bfloat16)
            fresh.append(jnp.exp2((new - top) * scale).astype(jnp.bfloat16))
            values = v_ref[pl.ds(k_at + g * group_cols, group_cols), :]
            held.append(_dot(cached, jnp.concatenate([values, ones[:group_cols]], axis=1)))
        values = jnp.concatenate([nv_ref[pl.ds(f_at, per * kv), :], ones[: per * kv]], axis=1)
        fresh = _dot(jnp.concatenate(fresh, axis=0), values)
        for g in range(groups):
            rows = slice(g * group_rows, (g + 1) * group_rows)
            mixed = fresh[rows, :] + held[g]
            mixed_ref[side, rows, :] = mixed[:, :width] / mixed[:, width:]
        for h in range(heads):
            a_ref[pl.ds(step * per, per), pl.ds(h * width, width)] = mixed_ref[
                side, pl.ds(h, per, stride=heads), :
            ].astype(jnp.bfloat16)
        rows = pl.ds(step * per, per)
        leave(a_ref.at[rows, :], a_hbm.at[rows, :])

    weights.wait()
    for columns, product in weights.products(a_ref[...]):
        out_ref[:, columns] = product.astype(jnp.bfloat16)
        leave(out_ref.at[:, columns], out_hbm.at[:, columns])
    sent_ref[:, pl.ds(0, heads * width)] = _dot(chosen_ref[...], a_ref[...]).astype(jnp.bfloat16)
    for r in range(replicas):
        leave(sent_ref.at[pl.ds(r * CAP, CAP), :], sent_hbm[r])
    for copy in leaving:
        copy.wait()


def plan_routes(slots, adapter_ref, placement_ref, chosen_ref, sent_ref):
    replicas = sent_ref.shape[0] // CAP
    requests = adapter_ref.shape[1]
    table = placement_ref.shape[1]
    matches = _iota((table, requests), 0) == adapter_ref[...]
    placed = jnp.broadcast_to(placement_ref[...].astype(jnp.float32), (8, table))
    slot = _dot(placed.astype(jnp.bfloat16), matches.astype(jnp.bfloat16)).astype(jnp.int32)
    slot = slot[0:1, :]
    holder = (slot // slots) ^ lax.axis_index("dp")
    inside = slot % slots
    of_holder = _iota((max(replicas, 8), requests), 0) == holder
    earlier = _iota((requests, requests), 0) < _iota((requests, requests), 1)
    before = _dot(of_holder.astype(jnp.bfloat16), earlier.astype(jnp.bfloat16))
    before = jnp.sum(jnp.where(of_holder, before, 0.0), axis=0, keepdims=True).astype(jnp.int32)
    target = holder * CAP + before
    here = _iota((replicas * CAP, requests), 0) == target
    chosen_ref[...] = here.astype(jnp.bfloat16)
    inner = jnp.sum(jnp.where(here, inside.astype(jnp.float32), 0.0), axis=1, keepdims=True)
    inner = jnp.broadcast_to(inner, (replicas * CAP, LANES)).astype(jnp.bfloat16)
    sent_ref[:, pl.ds(sent_ref.shape[1] - LANES, LANES)] = inner


def attend(
    query, keys, values, new_key, new_value, lengths, weight, request_adapter, placement,
    block, replicas, slots,
):
    requests, heads, width = query.shape
    cache, kv = keys.shape[1], keys.shape[2]
    steps = 4
    per = requests // steps
    columns = GROUP * cache * kv + per * kv
    features = heads * width
    chunk = chain_columns(block)[0][1]
    small = [lengths.reshape(1, -1), request_adapter.reshape(1, -1), placement.reshape(1, -1)]
    operands = [
        query.reshape(requests * heads, width),
        keys.reshape(requests * cache * kv, width),
        values.reshape(requests * cache * kv, width),
        new_key.reshape(requests * kv, width),
        new_value.reshape(requests * kv, width),
    ]
    return pl.pallas_call(
        functools.partial(attend_kernel, heads, kv, cache, steps, block, replicas, slots),
        in_specs=[ANY] * 9,
        out_specs=[ANY] * (3 + replicas),
        out_shape=[
            jax.ShapeDtypeStruct((requests, features), jnp.bfloat16),
            jax.ShapeDtypeStruct((requests, chunk), jnp.bfloat16),
            jax.ShapeDtypeStruct((replicas * CAP, requests), jnp.bfloat16),
        ]
        + [jax.ShapeDtypeStruct((CAP, features + LANES), jnp.bfloat16)] * replicas,
        scratch_shapes=[
            pltpu.VMEM((requests, features), jnp.bfloat16),
            pltpu.VMEM((requests, chunk), jnp.bfloat16),
            pltpu.VMEM((replicas * CAP, requests), jnp.bfloat16),
            pltpu.VMEM((replicas * CAP, features + LANES), jnp.bfloat16),
            pltpu.SemaphoreType.DMA((1 + steps + pl.cdiv(chunk, PIECE) + replicas,)),
        ]
        + [pltpu.VMEM(x.shape, x.dtype) for x in small + operands]
        + [
            pltpu.VMEM((2, per * heads, columns), jnp.float32),
            pltpu.VMEM((2, per * heads, width), jnp.float32),
            pltpu.SemaphoreType.DMA((3, steps)),
            pltpu.SemaphoreType.DMA((5,)),
        ]
        + Weights.scratch(weight.shape[0], chunk),
        compiler_params=pltpu.CompilerParams(vmem_limit_bytes=FULL_VMEM),
        name="attend",
    )(*small, *operands, weight)


def hop_kernel(step, block, start, arriving, after, *refs):
    if arriving:
        arrived_ref, *refs = refs
    a_ref, w_hbm, *refs = refs
    out_ref, held, sems = refs[after:]
    chunk = out_ref.shape[1]
    first = column_owner(step) * block + start
    weights = Weights(w_hbm, held, sems, first, chunk)
    weights.start()
    weights.wait()
    for columns, product in weights.products(a_ref[...]):
        if arriving:
            product = product + arrived_ref[:, columns].astype(jnp.float32)
        out_ref[:, columns] = product.astype(jnp.bfloat16)


def hop(step, chain, arrived, attended, weight, block, after=()):
    arriving = arrived is not None
    start, chunk = chain_columns(block)[chain]
    operands = ([arrived] if arriving else []) + [attended, weight, *after]
    return pl.pallas_call(
        functools.partial(hop_kernel, step, block, start, arriving, len(after)),
        in_specs=[VMEM] * (1 + arriving) + [ANY] + [ANY] * len(after),
        out_specs=VMEM,
        out_shape=jax.ShapeDtypeStruct((attended.shape[0], chunk), jnp.bfloat16),
        scratch_shapes=Weights.scratch(weight.shape[0], chunk),
        compiler_params=PARAMS,
        name="hop",
    )(*operands)


def down_kernel(replicas, after, *refs):
    received = refs[:replicas]
    down_ref = refs[replicas]
    mid_ref, inside_ref = refs[replicas + 1 + after :]
    slots, rank, width = down_ref.shape
    rows = jnp.concatenate([r[:, pl.ds(0, width)] for r in received], axis=0)
    inside = jnp.concatenate([r[:, pl.ds(width, LANES)] for r in received], axis=0)
    inside_ref[...] = inside
    projected = _dot(rows, down_ref[...].reshape(slots * rank, width), 1, 1)
    lane_slot = _iota(projected.shape, 1) // rank
    mine = lane_slot == inside[:, 0:1].astype(jnp.int32)
    projected = jnp.where(mine, projected, 0.0).astype(jnp.bfloat16)
    beside = LANES // rank
    some = projected.shape[0] // beside
    packed = 0.0
    for b in range(beside):
        lane = _iota((slots * rank, LANES), 1) - b * rank
        fold = _iota((slots * rank, LANES), 0) % rank == lane
        packed = packed + _dot(projected[b * some : (b + 1) * some, :], fold.astype(jnp.bfloat16))
    mid_ref[...] = packed.astype(jnp.bfloat16)


def down(received, slot_down_weight, after=()):
    replicas = len(received)
    rows = replicas * CAP
    return pl.pallas_call(
        functools.partial(down_kernel, replicas, len(after)),
        in_specs=[VMEM] * (replicas + 1) + [ANY] * len(after),
        out_specs=[VMEM, VMEM],
        out_shape=[
            jax.ShapeDtypeStruct((rows * slot_down_weight.shape[1] // LANES, LANES), jnp.bfloat16),
            jax.ShapeDtypeStruct((rows, LANES), jnp.bfloat16),
        ],
        compiler_params=PARAMS,
        name="down",
    )(*received, slot_down_weight, *after)


def up_kernel(parts, after, *refs):
    mids = refs[:parts]
    inside_ref, up_ref = refs[parts : parts + 2]
    out_refs = refs[parts + 2 + after :]
    slots, rank, width = up_ref.shape
    mid = mids[0][...].astype(jnp.float32)
    for m in mids[1:]:
        mid = mid + m[...].astype(jnp.float32)
    mid = mid.astype(jnp.bfloat16)
    wide = []
    for b in range(LANES // rank):
        lane = _iota((LANES, slots * rank), 0) - b * rank
        spread = _iota((LANES, slots * rank), 1) % rank == lane
        wide.append(_dot(mid, spread.astype(jnp.bfloat16)))
    wide = jnp.concatenate(wide, axis=0)
    mine = _iota(wide.shape, 1) // rank == inside_ref[:, 0:1].astype(jnp.int32)
    wide = jnp.where(mine, wide, 0.0).astype(jnp.bfloat16)
    delta = _dot(wide, up_ref[...].reshape(slots * rank, width)).astype(jnp.bfloat16)
    for r, out_ref in enumerate(out_refs):
        out_ref[...] = delta[r * CAP : (r + 1) * CAP, :]


def up(mids, inside, slot_up_weight, after=()):
    rows = inside.shape[0]
    replicas = rows // CAP
    width = slot_up_weight.shape[2]
    return pl.pallas_call(
        functools.partial(up_kernel, len(mids), len(after)),
        in_specs=[VMEM] * (len(mids) + 2) + [ANY] * len(after),
        out_specs=[VMEM] * replicas,
        out_shape=[jax.ShapeDtypeStruct((CAP, width), jnp.bfloat16)] * replicas,
        compiler_params=PARAMS,
        name="up",
    )(*mids, inside, slot_up_weight, *after)


def settle_kernel(step, replicas, after, *refs):
    returned = refs[:replicas]
    chosen_ref, a_ref, residual_ref, w_hbm = refs[replicas : replicas + 4]
    *out_refs, held, sems = refs[replicas + 4 + after :]
    width = residual_ref.shape[1]
    weights = Weights(w_hbm, held, sems, column_owner(step) * width, width)
    weights.start()
    rows = jnp.concatenate([r[...] for r in returned], axis=0)
    delta = _dot(chosen_ref[...], rows, 0, 0)
    total = residual_ref[...].astype(jnp.float32) + delta
    weights.wait()
    total = total + jnp.concatenate([p for _, p in weights.products(a_ref[...])], axis=1)
    for (start, chunk), out_ref in zip(chain_columns(width), out_refs):
        out_ref[...] = total[:, start : start + chunk]


def settle(step, returned, chosen, attended, residual, weight, after=()):
    replicas = len(returned)
    rows, width = residual.shape
    chains = chain_columns(width)
    return pl.pallas_call(
        functools.partial(settle_kernel, step, replicas, len(after)),
        in_specs=[VMEM] * (replicas + 3) + [ANY] * (1 + len(after)),
        out_specs=[VMEM] * len(chains),
        out_shape=[jax.ShapeDtypeStruct((rows, chunk), jnp.float32) for _, chunk in chains],
        scratch_shapes=Weights.scratch(weight.shape[0], width),
        compiler_params=PARAMS,
        name="settle",
    )(*returned, chosen, attended, residual, weight, *after)


def finish_kernel(start, arrived_ref, settled_ref, *refs):
    out_hbm, held, sems = refs[-3:]
    rows, chunk = arrived_ref.shape
    half = rows // 2
    copies = []
    for i in range(2):
        part = pl.ds(i * half, half)
        total = settled_ref[part, :] + arrived_ref[part, :].astype(jnp.float32)
        held[part, :] = total.astype(jnp.bfloat16)
        target = out_hbm.at[part, pl.ds(start, chunk)]
        copies.append(pltpu.make_async_copy(held.at[part, :], target, sems.at[i]))
        copies[-1].start()
    for copy in copies:
        copy.wait()


def finish(chain, arrived, settled, earlier, width):
    rows = arrived.shape[0]
    start, chunk = chain_columns(width)[chain]
    operands = [arrived, settled] + ([earlier] if earlier is not None else [])
    return pl.pallas_call(
        functools.partial(finish_kernel, start),
        in_specs=[VMEM, VMEM] + ([ANY] if earlier is not None else []),
        out_specs=ANY,
        out_shape=jax.ShapeDtypeStruct((rows, width), jnp.bfloat16),
        input_output_aliases={2: 0} if earlier is not None else {},
        scratch_shapes=[
            pltpu.VMEM((rows, chunk), jnp.bfloat16),
            pltpu.SemaphoreType.DMA((2,)),
        ],
        compiler_params=PARAMS,
        name="finish",
    )(*operands)


def hold_kernel(*refs):
    pass


def hold(x, after):
    return pl.pallas_call(
        hold_kernel,
        in_specs=[ANY] * (1 + len(after)),
        out_specs=ANY,
        out_shape=jax.ShapeDtypeStruct(x.shape, x.dtype),
        input_output_aliases={0: 0},
        compiler_params=PARAMS,
        name="hold",
    )(x, *after)


def per_device(
    residual,
    query,
    cached_key_rows,
    cached_value_rows,
    new_token_key,
    new_token_value,
    lengths,
    output_weight,
    slot_down_weight,
    slot_up_weight,
    placement,
    request_adapter,
):
    count = lax.axis_size("tensor")
    replicas = lax.axis_size("dp")
    block = residual.shape[1]
    order = ring_order(count)
    ring = [(order[p], order[(p + 1) % count]) for p in range(count)]

    def exchange(blocks):
        moved = [
            lax.ppermute(blocks[r], "dp", [(i, i ^ r) for i in range(replicas)])
            for r in range(1, replicas)
        ]
        return [blocks[0]] + moved

    def forward(x):
        return lax.ppermute(x, "tensor", ring)

    def next_hop(step, chain, after):
        arrived = forward(travelling[chain])
        travelling[chain] = hop(step, chain, arrived, attended, output_weight, block, after)

    attended, first, chosen, *leaving = attend(
        query, cached_key_rows, cached_value_rows, new_token_key, new_token_value, lengths,
        output_weight, request_adapter, placement, block, replicas, slot_down_weight.shape[0],
    )
    second = hop(0, 1, None, attended, output_weight, block)
    rows_here = exchange(leaving)
    mid, inside = down(rows_here, slot_down_weight, after=[second])
    rank_sums = [mid] + [
        lax.ppermute(mid, "tensor", [(i, (i + k) % count) for i in range(count)])
        for k in range(1, count)
    ]

    travelling = [first, second]
    next_hop(1, 0, after=[mid])
    travelling[0] = hold(travelling[0], after=rank_sums)
    next_hop(1, 1, after=[travelling[0]])
    next_hop(2, 0, after=[travelling[1]])
    deltas = up(rank_sums, inside, slot_up_weight, after=[travelling[0]])
    returned = exchange(deltas)
    next_hop(2, 1, after=returned)
    for step in range(3, count - 1):
        for chain in range(2):
            next_hop(step, chain, after=())
    settled = settle(
        count - 1, returned, chosen, attended, residual, output_weight, after=[travelling[1]]
    )
    out = None
    for chain in range(2):
        arrived = forward(travelling[chain])
        out = finish(chain, arrived, settled[chain], out, block)
    return out


def solution(mesh):
    placed = (
        P(("parts", "dp"), "tensor"),
        P(("parts", "dp"), "tensor", None),
        P(("parts", "dp"), None, "tensor", None),
        P(("parts", "dp"), None, "tensor", None),
        P(("parts", "dp"), "tensor", None),
        P(("parts", "dp"), "tensor", None),
        P(("parts", "dp")),
        P("tensor", None),
        P("dp", None, "tensor"),
        P("dp", None, "tensor"),
        P("parts"),
        P(("parts", "dp")),
    )
    return jax.shard_map(
        per_device,
        mesh=mesh,
        in_specs=placed,
        out_specs=P(("parts", "dp"), "tensor"),
        check_vma=False,
    )
```

```python
import functools
import math

import jax
import jax.numpy as jnp
from jax import lax
from jax.experimental import pallas as pl
from jax.experimental.pallas import tpu as pltpu
from jax.sharding import PartitionSpec as P

GROUP = 4
CAP = 64
LANES = 128
MASKED = -1e30
VMEM_LIMIT = 50 * 1024 * 1024
FULL_VMEM = 61 * 1024 * 1024
SHARES = ((1, 1),)
PIECE = 512
SPLIT = 4

VMEM = pl.BlockSpec(memory_space=pltpu.VMEM)
ANY = pl.BlockSpec(memory_space=pl.ANY)
PARAMS = pltpu.CompilerParams(vmem_limit_bytes=VMEM_LIMIT)


def _dot(a, b, left=1, right=0):
    return lax.dot_general(
        a, b, (((left,), (right,)), ((), ())), preferred_element_type=jnp.float32
    )


def _iota(shape, axis):
    return lax.broadcasted_iota(jnp.int32, shape, axis)


def right_owner(step):
    count = lax.axis_size("tensor")
    return jnp.minimum(lax.axis_index("tensor") + count - step, count - 1)


def left_owner(step):
    count = lax.axis_size("tensor")
    return jnp.maximum(lax.axis_index("tensor") + step - count, 0)


def one_way(step):
    return 2 * step <= lax.axis_size("tensor")


def outward_owner(step):
    count = lax.axis_size("tensor")
    rightward = lax.axis_index("tensor") < count // 2
    return jnp.where(rightward, right_owner(step), left_owner(step))


def chain_columns(width):
    shares = next(s for s in SHARES if width % (sum(s) * LANES) == 0)
    unit = width // sum(shares)
    return [(sum(shares[:c]) * unit, shares[c] * unit) for c in range(len(shares))]


class Weights:
    def __init__(self, w_ref, held, sems, first, width):
        depth = w_ref.shape[0] // SPLIT
        first = pl.multiple_of(first, LANES)
        self.held = held
        self.copies = [
            pltpu.make_async_copy(
                w_ref.at[pl.ds(s * depth, depth), pl.ds(first, width)],
                held.at[pl.ds(s * depth, depth), :],
                sems.at[s],
            )
            for s in range(SPLIT)
        ]

    def start(self):
        for copy in self.copies:
            copy.start()

    def wait(self):
        for copy in self.copies:
            copy.wait()

    def products(self, a):
        width = self.held.shape[1]
        for at in range(0, width, PIECE):
            columns = pl.ds(at, min(PIECE, width - at))
            yield columns, _dot(a, self.held[:, columns])

    @staticmethod
    def scratch(depth, width):
        return [
            pltpu.VMEM((depth, width), jnp.bfloat16),
            pltpu.SemaphoreType.DMA((SPLIT,)),
        ]


def row_max(arrays):
    full = None
    tops = []
    for x in arrays:
        width = x.shape[1]
        if width % LANES:
            tops.append(jnp.max(x, axis=1, keepdims=True))
            continue
        for at in range(0, width, LANES):
            tile = x[:, at : at + LANES]
            full = tile if full is None else jnp.maximum(full, tile)
    if full is not None:
        tops.append(jnp.max(full, axis=1, keepdims=True))
    return functools.reduce(jnp.maximum, tops)


def attend_kernel(
    heads, kv, cache, steps, block, replicas, slots,
    len_hbm, adapter_hbm, placement_hbm, q_hbm, k_hbm, v_hbm, nk_hbm, nv_hbm, w_hbm,
    *refs,
):
    a_hbm, out_hbm, chosen_hbm, *sent_hbm = refs[:5]
    (
        a_ref, out_ref, chosen_ref, sent_ref, out_sems,
        len_ref, adapter_ref, placement_ref, q_ref, k_ref, v_ref, nk_ref, nv_ref,
        scores_ref, mixed_ref, sems, small_sems, w_held, w_sems,
    ) = refs[5:]
    requests = len_ref.shape[1]
    width = q_hbm.shape[1]
    per = requests // steps
    groups = per // GROUP
    group_rows = GROUP * heads
    group_cols = GROUP * cache * kv
    per_kv = heads // kv
    scale = math.log2(math.e) / math.sqrt(width)

    def part(kind, step):
        source, target, count = (
            (q_hbm, q_ref, heads),
            (k_hbm, k_ref, cache * kv),
            (v_hbm, v_ref, cache * kv),
        )[kind]
        rows = pl.ds(step * per * count, per * count)
        return pltpu.make_async_copy(source.at[rows, :], target.at[rows, :], sems.at[kind, step])

    small = [
        pltpu.make_async_copy(source, target, small_sems.at[i])
        for i, (source, target) in enumerate(
            (
                (nk_hbm, nk_ref),
                (len_hbm, len_ref),
                (nv_hbm, nv_ref),
                (adapter_hbm, adapter_ref),
                (placement_hbm, placement_ref),
            )
        )
    ]
    leaving = []

    def leave(source, target):
        copy = pltpu.make_async_copy(source, target, out_sems.at[len(leaving)])
        copy.start()
        leaving.append(copy)

    chunk = out_ref.shape[1]
    weights = Weights(w_hbm, w_held, w_sems, outward_owner(1) * block, chunk)
    part(0, 0).start()
    part(1, 0).start()
    for copy in small[:2]:
        copy.start()
    part(0, 1).start()
    part(1, 1).start()
    part(2, 0).start()
    for copy in small[2:]:
        copy.start()
    part(2, 1).start()
    for step in range(2, steps):
        for kind in range(3):
            part(kind, step).start()
    weights.start()

    row = _iota((group_rows, group_cols), 0)
    col = _iota((group_rows, group_cols), 1)
    same = (row // heads == col // (cache * kv)) & ((row % heads) // per_kv == col % kv)
    own_bias = jnp.where(same, 0.0, MASKED)
    row = _iota((group_rows, per * kv), 0)
    col = _iota((group_rows, per * kv), 1)
    fresh_kv = (row % heads) // per_kv == col % kv
    fresh_distance = col // kv - row // heads
    ones = jnp.ones((max(group_cols, per * kv), LANES), jnp.bfloat16)

    def arrive(step):
        part(0, step).wait()
        part(1, step).wait()

    def scores(step):
        side = step % 2
        q_at = step * per * heads
        k_at = step * per * cache * kv
        for g in range(groups):
            scores_ref[side, pl.ds(g * group_rows, group_rows), pl.ds(0, group_cols)] = _dot(
                q_ref[pl.ds(q_at + g * group_rows, group_rows), :],
                k_ref[pl.ds(k_at + g * group_cols, group_cols), :],
                1,
                1,
            )
        scores_ref[side, :, pl.ds(group_cols, per * kv)] = _dot(
            q_ref[pl.ds(q_at, per * heads), :], nk_ref[pl.ds(step * per * kv, per * kv), :], 1, 1
        )

    for copy in small:
        copy.wait()
    plan_routes(slots, adapter_ref, placement_ref, chosen_ref, sent_ref)
    leave(chosen_ref, chosen_hbm)
    counts = len_ref[...].astype(jnp.float32)
    all_groups = requests // GROUP
    of_group = _iota((all_groups, requests), 1) // GROUP == _iota((all_groups, requests), 0)
    counts = jnp.where(of_group, counts, 0.0).astype(jnp.bfloat16)
    spread = _iota((requests, group_cols), 0) % GROUP == _iota((requests, group_cols), 1) // (cache * kv)
    counts = _dot(counts, spread.astype(jnp.bfloat16))
    position = (_iota((all_groups, group_cols), 1) // kv) % cache
    length_bias = jnp.where(position.astype(jnp.float32) < counts, 0.0, MASKED)

    arrive(0)
    scores(0)
    for step in range(steps):
        side = step % 2
        k_at = step * per * cache * kv
        f_at = step * per * kv
        part(2, step).wait()
        if step + 1 < steps:
            arrive(step + 1)
            scores(step + 1)
        held = []
        fresh = []
        for g in range(groups):
            rows = pl.ds(g * group_rows, group_rows)
            bias = own_bias + length_bias[step * groups + g : step * groups + g + 1, :]
            cached = scores_ref[side, rows, pl.ds(0, group_cols)] + bias
            new = scores_ref[side, rows, pl.ds(group_cols, per * kv)]
            new = jnp.where(fresh_kv & (fresh_distance == g * GROUP), new, MASKED)
            top = row_max([cached, new])
            cached = jnp.exp2((cached - top) * scale).astype(jnp.bfloat16)
            fresh.append(jnp.exp2((new - top) * scale).astype(jnp.bfloat16))
            values = v_ref[pl.ds(k_at + g * group_cols, group_cols), :]
            held.append(_dot(cached, jnp.concatenate([values, ones[:group_cols]], axis=1)))
        values = jnp.concatenate([nv_ref[pl.ds(f_at, per * kv), :], ones[: per * kv]], axis=1)
        fresh = _dot(jnp.concatenate(fresh, axis=0), values)
        for g in range(groups):
            rows = slice(g * group_rows, (g + 1) * group_rows)
            mixed = fresh[rows, :] + held[g]
            mixed_ref[side, rows, :] = mixed[:, :width] / mixed[:, width:]
        for h in range(heads):
            a_ref[pl.ds(step * per, per), pl.ds(h * width, width)] = mixed_ref[
                side, pl.ds(h, per, stride=heads), :
            ].astype(jnp.bfloat16)
        rows = pl.ds(step * per, per)
        leave(a_ref.at[rows, :], a_hbm.at[rows, :])

    weights.wait()
    for columns, product in weights.products(a_ref[...]):
        out_ref[:, columns] = product.astype(jnp.bfloat16)
        leave(out_ref.at[:, columns], out_hbm.at[:, columns])
    sent_ref[:, pl.ds(0, heads * width)] = _dot(chosen_ref[...], a_ref[...]).astype(jnp.bfloat16)
    half = sent_ref.shape[0] // 2
    for i, target in enumerate(sent_hbm):
        leave(sent_ref.at[pl.ds(i * half, half), :], target)
    for copy in leaving:
        copy.wait()


def plan_routes(slots, adapter_ref, placement_ref, chosen_ref, sent_ref):
    replicas = sent_ref.shape[0] // CAP
    requests = adapter_ref.shape[1]
    table = placement_ref.shape[1]
    matches = _iota((table, requests), 0) == adapter_ref[...]
    placed = jnp.broadcast_to(placement_ref[...].astype(jnp.float32), (8, table))
    slot = _dot(placed.astype(jnp.bfloat16), matches.astype(jnp.bfloat16)).astype(jnp.int32)
    slot = slot[0:1, :]
    holder = (slot // slots) ^ lax.axis_index("dp")
    inside = slot % slots
    of_holder = _iota((max(replicas, 8), requests), 0) == holder
    earlier = _iota((requests, requests), 0) < _iota((requests, requests), 1)
    before = _dot(of_holder.astype(jnp.bfloat16), earlier.astype(jnp.bfloat16))
    before = jnp.sum(jnp.where(of_holder, before, 0.0), axis=0, keepdims=True).astype(jnp.int32)
    target = holder * CAP + before
    here = _iota((replicas * CAP, requests), 0) == target
    chosen_ref[...] = here.astype(jnp.bfloat16)
    inner = jnp.sum(jnp.where(here, inside.astype(jnp.float32), 0.0), axis=1, keepdims=True)
    inner = jnp.broadcast_to(inner, (replicas * CAP, LANES)).astype(jnp.bfloat16)
    sent_ref[:, pl.ds(sent_ref.shape[1] - LANES, LANES)] = inner


def attend(
    query, keys, values, new_key, new_value, lengths, weight, request_adapter, placement,
    block, replicas, slots,
):
    requests, heads, width = query.shape
    cache, kv = keys.shape[1], keys.shape[2]
    steps = 4
    per = requests // steps
    columns = GROUP * cache * kv + per * kv
    features = heads * width
    chunk = chain_columns(block)[0][1]
    small = [lengths.reshape(1, -1), request_adapter.reshape(1, -1), placement.reshape(1, -1)]
    operands = [
        query.reshape(requests * heads, width),
        keys.reshape(requests * cache * kv, width),
        values.reshape(requests * cache * kv, width),
        new_key.reshape(requests * kv, width),
        new_value.reshape(requests * kv, width),
    ]
    return pl.pallas_call(
        functools.partial(attend_kernel, heads, kv, cache, steps, block, replicas, slots),
        in_specs=[ANY] * 9,
        out_specs=[ANY] * 5,
        out_shape=[
            jax.ShapeDtypeStruct((requests, features), jnp.bfloat16),
            jax.ShapeDtypeStruct((requests, chunk), jnp.bfloat16),
            jax.ShapeDtypeStruct((replicas * CAP, requests), jnp.bfloat16),
        ]
        + [jax.ShapeDtypeStruct((replicas // 2 * CAP, features + LANES), jnp.bfloat16)] * 2,
        scratch_shapes=[
            pltpu.VMEM((requests, features), jnp.bfloat16),
            pltpu.VMEM((requests, chunk), jnp.bfloat16),
            pltpu.VMEM((replicas * CAP, requests), jnp.bfloat16),
            pltpu.VMEM((replicas * CAP, features + LANES), jnp.bfloat16),
            pltpu.SemaphoreType.DMA((3 + steps + pl.cdiv(chunk, PIECE),)),
        ]
        + [pltpu.VMEM(x.shape, x.dtype) for x in small + operands]
        + [
            pltpu.VMEM((2, per * heads, columns), jnp.float32),
            pltpu.VMEM((2, per * heads, width), jnp.float32),
            pltpu.SemaphoreType.DMA((3, steps)),
            pltpu.SemaphoreType.DMA((5,)),
        ]
        + Weights.scratch(weight.shape[0], chunk),
        compiler_params=pltpu.CompilerParams(vmem_limit_bytes=FULL_VMEM),
        name="attend",
    )(*small, *operands, weight)


def hop_kernel(step, block, start, arrivals, after, *refs):
    arrived = refs[:arrivals]
    a_ref, w_hbm = refs[arrivals : arrivals + 2]
    refs = refs[arrivals + 2 + after :]
    owners = [outward_owner(step)] if one_way(step) else [right_owner(step), left_owner(step)]
    outs, held, sems = refs[: len(owners)], refs[len(owners) :: 2], refs[len(owners) + 1 :: 2]
    chunk = outs[0].shape[1]
    ways = []
    for owner, buffer, flags in zip(owners, held, sems):
        ways.append(Weights(w_hbm, buffer, flags, owner * block + start, chunk))
        ways[-1].start()
    for i, (weights, out_ref) in enumerate(zip(ways, outs)):
        weights.wait()
        for columns, product in weights.products(a_ref[...]):
            if arrivals:
                ref = arrived[min(i, arrivals - 1)]
                product = product + ref[:, columns].astype(jnp.float32)
            out_ref[:, columns] = product.astype(jnp.bfloat16)


def hop(step, chain, arrived, attended, weight, block, after=()):
    start, chunk = chain_columns(block)[chain]
    outs = 1 if one_way(step) else 2
    return pl.pallas_call(
        functools.partial(hop_kernel, step, block, start, len(arrived), len(after)),
        in_specs=[VMEM] * (len(arrived) + 1) + [ANY] * (1 + len(after)),
        out_specs=[VMEM] * outs,
        out_shape=[jax.ShapeDtypeStruct((attended.shape[0], chunk), jnp.bfloat16)] * outs,
        scratch_shapes=Weights.scratch(weight.shape[0], chunk) * outs,
        compiler_params=PARAMS,
        name="hop",
    )(*arrived, attended, weight, *after)


def down_kernel(places, arrays, after, *refs):
    down_ref = refs[arrays]
    mid_ref, inside_ref = refs[arrays + 1 + after :]
    slots, rank, width = down_ref.shape
    blocks = [refs[i].at[pl.ds(at, CAP), :] for i, at in places]
    rows = jnp.concatenate([b[:, pl.ds(0, width)] for b in blocks], axis=0)
    inside = jnp.concatenate([b[:, pl.ds(width, LANES)] for b in blocks], axis=0)
    inside_ref[...] = inside
    projected = _dot(rows, down_ref[...].reshape(slots * rank, width), 1, 1)
    lane_slot = _iota(projected.shape, 1) // rank
    mine = lane_slot == inside[:, 0:1].astype(jnp.int32)
    projected = jnp.where(mine, projected, 0.0).astype(jnp.bfloat16)
    beside = LANES // rank
    some = projected.shape[0] // beside
    packed = 0.0
    for b in range(beside):
        lane = _iota((slots * rank, LANES), 1) - b * rank
        fold = _iota((slots * rank, LANES), 0) % rank == lane
        packed = packed + _dot(projected[b * some : (b + 1) * some, :], fold.astype(jnp.bfloat16))
    mid_ref[...] = packed.astype(jnp.bfloat16)


def down(received, slot_down_weight, after=()):
    arrays, places = received
    rows = len(places) * CAP
    return pl.pallas_call(
        functools.partial(down_kernel, places, len(arrays), len(after)),
        in_specs=[VMEM] * (len(arrays) + 1) + [ANY] * len(after),
        out_specs=[VMEM, VMEM],
        out_shape=[
            jax.ShapeDtypeStruct((rows * slot_down_weight.shape[1] // LANES, LANES), jnp.bfloat16),
            jax.ShapeDtypeStruct((rows, LANES), jnp.bfloat16),
        ],
        compiler_params=PARAMS,
        name="down",
    )(*arrays, slot_down_weight, *after)


def up_kernel(parts, after, *refs):
    mids = refs[:parts]
    inside_ref, up_ref = refs[parts : parts + 2]
    out_refs = refs[parts + 2 + after :]
    slots, rank, width = up_ref.shape
    mid = mids[0][...].astype(jnp.float32)
    for m in mids[1:]:
        mid = mid + m[...].astype(jnp.float32)
    mid = mid.astype(jnp.bfloat16)
    wide = []
    for b in range(LANES // rank):
        lane = _iota((LANES, slots * rank), 0) - b * rank
        spread = _iota((LANES, slots * rank), 1) % rank == lane
        wide.append(_dot(mid, spread.astype(jnp.bfloat16)))
    wide = jnp.concatenate(wide, axis=0)
    mine = _iota(wide.shape, 1) // rank == inside_ref[:, 0:1].astype(jnp.int32)
    wide = jnp.where(mine, wide, 0.0).astype(jnp.bfloat16)
    delta = _dot(wide, up_ref[...].reshape(slots * rank, width)).astype(jnp.bfloat16)
    half = delta.shape[0] // 2
    for i, out_ref in enumerate(out_refs):
        out_ref[...] = delta[i * half : (i + 1) * half, :]


def up(mids, inside, slot_up_weight, after=()):
    rows = inside.shape[0]
    width = slot_up_weight.shape[2]
    return pl.pallas_call(
        functools.partial(up_kernel, len(mids), len(after)),
        in_specs=[VMEM] * (len(mids) + 2) + [ANY] * len(after),
        out_specs=[VMEM] * 2,
        out_shape=[jax.ShapeDtypeStruct((rows // 2, width), jnp.bfloat16)] * 2,
        compiler_params=PARAMS,
        name="up",
    )(*mids, inside, slot_up_weight, *after)


def settle_kernel(places, arrays, after, *refs):
    chosen_ref, a_ref, residual_ref, w_hbm = refs[arrays : arrays + 4]
    *out_refs, held, sems = refs[arrays + 4 + after :]
    width = residual_ref.shape[1]
    weights = Weights(w_hbm, held, sems, lax.axis_index("tensor") * width, width)
    weights.start()
    rows = jnp.concatenate([refs[i][pl.ds(at, CAP), :] for i, at in places], axis=0)
    delta = _dot(chosen_ref[...], rows, 0, 0)
    total = residual_ref[...].astype(jnp.float32) + delta
    weights.wait()
    total = total + jnp.concatenate([p for _, p in weights.products(a_ref[...])], axis=1)
    for (start, chunk), out_ref in zip(chain_columns(width), out_refs):
        out_ref[...] = total[:, start : start + chunk]


def settle(returned, chosen, attended, residual, weight, after=()):
    arrays, places = returned
    rows, width = residual.shape
    chains = chain_columns(width)
    return pl.pallas_call(
        functools.partial(settle_kernel, places, len(arrays), len(after)),
        in_specs=[VMEM] * (len(arrays) + 3) + [ANY] * (1 + len(after)),
        out_specs=[VMEM] * len(chains),
        out_shape=[jax.ShapeDtypeStruct((rows, chunk), jnp.float32) for _, chunk in chains],
        scratch_shapes=Weights.scratch(weight.shape[0], width),
        compiler_params=PARAMS,
        name="settle",
    )(*arrays, chosen, attended, residual, weight, *after)


def finish_kernel(start, right_ref, left_ref, settled_ref, *refs):
    out_hbm, held, sems = refs[-3:]
    rows, chunk = right_ref.shape
    half = rows // 2
    copies = []
    for i in range(2):
        part = pl.ds(i * half, half)
        total = right_ref[part, :].astype(jnp.float32) + left_ref[part, :].astype(jnp.float32)
        total = total + settled_ref[part, :]
        held[part, :] = total.astype(jnp.bfloat16)
        target = out_hbm.at[part, pl.ds(start, chunk)]
        copies.append(pltpu.make_async_copy(held.at[part, :], target, sems.at[i]))
        copies[-1].start()
    for copy in copies:
        copy.wait()


def finish(chain, arrived, settled, earlier, width):
    rows = settled.shape[0]
    start, chunk = chain_columns(width)[chain]
    operands = [*arrived, settled] + ([earlier] if earlier is not None else [])
    return pl.pallas_call(
        functools.partial(finish_kernel, start),
        in_specs=[VMEM] * 3 + ([ANY] if earlier is not None else []),
        out_specs=ANY,
        out_shape=jax.ShapeDtypeStruct((rows, width), jnp.bfloat16),
        input_output_aliases={3: 0} if earlier is not None else {},
        scratch_shapes=[
            pltpu.VMEM((rows, chunk), jnp.bfloat16),
            pltpu.SemaphoreType.DMA((2,)),
        ],
        compiler_params=PARAMS,
        name="finish",
    )(*operands)


def per_device(
    residual,
    query,
    cached_key_rows,
    cached_value_rows,
    new_token_key,
    new_token_value,
    lengths,
    output_weight,
    slot_down_weight,
    slot_up_weight,
    placement,
    request_adapter,
):
    count = lax.axis_size("tensor")
    replicas = lax.axis_size("dp")
    block = residual.shape[1]
    def exchange(near, far):
        arrays = [near, far]
        places = [(r * 2 // replicas, r % (replicas // 2) * CAP) for r in range(replicas)]
        reach = replicas // 2
        while reach:
            moving = [r for r in range(replicas) if r & reach]
            if 2 * reach == replicas:
                moved = far
            else:
                moved = jnp.concatenate(
                    [lax.slice_in_dim(arrays[i], at, at + CAP) for i, at in map(places.__getitem__, moving)]
                )
            arrays.append(lax.ppermute(moved, "dp", [(i, i ^ reach) for i in range(replicas)]))
            for j, r in enumerate(moving):
                places[r] = (len(arrays) - 1, j * CAP)
            reach //= 2
        used = sorted({i for i, _ in places})
        return [arrays[i] for i in used], [(used.index(i), at) for i, at in places]

    def pass_on(step, sums):
        rightward = [(i, i + 1) for i in range(step)]
        leftward = [(i, i - 1) for i in range(count - step, count)]
        if 2 * step < count - 1:
            return [lax.ppermute(sums[0], "tensor", rightward + leftward)]
        return [
            lax.ppermute(sums[0], "tensor", rightward),
            lax.ppermute(sums[-1], "tensor", leftward),
        ]

    def next_hop(step, chain, after):
        arrived = pass_on(step - 1, sums[chain])
        sums[chain] = hop(step, chain, arrived, attended, output_weight, block, after)

    attended, first, chosen, near, far = attend(
        query, cached_key_rows, cached_value_rows, new_token_key, new_token_value, lengths,
        output_weight, request_adapter, placement, block, replicas, slot_down_weight.shape[0],
    )
    sums = [[first], hop(1, 1, [], attended, output_weight, block)]
    rows_here = exchange(near, far)
    next_hop(2, 0, after=[*sums[1], *rows_here[0]])
    mid, inside = down(rows_here, slot_down_weight, after=sums[0])
    rank_sums = [mid] + [
        lax.ppermute(mid, "tensor", [(i, i ^ k) for i in range(count)]) for k in range(1, count)
    ]
    next_hop(2, 1, after=[rank_sums[0]])
    deltas = up(rank_sums, inside, slot_up_weight, after=sums[1])
    returned = exchange(*deltas)
    next_hop(3, 0, after=[deltas[0]])
    next_hop(3, 1, after=sums[0])
    for step in range(4, count):
        for chain in range(2):
            next_hop(step, chain, after=sums[1 - chain])
    settled = settle(returned, chosen, attended, residual, output_weight, after=sums[1])
    out = None
    for chain in range(2):
        arrived = pass_on(count - 1, sums[chain])
        out = finish(chain, arrived, settled[chain], out, block)
    return out


def solution(mesh):
    placed = (
        P(("parts", "dp"), "tensor"),
        P(("parts", "dp"), "tensor", None),
        P(("parts", "dp"), None, "tensor", None),
        P(("parts", "dp"), None, "tensor", None),
        P(("parts", "dp"), "tensor", None),
        P(("parts", "dp"), "tensor", None),
        P(("parts", "dp")),
        P("tensor", None),
        P("dp", None, "tensor"),
        P("dp", None, "tensor"),
        P("parts"),
        P(("parts", "dp")),
    )
    return jax.shard_map(
        per_device,
        mesh=mesh,
        in_specs=placed,
        out_specs=P(("parts", "dp"), "tensor"),
        check_vma=False,
    )
```

```python
import functools
import math

import jax
import jax.numpy as jnp
from jax import lax
from jax.experimental import pallas as pl
from jax.experimental.pallas import tpu as pltpu
from jax.sharding import PartitionSpec as P

GROUP = 4
CAP = 64
LANES = 128
MASKED = -1e30
VMEM_LIMIT = 50 * 1024 * 1024
FULL_VMEM = 61 * 1024 * 1024
SHARES = ((5, 3),)
PIECE = 512
SPLIT = 4

VMEM = pl.BlockSpec(memory_space=pltpu.VMEM)
ANY = pl.BlockSpec(memory_space=pl.ANY)
LONG = pl.CostEstimate(flops=20 * 10**9, transcendentals=0, bytes_accessed=40 * 10**6)
PARAMS = pltpu.CompilerParams(vmem_limit_bytes=VMEM_LIMIT)


def _dot(a, b, left=1, right=0):
    return lax.dot_general(
        a, b, (((left,), (right,)), ((), ())), preferred_element_type=jnp.float32
    )


def _iota(shape, axis):
    return lax.broadcasted_iota(jnp.int32, shape, axis)


def ring_order(count):
    return list(range(0, count, 2)) + list(range(1, count, 2))[::-1]


def column_owner(step):
    count = lax.axis_size("tensor")
    here = lax.axis_index("tensor")
    half = here // 2
    spot = jnp.where(here % 2 == 0, half, count - 1 - half)
    spot = lax.rem(spot - 1 - step + 2 * count, count)
    return jnp.where(2 * spot < count, 2 * spot, 2 * (count - spot) - 1)


def chain_columns(width):
    shares = next(s for s in SHARES if width % (sum(s) * LANES) == 0)
    unit = width // sum(shares)
    return [(sum(shares[:c]) * unit, shares[c] * unit) for c in range(len(shares))]


class Weights:
    def __init__(self, w_ref, held, sems, first, width):
        depth = w_ref.shape[0] // SPLIT
        first = pl.multiple_of(first, LANES)
        self.held = held
        self.copies = [
            pltpu.make_async_copy(
                w_ref.at[pl.ds(s * depth, depth), pl.ds(first, width)],
                held.at[pl.ds(s * depth, depth), :],
                sems.at[s],
            )
            for s in range(SPLIT)
        ]

    def start(self):
        for copy in self.copies:
            copy.start()

    def wait(self):
        for copy in self.copies:
            copy.wait()

    def products(self, a):
        width = self.held.shape[1]
        for at in range(0, width, PIECE):
            columns = pl.ds(at, min(PIECE, width - at))
            yield columns, _dot(a, self.held[:, columns])

    @staticmethod
    def scratch(depth, width):
        return [
            pltpu.VMEM((depth, width), jnp.bfloat16),
            pltpu.SemaphoreType.DMA((SPLIT,)),
        ]


def row_max(arrays):
    full = None
    tops = []
    for x in arrays:
        width = x.shape[1]
        if width % LANES:
            tops.append(jnp.max(x, axis=1, keepdims=True))
            continue
        for at in range(0, width, LANES):
            tile = x[:, at : at + LANES]
            full = tile if full is None else jnp.maximum(full, tile)
    if full is not None:
        tops.append(jnp.max(full, axis=1, keepdims=True))
    return functools.reduce(jnp.maximum, tops)


def attend_kernel(
    heads, kv, cache, steps, block, replicas, slots,
    len_hbm, adapter_hbm, placement_hbm, q_hbm, k_hbm, v_hbm, nk_hbm, nv_hbm, w_hbm,
    *refs,
):
    a_hbm, out_hbm, chosen_hbm, *sent_hbm = refs[: 3 + replicas]
    (
        a_ref, out_ref, chosen_ref, sent_ref, out_sems,
        len_ref, adapter_ref, placement_ref, q_ref, k_ref, v_ref, nk_ref, nv_ref,
        scores_ref, mixed_ref, sems, small_sems, w_held, w_sems,
    ) = refs[3 + replicas :]
    requests = len_ref.shape[1]
    width = q_hbm.shape[1]
    per = requests // steps
    groups = per // GROUP
    group_rows = GROUP * heads
    group_cols = GROUP * cache * kv
    per_kv = heads // kv
    scale = math.log2(math.e) / math.sqrt(width)

    def part(kind, step):
        source, target, count = (
            (q_hbm, q_ref, heads),
            (k_hbm, k_ref, cache * kv),
            (v_hbm, v_ref, cache * kv),
        )[kind]
        rows = pl.ds(step * per * count, per * count)
        return pltpu.make_async_copy(source.at[rows, :], target.at[rows, :], sems.at[kind, step])

    small = [
        pltpu.make_async_copy(source, target, small_sems.at[i])
        for i, (source, target) in enumerate(
            (
                (nk_hbm, nk_ref),
                (len_hbm, len_ref),
                (nv_hbm, nv_ref),
                (adapter_hbm, adapter_ref),
                (placement_hbm, placement_ref),
            )
        )
    ]
    leaving = []

    def leave(source, target):
        copy = pltpu.make_async_copy(source, target, out_sems.at[len(leaving)])
        copy.start()
        leaving.append(copy)

    chunk = out_ref.shape[1]
    weights = Weights(w_hbm, w_held, w_sems, column_owner(0) * block, chunk)
    part(0, 0).start()
    part(1, 0).start()
    for copy in small[:2]:
        copy.start()
    part(0, 1).start()
    part(1, 1).start()
    part(2, 0).start()
    for copy in small[2:]:
        copy.start()
    part(2, 1).start()
    for step in range(2, steps):
        for kind in range(3):
            part(kind, step).start()
    weights.start()

    row = _iota((group_rows, group_cols), 0)
    col = _iota((group_rows, group_cols), 1)
    same = (row // heads == col // (cache * kv)) & ((row % heads) // per_kv == col % kv)
    own_bias = jnp.where(same, 0.0, MASKED)
    row = _iota((group_rows, per * kv), 0)
    col = _iota((group_rows, per * kv), 1)
    fresh_kv = (row % heads) // per_kv == col % kv
    fresh_distance = col // kv - row // heads
    ones = jnp.ones((max(group_cols, per * kv), LANES), jnp.bfloat16)

    def arrive(step):
        part(0, step).wait()
        part(1, step).wait()

    def scores(step):
        side = step % 2
        q_at = step * per * heads
        k_at = step * per * cache * kv
        for g in range(groups):
            scores_ref[side, pl.ds(g * group_rows, group_rows), pl.ds(0, group_cols)] = _dot(
                q_ref[pl.ds(q_at + g * group_rows, group_rows), :],
                k_ref[pl.ds(k_at + g * group_cols, group_cols), :],
                1,
                1,
            )
        scores_ref[side, :, pl.ds(group_cols, per * kv)] = _dot(
            q_ref[pl.ds(q_at, per * heads), :], nk_ref[pl.ds(step * per * kv, per * kv), :], 1, 1
        )

    for copy in small:
        copy.wait()
    plan_routes(slots, adapter_ref, placement_ref, chosen_ref, sent_ref)
    leave(chosen_ref, chosen_hbm)
    counts = len_ref[...].astype(jnp.float32)
    all_groups = requests // GROUP
    of_group = _iota((all_groups, requests), 1) // GROUP == _iota((all_groups, requests), 0)
    counts = jnp.where(of_group, counts, 0.0).astype(jnp.bfloat16)
    spread = _iota((requests, group_cols), 0) % GROUP == _iota((requests, group_cols), 1) // (cache * kv)
    counts = _dot(counts, spread.astype(jnp.bfloat16))
    position = (_iota((all_groups, group_cols), 1) // kv) % cache
    length_bias = jnp.where(position.astype(jnp.float32) < counts, 0.0, MASKED)

    arrive(0)
    scores(0)
    for step in range(steps):
        side = step % 2
        k_at = step * per * cache * kv
        f_at = step * per * kv
        part(2, step).wait()
        if step + 1 < steps:
            arrive(step + 1)
            scores(step + 1)
        held = []
        fresh = []
        for g in range(groups):
            rows = pl.ds(g * group_rows, group_rows)
            bias = own_bias + length_bias[step * groups + g : step * groups + g + 1, :]
            cached = scores_ref[side, rows, pl.ds(0, group_cols)] + bias
            new = scores_ref[side, rows, pl.ds(group_cols, per * kv)]
            new = jnp.where(fresh_kv & (fresh_distance == g * GROUP), new, MASKED)
            top = row_max([cached, new])
            cached = jnp.exp2((cached - top) * scale).astype(jnp.bfloat16)
            fresh.append(jnp.exp2((new - top) * scale).astype(jnp.bfloat16))
            values = v_ref[pl.ds(k_at + g * group_cols, group_cols), :]
            held.append(_dot(cached, jnp.concatenate([values, ones[:group_cols]], axis=1)))
        values = jnp.concatenate([nv_ref[pl.ds(f_at, per * kv), :], ones[: per * kv]], axis=1)
        fresh = _dot(jnp.concatenate(fresh, axis=0), values)
        for g in range(groups):
            rows = slice(g * group_rows, (g + 1) * group_rows)
            mixed = fresh[rows, :] + held[g]
            mixed_ref[side, rows, :] = mixed[:, :width] / mixed[:, width:]
        for h in range(heads):
            a_ref[pl.ds(step * per, per), pl.ds(h * width, width)] = mixed_ref[
                side, pl.ds(h, per, stride=heads), :
            ].astype(jnp.bfloat16)
        rows = pl.ds(step * per, per)
        leave(a_ref.at[rows, :], a_hbm.at[rows, :])

    weights.wait()
    for columns, product in weights.products(a_ref[...]):
        out_ref[:, columns] = product.astype(jnp.bfloat16)
        leave(out_ref.at[:, columns], out_hbm.at[:, columns])
    sent_ref[:, pl.ds(0, heads * width)] = _dot(chosen_ref[...], a_ref[...]).astype(jnp.bfloat16)
    for r in range(replicas):
        leave(sent_ref.at[pl.ds(r * CAP, CAP), :], sent_hbm[r])
    for copy in leaving:
        copy.wait()


def plan_routes(slots, adapter_ref, placement_ref, chosen_ref, sent_ref):
    replicas = sent_ref.shape[0] // CAP
    requests = adapter_ref.shape[1]
    table = placement_ref.shape[1]
    matches = _iota((table, requests), 0) == adapter_ref[...]
    placed = jnp.broadcast_to(placement_ref[...].astype(jnp.float32), (8, table))
    slot = _dot(placed.astype(jnp.bfloat16), matches.astype(jnp.bfloat16)).astype(jnp.int32)
    slot = slot[0:1, :]
    holder = (slot // slots) ^ lax.axis_index("dp")
    inside = slot % slots
    of_holder = _iota((max(replicas, 8), requests), 0) == holder
    earlier = _iota((requests, requests), 0) < _iota((requests, requests), 1)
    before = _dot(of_holder.astype(jnp.bfloat16), earlier.astype(jnp.bfloat16))
    before = jnp.sum(jnp.where(of_holder, before, 0.0), axis=0, keepdims=True).astype(jnp.int32)
    target = holder * CAP + before
    here = _iota((replicas * CAP, requests), 0) == target
    chosen_ref[...] = here.astype(jnp.bfloat16)
    inner = jnp.sum(jnp.where(here, inside.astype(jnp.float32), 0.0), axis=1, keepdims=True)
    inner = jnp.broadcast_to(inner, (replicas * CAP, LANES)).astype(jnp.bfloat16)
    sent_ref[:, pl.ds(sent_ref.shape[1] - LANES, LANES)] = inner


def attend(
    query, keys, values, new_key, new_value, lengths, weight, request_adapter, placement,
    block, replicas, slots,
):
    requests, heads, width = query.shape
    cache, kv = keys.shape[1], keys.shape[2]
    steps = 4
    per = requests // steps
    columns = GROUP * cache * kv + per * kv
    features = heads * width
    chunk = chain_columns(block)[0][1]
    small = [lengths.reshape(1, -1), request_adapter.reshape(1, -1), placement.reshape(1, -1)]
    operands = [
        query.reshape(requests * heads, width),
        keys.reshape(requests * cache * kv, width),
        values.reshape(requests * cache * kv, width),
        new_key.reshape(requests * kv, width),
        new_value.reshape(requests * kv, width),
    ]
    return pl.pallas_call(
        functools.partial(attend_kernel, heads, kv, cache, steps, block, replicas, slots),
        in_specs=[ANY] * 9,
        out_specs=[ANY] * (3 + replicas),
        out_shape=[
            jax.ShapeDtypeStruct((requests, features), jnp.bfloat16),
            jax.ShapeDtypeStruct((requests, chunk), jnp.bfloat16),
            jax.ShapeDtypeStruct((replicas * CAP, requests), jnp.bfloat16),
        ]
        + [jax.ShapeDtypeStruct((CAP, features + LANES), jnp.bfloat16)] * replicas,
        scratch_shapes=[
            pltpu.VMEM((requests, features), jnp.bfloat16),
            pltpu.VMEM((requests, chunk), jnp.bfloat16),
            pltpu.VMEM((replicas * CAP, requests), jnp.bfloat16),
            pltpu.VMEM((replicas * CAP, features + LANES), jnp.bfloat16),
            pltpu.SemaphoreType.DMA((1 + steps + pl.cdiv(chunk, PIECE) + replicas,)),
        ]
        + [pltpu.VMEM(x.shape, x.dtype) for x in small + operands]
        + [
            pltpu.VMEM((2, per * heads, columns), jnp.float32),
            pltpu.VMEM((2, per * heads, width), jnp.float32),
            pltpu.SemaphoreType.DMA((3, steps)),
            pltpu.SemaphoreType.DMA((5,)),
        ]
        + Weights.scratch(weight.shape[0], chunk),
        compiler_params=pltpu.CompilerParams(vmem_limit_bytes=FULL_VMEM),
        name="attend",
    )(*small, *operands, weight)


def hop_kernel(step, block, start, arriving, after, *refs):
    if arriving:
        arrived_ref, *refs = refs
    a_ref, w_hbm, *refs = refs
    out_ref, held, sems = refs[after:]
    chunk = out_ref.shape[1]
    first = column_owner(step) * block + start
    weights = Weights(w_hbm, held, sems, first, chunk)
    weights.start()
    weights.wait()
    for columns, product in weights.products(a_ref[...]):
        if arriving:
            product = product + arrived_ref[:, columns].astype(jnp.float32)
        out_ref[:, columns] = product.astype(jnp.bfloat16)


def hop(step, chain, arrived, attended, weight, block, after=(), cost=None):
    arriving = arrived is not None
    start, chunk = chain_columns(block)[chain]
    operands = ([arrived] if arriving else []) + [attended, weight, *after]
    return pl.pallas_call(
        functools.partial(hop_kernel, step, block, start, arriving, len(after)),
        in_specs=[VMEM] * (1 + arriving) + [ANY] + [ANY] * len(after),
        out_specs=VMEM,
        out_shape=jax.ShapeDtypeStruct((attended.shape[0], chunk), jnp.bfloat16),
        scratch_shapes=Weights.scratch(weight.shape[0], chunk),
        compiler_params=PARAMS,
        cost_estimate=cost,
        name="hop",
    )(*operands)


def down_kernel(replicas, after, *refs):
    received = refs[:replicas]
    down_ref = refs[replicas]
    mid_ref, inside_ref = refs[replicas + 1 + after :]
    slots, rank, width = down_ref.shape
    rows = jnp.concatenate([r[:, pl.ds(0, width)] for r in received], axis=0)
    inside = jnp.concatenate([r[:, pl.ds(width, LANES)] for r in received], axis=0)
    inside_ref[...] = inside
    projected = _dot(rows, down_ref[...].reshape(slots * rank, width), 1, 1)
    lane_slot = _iota(projected.shape, 1) // rank
    mine = lane_slot == inside[:, 0:1].astype(jnp.int32)
    projected = jnp.where(mine, projected, 0.0).astype(jnp.bfloat16)
    beside = LANES // rank
    some = projected.shape[0] // beside
    packed = 0.0
    for b in range(beside):
        lane = _iota((slots * rank, LANES), 1) - b * rank
        fold = _iota((slots * rank, LANES), 0) % rank == lane
        packed = packed + _dot(projected[b * some : (b + 1) * some, :], fold.astype(jnp.bfloat16))
    mid_ref[...] = packed.astype(jnp.bfloat16)


def down(received, slot_down_weight, after=()):
    replicas = len(received)
    rows = replicas * CAP
    return pl.pallas_call(
        functools.partial(down_kernel, replicas, len(after)),
        in_specs=[VMEM] * (replicas + 1) + [ANY] * len(after),
        out_specs=[VMEM, VMEM],
        out_shape=[
            jax.ShapeDtypeStruct((rows * slot_down_weight.shape[1] // LANES, LANES), jnp.bfloat16),
            jax.ShapeDtypeStruct((rows, LANES), jnp.bfloat16),
        ],
        compiler_params=PARAMS,
        name="down",
    )(*received, slot_down_weight, *after)


def up_kernel(parts, after, *refs):
    mids = refs[:parts]
    inside_ref, up_ref = refs[parts : parts + 2]
    out_refs = refs[parts + 2 + after :]
    slots, rank, width = up_ref.shape
    mid = mids[0][...].astype(jnp.float32)
    for m in mids[1:]:
        mid = mid + m[...].astype(jnp.float32)
    mid = mid.astype(jnp.bfloat16)
    wide = []
    for b in range(LANES // rank):
        lane = _iota((LANES, slots * rank), 0) - b * rank
        spread = _iota((LANES, slots * rank), 1) % rank == lane
        wide.append(_dot(mid, spread.astype(jnp.bfloat16)))
    wide = jnp.concatenate(wide, axis=0)
    mine = _iota(wide.shape, 1) // rank == inside_ref[:, 0:1].astype(jnp.int32)
    wide = jnp.where(mine, wide, 0.0).astype(jnp.bfloat16)
    delta = _dot(wide, up_ref[...].reshape(slots * rank, width)).astype(jnp.bfloat16)
    for r, out_ref in enumerate(out_refs):
        out_ref[...] = delta[r * CAP : (r + 1) * CAP, :]


def up(mids, inside, slot_up_weight, after=()):
    rows = inside.shape[0]
    replicas = rows // CAP
    width = slot_up_weight.shape[2]
    return pl.pallas_call(
        functools.partial(up_kernel, len(mids), len(after)),
        in_specs=[VMEM] * (len(mids) + 2) + [ANY] * len(after),
        out_specs=[VMEM] * replicas,
        out_shape=[jax.ShapeDtypeStruct((CAP, width), jnp.bfloat16)] * replicas,
        compiler_params=PARAMS,
        name="up",
    )(*mids, inside, slot_up_weight, *after)


def settle_kernel(step, replicas, after, *refs):
    returned = refs[:replicas]
    chosen_ref, a_ref, residual_ref, w_hbm = refs[replicas : replicas + 4]
    *out_refs, held, sems = refs[replicas + 4 + after :]
    width = residual_ref.shape[1]
    weights = Weights(w_hbm, held, sems, column_owner(step) * width, width)
    weights.start()
    rows = jnp.concatenate([r[...] for r in returned], axis=0)
    delta = _dot(chosen_ref[...], rows, 0, 0)
    total = residual_ref[...].astype(jnp.float32) + delta
    weights.wait()
    total = total + jnp.concatenate([p for _, p in weights.products(a_ref[...])], axis=1)
    for (start, chunk), out_ref in zip(chain_columns(width), out_refs):
        out_ref[...] = total[:, start : start + chunk]


def settle(step, returned, chosen, attended, residual, weight, after=()):
    replicas = len(returned)
    rows, width = residual.shape
    chains = chain_columns(width)
    return pl.pallas_call(
        functools.partial(settle_kernel, step, replicas, len(after)),
        in_specs=[VMEM] * (replicas + 3) + [ANY] * (1 + len(after)),
        out_specs=[VMEM] * len(chains),
        out_shape=[jax.ShapeDtypeStruct((rows, chunk), jnp.float32) for _, chunk in chains],
        scratch_shapes=Weights.scratch(weight.shape[0], width),
        compiler_params=PARAMS,
        name="settle",
    )(*returned, chosen, attended, residual, weight, *after)


def finish_kernel(start, arrived_ref, settled_ref, *refs):
    out_hbm, held, sems = refs[-3:]
    rows, chunk = arrived_ref.shape
    half = rows // 2
    copies = []
    for i in range(2):
        part = pl.ds(i * half, half)
        total = settled_ref[part, :] + arrived_ref[part, :].astype(jnp.float32)
        held[part, :] = total.astype(jnp.bfloat16)
        target = out_hbm.at[part, pl.ds(start, chunk)]
        copies.append(pltpu.make_async_copy(held.at[part, :], target, sems.at[i]))
        copies[-1].start()
    for copy in copies:
        copy.wait()


def finish(chain, arrived, settled, earlier, width):
    rows = arrived.shape[0]
    start, chunk = chain_columns(width)[chain]
    operands = [arrived, settled] + ([earlier] if earlier is not None else [])
    return pl.pallas_call(
        functools.partial(finish_kernel, start),
        in_specs=[VMEM, VMEM] + ([ANY] if earlier is not None else []),
        out_specs=ANY,
        out_shape=jax.ShapeDtypeStruct((rows, width), jnp.bfloat16),
        input_output_aliases={2: 0} if earlier is not None else {},
        scratch_shapes=[
            pltpu.VMEM((rows, chunk), jnp.bfloat16),
            pltpu.SemaphoreType.DMA((2,)),
        ],
        compiler_params=PARAMS,
        name="finish",
    )(*operands)


def hold_kernel(*refs):
    pass


def hold(x, after):
    return pl.pallas_call(
        hold_kernel,
        in_specs=[ANY] * (1 + len(after)),
        out_specs=ANY,
        out_shape=jax.ShapeDtypeStruct(x.shape, x.dtype),
        input_output_aliases={0: 0},
        compiler_params=PARAMS,
        name="hold",
    )(x, *after)


def per_device(
    residual,
    query,
    cached_key_rows,
    cached_value_rows,
    new_token_key,
    new_token_value,
    lengths,
    output_weight,
    slot_down_weight,
    slot_up_weight,
    placement,
    request_adapter,
):
    count = lax.axis_size("tensor")
    replicas = lax.axis_size("dp")
    block = residual.shape[1]
    order = ring_order(count)
    ring = [(order[p], order[(p + 1) % count]) for p in range(count)]

    def exchange(blocks):
        moved = [
            lax.ppermute(blocks[r], "dp", [(i, i ^ r) for i in range(replicas)])
            for r in range(1, replicas)
        ]
        return [blocks[0]] + moved

    def forward(x):
        return lax.ppermute(x, "tensor", ring)

    def pair_sums(x):
        found = []
        for away in range(1, count // 2):
            pairs = [(p, (p + away) % (count // 2)) for p in range(count // 2)]
            near, far = [], []
            for p, q in pairs:
                sender = 2 * p if p < q else 2 * p + 1
                straight = 2 * q + (sender % 2)
                near.append((sender, straight))
                far.append((sender, straight ^ 1))
            one = lax.ppermute(x, "tensor", near)
            other = lax.ppermute(x, "tensor", far)
            found += [one, other]
        return found

    def next_hop(step, chain, after, cost=None):
        arrived = forward(travelling[chain])
        travelling[chain] = hop(step, chain, arrived, attended, output_weight, block, after, cost)

    attended, first, chosen, *leaving = attend(
        query, cached_key_rows, cached_value_rows, new_token_key, new_token_value, lengths,
        output_weight, request_adapter, placement, block, replicas, slot_down_weight.shape[0],
    )
    second = hop(0, 1, None, attended, output_weight, block)
    rows_here = exchange(leaving)
    mid, inside = down(rows_here, slot_down_weight, after=[second])
    travelling = [first, hold(second, after=[mid])]

    def added(a, b):
        return (a.astype(jnp.float32) + b.astype(jnp.float32)).astype(a.dtype)

    rank_sum = added(mid, lax.ppermute(mid, "tensor", [(i, i ^ 1) for i in range(count)]))
    rank_sums = [rank_sum] + pair_sums(rank_sum)
    next_hop(1, 0, after=[rank_sum, travelling[1]], cost=LONG)
    next_hop(1, 1, after=rank_sums[1:], cost=LONG)
    for step in range(2, count - 1):
        for chain in range(2):
            if (step, chain) == (2, 0):
                next_hop(step, chain, after=())
                deltas = up(rank_sums, inside, slot_up_weight, after=[travelling[0]])
                returned = exchange(deltas)
            else:
                next_hop(step, chain, after=[deltas[0]])
    settled = settle(
        count - 1, returned, chosen, attended, residual, output_weight, after=[travelling[1]]
    )
    out = None
    for chain in range(2):
        arrived = forward(travelling[chain])
        out = finish(chain, arrived, settled[chain], out, block)
    return out


def solution(mesh):
    placed = (
        P(("parts", "dp"), "tensor"),
        P(("parts", "dp"), "tensor", None),
        P(("parts", "dp"), None, "tensor", None),
        P(("parts", "dp"), None, "tensor", None),
        P(("parts", "dp"), "tensor", None),
        P(("parts", "dp"), "tensor", None),
        P(("parts", "dp")),
        P("tensor", None),
        P("dp", None, "tensor"),
        P("dp", None, "tensor"),
        P("parts"),
        P(("parts", "dp")),
    )
    return jax.shard_map(
        per_device,
        mesh=mesh,
        in_specs=placed,
        out_specs=P(("parts", "dp"), "tensor"),
        check_vma=False,
    )
```

```python
import functools
import math

import jax
import jax.numpy as jnp
from jax import lax
from jax.experimental import pallas as pl
from jax.experimental.pallas import tpu as pltpu
from jax.sharding import PartitionSpec as P

GROUP = 4
CAP = 64
LANES = 128
MASKED = -1e30
VMEM_LIMIT = 50 * 1024 * 1024
FULL_VMEM = 61 * 1024 * 1024
SHARES = ((5, 3),)
PIECE = 512
SPLIT = 4

VMEM = pl.BlockSpec(memory_space=pltpu.VMEM)
ANY = pl.BlockSpec(memory_space=pl.ANY)
LONG = pl.CostEstimate(flops=20 * 10**9, transcendentals=0, bytes_accessed=40 * 10**6)
MEDIUM = pl.CostEstimate(flops=3 * 10**9, transcendentals=0, bytes_accessed=6 * 10**6)
PARAMS = pltpu.CompilerParams(vmem_limit_bytes=VMEM_LIMIT)


def _dot(a, b, left=1, right=0):
    return lax.dot_general(
        a, b, (((left,), (right,)), ((), ())), preferred_element_type=jnp.float32
    )


def _iota(shape, axis):
    return lax.broadcasted_iota(jnp.int32, shape, axis)


def ring_order(count):
    return list(range(0, count, 2)) + list(range(1, count, 2))[::-1]


def column_owner(step):
    count = lax.axis_size("tensor")
    here = lax.axis_index("tensor")
    half = here // 2
    spot = jnp.where(here % 2 == 0, half, count - 1 - half)
    spot = lax.rem(spot - 1 - step + 2 * count, count)
    return jnp.where(2 * spot < count, 2 * spot, 2 * (count - spot) - 1)


def chain_columns(width):
    shares = next(s for s in SHARES if width % (sum(s) * LANES) == 0)
    unit = width // sum(shares)
    return [(sum(shares[:c]) * unit, shares[c] * unit) for c in range(len(shares))]


class Weights:
    def __init__(self, w_ref, held, sems, first, width):
        depth = w_ref.shape[0] // SPLIT
        first = pl.multiple_of(first, LANES)
        self.held = held
        self.copies = [
            pltpu.make_async_copy(
                w_ref.at[pl.ds(s * depth, depth), pl.ds(first, width)],
                held.at[pl.ds(s * depth, depth), :],
                sems.at[s],
            )
            for s in range(SPLIT)
        ]

    def start(self):
        for copy in self.copies:
            copy.start()

    def wait(self):
        for copy in self.copies:
            copy.wait()

    def products(self, a):
        width = self.held.shape[1]
        for at in range(0, width, PIECE):
            columns = pl.ds(at, min(PIECE, width - at))
            yield columns, _dot(a, self.held[:, columns])

    @staticmethod
    def scratch(depth, width):
        return [
            pltpu.VMEM((depth, width), jnp.bfloat16),
            pltpu.SemaphoreType.DMA((SPLIT,)),
        ]


def row_max(arrays):
    full = None
    tops = []
    for x in arrays:
        width = x.shape[1]
        if width % LANES:
            tops.append(jnp.max(x, axis=1, keepdims=True))
            continue
        for at in range(0, width, LANES):
            tile = x[:, at : at + LANES]
            full = tile if full is None else jnp.maximum(full, tile)
    if full is not None:
        tops.append(jnp.max(full, axis=1, keepdims=True))
    return functools.reduce(jnp.maximum, tops)


def attend_kernel(
    heads, kv, cache, steps, block, replicas, slots,
    len_hbm, adapter_hbm, placement_hbm, q_hbm, k_hbm, v_hbm, nk_hbm, nv_hbm, w_hbm,
    *refs,
):
    a_hbm, out_hbm, chosen_hbm, *sent_hbm = refs[: 3 + replicas]
    (
        a_ref, out_ref, chosen_ref, sent_ref, out_sems,
        len_ref, adapter_ref, placement_ref, q_ref, k_ref, v_ref, nk_ref, nv_ref,
        scores_ref, mixed_ref, sems, small_sems, w_held, w_sems,
    ) = refs[3 + replicas :]
    requests = len_ref.shape[1]
    width = q_hbm.shape[1]
    per = requests // steps
    groups = per // GROUP
    group_rows = GROUP * heads
    group_cols = GROUP * cache * kv
    per_kv = heads // kv
    scale = math.log2(math.e) / math.sqrt(width)

    def part(kind, step):
        source, target, count = (
            (q_hbm, q_ref, heads),
            (k_hbm, k_ref, cache * kv),
            (v_hbm, v_ref, cache * kv),
        )[kind]
        rows = pl.ds(step * per * count, per * count)
        return pltpu.make_async_copy(source.at[rows, :], target.at[rows, :], sems.at[kind, step])

    small = [
        pltpu.make_async_copy(source, target, small_sems.at[i])
        for i, (source, target) in enumerate(
            (
                (nk_hbm, nk_ref),
                (len_hbm, len_ref),
                (nv_hbm, nv_ref),
                (adapter_hbm, adapter_ref),
                (placement_hbm, placement_ref),
            )
        )
    ]
    leaving = []

    def leave(source, target):
        copy = pltpu.make_async_copy(source, target, out_sems.at[len(leaving)])
        copy.start()
        leaving.append(copy)

    chunk = out_ref.shape[1]
    weights = Weights(w_hbm, w_held, w_sems, column_owner(0) * block, chunk)
    part(0, 0).start()
    part(1, 0).start()
    for copy in small[:2]:
        copy.start()
    part(0, 1).start()
    part(1, 1).start()
    part(2, 0).start()
    for copy in small[2:]:
        copy.start()
    part(2, 1).start()
    for step in range(2, steps):
        for kind in range(3):
            part(kind, step).start()
    weights.start()

    row = _iota((group_rows, group_cols), 0)
    col = _iota((group_rows, group_cols), 1)
    same = (row // heads == col // (cache * kv)) & ((row % heads) // per_kv == col % kv)
    own_bias = jnp.where(same, 0.0, MASKED)
    row = _iota((group_rows, per * kv), 0)
    col = _iota((group_rows, per * kv), 1)
    fresh_kv = (row % heads) // per_kv == col % kv
    fresh_distance = col // kv - row // heads
    ones = jnp.ones((max(group_cols, per * kv), LANES), jnp.bfloat16)

    def arrive(step):
        part(0, step).wait()
        part(1, step).wait()

    def scores(step):
        side = step % 2
        q_at = step * per * heads
        k_at = step * per * cache * kv
        for g in range(groups):
            scores_ref[side, pl.ds(g * group_rows, group_rows), pl.ds(0, group_cols)] = _dot(
                q_ref[pl.ds(q_at + g * group_rows, group_rows), :],
                k_ref[pl.ds(k_at + g * group_cols, group_cols), :],
                1,
                1,
            )
        scores_ref[side, :, pl.ds(group_cols, per * kv)] = _dot(
            q_ref[pl.ds(q_at, per * heads), :], nk_ref[pl.ds(step * per * kv, per * kv), :], 1, 1
        )

    for copy in small:
        copy.wait()
    plan_routes(slots, adapter_ref, placement_ref, chosen_ref, sent_ref)
    leave(chosen_ref, chosen_hbm)
    counts = len_ref[...].astype(jnp.float32)
    all_groups = requests // GROUP
    of_group = _iota((all_groups, requests), 1) // GROUP == _iota((all_groups, requests), 0)
    counts = jnp.where(of_group, counts, 0.0).astype(jnp.bfloat16)
    spread = _iota((requests, group_cols), 0) % GROUP == _iota((requests, group_cols), 1) // (cache * kv)
    counts = _dot(counts, spread.astype(jnp.bfloat16))
    position = (_iota((all_groups, group_cols), 1) // kv) % cache
    length_bias = jnp.where(position.astype(jnp.float32) < counts, 0.0, MASKED)

    arrive(0)
    scores(0)
    for step in range(steps):
        side = step % 2
        k_at = step * per * cache * kv
        f_at = step * per * kv
        part(2, step).wait()
        if step + 1 < steps:
            arrive(step + 1)
            scores(step + 1)
        held = []
        fresh = []
        for g in range(groups):
            rows = pl.ds(g * group_rows, group_rows)
            bias = own_bias + length_bias[step * groups + g : step * groups + g + 1, :]
            cached = scores_ref[side, rows, pl.ds(0, group_cols)] + bias
            new = scores_ref[side, rows, pl.ds(group_cols, per * kv)]
            new = jnp.where(fresh_kv & (fresh_distance == g * GROUP), new, MASKED)
            top = row_max([cached, new])
            cached = jnp.exp2((cached - top) * scale).astype(jnp.bfloat16)
            fresh.append(jnp.exp2((new - top) * scale).astype(jnp.bfloat16))
            values = v_ref[pl.ds(k_at + g * group_cols, group_cols), :]
            held.append(_dot(cached, jnp.concatenate([values, ones[:group_cols]], axis=1)))
        values = jnp.concatenate([nv_ref[pl.ds(f_at, per * kv), :], ones[: per * kv]], axis=1)
        fresh = _dot(jnp.concatenate(fresh, axis=0), values)
        for g in range(groups):
            rows = slice(g * group_rows, (g + 1) * group_rows)
            mixed = fresh[rows, :] + held[g]
            mixed_ref[side, rows, :] = mixed[:, :width] / mixed[:, width:]
        for h in range(heads):
            a_ref[pl.ds(step * per, per), pl.ds(h * width, width)] = mixed_ref[
                side, pl.ds(h, per, stride=heads), :
            ].astype(jnp.bfloat16)
        rows = pl.ds(step * per, per)
        leave(a_ref.at[rows, :], a_hbm.at[rows, :])

    weights.wait()
    for columns, product in weights.products(a_ref[...]):
        out_ref[:, columns] = product.astype(jnp.bfloat16)
        leave(out_ref.at[:, columns], out_hbm.at[:, columns])
    sent_ref[:, pl.ds(0, heads * width)] = _dot(chosen_ref[...], a_ref[...]).astype(jnp.bfloat16)
    for r in range(replicas):
        leave(sent_ref.at[pl.ds(r * CAP, CAP), :], sent_hbm[r])
    for copy in leaving:
        copy.wait()


def plan_routes(slots, adapter_ref, placement_ref, chosen_ref, sent_ref):
    replicas = sent_ref.shape[0] // CAP
    requests = adapter_ref.shape[1]
    table = placement_ref.shape[1]
    matches = _iota((table, requests), 0) == adapter_ref[...]
    placed = jnp.broadcast_to(placement_ref[...].astype(jnp.float32), (8, table))
    slot = _dot(placed.astype(jnp.bfloat16), matches.astype(jnp.bfloat16)).astype(jnp.int32)
    slot = slot[0:1, :]
    holder = (slot // slots) ^ lax.axis_index("dp")
    inside = slot % slots
    of_holder = _iota((max(replicas, 8), requests), 0) == holder
    earlier = _iota((requests, requests), 0) < _iota((requests, requests), 1)
    before = _dot(of_holder.astype(jnp.bfloat16), earlier.astype(jnp.bfloat16))
    before = jnp.sum(jnp.where(of_holder, before, 0.0), axis=0, keepdims=True).astype(jnp.int32)
    target = holder * CAP + before
    here = _iota((replicas * CAP, requests), 0) == target
    chosen_ref[...] = here.astype(jnp.bfloat16)
    inner = jnp.sum(jnp.where(here, inside.astype(jnp.float32), 0.0), axis=1, keepdims=True)
    inner = jnp.broadcast_to(inner, (replicas * CAP, LANES)).astype(jnp.bfloat16)
    sent_ref[:, pl.ds(sent_ref.shape[1] - LANES, LANES)] = inner


def attend(
    query, keys, values, new_key, new_value, lengths, weight, request_adapter, placement,
    block, replicas, slots,
):
    requests, heads, width = query.shape
    cache, kv = keys.shape[1], keys.shape[2]
    steps = 4
    per = requests // steps
    columns = GROUP * cache * kv + per * kv
    features = heads * width
    chunk = chain_columns(block)[0][1]
    small = [lengths.reshape(1, -1), request_adapter.reshape(1, -1), placement.reshape(1, -1)]
    operands = [
        query.reshape(requests * heads, width),
        keys.reshape(requests * cache * kv, width),
        values.reshape(requests * cache * kv, width),
        new_key.reshape(requests * kv, width),
        new_value.reshape(requests * kv, width),
    ]
    return pl.pallas_call(
        functools.partial(attend_kernel, heads, kv, cache, steps, block, replicas, slots),
        in_specs=[ANY] * 9,
        out_specs=[ANY] * (3 + replicas),
        out_shape=[
            jax.ShapeDtypeStruct((requests, features), jnp.bfloat16),
            jax.ShapeDtypeStruct((requests, chunk), jnp.bfloat16),
            jax.ShapeDtypeStruct((replicas * CAP, requests), jnp.bfloat16),
        ]
        + [jax.ShapeDtypeStruct((CAP, features + LANES), jnp.bfloat16)] * replicas,
        scratch_shapes=[
            pltpu.VMEM((requests, features), jnp.bfloat16),
            pltpu.VMEM((requests, chunk), jnp.bfloat16),
            pltpu.VMEM((replicas * CAP, requests), jnp.bfloat16),
            pltpu.VMEM((replicas * CAP, features + LANES), jnp.bfloat16),
            pltpu.SemaphoreType.DMA((1 + steps + pl.cdiv(chunk, PIECE) + replicas,)),
        ]
        + [pltpu.VMEM(x.shape, x.dtype) for x in small + operands]
        + [
            pltpu.VMEM((2, per * heads, columns), jnp.float32),
            pltpu.VMEM((2, per * heads, width), jnp.float32),
            pltpu.SemaphoreType.DMA((3, steps)),
            pltpu.SemaphoreType.DMA((5,)),
        ]
        + Weights.scratch(weight.shape[0], chunk),
        compiler_params=pltpu.CompilerParams(vmem_limit_bytes=FULL_VMEM),
        name="attend",
    )(*small, *operands, weight)


def hop_kernel(step, block, start, arriving, after, *refs):
    if arriving:
        arrived_ref, *refs = refs
    a_ref, w_hbm, *refs = refs
    out_ref, held, sems = refs[after:]
    chunk = out_ref.shape[1]
    first = column_owner(step) * block + start
    weights = Weights(w_hbm, held, sems, first, chunk)
    weights.start()
    weights.wait()
    for columns, product in weights.products(a_ref[...]):
        if arriving:
            product = product + arrived_ref[:, columns].astype(jnp.float32)
        out_ref[:, columns] = product.astype(jnp.bfloat16)


def hop(step, chain, arrived, attended, weight, block, after=(), cost=None):
    arriving = arrived is not None
    start, chunk = chain_columns(block)[chain]
    operands = ([arrived] if arriving else []) + [attended, weight, *after]
    return pl.pallas_call(
        functools.partial(hop_kernel, step, block, start, arriving, len(after)),
        in_specs=[VMEM] * (1 + arriving) + [ANY] + [ANY] * len(after),
        out_specs=VMEM,
        out_shape=jax.ShapeDtypeStruct((attended.shape[0], chunk), jnp.bfloat16),
        scratch_shapes=Weights.scratch(weight.shape[0], chunk),
        compiler_params=PARAMS,
        cost_estimate=cost,
        name="hop",
    )(*operands)


def down_kernel(replicas, after, *refs):
    received = refs[:replicas]
    down_ref = refs[replicas]
    mid_ref, inside_ref = refs[replicas + 1 + after :]
    slots, rank, width = down_ref.shape
    rows = jnp.concatenate([r[:, pl.ds(0, width)] for r in received], axis=0)
    inside = jnp.concatenate([r[:, pl.ds(width, LANES)] for r in received], axis=0)
    inside_ref[...] = inside
    projected = _dot(rows, down_ref[...].reshape(slots * rank, width), 1, 1)
    lane_slot = _iota(projected.shape, 1) // rank
    mine = lane_slot == inside[:, 0:1].astype(jnp.int32)
    projected = jnp.where(mine, projected, 0.0).astype(jnp.bfloat16)
    beside = LANES // rank
    some = projected.shape[0] // beside
    packed = 0.0
    for b in range(beside):
        lane = _iota((slots * rank, LANES), 1) - b * rank
        fold = _iota((slots * rank, LANES), 0) % rank == lane
        packed = packed + _dot(projected[b * some : (b + 1) * some, :], fold.astype(jnp.bfloat16))
    mid_ref[...] = packed.astype(jnp.bfloat16)


def down(received, slot_down_weight, after=()):
    replicas = len(received)
    rows = replicas * CAP
    return pl.pallas_call(
        functools.partial(down_kernel, replicas, len(after)),
        in_specs=[VMEM] * (replicas + 1) + [ANY] * len(after),
        out_specs=[VMEM, VMEM],
        out_shape=[
            jax.ShapeDtypeStruct((rows * slot_down_weight.shape[1] // LANES, LANES), jnp.bfloat16),
            jax.ShapeDtypeStruct((rows, LANES), jnp.bfloat16),
        ],
        compiler_params=PARAMS,
        name="down",
    )(*received, slot_down_weight, *after)


def up_kernel(parts, after, *refs):
    mids = refs[:parts]
    inside_ref, up_ref = refs[parts : parts + 2]
    out_refs = refs[parts + 2 + after :]
    slots, rank, width = up_ref.shape
    mid = mids[0][...].astype(jnp.float32)
    for m in mids[1:]:
        mid = mid + m[...].astype(jnp.float32)
    mid = mid.astype(jnp.bfloat16)
    wide = []
    for b in range(LANES // rank):
        lane = _iota((LANES, slots * rank), 0) - b * rank
        spread = _iota((LANES, slots * rank), 1) % rank == lane
        wide.append(_dot(mid, spread.astype(jnp.bfloat16)))
    wide = jnp.concatenate(wide, axis=0)
    mine = _iota(wide.shape, 1) // rank == inside_ref[:, 0:1].astype(jnp.int32)
    wide = jnp.where(mine, wide, 0.0).astype(jnp.bfloat16)
    delta = _dot(wide, up_ref[...].reshape(slots * rank, width)).astype(jnp.bfloat16)
    for r, out_ref in enumerate(out_refs):
        out_ref[...] = delta[r * CAP : (r + 1) * CAP, :]


def up(mids, inside, slot_up_weight, after=()):
    rows = inside.shape[0]
    replicas = rows // CAP
    width = slot_up_weight.shape[2]
    return pl.pallas_call(
        functools.partial(up_kernel, len(mids), len(after)),
        in_specs=[VMEM] * (len(mids) + 2) + [ANY] * len(after),
        out_specs=[VMEM] * replicas,
        out_shape=[jax.ShapeDtypeStruct((CAP, width), jnp.bfloat16)] * replicas,
        compiler_params=PARAMS,
        name="up",
    )(*mids, inside, slot_up_weight, *after)


def settle_kernel(step, replicas, after, *refs):
    returned = refs[:replicas]
    chosen_ref, a_ref, residual_ref, w_hbm = refs[replicas : replicas + 4]
    *out_refs, held, sems = refs[replicas + 4 + after :]
    width = residual_ref.shape[1]
    weights = Weights(w_hbm, held, sems, column_owner(step) * width, width)
    weights.start()
    rows = jnp.concatenate([r[...] for r in returned], axis=0)
    delta = _dot(chosen_ref[...], rows, 0, 0)
    total = residual_ref[...].astype(jnp.float32) + delta
    weights.wait()
    total = total + jnp.concatenate([p for _, p in weights.products(a_ref[...])], axis=1)
    for (start, chunk), out_ref in zip(chain_columns(width), out_refs):
        out_ref[...] = total[:, start : start + chunk]


def settle(step, returned, chosen, attended, residual, weight, after=()):
    replicas = len(returned)
    rows, width = residual.shape
    chains = chain_columns(width)
    return pl.pallas_call(
        functools.partial(settle_kernel, step, replicas, len(after)),
        in_specs=[VMEM] * (replicas + 3) + [ANY] * (1 + len(after)),
        out_specs=[VMEM] * len(chains),
        out_shape=[jax.ShapeDtypeStruct((rows, chunk), jnp.float32) for _, chunk in chains],
        scratch_shapes=Weights.scratch(weight.shape[0], width),
        compiler_params=PARAMS,
        cost_estimate=LONG,
        name="settle",
    )(*returned, chosen, attended, residual, weight, *after)


def finish_kernel(start, arrived_ref, settled_ref, *refs):
    out_hbm, held, sems = refs[-3:]
    rows, chunk = arrived_ref.shape
    half = rows // 2
    copies = []
    for i in range(2):
        part = pl.ds(i * half, half)
        total = settled_ref[part, :] + arrived_ref[part, :].astype(jnp.float32)
        held[part, :] = total.astype(jnp.bfloat16)
        target = out_hbm.at[part, pl.ds(start, chunk)]
        copies.append(pltpu.make_async_copy(held.at[part, :], target, sems.at[i]))
        copies[-1].start()
    for copy in copies:
        copy.wait()


def finish(chain, arrived, settled, earlier, width):
    rows = arrived.shape[0]
    start, chunk = chain_columns(width)[chain]
    operands = [arrived, settled] + ([earlier] if earlier is not None else [])
    return pl.pallas_call(
        functools.partial(finish_kernel, start),
        in_specs=[VMEM, VMEM] + ([ANY] if earlier is not None else []),
        out_specs=ANY,
        out_shape=jax.ShapeDtypeStruct((rows, width), jnp.bfloat16),
        input_output_aliases={2: 0} if earlier is not None else {},
        scratch_shapes=[
            pltpu.VMEM((rows, chunk), jnp.bfloat16),
            pltpu.SemaphoreType.DMA((2,)),
        ],
        compiler_params=PARAMS,
        name="finish",
    )(*operands)


def hold_kernel(*refs):
    pass


def hold(x, after):
    return pl.pallas_call(
        hold_kernel,
        in_specs=[ANY] * (1 + len(after)),
        out_specs=ANY,
        out_shape=jax.ShapeDtypeStruct(x.shape, x.dtype),
        input_output_aliases={0: 0},
        compiler_params=PARAMS,
        name="hold",
    )(x, *after)


def per_device(
    residual,
    query,
    cached_key_rows,
    cached_value_rows,
    new_token_key,
    new_token_value,
    lengths,
    output_weight,
    slot_down_weight,
    slot_up_weight,
    placement,
    request_adapter,
):
    count = lax.axis_size("tensor")
    replicas = lax.axis_size("dp")
    block = residual.shape[1]
    order = ring_order(count)
    ring = [(order[p], order[(p + 1) % count]) for p in range(count)]

    def exchange(blocks):
        moved = [
            lax.ppermute(blocks[r], "dp", [(i, i ^ r) for i in range(replicas)])
            for r in range(1, replicas)
        ]
        return [blocks[0]] + moved

    def forward(x):
        return lax.ppermute(x, "tensor", ring)

    def pair_sums(x):
        found = []
        for away in range(1, count // 2):
            pairs = [(p, (p + away) % (count // 2)) for p in range(count // 2)]
            near, far = [], []
            for p, q in pairs:
                sender = 2 * p if p < q else 2 * p + 1
                straight = 2 * q + (sender % 2)
                near.append((sender, straight))
                far.append((sender, straight ^ 1))
            one = lax.ppermute(x, "tensor", near)
            other = lax.ppermute(x, "tensor", far)
            found += [one, other]
        return found

    def next_hop(step, chain, after, cost=None):
        arrived = forward(travelling[chain])
        travelling[chain] = hop(step, chain, arrived, attended, output_weight, block, after, cost)

    attended, first, chosen, *leaving = attend(
        query, cached_key_rows, cached_value_rows, new_token_key, new_token_value, lengths,
        output_weight, request_adapter, placement, block, replicas, slot_down_weight.shape[0],
    )
    second = hop(0, 1, None, attended, output_weight, block)
    rows_here = exchange(leaving)
    mid, inside = down(rows_here, slot_down_weight, after=[second])
    travelling = [first, hold(second, after=[mid])]

    def added(a, b):
        return (a.astype(jnp.float32) + b.astype(jnp.float32)).astype(a.dtype)

    rank_sum = added(mid, lax.ppermute(mid, "tensor", [(i, i ^ 1) for i in range(count)]))
    rank_sums = [rank_sum] + pair_sums(rank_sum)
    next_hop(1, 0, after=[rank_sum, travelling[1]], cost=LONG)
    next_hop(1, 1, after=[travelling[0]], cost=MEDIUM)
    for step in range(2, count - 1):
        for chain in range(2):
            if (step, chain) == (2, 0):
                next_hop(step, chain, after=rank_sums[1:], cost=LONG)
                deltas = up(rank_sums, inside, slot_up_weight, after=[travelling[0]])
                returned = exchange(deltas)
            else:
                next_hop(step, chain, after=[deltas[0]])
    settled = settle(
        count - 1, returned, chosen, attended, residual, output_weight, after=[travelling[1]]
    )
    out = None
    for chain in range(2):
        arrived = forward(travelling[chain])
        out = finish(chain, arrived, settled[chain], out, block)
    return out


def solution(mesh):
    placed = (
        P(("parts", "dp"), "tensor"),
        P(("parts", "dp"), "tensor", None),
        P(("parts", "dp"), None, "tensor", None),
        P(("parts", "dp"), None, "tensor", None),
        P(("parts", "dp"), "tensor", None),
        P(("parts", "dp"), "tensor", None),
        P(("parts", "dp")),
        P("tensor", None),
        P("dp", None, "tensor"),
        P("dp", None, "tensor"),
        P("parts"),
        P(("parts", "dp")),
    )
    return jax.shard_map(
        per_device,
        mesh=mesh,
        in_specs=placed,
        out_specs=P(("parts", "dp"), "tensor"),
        check_vma=False,
    )
```

```python
import functools
import math

import jax
import jax.numpy as jnp
from jax import lax
from jax.experimental import pallas as pl
from jax.experimental.pallas import tpu as pltpu
from jax.sharding import PartitionSpec as P

GROUP = 4
CAP = 64
LANES = 128
MASKED = -1e30
VMEM_LIMIT = 50 * 1024 * 1024
FULL_VMEM = 61 * 1024 * 1024
SHARES = ((5, 3),)
PIECE = 512
SPLIT = 4

VMEM = pl.BlockSpec(memory_space=pltpu.VMEM)
ANY = pl.BlockSpec(memory_space=pl.ANY)
LONG = pl.CostEstimate(flops=20 * 10**9, transcendentals=0, bytes_accessed=40 * 10**6)
MEDIUM = pl.CostEstimate(flops=4 * 10**9, transcendentals=0, bytes_accessed=8 * 10**6)
PARAMS = pltpu.CompilerParams(vmem_limit_bytes=VMEM_LIMIT)


def _dot(a, b, left=1, right=0):
    return lax.dot_general(
        a, b, (((left,), (right,)), ((), ())), preferred_element_type=jnp.float32
    )


def _iota(shape, axis):
    return lax.broadcasted_iota(jnp.int32, shape, axis)


def ring_order(count):
    return list(range(0, count, 2)) + list(range(1, count, 2))[::-1]


def column_owner(step):
    count = lax.axis_size("tensor")
    here = lax.axis_index("tensor")
    half = here // 2
    spot = jnp.where(here % 2 == 0, half, count - 1 - half)
    spot = lax.rem(spot - 1 - step + 2 * count, count)
    return jnp.where(2 * spot < count, 2 * spot, 2 * (count - spot) - 1)


def chain_columns(width):
    shares = next(s for s in SHARES if width % (sum(s) * LANES) == 0)
    unit = width // sum(shares)
    return [(sum(shares[:c]) * unit, shares[c] * unit) for c in range(len(shares))]


class Weights:
    def __init__(self, w_ref, held, sems, first, width):
        depth = w_ref.shape[0] // SPLIT
        first = pl.multiple_of(first, LANES)
        self.held = held
        self.copies = [
            pltpu.make_async_copy(
                w_ref.at[pl.ds(s * depth, depth), pl.ds(first, width)],
                held.at[pl.ds(s * depth, depth), :],
                sems.at[s],
            )
            for s in range(SPLIT)
        ]

    def start(self):
        for copy in self.copies:
            copy.start()

    def wait(self):
        for copy in self.copies:
            copy.wait()

    def products(self, a):
        width = self.held.shape[1]
        for at in range(0, width, PIECE):
            columns = pl.ds(at, min(PIECE, width - at))
            yield columns, _dot(a, self.held[:, columns])

    @staticmethod
    def scratch(depth, width):
        return [
            pltpu.VMEM((depth, width), jnp.bfloat16),
            pltpu.SemaphoreType.DMA((SPLIT,)),
        ]


def row_max(arrays):
    full = None
    tops = []
    for x in arrays:
        width = x.shape[1]
        if width % LANES:
            tops.append(jnp.max(x, axis=1, keepdims=True))
            continue
        for at in range(0, width, LANES):
            tile = x[:, at : at + LANES]
            full = tile if full is None else jnp.maximum(full, tile)
    if full is not None:
        tops.append(jnp.max(full, axis=1, keepdims=True))
    return functools.reduce(jnp.maximum, tops)


def attend_kernel(
    heads, kv, cache, steps, block, replicas, slots,
    len_hbm, adapter_hbm, placement_hbm, q_hbm, k_hbm, v_hbm, nk_hbm, nv_hbm, w_hbm,
    *refs,
):
    a_hbm, out_hbm, chosen_hbm, *sent_hbm = refs[: 3 + replicas]
    (
        a_ref, out_ref, chosen_ref, sent_ref, out_sems,
        len_ref, adapter_ref, placement_ref, q_ref, k_ref, v_ref, nk_ref, nv_ref,
        scores_ref, mixed_ref, sems, small_sems, w_held, w_sems,
    ) = refs[3 + replicas :]
    requests = len_ref.shape[1]
    width = q_hbm.shape[1]
    per = requests // steps
    groups = per // GROUP
    group_rows = GROUP * heads
    group_cols = GROUP * cache * kv
    per_kv = heads // kv
    scale = math.log2(math.e) / math.sqrt(width)

    def part(kind, step):
        source, target, count = (
            (q_hbm, q_ref, heads),
            (k_hbm, k_ref, cache * kv),
            (v_hbm, v_ref, cache * kv),
        )[kind]
        rows = pl.ds(step * per * count, per * count)
        return pltpu.make_async_copy(source.at[rows, :], target.at[rows, :], sems.at[kind, step])

    small = [
        pltpu.make_async_copy(source, target, small_sems.at[i])
        for i, (source, target) in enumerate(
            (
                (nk_hbm, nk_ref),
                (len_hbm, len_ref),
                (nv_hbm, nv_ref),
                (adapter_hbm, adapter_ref),
                (placement_hbm, placement_ref),
            )
        )
    ]
    leaving = []

    def leave(source, target):
        copy = pltpu.make_async_copy(source, target, out_sems.at[len(leaving)])
        copy.start()
        leaving.append(copy)

    chunk = out_ref.shape[1]
    weights = Weights(w_hbm, w_held, w_sems, column_owner(0) * block, chunk)
    part(0, 0).start()
    part(1, 0).start()
    for copy in small[:2]:
        copy.start()
    part(0, 1).start()
    part(1, 1).start()
    part(2, 0).start()
    for copy in small[2:]:
        copy.start()
    part(2, 1).start()
    for step in range(2, steps):
        for kind in range(3):
            part(kind, step).start()
    weights.start()

    row = _iota((group_rows, group_cols), 0)
    col = _iota((group_rows, group_cols), 1)
    same = (row // heads == col // (cache * kv)) & ((row % heads) // per_kv == col % kv)
    own_bias = jnp.where(same, 0.0, MASKED)
    row = _iota((group_rows, per * kv), 0)
    col = _iota((group_rows, per * kv), 1)
    fresh_kv = (row % heads) // per_kv == col % kv
    fresh_distance = col // kv - row // heads
    ones = jnp.ones((max(group_cols, per * kv), LANES), jnp.bfloat16)

    def arrive(step):
        part(0, step).wait()
        part(1, step).wait()

    def scores(step):
        side = step % 2
        q_at = step * per * heads
        k_at = step * per * cache * kv
        for g in range(groups):
            scores_ref[side, pl.ds(g * group_rows, group_rows), pl.ds(0, group_cols)] = _dot(
                q_ref[pl.ds(q_at + g * group_rows, group_rows), :],
                k_ref[pl.ds(k_at + g * group_cols, group_cols), :],
                1,
                1,
            )
        scores_ref[side, :, pl.ds(group_cols, per * kv)] = _dot(
            q_ref[pl.ds(q_at, per * heads), :], nk_ref[pl.ds(step * per * kv, per * kv), :], 1, 1
        )

    for copy in small:
        copy.wait()
    plan_routes(slots, adapter_ref, placement_ref, chosen_ref, sent_ref)
    leave(chosen_ref, chosen_hbm)
    counts = len_ref[...].astype(jnp.float32)
    all_groups = requests // GROUP
    of_group = _iota((all_groups, requests), 1) // GROUP == _iota((all_groups, requests), 0)
    counts = jnp.where(of_group, counts, 0.0).astype(jnp.bfloat16)
    spread = _iota((requests, group_cols), 0) % GROUP == _iota((requests, group_cols), 1) // (cache * kv)
    counts = _dot(counts, spread.astype(jnp.bfloat16))
    position = (_iota((all_groups, group_cols), 1) // kv) % cache
    length_bias = jnp.where(position.astype(jnp.float32) < counts, 0.0, MASKED)

    arrive(0)
    scores(0)
    for step in range(steps):
        side = step % 2
        k_at = step * per * cache * kv
        f_at = step * per * kv
        part(2, step).wait()
        if step + 1 < steps:
            arrive(step + 1)
            scores(step + 1)
        held = []
        fresh = []
        for g in range(groups):
            rows = pl.ds(g * group_rows, group_rows)
            bias = own_bias + length_bias[step * groups + g : step * groups + g + 1, :]
            cached = scores_ref[side, rows, pl.ds(0, group_cols)] + bias
            new = scores_ref[side, rows, pl.ds(group_cols, per * kv)]
            new = jnp.where(fresh_kv & (fresh_distance == g * GROUP), new, MASKED)
            top = row_max([cached, new])
            cached = jnp.exp2((cached - top) * scale).astype(jnp.bfloat16)
            fresh.append(jnp.exp2((new - top) * scale).astype(jnp.bfloat16))
            values = v_ref[pl.ds(k_at + g * group_cols, group_cols), :]
            held.append(_dot(cached, jnp.concatenate([values, ones[:group_cols]], axis=1)))
        values = jnp.concatenate([nv_ref[pl.ds(f_at, per * kv), :], ones[: per * kv]], axis=1)
        fresh = _dot(jnp.concatenate(fresh, axis=0), values)
        for g in range(groups):
            rows = slice(g * group_rows, (g + 1) * group_rows)
            mixed = fresh[rows, :] + held[g]
            mixed_ref[side, rows, :] = mixed[:, :width] / mixed[:, width:]
        for h in range(heads):
            a_ref[pl.ds(step * per, per), pl.ds(h * width, width)] = mixed_ref[
                side, pl.ds(h, per, stride=heads), :
            ].astype(jnp.bfloat16)
        rows = pl.ds(step * per, per)
        leave(a_ref.at[rows, :], a_hbm.at[rows, :])

    weights.wait()
    for columns, product in weights.products(a_ref[...]):
        out_ref[:, columns] = product.astype(jnp.bfloat16)
        leave(out_ref.at[:, columns], out_hbm.at[:, columns])
    sent_ref[:, pl.ds(0, heads * width)] = _dot(chosen_ref[...], a_ref[...]).astype(jnp.bfloat16)
    for r in range(replicas):
        leave(sent_ref.at[pl.ds(r * CAP, CAP), :], sent_hbm[r])
    for copy in leaving:
        copy.wait()


def plan_routes(slots, adapter_ref, placement_ref, chosen_ref, sent_ref):
    replicas = sent_ref.shape[0] // CAP
    requests = adapter_ref.shape[1]
    table = placement_ref.shape[1]
    matches = _iota((table, requests), 0) == adapter_ref[...]
    placed = jnp.broadcast_to(placement_ref[...].astype(jnp.float32), (8, table))
    slot = _dot(placed.astype(jnp.bfloat16), matches.astype(jnp.bfloat16)).astype(jnp.int32)
    slot = slot[0:1, :]
    holder = (slot // slots) ^ lax.axis_index("dp")
    inside = slot % slots
    of_holder = _iota((max(replicas, 8), requests), 0) == holder
    earlier = _iota((requests, requests), 0) < _iota((requests, requests), 1)
    before = _dot(of_holder.astype(jnp.bfloat16), earlier.astype(jnp.bfloat16))
    before = jnp.sum(jnp.where(of_holder, before, 0.0), axis=0, keepdims=True).astype(jnp.int32)
    target = holder * CAP + before
    here = _iota((replicas * CAP, requests), 0) == target
    chosen_ref[...] = here.astype(jnp.bfloat16)
    inner = jnp.sum(jnp.where(here, inside.astype(jnp.float32), 0.0), axis=1, keepdims=True)
    inner = jnp.broadcast_to(inner, (replicas * CAP, LANES)).astype(jnp.bfloat16)
    sent_ref[:, pl.ds(sent_ref.shape[1] - LANES, LANES)] = inner


def attend(
    query, keys, values, new_key, new_value, lengths, weight, request_adapter, placement,
    block, replicas, slots,
):
    requests, heads, width = query.shape
    cache, kv = keys.shape[1], keys.shape[2]
    steps = 4
    per = requests // steps
    columns = GROUP * cache * kv + per * kv
    features = heads * width
    chunk = chain_columns(block)[0][1]
    small = [lengths.reshape(1, -1), request_adapter.reshape(1, -1), placement.reshape(1, -1)]
    operands = [
        query.reshape(requests * heads, width),
        keys.reshape(requests * cache * kv, width),
        values.reshape(requests * cache * kv, width),
        new_key.reshape(requests * kv, width),
        new_value.reshape(requests * kv, width),
    ]
    return pl.pallas_call(
        functools.partial(attend_kernel, heads, kv, cache, steps, block, replicas, slots),
        in_specs=[ANY] * 9,
        out_specs=[ANY] * (3 + replicas),
        out_shape=[
            jax.ShapeDtypeStruct((requests, features), jnp.bfloat16),
            jax.ShapeDtypeStruct((requests, chunk), jnp.bfloat16),
            jax.ShapeDtypeStruct((replicas * CAP, requests), jnp.bfloat16),
        ]
        + [jax.ShapeDtypeStruct((CAP, features + LANES), jnp.bfloat16)] * replicas,
        scratch_shapes=[
            pltpu.VMEM((requests, features), jnp.bfloat16),
            pltpu.VMEM((requests, chunk), jnp.bfloat16),
            pltpu.VMEM((replicas * CAP, requests), jnp.bfloat16),
            pltpu.VMEM((replicas * CAP, features + LANES), jnp.bfloat16),
            pltpu.SemaphoreType.DMA((1 + steps + pl.cdiv(chunk, PIECE) + replicas,)),
        ]
        + [pltpu.VMEM(x.shape, x.dtype) for x in small + operands]
        + [
            pltpu.VMEM((2, per * heads, columns), jnp.float32),
            pltpu.VMEM((2, per * heads, width), jnp.float32),
            pltpu.SemaphoreType.DMA((3, steps)),
            pltpu.SemaphoreType.DMA((5,)),
        ]
        + Weights.scratch(weight.shape[0], chunk),
        compiler_params=pltpu.CompilerParams(vmem_limit_bytes=FULL_VMEM),
        name="attend",
    )(*small, *operands, weight)


def hop_kernel(step, block, start, arriving, after, *refs):
    if arriving:
        arrived_ref, *refs = refs
    a_ref, w_hbm, *refs = refs
    out_ref, held, sems = refs[after:]
    chunk = out_ref.shape[1]
    first = column_owner(step) * block + start
    weights = Weights(w_hbm, held, sems, first, chunk)
    weights.start()
    weights.wait()
    for columns, product in weights.products(a_ref[...]):
        if arriving:
            product = product + arrived_ref[:, columns].astype(jnp.float32)
        out_ref[:, columns] = product.astype(jnp.bfloat16)


def hop(step, chain, arrived, attended, weight, block, after=(), cost=None):
    arriving = arrived is not None
    start, chunk = chain_columns(block)[chain]
    operands = ([arrived] if arriving else []) + [attended, weight, *after]
    return pl.pallas_call(
        functools.partial(hop_kernel, step, block, start, arriving, len(after)),
        in_specs=[VMEM] * (1 + arriving) + [ANY] + [ANY] * len(after),
        out_specs=VMEM,
        out_shape=jax.ShapeDtypeStruct((attended.shape[0], chunk), jnp.bfloat16),
        scratch_shapes=Weights.scratch(weight.shape[0], chunk),
        compiler_params=PARAMS,
        cost_estimate=cost,
        name="hop",
    )(*operands)


def down_kernel(replicas, after, *refs):
    received = refs[:replicas]
    down_ref = refs[replicas]
    mid_ref, inside_ref = refs[replicas + 1 + after :]
    slots, rank, width = down_ref.shape
    rows = jnp.concatenate([r[:, pl.ds(0, width)] for r in received], axis=0)
    inside = jnp.concatenate([r[:, pl.ds(width, LANES)] for r in received], axis=0)
    inside_ref[...] = inside
    projected = _dot(rows, down_ref[...].reshape(slots * rank, width), 1, 1)
    lane_slot = _iota(projected.shape, 1) // rank
    mine = lane_slot == inside[:, 0:1].astype(jnp.int32)
    projected = jnp.where(mine, projected, 0.0).astype(jnp.bfloat16)
    beside = LANES // rank
    some = projected.shape[0] // beside
    packed = 0.0
    for b in range(beside):
        lane = _iota((slots * rank, LANES), 1) - b * rank
        fold = _iota((slots * rank, LANES), 0) % rank == lane
        packed = packed + _dot(projected[b * some : (b + 1) * some, :], fold.astype(jnp.bfloat16))
    mid_ref[...] = packed.astype(jnp.bfloat16)


def down(received, slot_down_weight, after=()):
    replicas = len(received)
    rows = replicas * CAP
    return pl.pallas_call(
        functools.partial(down_kernel, replicas, len(after)),
        in_specs=[VMEM] * (replicas + 1) + [ANY] * len(after),
        out_specs=[VMEM, VMEM],
        out_shape=[
            jax.ShapeDtypeStruct((rows * slot_down_weight.shape[1] // LANES, LANES), jnp.bfloat16),
            jax.ShapeDtypeStruct((rows, LANES), jnp.bfloat16),
        ],
        compiler_params=PARAMS,
        name="down",
    )(*received, slot_down_weight, *after)


def up_kernel(parts, after, *refs):
    mids = refs[:parts]
    inside_ref, up_ref = refs[parts : parts + 2]
    out_refs = refs[parts + 2 + after :]
    slots, rank, width = up_ref.shape
    mid = mids[0][...].astype(jnp.float32)
    for m in mids[1:]:
        mid = mid + m[...].astype(jnp.float32)
    mid = mid.astype(jnp.bfloat16)
    wide = []
    for b in range(LANES // rank):
        lane = _iota((LANES, slots * rank), 0) - b * rank
        spread = _iota((LANES, slots * rank), 1) % rank == lane
        wide.append(_dot(mid, spread.astype(jnp.bfloat16)))
    wide = jnp.concatenate(wide, axis=0)
    mine = _iota(wide.shape, 1) // rank == inside_ref[:, 0:1].astype(jnp.int32)
    wide = jnp.where(mine, wide, 0.0).astype(jnp.bfloat16)
    delta = _dot(wide, up_ref[...].reshape(slots * rank, width)).astype(jnp.bfloat16)
    for r, out_ref in enumerate(out_refs):
        out_ref[...] = delta[r * CAP : (r + 1) * CAP, :]


def up(mids, inside, slot_up_weight, after=()):
    rows = inside.shape[0]
    replicas = rows // CAP
    width = slot_up_weight.shape[2]
    return pl.pallas_call(
        functools.partial(up_kernel, len(mids), len(after)),
        in_specs=[VMEM] * (len(mids) + 2) + [ANY] * len(after),
        out_specs=[VMEM] * replicas,
        out_shape=[jax.ShapeDtypeStruct((CAP, width), jnp.bfloat16)] * replicas,
        compiler_params=PARAMS,
        name="up",
    )(*mids, inside, slot_up_weight, *after)


def settle_kernel(step, replicas, after, *refs):
    returned = refs[:replicas]
    chosen_ref, a_ref, residual_ref, w_hbm = refs[replicas : replicas + 4]
    *out_refs, held, sems = refs[replicas + 4 + after :]
    width = residual_ref.shape[1]
    weights = Weights(w_hbm, held, sems, column_owner(step) * width, width)
    weights.start()
    rows = jnp.concatenate([r[...] for r in returned], axis=0)
    delta = _dot(chosen_ref[...], rows, 0, 0)
    total = residual_ref[...].astype(jnp.float32) + delta
    weights.wait()
    total = total + jnp.concatenate([p for _, p in weights.products(a_ref[...])], axis=1)
    for (start, chunk), out_ref in zip(chain_columns(width), out_refs):
        out_ref[...] = total[:, start : start + chunk]


def settle(step, returned, chosen, attended, residual, weight, after=()):
    replicas = len(returned)
    rows, width = residual.shape
    chains = chain_columns(width)
    return pl.pallas_call(
        functools.partial(settle_kernel, step, replicas, len(after)),
        in_specs=[VMEM] * (replicas + 3) + [ANY] * (1 + len(after)),
        out_specs=[VMEM] * len(chains),
        out_shape=[jax.ShapeDtypeStruct((rows, chunk), jnp.float32) for _, chunk in chains],
        scratch_shapes=Weights.scratch(weight.shape[0], width),
        compiler_params=PARAMS,
        cost_estimate=MEDIUM,
        name="settle",
    )(*returned, chosen, attended, residual, weight, *after)


def finish_kernel(start, arrived_ref, settled_ref, *refs):
    out_hbm, held, sems = refs[-3:]
    rows, chunk = arrived_ref.shape
    half = rows // 2
    copies = []
    for i in range(2):
        part = pl.ds(i * half, half)
        total = settled_ref[part, :] + arrived_ref[part, :].astype(jnp.float32)
        held[part, :] = total.astype(jnp.bfloat16)
        target = out_hbm.at[part, pl.ds(start, chunk)]
        copies.append(pltpu.make_async_copy(held.at[part, :], target, sems.at[i]))
        copies[-1].start()
    for copy in copies:
        copy.wait()


def finish(chain, arrived, settled, earlier, width):
    rows = arrived.shape[0]
    start, chunk = chain_columns(width)[chain]
    operands = [arrived, settled] + ([earlier] if earlier is not None else [])
    return pl.pallas_call(
        functools.partial(finish_kernel, start),
        in_specs=[VMEM, VMEM] + ([ANY] if earlier is not None else []),
        out_specs=ANY,
        out_shape=jax.ShapeDtypeStruct((rows, width), jnp.bfloat16),
        input_output_aliases={2: 0} if earlier is not None else {},
        scratch_shapes=[
            pltpu.VMEM((rows, chunk), jnp.bfloat16),
            pltpu.SemaphoreType.DMA((2,)),
        ],
        compiler_params=PARAMS,
        name="finish",
    )(*operands)


def hold_kernel(*refs):
    pass


def hold(x, after):
    return pl.pallas_call(
        hold_kernel,
        in_specs=[ANY] * (1 + len(after)),
        out_specs=ANY,
        out_shape=jax.ShapeDtypeStruct(x.shape, x.dtype),
        input_output_aliases={0: 0},
        compiler_params=PARAMS,
        name="hold",
    )(x, *after)


def per_device(
    residual,
    query,
    cached_key_rows,
    cached_value_rows,
    new_token_key,
    new_token_value,
    lengths,
    output_weight,
    slot_down_weight,
    slot_up_weight,
    placement,
    request_adapter,
):
    count = lax.axis_size("tensor")
    replicas = lax.axis_size("dp")
    block = residual.shape[1]
    order = ring_order(count)
    ring = [(order[p], order[(p + 1) % count]) for p in range(count)]

    def exchange(blocks):
        moved = [
            lax.ppermute(blocks[r], "dp", [(i, i ^ r) for i in range(replicas)])
            for r in range(1, replicas)
        ]
        return [blocks[0]] + moved

    def forward(x):
        return lax.ppermute(x, "tensor", ring)

    def pair_sums(x):
        found = []
        for away in range(1, count // 2):
            pairs = [(p, (p + away) % (count // 2)) for p in range(count // 2)]
            near, far = [], []
            for p, q in pairs:
                sender = 2 * p if p < q else 2 * p + 1
                straight = 2 * q + (sender % 2)
                near.append((sender, straight))
                far.append((sender, straight ^ 1))
            one = lax.ppermute(x, "tensor", near)
            other = lax.ppermute(x, "tensor", far)
            found += [one, other]
        return found

    def next_hop(step, chain, after, cost=None):
        arrived = forward(travelling[chain])
        travelling[chain] = hop(step, chain, arrived, attended, output_weight, block, after, cost)

    attended, first, chosen, *leaving = attend(
        query, cached_key_rows, cached_value_rows, new_token_key, new_token_value, lengths,
        output_weight, request_adapter, placement, block, replicas, slot_down_weight.shape[0],
    )
    second = hop(0, 1, None, attended, output_weight, block)
    rows_here = exchange(leaving)
    mid, inside = down(rows_here, slot_down_weight, after=[second])
    travelling = [first, hold(second, after=[mid])]

    def added(a, b):
        return (a.astype(jnp.float32) + b.astype(jnp.float32)).astype(a.dtype)

    rank_sum = added(mid, lax.ppermute(mid, "tensor", [(i, i ^ 1) for i in range(count)]))
    rank_sums = [rank_sum] + pair_sums(rank_sum)
    next_hop(1, 0, after=[rank_sum, travelling[1]], cost=LONG)
    next_hop(1, 1, after=[travelling[0]], cost=MEDIUM)
    for step in range(2, count - 1):
        for chain in range(2):
            if (step, chain) == (2, 0):
                next_hop(step, chain, after=(), cost=LONG)
                deltas = up(rank_sums, inside, slot_up_weight, after=[travelling[0]])
                returned = exchange(deltas)
            else:
                next_hop(step, chain, after=[deltas[0]])
    settled = settle(
        count - 1, returned, chosen, attended, residual, output_weight, after=[travelling[1]]
    )
    out = None
    for chain in range(2):
        arrived = forward(travelling[chain])
        out = finish(chain, arrived, settled[chain], out, block)
    return out


def solution(mesh):
    placed = (
        P(("parts", "dp"), "tensor"),
        P(("parts", "dp"), "tensor", None),
        P(("parts", "dp"), None, "tensor", None),
        P(("parts", "dp"), None, "tensor", None),
        P(("parts", "dp"), "tensor", None),
        P(("parts", "dp"), "tensor", None),
        P(("parts", "dp")),
        P("tensor", None),
        P("dp", None, "tensor"),
        P("dp", None, "tensor"),
        P("parts"),
        P(("parts", "dp")),
    )
    return jax.shard_map(
        per_device,
        mesh=mesh,
        in_specs=placed,
        out_specs=P(("parts", "dp"), "tensor"),
        check_vma=False,
    )
```

```python
import functools
import math

import jax
import jax.numpy as jnp
from jax import lax
from jax.experimental import pallas as pl
from jax.experimental.pallas import tpu as pltpu
from jax.sharding import PartitionSpec as P

GROUP = 4
CAP = 64
LANES = 128
SPAN = 64
MASKED = -1e30
VMEM_LIMIT = 50 * 1024 * 1024
FULL_VMEM = 61 * 1024 * 1024
SHARES = ((5, 3),)
PIECE = 512
SPLIT = 4

VMEM = pl.BlockSpec(memory_space=pltpu.VMEM)
ANY = pl.BlockSpec(memory_space=pl.ANY)
LONG = pl.CostEstimate(flops=20 * 10**9, transcendentals=0, bytes_accessed=40 * 10**6)
MEDIUM = pl.CostEstimate(flops=4 * 10**9, transcendentals=0, bytes_accessed=8 * 10**6)
PARAMS = pltpu.CompilerParams(vmem_limit_bytes=VMEM_LIMIT)


def _dot(a, b, left=1, right=0):
    return lax.dot_general(
        a, b, (((left,), (right,)), ((), ())), preferred_element_type=jnp.float32
    )


def _iota(shape, axis):
    return lax.broadcasted_iota(jnp.int32, shape, axis)


def ring_order(count):
    return list(range(0, count, 2)) + list(range(1, count, 2))[::-1]


def column_owner(step):
    count = lax.axis_size("tensor")
    here = lax.axis_index("tensor")
    half = here // 2
    spot = jnp.where(here % 2 == 0, half, count - 1 - half)
    spot = lax.rem(spot - 1 - step + 2 * count, count)
    return jnp.where(2 * spot < count, 2 * spot, 2 * (count - spot) - 1)


def chain_columns(width):
    shares = next(s for s in SHARES if width % (sum(s) * LANES) == 0)
    unit = width // sum(shares)
    return [(sum(shares[:c]) * unit, shares[c] * unit) for c in range(len(shares))]


class Weights:
    def __init__(self, w_ref, held, sems, first, width):
        depth = w_ref.shape[0] // SPLIT
        first = pl.multiple_of(first, LANES)
        self.held = held
        self.copies = [
            pltpu.make_async_copy(
                w_ref.at[pl.ds(s * depth, depth), pl.ds(first, width)],
                held.at[pl.ds(s * depth, depth), :],
                sems.at[s],
            )
            for s in range(SPLIT)
        ]

    def start(self):
        for copy in self.copies:
            copy.start()

    def wait(self):
        for copy in self.copies:
            copy.wait()

    def products(self, a):
        width = self.held.shape[1]
        for at in range(0, width, PIECE):
            columns = pl.ds(at, min(PIECE, width - at))
            yield columns, _dot(a, self.held[:, columns])

    @staticmethod
    def scratch(depth, width):
        return [
            pltpu.VMEM((depth, width), jnp.bfloat16),
            pltpu.SemaphoreType.DMA((SPLIT,)),
        ]


def row_max(arrays):
    full = None
    tops = []
    for x in arrays:
        width = x.shape[1]
        if width % LANES:
            tops.append(jnp.max(x, axis=1, keepdims=True))
            continue
        for at in range(0, width, LANES):
            tile = x[:, at : at + LANES]
            full = tile if full is None else jnp.maximum(full, tile)
    if full is not None:
        tops.append(jnp.max(full, axis=1, keepdims=True))
    return functools.reduce(jnp.maximum, tops)


def attend_kernel(
    heads, kv, cache, steps, block, replicas, slots,
    len_hbm, adapter_hbm, placement_hbm, q_hbm, k_hbm, v_hbm, nk_hbm, nv_hbm, w_hbm,
    *refs,
):
    a_hbm, out_hbm, chosen_hbm, *sent_hbm = refs[: 3 + replicas]
    (
        a_ref, out_ref, chosen_ref, sent_ref, out_sems,
        len_ref, adapter_ref, placement_ref, q_ref, k_ref, v_ref, nk_ref, nv_ref,
        scores_ref, mixed_ref, fresh_bias_ref, sems, small_sems, w_held, w_sems,
    ) = refs[3 + replicas :]
    requests = len_ref.shape[1]
    width = q_hbm.shape[1]
    per = requests // steps
    groups = per // GROUP
    group_rows = GROUP * heads
    group_cols = GROUP * cache * kv
    per_kv = heads // kv
    scale = math.log2(math.e) / math.sqrt(width)

    def part(kind, step):
        source, target, count = (
            (q_hbm, q_ref, heads),
            (k_hbm, k_ref, cache * kv),
            (v_hbm, v_ref, cache * kv),
        )[kind]
        rows = pl.ds(step * per * count, per * count)
        return pltpu.make_async_copy(source.at[rows, :], target.at[rows, :], sems.at[kind, step])

    small = [
        pltpu.make_async_copy(source, target, small_sems.at[i])
        for i, (source, target) in enumerate(
            (
                (nk_hbm, nk_ref),
                (len_hbm, len_ref),
                (nv_hbm, nv_ref),
                (adapter_hbm, adapter_ref),
                (placement_hbm, placement_ref),
            )
        )
    ]
    leaving = []

    def leave(source, target):
        copy = pltpu.make_async_copy(source, target, out_sems.at[len(leaving)])
        copy.start()
        leaving.append(copy)

    def multiply(first, count):
        rows = pl.ds(first, count)
        for columns, product in weights.products(a_ref[rows, :]):
            out_ref[rows, columns] = product.astype(jnp.bfloat16)
        leave(out_ref.at[rows, :], out_hbm.at[rows, :])

    chunk = out_ref.shape[1]
    weights = Weights(w_hbm, w_held, w_sems, column_owner(0) * block, chunk)
    part(0, 0).start()
    part(1, 0).start()
    for copy in small[:2]:
        copy.start()
    part(0, 1).start()
    part(1, 1).start()
    part(2, 0).start()
    for copy in small[2:]:
        copy.start()
    part(2, 1).start()
    for step in range(2, steps):
        for kind in range(3):
            part(kind, step).start()
    weights.start()

    row = _iota((group_rows, group_cols), 0)
    col = _iota((group_rows, group_cols), 1)
    same = (row // heads == col // (cache * kv)) & ((row % heads) // per_kv == col % kv)
    own_bias = jnp.where(same, 0.0, MASKED)
    row = _iota(fresh_bias_ref.shape, 0)
    col = _iota(fresh_bias_ref.shape, 1)
    same = (row // heads == col // kv) & ((row % heads) // per_kv == col % kv)
    fresh_bias_ref[...] = jnp.where(same, 0.0, MASKED)
    fresh_cols = SPAN * kv
    span_rows = SPAN * heads
    span_groups = SPAN // GROUP
    ones = jnp.ones((max(group_cols, fresh_cols), LANES), jnp.bfloat16)

    def arrive(step):
        part(0, step).wait()
        part(1, step).wait()

    def scores(step):
        side = step % 2
        q_at = step * per * heads
        k_at = step * per * cache * kv
        for g in range(groups):
            scores_ref[side, pl.ds(g * group_rows, group_rows), pl.ds(0, group_cols)] = _dot(
                q_ref[pl.ds(q_at + g * group_rows, group_rows), :],
                k_ref[pl.ds(k_at + g * group_cols, group_cols), :],
                1,
                1,
            )
        for span in range(per // SPAN):
            rows = pl.ds(span * span_rows, span_rows)
            scores_ref[side, rows, pl.ds(group_cols, fresh_cols)] = _dot(
                q_ref[pl.ds(q_at + span * span_rows, span_rows), :],
                nk_ref[pl.ds(step * per * kv + span * fresh_cols, fresh_cols), :],
                1,
                1,
            )

    for copy in small:
        copy.wait()
    plan_routes(slots, adapter_ref, placement_ref, chosen_ref, sent_ref)
    leave(chosen_ref, chosen_hbm)
    counts = len_ref[...].astype(jnp.float32)
    all_groups = requests // GROUP
    of_group = _iota((all_groups, requests), 1) // GROUP == _iota((all_groups, requests), 0)
    counts = jnp.where(of_group, counts, 0.0).astype(jnp.bfloat16)
    spread = _iota((requests, group_cols), 0) % GROUP == _iota((requests, group_cols), 1) // (cache * kv)
    counts = _dot(counts, spread.astype(jnp.bfloat16))
    position = (_iota((all_groups, group_cols), 1) // kv) % cache
    length_bias = jnp.where(position.astype(jnp.float32) < counts, 0.0, MASKED)

    arrive(0)
    scores(0)
    for step in range(steps):
        side = step % 2
        k_at = step * per * cache * kv
        f_at = step * per * kv
        part(2, step).wait()
        if step + 1 < steps:
            arrive(step + 1)
            scores(step + 1)
        if step == steps - 1:
            weights.wait()
            multiply(0, requests - per)
        for span in range(per // SPAN):
            cached_weights = []
            fresh_weights = []
            mixed = []
            for g in range(span * span_groups, (span + 1) * span_groups):
                rows = pl.ds(g * group_rows, group_rows)
                bias = own_bias + length_bias[step * groups + g : step * groups + g + 1, :]
                cached = scores_ref[side, rows, pl.ds(0, group_cols)] + bias
                inner = pl.ds((g % span_groups) * group_rows, group_rows)
                new = scores_ref[side, rows, pl.ds(group_cols, fresh_cols)]
                new = new + fresh_bias_ref[inner, :]
                top = row_max([cached, new])
                cached = jnp.exp2((cached - top) * scale).astype(jnp.bfloat16)
                cached_weights.append(cached)
                fresh_weights.append(jnp.exp2((new - top) * scale).astype(jnp.bfloat16))
                mixed.append(_dot(cached, v_ref[pl.ds(k_at + g * group_cols, group_cols), :]))
            fresh = jnp.concatenate(fresh_weights, axis=0)
            values = nv_ref[pl.ds(f_at + span * fresh_cols, fresh_cols), :]
            mixed = jnp.concatenate(mixed, axis=0) + _dot(fresh, values)
            total = _dot(jnp.concatenate(cached_weights, axis=0), ones[:group_cols])
            total = total + _dot(fresh, ones[:fresh_cols])
            rows = pl.ds(span * span_rows, span_rows)
            mixed_ref[side, rows, :] = mixed / total
        for h in range(heads):
            a_ref[pl.ds(step * per, per), pl.ds(h * width, width)] = mixed_ref[
                side, pl.ds(h, per, stride=heads), :
            ].astype(jnp.bfloat16)
        rows = pl.ds(step * per, per)
        leave(a_ref.at[rows, :], a_hbm.at[rows, :])

    multiply(requests - per, per)
    sent_ref[:, pl.ds(0, heads * width)] = _dot(chosen_ref[...], a_ref[...]).astype(jnp.bfloat16)
    for r in range(replicas):
        leave(sent_ref.at[pl.ds(r * CAP, CAP), :], sent_hbm[r])
    for copy in leaving:
        copy.wait()


def plan_routes(slots, adapter_ref, placement_ref, chosen_ref, sent_ref):
    replicas = sent_ref.shape[0] // CAP
    requests = adapter_ref.shape[1]
    table = placement_ref.shape[1]
    matches = _iota((table, requests), 0) == adapter_ref[...]
    placed = jnp.broadcast_to(placement_ref[...].astype(jnp.float32), (8, table))
    slot = _dot(placed.astype(jnp.bfloat16), matches.astype(jnp.bfloat16)).astype(jnp.int32)
    slot = slot[0:1, :]
    holder = (slot // slots) ^ lax.axis_index("dp")
    inside = slot % slots
    of_holder = _iota((max(replicas, 8), requests), 0) == holder
    earlier = _iota((requests, requests), 0) < _iota((requests, requests), 1)
    before = _dot(of_holder.astype(jnp.bfloat16), earlier.astype(jnp.bfloat16))
    before = jnp.sum(jnp.where(of_holder, before, 0.0), axis=0, keepdims=True).astype(jnp.int32)
    target = holder * CAP + before
    here = _iota((replicas * CAP, requests), 0) == target
    chosen_ref[...] = here.astype(jnp.bfloat16)
    inner = jnp.sum(jnp.where(here, inside.astype(jnp.float32), 0.0), axis=1, keepdims=True)
    inner = jnp.broadcast_to(inner, (replicas * CAP, LANES)).astype(jnp.bfloat16)
    sent_ref[:, pl.ds(sent_ref.shape[1] - LANES, LANES)] = inner


def attend(
    query, keys, values, new_key, new_value, lengths, weight, request_adapter, placement,
    block, replicas, slots,
):
    requests, heads, width = query.shape
    cache, kv = keys.shape[1], keys.shape[2]
    steps = 2
    per = requests // steps
    columns = GROUP * cache * kv + SPAN * kv
    features = heads * width
    chunk = chain_columns(block)[0][1]
    small = [lengths.reshape(1, -1), request_adapter.reshape(1, -1), placement.reshape(1, -1)]
    operands = [
        query.reshape(requests * heads, width),
        keys.reshape(requests * cache * kv, width),
        values.reshape(requests * cache * kv, width),
        new_key.reshape(requests * kv, width),
        new_value.reshape(requests * kv, width),
    ]
    return pl.pallas_call(
        functools.partial(attend_kernel, heads, kv, cache, steps, block, replicas, slots),
        in_specs=[ANY] * 9,
        out_specs=[ANY] * (3 + replicas),
        out_shape=[
            jax.ShapeDtypeStruct((requests, features), jnp.bfloat16),
            jax.ShapeDtypeStruct((requests, chunk), jnp.bfloat16),
            jax.ShapeDtypeStruct((replicas * CAP, requests), jnp.bfloat16),
        ]
        + [jax.ShapeDtypeStruct((CAP, features + LANES), jnp.bfloat16)] * replicas,
        scratch_shapes=[
            pltpu.VMEM((requests, features), jnp.bfloat16),
            pltpu.VMEM((requests, chunk), jnp.bfloat16),
            pltpu.VMEM((replicas * CAP, requests), jnp.bfloat16),
            pltpu.VMEM((replicas * CAP, features + LANES), jnp.bfloat16),
            pltpu.SemaphoreType.DMA((1 + steps + 2 + replicas,)),
        ]
        + [pltpu.VMEM(x.shape, x.dtype) for x in small + operands]
        + [
            pltpu.VMEM((2, per * heads, columns), jnp.float32),
            pltpu.VMEM((2, per * heads, width), jnp.float32),
            pltpu.VMEM((SPAN * heads, SPAN * kv), jnp.float32),
            pltpu.SemaphoreType.DMA((3, steps)),
            pltpu.SemaphoreType.DMA((5,)),
        ]
        + Weights.scratch(weight.shape[0], chunk),
        compiler_params=pltpu.CompilerParams(vmem_limit_bytes=FULL_VMEM),
        name="attend",
    )(*small, *operands, weight)


def hop_kernel(step, block, start, arriving, after, *refs):
    if arriving:
        arrived_ref, *refs = refs
    a_ref, w_hbm, *refs = refs
    out_ref, held, sems = refs[after:]
    chunk = out_ref.shape[1]
    first = column_owner(step) * block + start
    weights = Weights(w_hbm, held, sems, first, chunk)
    weights.start()
    weights.wait()
    for columns, product in weights.products(a_ref[...]):
        if arriving:
            product = product + arrived_ref[:, columns].astype(jnp.float32)
        out_ref[:, columns] = product.astype(jnp.bfloat16)


def hop(step, chain, arrived, attended, weight, block, after=(), cost=None):
    arriving = arrived is not None
    start, chunk = chain_columns(block)[chain]
    operands = ([arrived] if arriving else []) + [attended, weight, *after]
    return pl.pallas_call(
        functools.partial(hop_kernel, step, block, start, arriving, len(after)),
        in_specs=[VMEM] * (1 + arriving) + [ANY] + [ANY] * len(after),
        out_specs=VMEM,
        out_shape=jax.ShapeDtypeStruct((attended.shape[0], chunk), jnp.bfloat16),
        scratch_shapes=Weights.scratch(weight.shape[0], chunk),
        compiler_params=PARAMS,
        cost_estimate=cost,
        name="hop",
    )(*operands)


def down_kernel(replicas, after, *refs):
    received = refs[:replicas]
    down_ref = refs[replicas]
    mid_ref, inside_ref = refs[replicas + 1 + after :]
    slots, rank, width = down_ref.shape
    rows = jnp.concatenate([r[:, pl.ds(0, width)] for r in received], axis=0)
    inside = jnp.concatenate([r[:, pl.ds(width, LANES)] for r in received], axis=0)
    inside_ref[...] = inside
    projected = _dot(rows, down_ref[...].reshape(slots * rank, width), 1, 1)
    lane_slot = _iota(projected.shape, 1) // rank
    mine = lane_slot == inside[:, 0:1].astype(jnp.int32)
    projected = jnp.where(mine, projected, 0.0).astype(jnp.bfloat16)
    beside = LANES // rank
    some = projected.shape[0] // beside
    packed = 0.0
    for b in range(beside):
        lane = _iota((slots * rank, LANES), 1) - b * rank
        fold = _iota((slots * rank, LANES), 0) % rank == lane
        packed = packed + _dot(projected[b * some : (b + 1) * some, :], fold.astype(jnp.bfloat16))
    mid_ref[...] = packed.astype(jnp.bfloat16)


def down(received, slot_down_weight, after=()):
    replicas = len(received)
    rows = replicas * CAP
    return pl.pallas_call(
        functools.partial(down_kernel, replicas, len(after)),
        in_specs=[VMEM] * (replicas + 1) + [ANY] * len(after),
        out_specs=[VMEM, VMEM],
        out_shape=[
            jax.ShapeDtypeStruct((rows * slot_down_weight.shape[1] // LANES, LANES), jnp.bfloat16),
            jax.ShapeDtypeStruct((rows, LANES), jnp.bfloat16),
        ],
        compiler_params=PARAMS,
        name="down",
    )(*received, slot_down_weight, *after)


def up_kernel(parts, after, *refs):
    mids = refs[:parts]
    inside_ref, up_ref = refs[parts : parts + 2]
    out_refs = refs[parts + 2 + after :]
    slots, rank, width = up_ref.shape
    mid = mids[0][...].astype(jnp.float32)
    for m in mids[1:]:
        mid = mid + m[...].astype(jnp.float32)
    mid = mid.astype(jnp.bfloat16)
    wide = []
    for b in range(LANES // rank):
        lane = _iota((LANES, slots * rank), 0) - b * rank
        spread = _iota((LANES, slots * rank), 1) % rank == lane
        wide.append(_dot(mid, spread.astype(jnp.bfloat16)))
    wide = jnp.concatenate(wide, axis=0)
    mine = _iota(wide.shape, 1) // rank == inside_ref[:, 0:1].astype(jnp.int32)
    wide = jnp.where(mine, wide, 0.0).astype(jnp.bfloat16)
    delta = _dot(wide, up_ref[...].reshape(slots * rank, width)).astype(jnp.bfloat16)
    for r, out_ref in enumerate(out_refs):
        out_ref[...] = delta[r * CAP : (r + 1) * CAP, :]


def up(mids, inside, slot_up_weight, after=()):
    rows = inside.shape[0]
    replicas = rows // CAP
    width = slot_up_weight.shape[2]
    return pl.pallas_call(
        functools.partial(up_kernel, len(mids), len(after)),
        in_specs=[VMEM] * (len(mids) + 2) + [ANY] * len(after),
        out_specs=[VMEM] * replicas,
        out_shape=[jax.ShapeDtypeStruct((CAP, width), jnp.bfloat16)] * replicas,
        compiler_params=PARAMS,
        name="up",
    )(*mids, inside, slot_up_weight, *after)


def settle_kernel(step, replicas, after, *refs):
    returned = refs[:replicas]
    chosen_ref, a_ref, residual_ref, w_hbm = refs[replicas : replicas + 4]
    *out_refs, held, sems = refs[replicas + 4 + after :]
    width = residual_ref.shape[1]
    weights = Weights(w_hbm, held, sems, column_owner(step) * width, width)
    weights.start()
    rows = jnp.concatenate([r[...] for r in returned], axis=0)
    delta = _dot(chosen_ref[...], rows, 0, 0)
    total = residual_ref[...].astype(jnp.float32) + delta
    weights.wait()
    total = total + jnp.concatenate([p for _, p in weights.products(a_ref[...])], axis=1)
    for (start, chunk), out_ref in zip(chain_columns(width), out_refs):
        out_ref[...] = total[:, start : start + chunk]


def settle(step, returned, chosen, attended, residual, weight, after=()):
    replicas = len(returned)
    rows, width = residual.shape
    chains = chain_columns(width)
    return pl.pallas_call(
        functools.partial(settle_kernel, step, replicas, len(after)),
        in_specs=[VMEM] * (replicas + 3) + [ANY] * (1 + len(after)),
        out_specs=[VMEM] * len(chains),
        out_shape=[jax.ShapeDtypeStruct((rows, chunk), jnp.float32) for _, chunk in chains],
        scratch_shapes=Weights.scratch(weight.shape[0], width),
        compiler_params=PARAMS,
        cost_estimate=MEDIUM,
        name="settle",
    )(*returned, chosen, attended, residual, weight, *after)


def finish_kernel(start, arrived_ref, settled_ref, *refs):
    out_hbm, held, sems = refs[-3:]
    rows, chunk = arrived_ref.shape
    half = rows // 2
    copies = []
    for i in range(2):
        part = pl.ds(i * half, half)
        total = settled_ref[part, :] + arrived_ref[part, :].astype(jnp.float32)
        held[part, :] = total.astype(jnp.bfloat16)
        target = out_hbm.at[part, pl.ds(start, chunk)]
        copies.append(pltpu.make_async_copy(held.at[part, :], target, sems.at[i]))
        copies[-1].start()
    for copy in copies:
        copy.wait()


def finish(chain, arrived, settled, earlier, width):
    rows = arrived.shape[0]
    start, chunk = chain_columns(width)[chain]
    operands = [arrived, settled] + ([earlier] if earlier is not None else [])
    return pl.pallas_call(
        functools.partial(finish_kernel, start),
        in_specs=[VMEM, VMEM] + ([ANY] if earlier is not None else []),
        out_specs=ANY,
        out_shape=jax.ShapeDtypeStruct((rows, width), jnp.bfloat16),
        input_output_aliases={2: 0} if earlier is not None else {},
        scratch_shapes=[
            pltpu.VMEM((rows, chunk), jnp.bfloat16),
            pltpu.SemaphoreType.DMA((2,)),
        ],
        compiler_params=PARAMS,
        name="finish",
    )(*operands)


def hold_kernel(*refs):
    pass


def hold(x, after):
    return pl.pallas_call(
        hold_kernel,
        in_specs=[ANY] * (1 + len(after)),
        out_specs=ANY,
        out_shape=jax.ShapeDtypeStruct(x.shape, x.dtype),
        input_output_aliases={0: 0},
        compiler_params=PARAMS,
        name="hold",
    )(x, *after)


def per_device(
    residual,
    query,
    cached_key_rows,
    cached_value_rows,
    new_token_key,
    new_token_value,
    lengths,
    output_weight,
    slot_down_weight,
    slot_up_weight,
    placement,
    request_adapter,
):
    count = lax.axis_size("tensor")
    replicas = lax.axis_size("dp")
    block = residual.shape[1]
    order = ring_order(count)
    ring = [(order[p], order[(p + 1) % count]) for p in range(count)]

    def exchange(blocks):
        moved = [
            lax.ppermute(blocks[r], "dp", [(i, i ^ r) for i in range(replicas)])
            for r in range(1, replicas)
        ]
        return [blocks[0]] + moved

    def forward(x):
        return lax.ppermute(x, "tensor", ring)

    def pair_sums(x):
        found = []
        for away in range(1, count // 2):
            pairs = [(p, (p + away) % (count // 2)) for p in range(count // 2)]
            near, far = [], []
            for p, q in pairs:
                sender = 2 * p if p < q else 2 * p + 1
                straight = 2 * q + (sender % 2)
                near.append((sender, straight))
                far.append((sender, straight ^ 1))
            one = lax.ppermute(x, "tensor", near)
            other = lax.ppermute(x, "tensor", far)
            found += [one, other]
        return found

    def next_hop(step, chain, after, cost=None):
        arrived = forward(travelling[chain])
        travelling[chain] = hop(step, chain, arrived, attended, output_weight, block, after, cost)

    attended, first, chosen, *leaving = attend(
        query, cached_key_rows, cached_value_rows, new_token_key, new_token_value, lengths,
        output_weight, request_adapter, placement, block, replicas, slot_down_weight.shape[0],
    )
    second = hop(0, 1, None, attended, output_weight, block)
    rows_here = exchange(leaving)
    mid, inside = down(rows_here, slot_down_weight, after=[second])
    travelling = [first, hold(second, after=[mid])]

    def added(a, b):
        return (a.astype(jnp.float32) + b.astype(jnp.float32)).astype(a.dtype)

    rank_sum = added(mid, lax.ppermute(mid, "tensor", [(i, i ^ 1) for i in range(count)]))
    rank_sums = [rank_sum] + pair_sums(rank_sum)
    next_hop(1, 0, after=[rank_sum, travelling[1]], cost=LONG)
    next_hop(1, 1, after=[travelling[0]], cost=MEDIUM)
    for step in range(2, count - 1):
        for chain in range(2):
            if (step, chain) == (2, 0):
                next_hop(step, chain, after=(), cost=LONG)
                deltas = up(rank_sums, inside, slot_up_weight, after=[travelling[0]])
                returned = exchange(deltas)
            else:
                next_hop(step, chain, after=[deltas[0]])
    settled = settle(
        count - 1, returned, chosen, attended, residual, output_weight, after=[travelling[1]]
    )
    out = None
    for chain in range(2):
        arrived = forward(travelling[chain])
        out = finish(chain, arrived, settled[chain], out, block)
    return out


def solution(mesh):
    placed = (
        P(("parts", "dp"), "tensor"),
        P(("parts", "dp"), "tensor", None),
        P(("parts", "dp"), None, "tensor", None),
        P(("parts", "dp"), None, "tensor", None),
        P(("parts", "dp"), "tensor", None),
        P(("parts", "dp"), "tensor", None),
        P(("parts", "dp")),
        P("tensor", None),
        P("dp", None, "tensor"),
        P("dp", None, "tensor"),
        P("parts"),
        P(("parts", "dp")),
    )
    return jax.shard_map(
        per_device,
        mesh=mesh,
        in_specs=placed,
        out_specs=P(("parts", "dp"), "tensor"),
        check_vma=False,
    )
```

```python
import functools
import math

import jax
import jax.numpy as jnp
from jax import lax
from jax.experimental import pallas as pl
from jax.experimental.pallas import tpu as pltpu
from jax.sharding import PartitionSpec as P

GROUP = 4
CAP = 64
LANES = 128
SPAN = 64
MASKED = -1e30
VMEM_LIMIT = 50 * 1024 * 1024
FULL_VMEM = 61 * 1024 * 1024
SHARES = ((5, 3),)
PIECE = 512
SPLIT = 4

VMEM = pl.BlockSpec(memory_space=pltpu.VMEM)
ANY = pl.BlockSpec(memory_space=pl.ANY)
LONG = pl.CostEstimate(flops=20 * 10**9, transcendentals=0, bytes_accessed=40 * 10**6)
MEDIUM = pl.CostEstimate(flops=4 * 10**9, transcendentals=0, bytes_accessed=8 * 10**6)
PARAMS = pltpu.CompilerParams(vmem_limit_bytes=VMEM_LIMIT)


def _dot(a, b, left=1, right=0):
    return lax.dot_general(
        a, b, (((left,), (right,)), ((), ())), preferred_element_type=jnp.float32
    )


def _iota(shape, axis):
    return lax.broadcasted_iota(jnp.int32, shape, axis)


def ring_order(count):
    return list(range(0, count, 2)) + list(range(1, count, 2))[::-1]


def column_owner(step):
    count = lax.axis_size("tensor")
    here = lax.axis_index("tensor")
    half = here // 2
    spot = jnp.where(here % 2 == 0, half, count - 1 - half)
    spot = lax.rem(spot - 1 - step + 2 * count, count)
    return jnp.where(2 * spot < count, 2 * spot, 2 * (count - spot) - 1)


def chain_columns(width):
    shares = next(s for s in SHARES if width % (sum(s) * LANES) == 0)
    unit = width // sum(shares)
    return [(sum(shares[:c]) * unit, shares[c] * unit) for c in range(len(shares))]


class Weights:
    def __init__(self, w_ref, held, sems, first, width):
        depth = w_ref.shape[0] // SPLIT
        first = pl.multiple_of(first, LANES)
        self.held = held
        self.copies = [
            pltpu.make_async_copy(
                w_ref.at[pl.ds(s * depth, depth), pl.ds(first, width)],
                held.at[pl.ds(s * depth, depth), :],
                sems.at[s],
            )
            for s in range(SPLIT)
        ]

    def start(self):
        for copy in self.copies:
            copy.start()

    def wait(self):
        for copy in self.copies:
            copy.wait()

    def products(self, a):
        width = self.held.shape[1]
        for at in range(0, width, PIECE):
            columns = pl.ds(at, min(PIECE, width - at))
            yield columns, _dot(a, self.held[:, columns])

    @staticmethod
    def scratch(depth, width):
        return [
            pltpu.VMEM((depth, width), jnp.bfloat16),
            pltpu.SemaphoreType.DMA((SPLIT,)),
        ]


def row_max(arrays):
    full = None
    tops = []
    for x in arrays:
        width = x.shape[1]
        if width % LANES:
            tops.append(jnp.max(x, axis=1, keepdims=True))
            continue
        for at in range(0, width, LANES):
            tile = x[:, at : at + LANES]
            full = tile if full is None else jnp.maximum(full, tile)
    if full is not None:
        tops.append(jnp.max(full, axis=1, keepdims=True))
    return functools.reduce(jnp.maximum, tops)


def attend_kernel(
    heads, kv, cache, steps, block, replicas, slots,
    len_hbm, adapter_hbm, placement_hbm, q_hbm, k_hbm, v_hbm, nk_hbm, nv_hbm, w_hbm,
    *refs,
):
    a_hbm, out_hbm, chosen_hbm, *sent_hbm = refs[: 3 + replicas]
    (
        a_ref, out_ref, chosen_ref, sent_ref, out_sems,
        len_ref, adapter_ref, placement_ref, q_ref, k_ref, v_ref, nk_ref, nv_ref,
        scores_ref, mixed_ref, fresh_bias_ref, sems, small_sems, w_held, w_sems,
    ) = refs[3 + replicas :]
    requests = len_ref.shape[1]
    width = q_hbm.shape[1]
    per = requests // steps
    groups = per // GROUP
    group_rows = GROUP * heads
    group_cols = GROUP * cache * kv
    per_kv = heads // kv
    scale = math.log2(math.e) / math.sqrt(width)

    def part(kind, step):
        source, target, count = (
            (q_hbm, q_ref, heads),
            (k_hbm, k_ref, cache * kv),
            (v_hbm, v_ref, cache * kv),
        )[kind]
        rows = pl.ds(step * per * count, per * count)
        return pltpu.make_async_copy(source.at[rows, :], target.at[rows, :], sems.at[kind, step])

    small = [
        pltpu.make_async_copy(source, target, small_sems.at[i])
        for i, (source, target) in enumerate(
            (
                (nk_hbm, nk_ref),
                (len_hbm, len_ref),
                (nv_hbm, nv_ref),
                (adapter_hbm, adapter_ref),
                (placement_hbm, placement_ref),
            )
        )
    ]
    leaving = []

    def leave(source, target):
        copy = pltpu.make_async_copy(source, target, out_sems.at[len(leaving)])
        copy.start()
        leaving.append(copy)

    def multiply(first, count):
        rows = pl.ds(first, count)
        for columns, product in weights.products(a_ref[rows, :]):
            out_ref[rows, columns] = product.astype(jnp.bfloat16)
        leave(out_ref.at[rows, :], out_hbm.at[rows, :])

    chunk = out_ref.shape[1]
    weights = Weights(w_hbm, w_held, w_sems, column_owner(0) * block, chunk)
    part(0, 0).start()
    part(1, 0).start()
    for copy in small[:2]:
        copy.start()
    part(0, 1).start()
    part(1, 1).start()
    part(2, 0).start()
    for copy in small[2:]:
        copy.start()
    part(2, 1).start()
    for step in range(2, steps):
        for kind in range(3):
            part(kind, step).start()
    weights.start()

    row = _iota((group_rows, group_cols), 0)
    col = _iota((group_rows, group_cols), 1)
    same = (row // heads == col // (cache * kv)) & ((row % heads) // per_kv == col % kv)
    own_bias = jnp.where(same, 0.0, MASKED)
    row = _iota(fresh_bias_ref.shape, 0)
    col = _iota(fresh_bias_ref.shape, 1)
    same = (row // heads == col // kv) & ((row % heads) // per_kv == col % kv)
    fresh_bias_ref[...] = jnp.where(same, 0.0, MASKED)
    fresh_cols = SPAN * kv
    span_rows = SPAN * heads
    span_groups = SPAN // GROUP
    ones = jnp.ones((max(group_cols, fresh_cols), LANES), jnp.bfloat16)

    def arrive(step):
        part(0, step).wait()
        part(1, step).wait()

    def scores(step):
        side = step % 2
        q_at = step * per * heads
        k_at = step * per * cache * kv
        for g in range(groups):
            scores_ref[side, pl.ds(g * group_rows, group_rows), pl.ds(0, group_cols)] = _dot(
                q_ref[pl.ds(q_at + g * group_rows, group_rows), :],
                k_ref[pl.ds(k_at + g * group_cols, group_cols), :],
                1,
                1,
            )
        for span in range(per // SPAN):
            rows = pl.ds(span * span_rows, span_rows)
            scores_ref[side, rows, pl.ds(group_cols, fresh_cols)] = _dot(
                q_ref[pl.ds(q_at + span * span_rows, span_rows), :],
                nk_ref[pl.ds(step * per * kv + span * fresh_cols, fresh_cols), :],
                1,
                1,
            )

    for copy in small:
        copy.wait()
    counts = len_ref[...].astype(jnp.float32)
    all_groups = requests // GROUP
    of_group = _iota((all_groups, requests), 1) // GROUP == _iota((all_groups, requests), 0)
    counts = jnp.where(of_group, counts, 0.0).astype(jnp.bfloat16)
    spread = _iota((requests, group_cols), 0) % GROUP == _iota((requests, group_cols), 1) // (cache * kv)
    counts = _dot(counts, spread.astype(jnp.bfloat16))
    position = (_iota((all_groups, group_cols), 1) // kv) % cache
    length_bias = jnp.where(position.astype(jnp.float32) < counts, 0.0, MASKED)

    arrive(0)
    scores(0)
    for step in range(steps):
        side = step % 2
        k_at = step * per * cache * kv
        f_at = step * per * kv
        part(2, step).wait()
        if step + 1 < steps:
            arrive(step + 1)
            scores(step + 1)
        if step == 0:
            plan_routes(slots, adapter_ref, placement_ref, chosen_ref, sent_ref)
            leave(chosen_ref, chosen_hbm)
        if step == steps - 1:
            weights.wait()
            multiply(0, requests - per)
        for span in range(per // SPAN):
            cached_weights = []
            fresh_weights = []
            mixed = []
            for g in range(span * span_groups, (span + 1) * span_groups):
                rows = pl.ds(g * group_rows, group_rows)
                bias = own_bias + length_bias[step * groups + g : step * groups + g + 1, :]
                cached = scores_ref[side, rows, pl.ds(0, group_cols)] + bias
                inner = pl.ds((g % span_groups) * group_rows, group_rows)
                new = scores_ref[side, rows, pl.ds(group_cols, fresh_cols)]
                new = new + fresh_bias_ref[inner, :]
                top = row_max([cached, new])
                cached = jnp.exp2((cached - top) * scale).astype(jnp.bfloat16)
                cached_weights.append(cached)
                fresh_weights.append(jnp.exp2((new - top) * scale).astype(jnp.bfloat16))
                mixed.append(_dot(cached, v_ref[pl.ds(k_at + g * group_cols, group_cols), :]))
            fresh = jnp.concatenate(fresh_weights, axis=0)
            values = nv_ref[pl.ds(f_at + span * fresh_cols, fresh_cols), :]
            mixed = jnp.concatenate(mixed, axis=0) + _dot(fresh, values)
            total = _dot(jnp.concatenate(cached_weights, axis=0), ones[:group_cols])
            total = total + _dot(fresh, ones[:fresh_cols])
            rows = pl.ds(span * span_rows, span_rows)
            inverse = pl.reciprocal(total, approx=True)
            mixed_ref[side, rows, :] = mixed * (inverse * (2.0 - total * inverse))
        for h in range(heads):
            a_ref[pl.ds(step * per, per), pl.ds(h * width, width)] = mixed_ref[
                side, pl.ds(h, per, stride=heads), :
            ].astype(jnp.bfloat16)
        rows = pl.ds(step * per, per)
        leave(a_ref.at[rows, :], a_hbm.at[rows, :])

    sent_ref[:, pl.ds(0, heads * width)] = _dot(chosen_ref[...], a_ref[...]).astype(jnp.bfloat16)
    for r in range(replicas):
        leave(sent_ref.at[pl.ds(r * CAP, CAP), :], sent_hbm[r])
    multiply(requests - per, per)
    for copy in leaving:
        copy.wait()


def plan_routes(slots, adapter_ref, placement_ref, chosen_ref, sent_ref):
    replicas = sent_ref.shape[0] // CAP
    requests = adapter_ref.shape[1]
    table = placement_ref.shape[1]
    matches = _iota((table, requests), 0) == adapter_ref[...]
    placed = jnp.broadcast_to(placement_ref[...].astype(jnp.float32), (8, table))
    slot = _dot(placed.astype(jnp.bfloat16), matches.astype(jnp.bfloat16)).astype(jnp.int32)
    slot = slot[0:1, :]
    holder = (slot // slots) ^ lax.axis_index("dp")
    inside = slot % slots
    of_holder = _iota((max(replicas, 8), requests), 0) == holder
    earlier = _iota((requests, requests), 0) < _iota((requests, requests), 1)
    before = _dot(of_holder.astype(jnp.bfloat16), earlier.astype(jnp.bfloat16))
    before = jnp.sum(jnp.where(of_holder, before, 0.0), axis=0, keepdims=True).astype(jnp.int32)
    target = holder * CAP + before
    here = _iota((replicas * CAP, requests), 0) == target
    chosen_ref[...] = here.astype(jnp.bfloat16)
    inner = jnp.sum(jnp.where(here, inside.astype(jnp.float32), 0.0), axis=1, keepdims=True)
    inner = jnp.broadcast_to(inner, (replicas * CAP, LANES)).astype(jnp.bfloat16)
    sent_ref[:, pl.ds(sent_ref.shape[1] - LANES, LANES)] = inner


def attend(
    query, keys, values, new_key, new_value, lengths, weight, request_adapter, placement,
    block, replicas, slots,
):
    requests, heads, width = query.shape
    cache, kv = keys.shape[1], keys.shape[2]
    steps = 2
    per = requests // steps
    columns = GROUP * cache * kv + SPAN * kv
    features = heads * width
    chunk = chain_columns(block)[0][1]
    small = [lengths.reshape(1, -1), request_adapter.reshape(1, -1), placement.reshape(1, -1)]
    operands = [
        query.reshape(requests * heads, width),
        keys.reshape(requests * cache * kv, width),
        values.reshape(requests * cache * kv, width),
        new_key.reshape(requests * kv, width),
        new_value.reshape(requests * kv, width),
    ]
    return pl.pallas_call(
        functools.partial(attend_kernel, heads, kv, cache, steps, block, replicas, slots),
        in_specs=[ANY] * 9,
        out_specs=[ANY] * (3 + replicas),
        out_shape=[
            jax.ShapeDtypeStruct((requests, features), jnp.bfloat16),
            jax.ShapeDtypeStruct((requests, chunk), jnp.bfloat16),
            jax.ShapeDtypeStruct((replicas * CAP, requests), jnp.bfloat16),
        ]
        + [jax.ShapeDtypeStruct((CAP, features + LANES), jnp.bfloat16)] * replicas,
        scratch_shapes=[
            pltpu.VMEM((requests, features), jnp.bfloat16),
            pltpu.VMEM((requests, chunk), jnp.bfloat16),
            pltpu.VMEM((replicas * CAP, requests), jnp.bfloat16),
            pltpu.VMEM((replicas * CAP, features + LANES), jnp.bfloat16),
            pltpu.SemaphoreType.DMA((1 + steps + 2 + replicas,)),
        ]
        + [pltpu.VMEM(x.shape, x.dtype) for x in small + operands]
        + [
            pltpu.VMEM((2, per * heads, columns), jnp.float32),
            pltpu.VMEM((2, per * heads, width), jnp.float32),
            pltpu.VMEM((SPAN * heads, SPAN * kv), jnp.float32),
            pltpu.SemaphoreType.DMA((3, steps)),
            pltpu.SemaphoreType.DMA((5,)),
        ]
        + Weights.scratch(weight.shape[0], chunk),
        compiler_params=pltpu.CompilerParams(vmem_limit_bytes=FULL_VMEM),
        name="attend",
    )(*small, *operands, weight)


def hop_kernel(step, block, start, arriving, after, *refs):
    if arriving:
        arrived_ref, *refs = refs
    a_ref, w_hbm, *refs = refs
    out_ref, held, sems = refs[after:]
    chunk = out_ref.shape[1]
    first = column_owner(step) * block + start
    weights = Weights(w_hbm, held, sems, first, chunk)
    weights.start()
    weights.wait()
    for columns, product in weights.products(a_ref[...]):
        if arriving:
            product = product + arrived_ref[:, columns].astype(jnp.float32)
        out_ref[:, columns] = product.astype(jnp.bfloat16)


def hop(step, chain, arrived, attended, weight, block, after=(), cost=None):
    arriving = arrived is not None
    start, chunk = chain_columns(block)[chain]
    operands = ([arrived] if arriving else []) + [attended, weight, *after]
    return pl.pallas_call(
        functools.partial(hop_kernel, step, block, start, arriving, len(after)),
        in_specs=[VMEM] * (1 + arriving) + [ANY] + [ANY] * len(after),
        out_specs=VMEM,
        out_shape=jax.ShapeDtypeStruct((attended.shape[0], chunk), jnp.bfloat16),
        scratch_shapes=Weights.scratch(weight.shape[0], chunk),
        compiler_params=PARAMS,
        cost_estimate=cost,
        name="hop",
    )(*operands)


def down_kernel(replicas, after, *refs):
    received = refs[:replicas]
    down_ref = refs[replicas]
    mid_ref, inside_ref = refs[replicas + 1 + after :]
    slots, rank, width = down_ref.shape
    rows = jnp.concatenate([r[:, pl.ds(0, width)] for r in received], axis=0)
    inside = jnp.concatenate([r[:, pl.ds(width, LANES)] for r in received], axis=0)
    inside_ref[...] = inside
    projected = _dot(rows, down_ref[...].reshape(slots * rank, width), 1, 1)
    lane_slot = _iota(projected.shape, 1) // rank
    mine = lane_slot == inside[:, 0:1].astype(jnp.int32)
    projected = jnp.where(mine, projected, 0.0).astype(jnp.bfloat16)
    beside = LANES // rank
    some = projected.shape[0] // beside
    packed = 0.0
    for b in range(beside):
        lane = _iota((slots * rank, LANES), 1) - b * rank
        fold = _iota((slots * rank, LANES), 0) % rank == lane
        packed = packed + _dot(projected[b * some : (b + 1) * some, :], fold.astype(jnp.bfloat16))
    mid_ref[...] = packed.astype(jnp.bfloat16)


def down(received, slot_down_weight, after=()):
    replicas = len(received)
    rows = replicas * CAP
    return pl.pallas_call(
        functools.partial(down_kernel, replicas, len(after)),
        in_specs=[VMEM] * (replicas + 1) + [ANY] * len(after),
        out_specs=[VMEM, VMEM],
        out_shape=[
            jax.ShapeDtypeStruct((rows * slot_down_weight.shape[1] // LANES, LANES), jnp.bfloat16),
            jax.ShapeDtypeStruct((rows, LANES), jnp.bfloat16),
        ],
        compiler_params=PARAMS,
        name="down",
    )(*received, slot_down_weight, *after)


def up_kernel(parts, after, *refs):
    mids = refs[:parts]
    inside_ref, up_ref = refs[parts : parts + 2]
    out_refs = refs[parts + 2 + after :]
    slots, rank, width = up_ref.shape
    mid = mids[0][...].astype(jnp.float32)
    for m in mids[1:]:
        mid = mid + m[...].astype(jnp.float32)
    mid = mid.astype(jnp.bfloat16)
    wide = []
    for b in range(LANES // rank):
        lane = _iota((LANES, slots * rank), 0) - b * rank
        spread = _iota((LANES, slots * rank), 1) % rank == lane
        wide.append(_dot(mid, spread.astype(jnp.bfloat16)))
    wide = jnp.concatenate(wide, axis=0)
    mine = _iota(wide.shape, 1) // rank == inside_ref[:, 0:1].astype(jnp.int32)
    wide = jnp.where(mine, wide, 0.0).astype(jnp.bfloat16)
    delta = _dot(wide, up_ref[...].reshape(slots * rank, width)).astype(jnp.bfloat16)
    for r, out_ref in enumerate(out_refs):
        out_ref[...] = delta[r * CAP : (r + 1) * CAP, :]


def up(mids, inside, slot_up_weight, after=()):
    rows = inside.shape[0]
    replicas = rows // CAP
    width = slot_up_weight.shape[2]
    return pl.pallas_call(
        functools.partial(up_kernel, len(mids), len(after)),
        in_specs=[VMEM] * (len(mids) + 2) + [ANY] * len(after),
        out_specs=[VMEM] * replicas,
        out_shape=[jax.ShapeDtypeStruct((CAP, width), jnp.bfloat16)] * replicas,
        compiler_params=PARAMS,
        name="up",
    )(*mids, inside, slot_up_weight, *after)


def settle_kernel(step, replicas, after, *refs):
    returned = refs[:replicas]
    chosen_ref, a_ref, residual_ref, w_hbm = refs[replicas : replicas + 4]
    *out_refs, held, sems = refs[replicas + 4 + after :]
    width = residual_ref.shape[1]
    weights = Weights(w_hbm, held, sems, column_owner(step) * width, width)
    weights.start()
    rows = jnp.concatenate([r[...] for r in returned], axis=0)
    delta = _dot(chosen_ref[...], rows, 0, 0)
    total = residual_ref[...].astype(jnp.float32) + delta
    weights.wait()
    total = total + jnp.concatenate([p for _, p in weights.products(a_ref[...])], axis=1)
    for (start, chunk), out_ref in zip(chain_columns(width), out_refs):
        out_ref[...] = total[:, start : start + chunk]


def settle(step, returned, chosen, attended, residual, weight, after=()):
    replicas = len(returned)
    rows, width = residual.shape
    chains = chain_columns(width)
    return pl.pallas_call(
        functools.partial(settle_kernel, step, replicas, len(after)),
        in_specs=[VMEM] * (replicas + 3) + [ANY] * (1 + len(after)),
        out_specs=[VMEM] * len(chains),
        out_shape=[jax.ShapeDtypeStruct((rows, chunk), jnp.float32) for _, chunk in chains],
        scratch_shapes=Weights.scratch(weight.shape[0], width),
        compiler_params=PARAMS,
        cost_estimate=MEDIUM,
        name="settle",
    )(*returned, chosen, attended, residual, weight, *after)


def finish_kernel(start, arrived_ref, settled_ref, *refs):
    out_hbm, held, sems = refs[-3:]
    rows, chunk = arrived_ref.shape
    half = rows // 2
    copies = []
    for i in range(2):
        part = pl.ds(i * half, half)
        total = settled_ref[part, :] + arrived_ref[part, :].astype(jnp.float32)
        held[part, :] = total.astype(jnp.bfloat16)
        target = out_hbm.at[part, pl.ds(start, chunk)]
        copies.append(pltpu.make_async_copy(held.at[part, :], target, sems.at[i]))
        copies[-1].start()
    for copy in copies:
        copy.wait()


def finish(chain, arrived, settled, earlier, width):
    rows = arrived.shape[0]
    start, chunk = chain_columns(width)[chain]
    operands = [arrived, settled] + ([earlier] if earlier is not None else [])
    return pl.pallas_call(
        functools.partial(finish_kernel, start),
        in_specs=[VMEM, VMEM] + ([ANY] if earlier is not None else []),
        out_specs=ANY,
        out_shape=jax.ShapeDtypeStruct((rows, width), jnp.bfloat16),
        input_output_aliases={2: 0} if earlier is not None else {},
        scratch_shapes=[
            pltpu.VMEM((rows, chunk), jnp.bfloat16),
            pltpu.SemaphoreType.DMA((2,)),
        ],
        compiler_params=PARAMS,
        name="finish",
    )(*operands)


def hold_kernel(*refs):
    pass


def hold(x, after):
    return pl.pallas_call(
        hold_kernel,
        in_specs=[ANY] * (1 + len(after)),
        out_specs=ANY,
        out_shape=jax.ShapeDtypeStruct(x.shape, x.dtype),
        input_output_aliases={0: 0},
        compiler_params=PARAMS,
        name="hold",
    )(x, *after)


def per_device(
    residual,
    query,
    cached_key_rows,
    cached_value_rows,
    new_token_key,
    new_token_value,
    lengths,
    output_weight,
    slot_down_weight,
    slot_up_weight,
    placement,
    request_adapter,
):
    count = lax.axis_size("tensor")
    replicas = lax.axis_size("dp")
    block = residual.shape[1]
    order = ring_order(count)
    ring = [(order[p], order[(p + 1) % count]) for p in range(count)]

    def exchange(blocks):
        moved = [
            lax.ppermute(blocks[r], "dp", [(i, i ^ r) for i in range(replicas)])
            for r in range(1, replicas)
        ]
        return [blocks[0]] + moved

    def forward(x):
        return lax.ppermute(x, "tensor", ring)

    def pair_sums(x):
        found = []
        for away in range(1, count // 2):
            pairs = [(p, (p + away) % (count // 2)) for p in range(count // 2)]
            near, far = [], []
            for p, q in pairs:
                sender = 2 * p if p < q else 2 * p + 1
                straight = 2 * q + (sender % 2)
                near.append((sender, straight))
                far.append((sender, straight ^ 1))
            one = lax.ppermute(x, "tensor", near)
            other = lax.ppermute(x, "tensor", far)
            found += [one, other]
        return found

    def next_hop(step, chain, after, cost=None):
        arrived = forward(travelling[chain])
        travelling[chain] = hop(step, chain, arrived, attended, output_weight, block, after, cost)

    attended, first, chosen, *leaving = attend(
        query, cached_key_rows, cached_value_rows, new_token_key, new_token_value, lengths,
        output_weight, request_adapter, placement, block, replicas, slot_down_weight.shape[0],
    )
    second = hop(0, 1, None, attended, output_weight, block)
    rows_here = exchange(leaving)
    mid, inside = down(rows_here, slot_down_weight, after=[second])
    travelling = [first, hold(second, after=[mid])]

    def added(a, b):
        return (a.astype(jnp.float32) + b.astype(jnp.float32)).astype(a.dtype)

    rank_sum = added(mid, lax.ppermute(mid, "tensor", [(i, i ^ 1) for i in range(count)]))
    rank_sums = [rank_sum] + pair_sums(rank_sum)
    next_hop(1, 0, after=[rank_sum, travelling[1]], cost=LONG)
    next_hop(1, 1, after=[travelling[0]], cost=MEDIUM)
    for step in range(2, count - 1):
        for chain in range(2):
            if (step, chain) == (2, 0):
                next_hop(step, chain, after=(), cost=LONG)
                deltas = up(rank_sums, inside, slot_up_weight, after=[travelling[0]])
                returned = exchange(deltas)
            else:
                next_hop(step, chain, after=[deltas[0]])
    settled = settle(
        count - 1, returned, chosen, attended, residual, output_weight, after=[travelling[1]]
    )
    out = None
    for chain in range(2):
        arrived = forward(travelling[chain])
        out = finish(chain, arrived, settled[chain], out, block)
    return out


def solution(mesh):
    placed = (
        P(("parts", "dp"), "tensor"),
        P(("parts", "dp"), "tensor", None),
        P(("parts", "dp"), None, "tensor", None),
        P(("parts", "dp"), None, "tensor", None),
        P(("parts", "dp"), "tensor", None),
        P(("parts", "dp"), "tensor", None),
        P(("parts", "dp")),
        P("tensor", None),
        P("dp", None, "tensor"),
        P("dp", None, "tensor"),
        P("parts"),
        P(("parts", "dp")),
    )
    return jax.shard_map(
        per_device,
        mesh=mesh,
        in_specs=placed,
        out_specs=P(("parts", "dp"), "tensor"),
        check_vma=False,
    )
```

```python
import functools
import math

import jax
import jax.numpy as jnp
from jax import lax
from jax.experimental import pallas as pl
from jax.experimental.pallas import tpu as pltpu
from jax.sharding import PartitionSpec as P

GROUP = 4
CAP = 64
LANES = 128
SPAN = 64
MASKED = -1e30
VMEM_LIMIT = 50 * 1024 * 1024
FULL_VMEM = 61 * 1024 * 1024
SHARES = ((9, 7), (5, 3))
PIECE = 512
SPLIT = 4

VMEM = pl.BlockSpec(memory_space=pltpu.VMEM)
ANY = pl.BlockSpec(memory_space=pl.ANY)
SETTLE = pl.CostEstimate(flops=33 * 10**8, transcendentals=0, bytes_accessed=66 * 10**5)
LONG = pl.CostEstimate(flops=20 * 10**9, transcendentals=0, bytes_accessed=40 * 10**6)
MEDIUM = pl.CostEstimate(flops=4 * 10**9, transcendentals=0, bytes_accessed=8 * 10**6)
PARAMS = pltpu.CompilerParams(vmem_limit_bytes=VMEM_LIMIT)


def _dot(a, b, left=1, right=0):
    return lax.dot_general(
        a, b, (((left,), (right,)), ((), ())), preferred_element_type=jnp.float32
    )


def _iota(shape, axis):
    return lax.broadcasted_iota(jnp.int32, shape, axis)


def ring_order(count):
    return list(range(0, count, 2)) + list(range(1, count, 2))[::-1]


def column_owner(step):
    count = lax.axis_size("tensor")
    here = lax.axis_index("tensor")
    half = here // 2
    spot = jnp.where(here % 2 == 0, half, count - 1 - half)
    spot = lax.rem(spot - 1 - step + 2 * count, count)
    return jnp.where(2 * spot < count, 2 * spot, 2 * (count - spot) - 1)


def chain_columns(width):
    shares = next(s for s in SHARES if width % (sum(s) * LANES) == 0)
    unit = width // sum(shares)
    return [(sum(shares[:c]) * unit, shares[c] * unit) for c in range(len(shares))]


class Weights:
    def __init__(self, w_ref, held, sems, first, width):
        depth = w_ref.shape[0] // SPLIT
        first = pl.multiple_of(first, LANES)
        self.held = held
        self.copies = [
            pltpu.make_async_copy(
                w_ref.at[pl.ds(s * depth, depth), pl.ds(first, width)],
                held.at[pl.ds(s * depth, depth), :],
                sems.at[s],
            )
            for s in range(SPLIT)
        ]

    def start(self):
        for copy in self.copies:
            copy.start()

    def wait(self):
        for copy in self.copies:
            copy.wait()

    def products(self, a):
        width = self.held.shape[1]
        for at in range(0, width, PIECE):
            columns = pl.ds(at, min(PIECE, width - at))
            yield columns, _dot(a, self.held[:, columns])

    @staticmethod
    def scratch(depth, width):
        return [
            pltpu.VMEM((depth, width), jnp.bfloat16),
            pltpu.SemaphoreType.DMA((SPLIT,)),
        ]


def row_max(arrays):
    full = None
    tops = []
    for x in arrays:
        width = x.shape[1]
        if width % LANES:
            tops.append(jnp.max(x, axis=1, keepdims=True))
            continue
        for at in range(0, width, LANES):
            tile = x[:, at : at + LANES]
            full = tile if full is None else jnp.maximum(full, tile)
    if full is not None:
        tops.append(jnp.max(full, axis=1, keepdims=True))
    return functools.reduce(jnp.maximum, tops)


def attend_kernel(
    heads, kv, cache, steps, block, replicas, slots,
    len_hbm, adapter_hbm, placement_hbm, q_hbm, k_hbm, v_hbm, nk_hbm, nv_hbm, w_hbm,
    *refs,
):
    a_hbm, out_hbm, chosen_hbm, *sent_hbm = refs[: 3 + replicas]
    (
        a_ref, out_ref, chosen_ref, sent_ref, out_sems,
        len_ref, adapter_ref, placement_ref, q_ref, k_ref, v_ref, nk_ref, nv_ref,
        scores_ref, mixed_ref, fresh_bias_ref, sems, small_sems, w_held, w_sems,
    ) = refs[3 + replicas :]
    requests = len_ref.shape[1]
    width = q_hbm.shape[1]
    per = requests // steps
    groups = per // GROUP
    group_rows = GROUP * heads
    group_cols = GROUP * cache * kv
    per_kv = heads // kv
    scale = math.log2(math.e) / math.sqrt(width)

    def part(kind, step):
        source, target, count = (
            (q_hbm, q_ref, heads),
            (k_hbm, k_ref, cache * kv),
            (v_hbm, v_ref, cache * kv),
        )[kind]
        rows = pl.ds(step * per * count, per * count)
        return pltpu.make_async_copy(source.at[rows, :], target.at[rows, :], sems.at[kind, step])

    small = [
        pltpu.make_async_copy(source, target, small_sems.at[i])
        for i, (source, target) in enumerate(
            (
                (nk_hbm, nk_ref),
                (len_hbm, len_ref),
                (nv_hbm, nv_ref),
                (adapter_hbm, adapter_ref),
                (placement_hbm, placement_ref),
            )
        )
    ]
    leaving = []

    def leave(source, target):
        copy = pltpu.make_async_copy(source, target, out_sems.at[len(leaving)])
        copy.start()
        leaving.append(copy)

    def multiply(first, count):
        rows = pl.ds(first, count)
        for columns, product in weights.products(a_ref[rows, :]):
            out_ref[rows, columns] = product.astype(jnp.bfloat16)
        leave(out_ref.at[rows, :], out_hbm.at[rows, :])

    chunk = out_ref.shape[1]
    weights = Weights(w_hbm, w_held, w_sems, column_owner(0) * block, chunk)
    part(0, 0).start()
    part(1, 0).start()
    for copy in small[:2]:
        copy.start()
    part(0, 1).start()
    part(1, 1).start()
    part(2, 0).start()
    for copy in small[2:]:
        copy.start()
    part(2, 1).start()
    for step in range(2, steps):
        for kind in range(3):
            part(kind, step).start()
    weights.start()

    row = _iota((group_rows, group_cols), 0)
    col = _iota((group_rows, group_cols), 1)
    same = (row // heads == col // (cache * kv)) & ((row % heads) // per_kv == col % kv)
    own_bias = jnp.where(same, 0.0, MASKED)
    row = _iota(fresh_bias_ref.shape, 0)
    col = _iota(fresh_bias_ref.shape, 1)
    same = (row // heads == col // kv) & ((row % heads) // per_kv == col % kv)
    fresh_bias_ref[...] = jnp.where(same, 0.0, MASKED)
    fresh_cols = SPAN * kv
    span_rows = SPAN * heads
    span_groups = SPAN // GROUP
    ones = jnp.ones((max(group_cols, fresh_cols), LANES), jnp.bfloat16)

    def arrive(step):
        part(0, step).wait()
        part(1, step).wait()

    def scores(step):
        side = step % 2
        q_at = step * per * heads
        k_at = step * per * cache * kv
        for g in range(groups):
            scores_ref[side, pl.ds(g * group_rows, group_rows), pl.ds(0, group_cols)] = _dot(
                q_ref[pl.ds(q_at + g * group_rows, group_rows), :],
                k_ref[pl.ds(k_at + g * group_cols, group_cols), :],
                1,
                1,
            )
        for span in range(per // SPAN):
            rows = pl.ds(span * span_rows, span_rows)
            scores_ref[side, rows, pl.ds(group_cols, fresh_cols)] = _dot(
                q_ref[pl.ds(q_at + span * span_rows, span_rows), :],
                nk_ref[pl.ds(step * per * kv + span * fresh_cols, fresh_cols), :],
                1,
                1,
            )

    for copy in small:
        copy.wait()
    counts = len_ref[...].astype(jnp.float32)
    all_groups = requests // GROUP
    of_group = _iota((all_groups, requests), 1) // GROUP == _iota((all_groups, requests), 0)
    counts = jnp.where(of_group, counts, 0.0).astype(jnp.bfloat16)
    spread = _iota((requests, group_cols), 0) % GROUP == _iota((requests, group_cols), 1) // (cache * kv)
    counts = _dot(counts, spread.astype(jnp.bfloat16))
    position = (_iota((all_groups, group_cols), 1) // kv) % cache
    length_bias = jnp.where(position.astype(jnp.float32) < counts, 0.0, MASKED)

    arrive(0)
    scores(0)
    for step in range(steps):
        side = step % 2
        k_at = step * per * cache * kv
        f_at = step * per * kv
        part(2, step).wait()
        if step + 1 < steps:
            arrive(step + 1)
            scores(step + 1)
        if step == 0:
            plan_routes(slots, adapter_ref, placement_ref, chosen_ref, sent_ref)
            leave(chosen_ref, chosen_hbm)
        if step == steps - 1:
            weights.wait()
            multiply(0, requests - per)
        for span in range(per // SPAN):
            cached_weights = []
            fresh_weights = []
            mixed = []
            for g in range(span * span_groups, (span + 1) * span_groups):
                rows = pl.ds(g * group_rows, group_rows)
                bias = own_bias + length_bias[step * groups + g : step * groups + g + 1, :]
                cached = scores_ref[side, rows, pl.ds(0, group_cols)] + bias
                inner = pl.ds((g % span_groups) * group_rows, group_rows)
                new = scores_ref[side, rows, pl.ds(group_cols, fresh_cols)]
                new = new + fresh_bias_ref[inner, :]
                top = row_max([cached, new])
                cached = jnp.exp2((cached - top) * scale).astype(jnp.bfloat16)
                cached_weights.append(cached)
                fresh_weights.append(jnp.exp2((new - top) * scale).astype(jnp.bfloat16))
                mixed.append(_dot(cached, v_ref[pl.ds(k_at + g * group_cols, group_cols), :]))
            fresh = jnp.concatenate(fresh_weights, axis=0)
            values = nv_ref[pl.ds(f_at + span * fresh_cols, fresh_cols), :]
            mixed = jnp.concatenate(mixed, axis=0) + _dot(fresh, values)
            total = _dot(jnp.concatenate(cached_weights, axis=0), ones[:group_cols])
            total = total + _dot(fresh, ones[:fresh_cols])
            rows = pl.ds(span * span_rows, span_rows)
            inverse = pl.reciprocal(total, approx=True)
            mixed_ref[side, rows, :] = mixed * (inverse * (2.0 - total * inverse))
        for h in range(heads):
            a_ref[pl.ds(step * per, per), pl.ds(h * width, width)] = mixed_ref[
                side, pl.ds(h, per, stride=heads), :
            ].astype(jnp.bfloat16)
        rows = pl.ds(step * per, per)
        leave(a_ref.at[rows, :], a_hbm.at[rows, :])

    sent_ref[:, pl.ds(0, heads * width)] = _dot(chosen_ref[...], a_ref[...]).astype(jnp.bfloat16)
    for r in range(replicas):
        leave(sent_ref.at[pl.ds(r * CAP, CAP), :], sent_hbm[r])
    multiply(requests - per, per)
    for copy in leaving:
        copy.wait()


def plan_routes(slots, adapter_ref, placement_ref, chosen_ref, sent_ref):
    replicas = sent_ref.shape[0] // CAP
    requests = adapter_ref.shape[1]
    table = placement_ref.shape[1]
    matches = _iota((table, requests), 0) == adapter_ref[...]
    placed = jnp.broadcast_to(placement_ref[...].astype(jnp.float32), (8, table))
    slot = _dot(placed.astype(jnp.bfloat16), matches.astype(jnp.bfloat16)).astype(jnp.int32)
    slot = slot[0:1, :]
    holder = (slot // slots) ^ lax.axis_index("dp")
    inside = slot % slots
    of_holder = _iota((max(replicas, 8), requests), 0) == holder
    earlier = _iota((requests, requests), 0) < _iota((requests, requests), 1)
    before = _dot(of_holder.astype(jnp.bfloat16), earlier.astype(jnp.bfloat16))
    before = jnp.sum(jnp.where(of_holder, before, 0.0), axis=0, keepdims=True).astype(jnp.int32)
    target = holder * CAP + before
    here = _iota((replicas * CAP, requests), 0) == target
    chosen_ref[...] = here.astype(jnp.bfloat16)
    inner = jnp.sum(jnp.where(here, inside.astype(jnp.float32), 0.0), axis=1, keepdims=True)
    inner = jnp.broadcast_to(inner, (replicas * CAP, LANES)).astype(jnp.bfloat16)
    sent_ref[:, pl.ds(sent_ref.shape[1] - LANES, LANES)] = inner


def attend(
    query, keys, values, new_key, new_value, lengths, weight, request_adapter, placement,
    block, replicas, slots,
):
    requests, heads, width = query.shape
    cache, kv = keys.shape[1], keys.shape[2]
    steps = 2
    per = requests // steps
    columns = GROUP * cache * kv + SPAN * kv
    features = heads * width
    chunk = chain_columns(block)[0][1]
    small = [lengths.reshape(1, -1), request_adapter.reshape(1, -1), placement.reshape(1, -1)]
    operands = [
        query.reshape(requests * heads, width),
        keys.reshape(requests * cache * kv, width),
        values.reshape(requests * cache * kv, width),
        new_key.reshape(requests * kv, width),
        new_value.reshape(requests * kv, width),
    ]
    return pl.pallas_call(
        functools.partial(attend_kernel, heads, kv, cache, steps, block, replicas, slots),
        in_specs=[ANY] * 9,
        out_specs=[ANY] * (3 + replicas),
        out_shape=[
            jax.ShapeDtypeStruct((requests, features), jnp.bfloat16),
            jax.ShapeDtypeStruct((requests, chunk), jnp.bfloat16),
            jax.ShapeDtypeStruct((replicas * CAP, requests), jnp.bfloat16),
        ]
        + [jax.ShapeDtypeStruct((CAP, features + LANES), jnp.bfloat16)] * replicas,
        scratch_shapes=[
            pltpu.VMEM((requests, features), jnp.bfloat16),
            pltpu.VMEM((requests, chunk), jnp.bfloat16),
            pltpu.VMEM((replicas * CAP, requests), jnp.bfloat16),
            pltpu.VMEM((replicas * CAP, features + LANES), jnp.bfloat16),
            pltpu.SemaphoreType.DMA((1 + steps + 2 + replicas,)),
        ]
        + [pltpu.VMEM(x.shape, x.dtype) for x in small + operands]
        + [
            pltpu.VMEM((2, per * heads, columns), jnp.float32),
            pltpu.VMEM((2, per * heads, width), jnp.float32),
            pltpu.VMEM((SPAN * heads, SPAN * kv), jnp.float32),
            pltpu.SemaphoreType.DMA((3, steps)),
            pltpu.SemaphoreType.DMA((5,)),
        ]
        + Weights.scratch(weight.shape[0], chunk),
        compiler_params=pltpu.CompilerParams(vmem_limit_bytes=FULL_VMEM),
        name="attend",
    )(*small, *operands, weight)


def hop_kernel(step, block, start, arriving, after, *refs):
    if arriving:
        arrived_ref, *refs = refs
    a_ref, w_hbm, *refs = refs
    out_ref, held, sems = refs[after:]
    chunk = out_ref.shape[1]
    first = column_owner(step) * block + start
    weights = Weights(w_hbm, held, sems, first, chunk)
    weights.start()
    weights.wait()
    for columns, product in weights.products(a_ref[...]):
        if arriving:
            product = product + arrived_ref[:, columns].astype(jnp.float32)
        out_ref[:, columns] = product.astype(jnp.bfloat16)


def hop(step, chain, arrived, attended, weight, block, after=(), cost=None):
    arriving = arrived is not None
    start, chunk = chain_columns(block)[chain]
    operands = ([arrived] if arriving else []) + [attended, weight, *after]
    return pl.pallas_call(
        functools.partial(hop_kernel, step, block, start, arriving, len(after)),
        in_specs=[VMEM] * (1 + arriving) + [ANY] + [ANY] * len(after),
        out_specs=VMEM,
        out_shape=jax.ShapeDtypeStruct((attended.shape[0], chunk), jnp.bfloat16),
        scratch_shapes=Weights.scratch(weight.shape[0], chunk),
        compiler_params=PARAMS,
        cost_estimate=cost,
        name="hop",
    )(*operands)


def down_kernel(replicas, after, *refs):
    received = refs[:replicas]
    down_ref = refs[replicas]
    mid_ref, inside_ref = refs[replicas + 1 + after :]
    slots, rank, width = down_ref.shape
    rows = jnp.concatenate([r[:, pl.ds(0, width)] for r in received], axis=0)
    inside = jnp.concatenate([r[:, pl.ds(width, LANES)] for r in received], axis=0)
    inside_ref[...] = inside
    projected = _dot(rows, down_ref[...].reshape(slots * rank, width), 1, 1)
    lane_slot = _iota(projected.shape, 1) // rank
    mine = lane_slot == inside[:, 0:1].astype(jnp.int32)
    projected = jnp.where(mine, projected, 0.0).astype(jnp.bfloat16)
    beside = LANES // rank
    some = projected.shape[0] // beside
    packed = 0.0
    for b in range(beside):
        lane = _iota((slots * rank, LANES), 1) - b * rank
        fold = _iota((slots * rank, LANES), 0) % rank == lane
        packed = packed + _dot(projected[b * some : (b + 1) * some, :], fold.astype(jnp.bfloat16))
    mid_ref[...] = packed.astype(jnp.bfloat16)


def down(received, slot_down_weight, after=()):
    replicas = len(received)
    rows = replicas * CAP
    return pl.pallas_call(
        functools.partial(down_kernel, replicas, len(after)),
        in_specs=[VMEM] * (replicas + 1) + [ANY] * len(after),
        out_specs=[VMEM, VMEM],
        out_shape=[
            jax.ShapeDtypeStruct((rows * slot_down_weight.shape[1] // LANES, LANES), jnp.bfloat16),
            jax.ShapeDtypeStruct((rows, LANES), jnp.bfloat16),
        ],
        compiler_params=PARAMS,
        name="down",
    )(*received, slot_down_weight, *after)


def up_kernel(parts, after, *refs):
    mids = refs[:parts]
    inside_ref, up_ref = refs[parts : parts + 2]
    out_refs = refs[parts + 2 + after :]
    slots, rank, width = up_ref.shape
    mid = mids[0][...].astype(jnp.float32)
    for m in mids[1:]:
        mid = mid + m[...].astype(jnp.float32)
    mid = mid.astype(jnp.bfloat16)
    wide = []
    for b in range(LANES // rank):
        lane = _iota((LANES, slots * rank), 0) - b * rank
        spread = _iota((LANES, slots * rank), 1) % rank == lane
        wide.append(_dot(mid, spread.astype(jnp.bfloat16)))
    wide = jnp.concatenate(wide, axis=0)
    mine = _iota(wide.shape, 1) // rank == inside_ref[:, 0:1].astype(jnp.int32)
    wide = jnp.where(mine, wide, 0.0).astype(jnp.bfloat16)
    delta = _dot(wide, up_ref[...].reshape(slots * rank, width)).astype(jnp.bfloat16)
    for r, out_ref in enumerate(out_refs):
        out_ref[...] = delta[r * CAP : (r + 1) * CAP, :]


def up(mids, inside, slot_up_weight, after=()):
    rows = inside.shape[0]
    replicas = rows // CAP
    width = slot_up_weight.shape[2]
    return pl.pallas_call(
        functools.partial(up_kernel, len(mids), len(after)),
        in_specs=[VMEM] * (len(mids) + 2) + [ANY] * len(after),
        out_specs=[VMEM] * replicas,
        out_shape=[jax.ShapeDtypeStruct((CAP, width), jnp.bfloat16)] * replicas,
        compiler_params=PARAMS,
        name="up",
    )(*mids, inside, slot_up_weight, *after)


def settle_kernel(step, replicas, after, *refs):
    returned = refs[:replicas]
    chosen_ref, a_ref, residual_ref, w_hbm = refs[replicas : replicas + 4]
    *out_refs, held, sems = refs[replicas + 4 + after :]
    width = residual_ref.shape[1]
    weights = Weights(w_hbm, held, sems, column_owner(step) * width, width)
    weights.start()
    rows = jnp.concatenate([r[...] for r in returned], axis=0)
    delta = _dot(chosen_ref[...], rows, 0, 0)
    total = residual_ref[...].astype(jnp.float32) + delta
    weights.wait()
    total = total + jnp.concatenate([p for _, p in weights.products(a_ref[...])], axis=1)
    for (start, chunk), out_ref in zip(chain_columns(width), out_refs):
        out_ref[...] = total[:, start : start + chunk]


def settle(step, returned, chosen, attended, residual, weight, after=()):
    replicas = len(returned)
    rows, width = residual.shape
    chains = chain_columns(width)
    return pl.pallas_call(
        functools.partial(settle_kernel, step, replicas, len(after)),
        in_specs=[VMEM] * (replicas + 3) + [ANY] * (1 + len(after)),
        out_specs=[VMEM] * len(chains),
        out_shape=[jax.ShapeDtypeStruct((rows, chunk), jnp.float32) for _, chunk in chains],
        scratch_shapes=Weights.scratch(weight.shape[0], width),
        compiler_params=PARAMS,
        cost_estimate=SETTLE,
        name="settle",
    )(*returned, chosen, attended, residual, weight, *after)


def finish_kernel(start, arrived_ref, settled_ref, *refs):
    out_hbm, held, sems = refs[-3:]
    rows, chunk = arrived_ref.shape
    half = rows // 2
    copies = []
    for i in range(2):
        part = pl.ds(i * half, half)
        total = settled_ref[part, :] + arrived_ref[part, :].astype(jnp.float32)
        held[part, :] = total.astype(jnp.bfloat16)
        target = out_hbm.at[part, pl.ds(start, chunk)]
        copies.append(pltpu.make_async_copy(held.at[part, :], target, sems.at[i]))
        copies[-1].start()
    for copy in copies:
        copy.wait()


def finish(chain, arrived, settled, earlier, width):
    rows = arrived.shape[0]
    start, chunk = chain_columns(width)[chain]
    operands = [arrived, settled] + ([earlier] if earlier is not None else [])
    return pl.pallas_call(
        functools.partial(finish_kernel, start),
        in_specs=[VMEM, VMEM] + ([ANY] if earlier is not None else []),
        out_specs=ANY,
        out_shape=jax.ShapeDtypeStruct((rows, width), jnp.bfloat16),
        input_output_aliases={2: 0} if earlier is not None else {},
        scratch_shapes=[
            pltpu.VMEM((rows, chunk), jnp.bfloat16),
            pltpu.SemaphoreType.DMA((2,)),
        ],
        compiler_params=PARAMS,
        name="finish",
    )(*operands)


def hold_kernel(*refs):
    pass


def hold(x, after):
    return pl.pallas_call(
        hold_kernel,
        in_specs=[ANY] * (1 + len(after)),
        out_specs=ANY,
        out_shape=jax.ShapeDtypeStruct(x.shape, x.dtype),
        input_output_aliases={0: 0},
        compiler_params=PARAMS,
        name="hold",
    )(x, *after)


def per_device(
    residual,
    query,
    cached_key_rows,
    cached_value_rows,
    new_token_key,
    new_token_value,
    lengths,
    output_weight,
    slot_down_weight,
    slot_up_weight,
    placement,
    request_adapter,
):
    count = lax.axis_size("tensor")
    replicas = lax.axis_size("dp")
    block = residual.shape[1]
    order = ring_order(count)
    ring = [(order[p], order[(p + 1) % count]) for p in range(count)]

    def exchange(blocks):
        moved = [
            lax.ppermute(blocks[r], "dp", [(i, i ^ r) for i in range(replicas)])
            for r in range(1, replicas)
        ]
        return [blocks[0]] + moved

    def forward(x):
        return lax.ppermute(x, "tensor", ring)

    def pair_sums(x):
        found = []
        for away in range(1, count // 2):
            pairs = [(p, (p + away) % (count // 2)) for p in range(count // 2)]
            near, far = [], []
            for p, q in pairs:
                sender = 2 * p if p < q else 2 * p + 1
                straight = 2 * q + (sender % 2)
                near.append((sender, straight))
                far.append((sender, straight ^ 1))
            one = lax.ppermute(x, "tensor", near)
            other = lax.ppermute(x, "tensor", far)
            found += [one, other]
        return found

    def next_hop(step, chain, after, cost=None):
        arrived = forward(travelling[chain])
        travelling[chain] = hop(step, chain, arrived, attended, output_weight, block, after, cost)

    attended, first, chosen, *leaving = attend(
        query, cached_key_rows, cached_value_rows, new_token_key, new_token_value, lengths,
        output_weight, request_adapter, placement, block, replicas, slot_down_weight.shape[0],
    )
    second = hop(0, 1, None, attended, output_weight, block)
    rows_here = exchange(leaving)
    mid, inside = down(rows_here, slot_down_weight, after=[second])
    travelling = [first, hold(second, after=[mid])]

    def added(a, b):
        return (a.astype(jnp.float32) + b.astype(jnp.float32)).astype(a.dtype)

    rank_sum = added(mid, lax.ppermute(mid, "tensor", [(i, i ^ 1) for i in range(count)]))
    rank_sums = [rank_sum] + pair_sums(rank_sum)
    next_hop(1, 0, after=[rank_sum, travelling[1]], cost=LONG)
    next_hop(1, 1, after=[travelling[0]], cost=MEDIUM)
    for step in range(2, count - 1):
        for chain in range(2):
            if (step, chain) == (2, 0):
                next_hop(step, chain, after=(), cost=LONG)
                deltas = up(rank_sums, inside, slot_up_weight, after=[travelling[0]])
                returned = exchange(deltas)
            else:
                next_hop(step, chain, after=[deltas[0]])
    settled = settle(
        count - 1, returned, chosen, attended, residual, output_weight, after=[travelling[1]]
    )
    out = None
    for chain in range(2):
        arrived = forward(travelling[chain])
        out = finish(chain, arrived, settled[chain], out, block)
    return out


def solution(mesh):
    placed = (
        P(("parts", "dp"), "tensor"),
        P(("parts", "dp"), "tensor", None),
        P(("parts", "dp"), None, "tensor", None),
        P(("parts", "dp"), None, "tensor", None),
        P(("parts", "dp"), "tensor", None),
        P(("parts", "dp"), "tensor", None),
        P(("parts", "dp")),
        P("tensor", None),
        P("dp", None, "tensor"),
        P("dp", None, "tensor"),
        P("parts"),
        P(("parts", "dp")),
    )
    return jax.shard_map(
        per_device,
        mesh=mesh,
        in_specs=placed,
        out_specs=P(("parts", "dp"), "tensor"),
        check_vma=False,
    )
```

```python
import functools
import math

import jax
import jax.numpy as jnp
from jax import lax
from jax.experimental import pallas as pl
from jax.experimental.pallas import tpu as pltpu
from jax.sharding import PartitionSpec as P

GROUP = 4
CAP = 64
LANES = 128
SPAN = 64
MASKED = -1e30
VMEM_LIMIT = 50 * 1024 * 1024
FULL_VMEM = 61 * 1024 * 1024
SHARES = ((5, 3),)
PIECE = 512
SPLIT = 4

VMEM = pl.BlockSpec(memory_space=pltpu.VMEM)
ANY = pl.BlockSpec(memory_space=pl.ANY)
LONG = pl.CostEstimate(flops=20 * 10**9, transcendentals=0, bytes_accessed=40 * 10**6)
MEDIUM = pl.CostEstimate(flops=4 * 10**9, transcendentals=0, bytes_accessed=8 * 10**6)
PARAMS = pltpu.CompilerParams(vmem_limit_bytes=VMEM_LIMIT)


def _dot(a, b, left=1, right=0):
    return lax.dot_general(
        a, b, (((left,), (right,)), ((), ())), preferred_element_type=jnp.float32
    )


def _iota(shape, axis):
    return lax.broadcasted_iota(jnp.int32, shape, axis)


def ring_order(count):
    return list(range(0, count, 2)) + list(range(1, count, 2))[::-1]


def column_owner(step):
    count = lax.axis_size("tensor")
    here = lax.axis_index("tensor")
    half = here // 2
    spot = jnp.where(here % 2 == 0, half, count - 1 - half)
    spot = lax.rem(spot - 1 - step + 2 * count, count)
    return jnp.where(2 * spot < count, 2 * spot, 2 * (count - spot) - 1)


def chain_columns(width):
    shares = next(s for s in SHARES if width % (sum(s) * LANES) == 0)
    unit = width // sum(shares)
    return [(sum(shares[:c]) * unit, shares[c] * unit) for c in range(len(shares))]


class Weights:
    def __init__(self, w_ref, held, sems, first, width):
        depth = w_ref.shape[0] // SPLIT
        first = pl.multiple_of(first, LANES)
        self.held = held
        self.copies = [
            pltpu.make_async_copy(
                w_ref.at[pl.ds(s * depth, depth), pl.ds(first, width)],
                held.at[pl.ds(s * depth, depth), :],
                sems.at[s],
            )
            for s in range(SPLIT)
        ]

    def start(self):
        for copy in self.copies:
            copy.start()

    def wait(self):
        for copy in self.copies:
            copy.wait()

    def products(self, a):
        width = self.held.shape[1]
        for at in range(0, width, PIECE):
            columns = pl.ds(at, min(PIECE, width - at))
            yield columns, _dot(a, self.held[:, columns])

    @staticmethod
    def scratch(depth, width):
        return [
            pltpu.VMEM((depth, width), jnp.bfloat16),
            pltpu.SemaphoreType.DMA((SPLIT,)),
        ]


def row_max(arrays):
    full = None
    tops = []
    for x in arrays:
        width = x.shape[1]
        if width % LANES:
            tops.append(jnp.max(x, axis=1, keepdims=True))
            continue
        for at in range(0, width, LANES):
            tile = x[:, at : at + LANES]
            full = tile if full is None else jnp.maximum(full, tile)
    if full is not None:
        tops.append(jnp.max(full, axis=1, keepdims=True))
    return functools.reduce(jnp.maximum, tops)


def attend_kernel(
    heads, kv, cache, steps, block, replicas, slots,
    len_hbm, adapter_hbm, placement_hbm, q_hbm, k_hbm, v_hbm, nk_hbm, nv_hbm, w_hbm,
    *refs,
):
    a_hbm, out_hbm, chosen_hbm, *sent_hbm = refs[: 3 + replicas]
    (
        a_ref, out_ref, chosen_ref, sent_ref, out_sems,
        len_ref, adapter_ref, placement_ref, q_ref, k_ref, v_ref, nk_ref, nv_ref,
        scores_ref, mixed_ref, fresh_bias_ref, sems, small_sems, w_held, w_sems,
    ) = refs[3 + replicas :]
    requests = len_ref.shape[1]
    width = q_hbm.shape[1]
    per = requests // steps
    groups = per // GROUP
    group_rows = GROUP * heads
    group_cols = GROUP * cache * kv
    per_kv = heads // kv
    scale = math.log2(math.e) / math.sqrt(width)

    def part(kind, step):
        source, target, count = (
            (q_hbm, q_ref, heads),
            (k_hbm, k_ref, cache * kv),
            (v_hbm, v_ref, cache * kv),
        )[kind]
        rows = pl.ds(step * per * count, per * count)
        return pltpu.make_async_copy(source.at[rows, :], target.at[rows, :], sems.at[kind, step])

    small = [
        pltpu.make_async_copy(source, target, small_sems.at[i])
        for i, (source, target) in enumerate(
            (
                (nk_hbm, nk_ref),
                (len_hbm, len_ref),
                (nv_hbm, nv_ref),
                (adapter_hbm, adapter_ref),
                (placement_hbm, placement_ref),
            )
        )
    ]
    leaving = []

    def leave(source, target):
        copy = pltpu.make_async_copy(source, target, out_sems.at[len(leaving)])
        copy.start()
        leaving.append(copy)

    def multiply(first, count):
        rows = pl.ds(first, count)
        for columns, product in weights.products(a_ref[rows, :]):
            out_ref[rows, columns] = product.astype(jnp.bfloat16)
        leave(out_ref.at[rows, :], out_hbm.at[rows, :])

    chunk = out_ref.shape[1]
    weights = Weights(w_hbm, w_held, w_sems, column_owner(0) * block, chunk)
    part(0, 0).start()
    part(1, 0).start()
    for copy in small[:2]:
        copy.start()
    part(0, 1).start()
    part(1, 1).start()
    part(2, 0).start()
    for copy in small[2:]:
        copy.start()
    part(2, 1).start()
    for step in range(2, steps):
        for kind in range(3):
            part(kind, step).start()
    weights.start()

    row = _iota((group_rows, group_cols), 0)
    col = _iota((group_rows, group_cols), 1)
    same = (row // heads == col // (cache * kv)) & ((row % heads) // per_kv == col % kv)
    own_bias = jnp.where(same, 0.0, MASKED)
    row = _iota(fresh_bias_ref.shape, 0)
    col = _iota(fresh_bias_ref.shape, 1)
    same = (row // heads == col // kv) & ((row % heads) // per_kv == col % kv)
    fresh_bias_ref[...] = jnp.where(same, 0.0, MASKED)
    fresh_cols = SPAN * kv
    span_rows = SPAN * heads
    span_groups = SPAN // GROUP
    ones = jnp.ones((max(group_cols, fresh_cols), LANES), jnp.bfloat16)

    def arrive(step):
        part(0, step).wait()
        part(1, step).wait()

    def scores(step):
        side = step % 2
        q_at = step * per * heads
        k_at = step * per * cache * kv
        for g in range(groups):
            scores_ref[side, pl.ds(g * group_rows, group_rows), pl.ds(0, group_cols)] = _dot(
                q_ref[pl.ds(q_at + g * group_rows, group_rows), :],
                k_ref[pl.ds(k_at + g * group_cols, group_cols), :],
                1,
                1,
            )
        for span in range(per // SPAN):
            rows = pl.ds(span * span_rows, span_rows)
            scores_ref[side, rows, pl.ds(group_cols, fresh_cols)] = _dot(
                q_ref[pl.ds(q_at + span * span_rows, span_rows), :],
                nk_ref[pl.ds(step * per * kv + span * fresh_cols, fresh_cols), :],
                1,
                1,
            )

    for copy in small:
        copy.wait()
    counts = len_ref[...].astype(jnp.float32)
    all_groups = requests // GROUP
    of_group = _iota((all_groups, requests), 1) // GROUP == _iota((all_groups, requests), 0)
    counts = jnp.where(of_group, counts, 0.0).astype(jnp.bfloat16)
    spread = _iota((requests, group_cols), 0) % GROUP == _iota((requests, group_cols), 1) // (cache * kv)
    counts = _dot(counts, spread.astype(jnp.bfloat16))
    position = (_iota((all_groups, group_cols), 1) // kv) % cache
    length_bias = jnp.where(position.astype(jnp.float32) < counts, 0.0, MASKED)

    arrive(0)
    scores(0)
    for step in range(steps):
        side = step % 2
        k_at = step * per * cache * kv
        f_at = step * per * kv
        part(2, step).wait()
        if step + 1 < steps:
            arrive(step + 1)
            scores(step + 1)
        if step == 0:
            plan_routes(slots, adapter_ref, placement_ref, chosen_ref, sent_ref)
            leave(chosen_ref, chosen_hbm)
        for span in range(per // SPAN):
            if step == steps - 1 and span == per // SPAN - 1:
                weights.wait()
                multiply(0, requests - per)
            cached_weights = []
            fresh_weights = []
            mixed = []
            for g in range(span * span_groups, (span + 1) * span_groups):
                rows = pl.ds(g * group_rows, group_rows)
                bias = own_bias + length_bias[step * groups + g : step * groups + g + 1, :]
                cached = scores_ref[side, rows, pl.ds(0, group_cols)] + bias
                inner = pl.ds((g % span_groups) * group_rows, group_rows)
                new = scores_ref[side, rows, pl.ds(group_cols, fresh_cols)]
                new = new + fresh_bias_ref[inner, :]
                top = row_max([cached, new])
                cached = jnp.exp2((cached - top) * scale).astype(jnp.bfloat16)
                cached_weights.append(cached)
                fresh_weights.append(jnp.exp2((new - top) * scale).astype(jnp.bfloat16))
                mixed.append(_dot(cached, v_ref[pl.ds(k_at + g * group_cols, group_cols), :]))
            fresh = jnp.concatenate(fresh_weights, axis=0)
            values = nv_ref[pl.ds(f_at + span * fresh_cols, fresh_cols), :]
            mixed = jnp.concatenate(mixed, axis=0) + _dot(fresh, values)
            total = _dot(jnp.concatenate(cached_weights, axis=0), ones[:group_cols])
            total = total + _dot(fresh, ones[:fresh_cols])
            rows = pl.ds(span * span_rows, span_rows)
            inverse = pl.reciprocal(total, approx=True)
            mixed_ref[side, rows, :] = mixed * (inverse * (2.0 - total * inverse))
        for h in range(heads):
            a_ref[pl.ds(step * per, per), pl.ds(h * width, width)] = mixed_ref[
                side, pl.ds(h, per, stride=heads), :
            ].astype(jnp.bfloat16)
        rows = pl.ds(step * per, per)
        leave(a_ref.at[rows, :], a_hbm.at[rows, :])

    sent_ref[:, pl.ds(0, heads * width)] = _dot(chosen_ref[...], a_ref[...]).astype(jnp.bfloat16)
    for r in range(replicas):
        leave(sent_ref.at[pl.ds(r * CAP, CAP), :], sent_hbm[r])
    multiply(requests - per, per)
    for copy in leaving:
        copy.wait()


def plan_routes(slots, adapter_ref, placement_ref, chosen_ref, sent_ref):
    replicas = sent_ref.shape[0] // CAP
    requests = adapter_ref.shape[1]
    table = placement_ref.shape[1]
    matches = _iota((table, requests), 0) == adapter_ref[...]
    placed = jnp.broadcast_to(placement_ref[...].astype(jnp.float32), (8, table))
    slot = _dot(placed.astype(jnp.bfloat16), matches.astype(jnp.bfloat16)).astype(jnp.int32)
    slot = slot[0:1, :]
    holder = (slot // slots) ^ lax.axis_index("dp")
    inside = slot % slots
    of_holder = _iota((max(replicas, 8), requests), 0) == holder
    earlier = _iota((requests, requests), 0) < _iota((requests, requests), 1)
    before = _dot(of_holder.astype(jnp.bfloat16), earlier.astype(jnp.bfloat16))
    before = jnp.sum(jnp.where(of_holder, before, 0.0), axis=0, keepdims=True).astype(jnp.int32)
    target = holder * CAP + before
    here = _iota((replicas * CAP, requests), 0) == target
    chosen_ref[...] = here.astype(jnp.bfloat16)
    inner = jnp.sum(jnp.where(here, inside.astype(jnp.float32), 0.0), axis=1, keepdims=True)
    inner = jnp.broadcast_to(inner, (replicas * CAP, LANES)).astype(jnp.bfloat16)
    sent_ref[:, pl.ds(sent_ref.shape[1] - LANES, LANES)] = inner


def attend(
    query, keys, values, new_key, new_value, lengths, weight, request_adapter, placement,
    block, replicas, slots,
):
    requests, heads, width = query.shape
    cache, kv = keys.shape[1], keys.shape[2]
    steps = 2
    per = requests // steps
    columns = GROUP * cache * kv + SPAN * kv
    features = heads * width
    chunk = chain_columns(block)[0][1]
    small = [lengths.reshape(1, -1), request_adapter.reshape(1, -1), placement.reshape(1, -1)]
    operands = [
        query.reshape(requests * heads, width),
        keys.reshape(requests * cache * kv, width),
        values.reshape(requests * cache * kv, width),
        new_key.reshape(requests * kv, width),
        new_value.reshape(requests * kv, width),
    ]
    return pl.pallas_call(
        functools.partial(attend_kernel, heads, kv, cache, steps, block, replicas, slots),
        in_specs=[ANY] * 9,
        out_specs=[ANY] * (3 + replicas),
        out_shape=[
            jax.ShapeDtypeStruct((requests, features), jnp.bfloat16),
            jax.ShapeDtypeStruct((requests, chunk), jnp.bfloat16),
            jax.ShapeDtypeStruct((replicas * CAP, requests), jnp.bfloat16),
        ]
        + [jax.ShapeDtypeStruct((CAP, features + LANES), jnp.bfloat16)] * replicas,
        scratch_shapes=[
            pltpu.VMEM((requests, features), jnp.bfloat16),
            pltpu.VMEM((requests, chunk), jnp.bfloat16),
            pltpu.VMEM((replicas * CAP, requests), jnp.bfloat16),
            pltpu.VMEM((replicas * CAP, features + LANES), jnp.bfloat16),
            pltpu.SemaphoreType.DMA((1 + steps + 2 + replicas,)),
        ]
        + [pltpu.VMEM(x.shape, x.dtype) for x in small + operands]
        + [
            pltpu.VMEM((2, per * heads, columns), jnp.float32),
            pltpu.VMEM((2, per * heads, width), jnp.float32),
            pltpu.VMEM((SPAN * heads, SPAN * kv), jnp.float32),
            pltpu.SemaphoreType.DMA((3, steps)),
            pltpu.SemaphoreType.DMA((5,)),
        ]
        + Weights.scratch(weight.shape[0], chunk),
        compiler_params=pltpu.CompilerParams(vmem_limit_bytes=FULL_VMEM),
        name="attend",
    )(*small, *operands, weight)


def hop_kernel(step, block, start, arriving, after, *refs):
    if arriving:
        arrived_ref, *refs = refs
    a_ref, w_hbm, *refs = refs
    out_ref, held, sems = refs[after:]
    chunk = out_ref.shape[1]
    first = column_owner(step) * block + start
    weights = Weights(w_hbm, held, sems, first, chunk)
    weights.start()
    weights.wait()
    for columns, product in weights.products(a_ref[...]):
        if arriving:
            product = product + arrived_ref[:, columns].astype(jnp.float32)
        out_ref[:, columns] = product.astype(jnp.bfloat16)


def hop(step, chain, arrived, attended, weight, block, after=(), cost=None):
    arriving = arrived is not None
    start, chunk = chain_columns(block)[chain]
    operands = ([arrived] if arriving else []) + [attended, weight, *after]
    return pl.pallas_call(
        functools.partial(hop_kernel, step, block, start, arriving, len(after)),
        in_specs=[VMEM] * (1 + arriving) + [ANY] + [ANY] * len(after),
        out_specs=VMEM,
        out_shape=jax.ShapeDtypeStruct((attended.shape[0], chunk), jnp.bfloat16),
        scratch_shapes=Weights.scratch(weight.shape[0], chunk),
        compiler_params=PARAMS,
        cost_estimate=cost,
        name="hop",
    )(*operands)


def down_kernel(replicas, after, *refs):
    received = refs[:replicas]
    down_ref = refs[replicas]
    mid_ref, inside_ref = refs[replicas + 1 + after :]
    slots, rank, width = down_ref.shape
    rows = jnp.concatenate([r[:, pl.ds(0, width)] for r in received], axis=0)
    inside = jnp.concatenate([r[:, pl.ds(width, LANES)] for r in received], axis=0)
    inside_ref[...] = inside
    projected = _dot(rows, down_ref[...].reshape(slots * rank, width), 1, 1)
    lane_slot = _iota(projected.shape, 1) // rank
    mine = lane_slot == inside[:, 0:1].astype(jnp.int32)
    projected = jnp.where(mine, projected, 0.0).astype(jnp.bfloat16)
    beside = LANES // rank
    some = projected.shape[0] // beside
    packed = 0.0
    for b in range(beside):
        lane = _iota((slots * rank, LANES), 1) - b * rank
        fold = _iota((slots * rank, LANES), 0) % rank == lane
        packed = packed + _dot(projected[b * some : (b + 1) * some, :], fold.astype(jnp.bfloat16))
    mid_ref[...] = packed.astype(jnp.bfloat16)


def down(received, slot_down_weight, after=()):
    replicas = len(received)
    rows = replicas * CAP
    return pl.pallas_call(
        functools.partial(down_kernel, replicas, len(after)),
        in_specs=[VMEM] * (replicas + 1) + [ANY] * len(after),
        out_specs=[VMEM, VMEM],
        out_shape=[
            jax.ShapeDtypeStruct((rows * slot_down_weight.shape[1] // LANES, LANES), jnp.bfloat16),
            jax.ShapeDtypeStruct((rows, LANES), jnp.bfloat16),
        ],
        compiler_params=PARAMS,
        name="down",
    )(*received, slot_down_weight, *after)


def up_kernel(parts, after, *refs):
    mids = refs[:parts]
    inside_ref, up_ref = refs[parts : parts + 2]
    out_refs = refs[parts + 2 + after :]
    slots, rank, width = up_ref.shape
    mid = mids[0][...].astype(jnp.float32)
    for m in mids[1:]:
        mid = mid + m[...].astype(jnp.float32)
    mid = mid.astype(jnp.bfloat16)
    wide = []
    for b in range(LANES // rank):
        lane = _iota((LANES, slots * rank), 0) - b * rank
        spread = _iota((LANES, slots * rank), 1) % rank == lane
        wide.append(_dot(mid, spread.astype(jnp.bfloat16)))
    wide = jnp.concatenate(wide, axis=0)
    mine = _iota(wide.shape, 1) // rank == inside_ref[:, 0:1].astype(jnp.int32)
    wide = jnp.where(mine, wide, 0.0).astype(jnp.bfloat16)
    delta = _dot(wide, up_ref[...].reshape(slots * rank, width)).astype(jnp.bfloat16)
    for r, out_ref in enumerate(out_refs):
        out_ref[...] = delta[r * CAP : (r + 1) * CAP, :]


def up(mids, inside, slot_up_weight, after=()):
    rows = inside.shape[0]
    replicas = rows // CAP
    width = slot_up_weight.shape[2]
    return pl.pallas_call(
        functools.partial(up_kernel, len(mids), len(after)),
        in_specs=[VMEM] * (len(mids) + 2) + [ANY] * len(after),
        out_specs=[VMEM] * replicas,
        out_shape=[jax.ShapeDtypeStruct((CAP, width), jnp.bfloat16)] * replicas,
        compiler_params=PARAMS,
        name="up",
    )(*mids, inside, slot_up_weight, *after)


def settle_kernel(step, replicas, after, *refs):
    returned = refs[:replicas]
    chosen_ref, a_ref, residual_ref, w_hbm = refs[replicas : replicas + 4]
    *out_refs, held, sems = refs[replicas + 4 + after :]
    width = residual_ref.shape[1]
    weights = Weights(w_hbm, held, sems, column_owner(step) * width, width)
    weights.start()
    rows = jnp.concatenate([r[...] for r in returned], axis=0)
    delta = _dot(chosen_ref[...], rows, 0, 0)
    total = residual_ref[...].astype(jnp.float32) + delta
    weights.wait()
    total = total + jnp.concatenate([p for _, p in weights.products(a_ref[...])], axis=1)
    for (start, chunk), out_ref in zip(chain_columns(width), out_refs):
        out_ref[...] = total[:, start : start + chunk]


def settle(step, returned, chosen, attended, residual, weight, after=()):
    replicas = len(returned)
    rows, width = residual.shape
    chains = chain_columns(width)
    return pl.pallas_call(
        functools.partial(settle_kernel, step, replicas, len(after)),
        in_specs=[VMEM] * (replicas + 3) + [ANY] * (1 + len(after)),
        out_specs=[VMEM] * len(chains),
        out_shape=[jax.ShapeDtypeStruct((rows, chunk), jnp.float32) for _, chunk in chains],
        scratch_shapes=Weights.scratch(weight.shape[0], width),
        compiler_params=PARAMS,
        cost_estimate=MEDIUM,
        name="settle",
    )(*returned, chosen, attended, residual, weight, *after)


def finish_kernel(start, arrived_ref, settled_ref, *refs):
    out_hbm, held, sems = refs[-3:]
    rows, chunk = arrived_ref.shape
    half = rows // 2
    copies = []
    for i in range(2):
        part = pl.ds(i * half, half)
        total = settled_ref[part, :] + arrived_ref[part, :].astype(jnp.float32)
        held[part, :] = total.astype(jnp.bfloat16)
        target = out_hbm.at[part, pl.ds(start, chunk)]
        copies.append(pltpu.make_async_copy(held.at[part, :], target, sems.at[i]))
        copies[-1].start()
    for copy in copies:
        copy.wait()


def finish(chain, arrived, settled, earlier, width):
    rows = arrived.shape[0]
    start, chunk = chain_columns(width)[chain]
    operands = [arrived, settled] + ([earlier] if earlier is not None else [])
    return pl.pallas_call(
        functools.partial(finish_kernel, start),
        in_specs=[VMEM, VMEM] + ([ANY] if earlier is not None else []),
        out_specs=ANY,
        out_shape=jax.ShapeDtypeStruct((rows, width), jnp.bfloat16),
        input_output_aliases={2: 0} if earlier is not None else {},
        scratch_shapes=[
            pltpu.VMEM((rows, chunk), jnp.bfloat16),
            pltpu.SemaphoreType.DMA((2,)),
        ],
        compiler_params=PARAMS,
        name="finish",
    )(*operands)


def hold_kernel(*refs):
    pass


def hold(x, after):
    return pl.pallas_call(
        hold_kernel,
        in_specs=[ANY] * (1 + len(after)),
        out_specs=ANY,
        out_shape=jax.ShapeDtypeStruct(x.shape, x.dtype),
        input_output_aliases={0: 0},
        compiler_params=PARAMS,
        name="hold",
    )(x, *after)


def per_device(
    residual,
    query,
    cached_key_rows,
    cached_value_rows,
    new_token_key,
    new_token_value,
    lengths,
    output_weight,
    slot_down_weight,
    slot_up_weight,
    placement,
    request_adapter,
):
    count = lax.axis_size("tensor")
    replicas = lax.axis_size("dp")
    block = residual.shape[1]
    order = ring_order(count)
    ring = [(order[p], order[(p + 1) % count]) for p in range(count)]

    def exchange(blocks):
        moved = [
            lax.ppermute(blocks[r], "dp", [(i, i ^ r) for i in range(replicas)])
            for r in range(1, replicas)
        ]
        return [blocks[0]] + moved

    def forward(x):
        return lax.ppermute(x, "tensor", ring)

    def pair_sums(x):
        found = []
        for away in range(1, count // 2):
            pairs = [(p, (p + away) % (count // 2)) for p in range(count // 2)]
            near, far = [], []
            for p, q in pairs:
                sender = 2 * p if p < q else 2 * p + 1
                straight = 2 * q + (sender % 2)
                near.append((sender, straight))
                far.append((sender, straight ^ 1))
            one = lax.ppermute(x, "tensor", near)
            other = lax.ppermute(x, "tensor", far)
            found += [one, other]
        return found

    def next_hop(step, chain, after, cost=None):
        arrived = forward(travelling[chain])
        travelling[chain] = hop(step, chain, arrived, attended, output_weight, block, after, cost)

    attended, first, chosen, *leaving = attend(
        query, cached_key_rows, cached_value_rows, new_token_key, new_token_value, lengths,
        output_weight, request_adapter, placement, block, replicas, slot_down_weight.shape[0],
    )
    second = hop(0, 1, None, attended, output_weight, block)
    rows_here = exchange(leaving)
    mid, inside = down(rows_here, slot_down_weight, after=[second])
    travelling = [first, hold(second, after=[mid])]

    def added(a, b):
        return (a.astype(jnp.float32) + b.astype(jnp.float32)).astype(a.dtype)

    rank_sum = added(mid, lax.ppermute(mid, "tensor", [(i, i ^ 1) for i in range(count)]))
    rank_sums = [rank_sum] + pair_sums(rank_sum)
    next_hop(1, 0, after=[rank_sum, travelling[1]], cost=LONG)
    next_hop(1, 1, after=[travelling[0]], cost=MEDIUM)
    for step in range(2, count - 1):
        for chain in range(2):
            if (step, chain) == (2, 0):
                next_hop(step, chain, after=(), cost=LONG)
                deltas = up(rank_sums, inside, slot_up_weight, after=[travelling[0]])
                returned = exchange(deltas)
            else:
                next_hop(step, chain, after=[deltas[0]])
    settled = settle(
        count - 1, returned, chosen, attended, residual, output_weight, after=[travelling[1]]
    )
    out = None
    for chain in range(2):
        arrived = forward(travelling[chain])
        out = finish(chain, arrived, settled[chain], out, block)
    return out


def solution(mesh):
    placed = (
        P(("parts", "dp"), "tensor"),
        P(("parts", "dp"), "tensor", None),
        P(("parts", "dp"), None, "tensor", None),
        P(("parts", "dp"), None, "tensor", None),
        P(("parts", "dp"), "tensor", None),
        P(("parts", "dp"), "tensor", None),
        P(("parts", "dp")),
        P("tensor", None),
        P("dp", None, "tensor"),
        P("dp", None, "tensor"),
        P("parts"),
        P(("parts", "dp")),
    )
    return jax.shard_map(
        per_device,
        mesh=mesh,
        in_specs=placed,
        out_specs=P(("parts", "dp"), "tensor"),
        check_vma=False,
    )
```

```python
import functools
import math

import jax
import jax.numpy as jnp
from jax import lax
from jax.experimental import pallas as pl
from jax.experimental.pallas import tpu as pltpu
from jax.sharding import PartitionSpec as P

GROUP = 4
CAP = 64
LANES = 128
SPAN = 64
MASKED = -1e30
VMEM_LIMIT = 50 * 1024 * 1024
FULL_VMEM = 61 * 1024 * 1024
SHARES = ((5, 3),)
PIECE = 512
SPLIT = 4

VMEM = pl.BlockSpec(memory_space=pltpu.VMEM)
ANY = pl.BlockSpec(memory_space=pl.ANY)
LONG = pl.CostEstimate(flops=20 * 10**9, transcendentals=0, bytes_accessed=40 * 10**6)
MEDIUM = pl.CostEstimate(flops=4 * 10**9, transcendentals=0, bytes_accessed=8 * 10**6)
PARAMS = pltpu.CompilerParams(vmem_limit_bytes=VMEM_LIMIT)


def _dot(a, b, left=1, right=0):
    return lax.dot_general(
        a, b, (((left,), (right,)), ((), ())), preferred_element_type=jnp.float32
    )


def _iota(shape, axis):
    return lax.broadcasted_iota(jnp.int32, shape, axis)


def ring_order(count):
    return list(range(0, count, 2)) + list(range(1, count, 2))[::-1]


def column_owner(step):
    count = lax.axis_size("tensor")
    here = lax.axis_index("tensor")
    half = here // 2
    spot = jnp.where(here % 2 == 0, half, count - 1 - half)
    spot = lax.rem(spot - 1 - step + 2 * count, count)
    return jnp.where(2 * spot < count, 2 * spot, 2 * (count - spot) - 1)


def chain_columns(width):
    shares = next(s for s in SHARES if width % (sum(s) * LANES) == 0)
    unit = width // sum(shares)
    return [(sum(shares[:c]) * unit, shares[c] * unit) for c in range(len(shares))]


class Weights:
    def __init__(self, w_ref, held, sems, first, width):
        depth = w_ref.shape[0] // SPLIT
        first = pl.multiple_of(first, LANES)
        self.held = held
        self.copies = [
            pltpu.make_async_copy(
                w_ref.at[pl.ds(s * depth, depth), pl.ds(first, width)],
                held.at[pl.ds(s * depth, depth), :],
                sems.at[s],
            )
            for s in range(SPLIT)
        ]

    def start(self):
        for copy in self.copies:
            copy.start()

    def wait(self):
        for copy in self.copies:
            copy.wait()

    def products(self, a):
        width = self.held.shape[1]
        for at in range(0, width, PIECE):
            columns = pl.ds(at, min(PIECE, width - at))
            yield columns, _dot(a, self.held[:, columns])

    @staticmethod
    def scratch(depth, width):
        return [
            pltpu.VMEM((depth, width), jnp.bfloat16),
            pltpu.SemaphoreType.DMA((SPLIT,)),
        ]


def row_max(arrays):
    full = None
    tops = []
    for x in arrays:
        width = x.shape[1]
        if width % LANES:
            tops.append(jnp.max(x, axis=1, keepdims=True))
            continue
        for at in range(0, width, LANES):
            tile = x[:, at : at + LANES]
            full = tile if full is None else jnp.maximum(full, tile)
    if full is not None:
        tops.append(jnp.max(full, axis=1, keepdims=True))
    return functools.reduce(jnp.maximum, tops)


def attend_kernel(
    heads, kv, cache, steps, block, replicas, slots,
    len_hbm, adapter_hbm, placement_hbm, q_hbm, k_hbm, v_hbm, nk_hbm, nv_hbm, w_hbm,
    *refs,
):
    a_hbm, out_hbm, chosen_hbm, *sent_hbm = refs[: 3 + replicas]
    (
        a_ref, out_ref, chosen_ref, sent_ref, out_sems,
        len_ref, adapter_ref, placement_ref, q_ref, k_ref, v_ref, nk_ref, nv_ref,
        scores_ref, mixed_ref, fresh_bias_ref, sems, small_sems, w_held, w_sems,
    ) = refs[3 + replicas :]
    requests = len_ref.shape[1]
    width = q_hbm.shape[1]
    per = requests // steps
    groups = per // GROUP
    group_rows = GROUP * heads
    group_cols = GROUP * cache * kv
    per_kv = heads // kv
    scale = math.log2(math.e) / math.sqrt(width)

    def part(kind, step):
        source, target, count = (
            (q_hbm, q_ref, heads),
            (k_hbm, k_ref, cache * kv),
            (v_hbm, v_ref, cache * kv),
        )[kind]
        rows = pl.ds(step * per * count, per * count)
        return pltpu.make_async_copy(source.at[rows, :], target.at[rows, :], sems.at[kind, step])

    small = [
        pltpu.make_async_copy(source, target, small_sems.at[i])
        for i, (source, target) in enumerate(
            (
                (nk_hbm, nk_ref),
                (len_hbm, len_ref),
                (nv_hbm, nv_ref),
                (adapter_hbm, adapter_ref),
                (placement_hbm, placement_ref),
            )
        )
    ]
    leaving = []

    def leave(source, target):
        copy = pltpu.make_async_copy(source, target, out_sems.at[len(leaving)])
        copy.start()
        leaving.append(copy)

    def multiply(first, count):
        rows = pl.ds(first, count)
        for columns, product in weights.products(a_ref[rows, :]):
            out_ref[rows, columns] = product.astype(jnp.bfloat16)
        leave(out_ref.at[rows, :], out_hbm.at[rows, :])

    chunk = out_ref.shape[1]
    weights = Weights(w_hbm, w_held, w_sems, column_owner(0) * block, chunk)
    part(0, 0).start()
    part(1, 0).start()
    for copy in small[:2]:
        copy.start()
    part(0, 1).start()
    part(1, 1).start()
    part(2, 0).start()
    for copy in small[2:]:
        copy.start()
    part(2, 1).start()
    for step in range(2, steps):
        for kind in range(3):
            part(kind, step).start()
    weights.start()

    row = _iota((group_rows, group_cols), 0)
    col = _iota((group_rows, group_cols), 1)
    same = (row // heads == col // (cache * kv)) & ((row % heads) // per_kv == col % kv)
    own_bias = jnp.where(same, 0.0, MASKED)
    row = _iota(fresh_bias_ref.shape, 0)
    col = _iota(fresh_bias_ref.shape, 1)
    same = (row // heads == col // kv) & ((row % heads) // per_kv == col % kv)
    fresh_bias_ref[...] = jnp.where(same, 0.0, MASKED)
    fresh_cols = SPAN * kv
    span_rows = SPAN * heads
    span_groups = SPAN // GROUP
    ones = jnp.ones((max(group_cols, fresh_cols), LANES), jnp.bfloat16)

    def arrive(step):
        part(0, step).wait()
        part(1, step).wait()

    def scores(step):
        side = step % 2
        q_at = step * per * heads
        k_at = step * per * cache * kv
        for g in range(groups):
            scores_ref[side, pl.ds(g * group_rows, group_rows), pl.ds(0, group_cols)] = _dot(
                q_ref[pl.ds(q_at + g * group_rows, group_rows), :],
                k_ref[pl.ds(k_at + g * group_cols, group_cols), :],
                1,
                1,
            )
        for span in range(per // SPAN):
            rows = pl.ds(span * span_rows, span_rows)
            scores_ref[side, rows, pl.ds(group_cols, fresh_cols)] = _dot(
                q_ref[pl.ds(q_at + span * span_rows, span_rows), :],
                nk_ref[pl.ds(step * per * kv + span * fresh_cols, fresh_cols), :],
                1,
                1,
            )

    for copy in small[:2]:
        copy.wait()
    counts = len_ref[...].astype(jnp.float32)
    all_groups = requests // GROUP
    of_group = _iota((all_groups, requests), 1) // GROUP == _iota((all_groups, requests), 0)
    counts = jnp.where(of_group, counts, 0.0).astype(jnp.bfloat16)
    spread = _iota((requests, group_cols), 0) % GROUP == _iota((requests, group_cols), 1) // (cache * kv)
    counts = _dot(counts, spread.astype(jnp.bfloat16))
    position = (_iota((all_groups, group_cols), 1) // kv) % cache
    length_bias = jnp.where(position.astype(jnp.float32) < counts, 0.0, MASKED)

    arrive(0)
    scores(0)
    for step in range(steps):
        side = step % 2
        k_at = step * per * cache * kv
        f_at = step * per * kv
        part(2, step).wait()
        if step == 0:
            for copy in small[2:]:
                copy.wait()
        if step + 1 < steps:
            arrive(step + 1)
            scores(step + 1)
        if step == 0:
            plan_routes(slots, adapter_ref, placement_ref, chosen_ref, sent_ref)
        if step == steps - 1:
            weights.wait()
            multiply(0, requests - per)
        for span in range(per // SPAN):
            cached_weights = []
            fresh_weights = []
            mixed = []
            for g in range(span * span_groups, (span + 1) * span_groups):
                rows = pl.ds(g * group_rows, group_rows)
                bias = own_bias + length_bias[step * groups + g : step * groups + g + 1, :]
                cached = scores_ref[side, rows, pl.ds(0, group_cols)] + bias
                inner = pl.ds((g % span_groups) * group_rows, group_rows)
                new = scores_ref[side, rows, pl.ds(group_cols, fresh_cols)]
                new = new + fresh_bias_ref[inner, :]
                top = row_max([cached, new])
                cached = jnp.exp2((cached - top) * scale).astype(jnp.bfloat16)
                cached_weights.append(cached)
                fresh_weights.append(jnp.exp2((new - top) * scale).astype(jnp.bfloat16))
                mixed.append(_dot(cached, v_ref[pl.ds(k_at + g * group_cols, group_cols), :]))
            fresh = jnp.concatenate(fresh_weights, axis=0)
            values = nv_ref[pl.ds(f_at + span * fresh_cols, fresh_cols), :]
            mixed = jnp.concatenate(mixed, axis=0) + _dot(fresh, values)
            total = _dot(jnp.concatenate(cached_weights, axis=0), ones[:group_cols])
            total = total + _dot(fresh, ones[:fresh_cols])
            rows = pl.ds(span * span_rows, span_rows)
            inverse = pl.reciprocal(total, approx=True)
            mixed_ref[side, rows, :] = mixed * (inverse * (2.0 - total * inverse))
        for h in range(heads):
            a_ref[pl.ds(step * per, per), pl.ds(h * width, width)] = mixed_ref[
                side, pl.ds(h, per, stride=heads), :
            ].astype(jnp.bfloat16)
        rows = pl.ds(step * per, per)
        leave(a_ref.at[rows, :], a_hbm.at[rows, :])

    sent_ref[:, pl.ds(0, heads * width)] = _dot(chosen_ref[...], a_ref[...]).astype(jnp.bfloat16)
    leave(chosen_ref, chosen_hbm)
    for r in range(replicas):
        leave(sent_ref.at[pl.ds(r * CAP, CAP), :], sent_hbm[r])
    multiply(requests - per, per)
    for copy in leaving:
        copy.wait()


def plan_routes(slots, adapter_ref, placement_ref, chosen_ref, sent_ref):
    replicas = sent_ref.shape[0] // CAP
    requests = adapter_ref.shape[1]
    table = placement_ref.shape[1]
    matches = _iota((table, requests), 0) == adapter_ref[...]
    placed = jnp.broadcast_to(placement_ref[...].astype(jnp.float32), (8, table))
    slot = _dot(placed.astype(jnp.bfloat16), matches.astype(jnp.bfloat16)).astype(jnp.int32)
    slot = slot[0:1, :]
    holder = (slot // slots) ^ lax.axis_index("dp")
    inside = slot % slots
    of_holder = _iota((max(replicas, 8), requests), 0) == holder
    earlier = _iota((requests, requests), 0) < _iota((requests, requests), 1)
    before = _dot(of_holder.astype(jnp.bfloat16), earlier.astype(jnp.bfloat16))
    before = jnp.sum(jnp.where(of_holder, before, 0.0), axis=0, keepdims=True).astype(jnp.int32)
    target = holder * CAP + before
    here = _iota((replicas * CAP, requests), 0) == target
    chosen_ref[...] = here.astype(jnp.bfloat16)
    inner = jnp.sum(jnp.where(here, inside.astype(jnp.float32), 0.0), axis=1, keepdims=True)
    inner = jnp.broadcast_to(inner, (replicas * CAP, LANES)).astype(jnp.bfloat16)
    sent_ref[:, pl.ds(sent_ref.shape[1] - LANES, LANES)] = inner


def attend(
    query, keys, values, new_key, new_value, lengths, weight, request_adapter, placement,
    block, replicas, slots,
):
    requests, heads, width = query.shape
    cache, kv = keys.shape[1], keys.shape[2]
    steps = 2
    per = requests // steps
    columns = GROUP * cache * kv + SPAN * kv
    features = heads * width
    chunk = chain_columns(block)[0][1]
    small = [lengths.reshape(1, -1), request_adapter.reshape(1, -1), placement.reshape(1, -1)]
    operands = [
        query.reshape(requests * heads, width),
        keys.reshape(requests * cache * kv, width),
        values.reshape(requests * cache * kv, width),
        new_key.reshape(requests * kv, width),
        new_value.reshape(requests * kv, width),
    ]
    return pl.pallas_call(
        functools.partial(attend_kernel, heads, kv, cache, steps, block, replicas, slots),
        in_specs=[ANY] * 9,
        out_specs=[ANY] * (3 + replicas),
        out_shape=[
            jax.ShapeDtypeStruct((requests, features), jnp.bfloat16),
            jax.ShapeDtypeStruct((requests, chunk), jnp.bfloat16),
            jax.ShapeDtypeStruct((replicas * CAP, requests), jnp.bfloat16),
        ]
        + [jax.ShapeDtypeStruct((CAP, features + LANES), jnp.bfloat16)] * replicas,
        scratch_shapes=[
            pltpu.VMEM((requests, features), jnp.bfloat16),
            pltpu.VMEM((requests, chunk), jnp.bfloat16),
            pltpu.VMEM((replicas * CAP, requests), jnp.bfloat16),
            pltpu.VMEM((replicas * CAP, features + LANES), jnp.bfloat16),
            pltpu.SemaphoreType.DMA((1 + steps + 2 + replicas,)),
        ]
        + [pltpu.VMEM(x.shape, x.dtype) for x in small + operands]
        + [
            pltpu.VMEM((2, per * heads, columns), jnp.float32),
            pltpu.VMEM((2, per * heads, width), jnp.float32),
            pltpu.VMEM((SPAN * heads, SPAN * kv), jnp.float32),
            pltpu.SemaphoreType.DMA((3, steps)),
            pltpu.SemaphoreType.DMA((5,)),
        ]
        + Weights.scratch(weight.shape[0], chunk),
        compiler_params=pltpu.CompilerParams(vmem_limit_bytes=FULL_VMEM),
        name="attend",
    )(*small, *operands, weight)


def hop_kernel(step, block, start, arriving, after, *refs):
    if arriving:
        arrived_ref, *refs = refs
    a_ref, w_hbm, *refs = refs
    out_ref, held, sems = refs[after:]
    chunk = out_ref.shape[1]
    first = column_owner(step) * block + start
    weights = Weights(w_hbm, held, sems, first, chunk)
    weights.start()
    weights.wait()
    for columns, product in weights.products(a_ref[...]):
        if arriving:
            product = product + arrived_ref[:, columns].astype(jnp.float32)
        out_ref[:, columns] = product.astype(jnp.bfloat16)


def hop(step, chain, arrived, attended, weight, block, after=(), cost=None):
    arriving = arrived is not None
    start, chunk = chain_columns(block)[chain]
    operands = ([arrived] if arriving else []) + [attended, weight, *after]
    return pl.pallas_call(
        functools.partial(hop_kernel, step, block, start, arriving, len(after)),
        in_specs=[VMEM] * (1 + arriving) + [ANY] + [ANY] * len(after),
        out_specs=VMEM,
        out_shape=jax.ShapeDtypeStruct((attended.shape[0], chunk), jnp.bfloat16),
        scratch_shapes=Weights.scratch(weight.shape[0], chunk),
        compiler_params=PARAMS,
        cost_estimate=cost,
        name="hop",
    )(*operands)


def down_kernel(replicas, after, *refs):
    received = refs[:replicas]
    down_ref = refs[replicas]
    mid_ref, inside_ref = refs[replicas + 1 + after :]
    slots, rank, width = down_ref.shape
    rows = jnp.concatenate([r[:, pl.ds(0, width)] for r in received], axis=0)
    inside = jnp.concatenate([r[:, pl.ds(width, LANES)] for r in received], axis=0)
    inside_ref[...] = inside
    projected = _dot(rows, down_ref[...].reshape(slots * rank, width), 1, 1)
    lane_slot = _iota(projected.shape, 1) // rank
    mine = lane_slot == inside[:, 0:1].astype(jnp.int32)
    projected = jnp.where(mine, projected, 0.0).astype(jnp.bfloat16)
    beside = LANES // rank
    some = projected.shape[0] // beside
    packed = 0.0
    for b in range(beside):
        lane = _iota((slots * rank, LANES), 1) - b * rank
        fold = _iota((slots * rank, LANES), 0) % rank == lane
        packed = packed + _dot(projected[b * some : (b + 1) * some, :], fold.astype(jnp.bfloat16))
    mid_ref[...] = packed.astype(jnp.bfloat16)


def down(received, slot_down_weight, after=()):
    replicas = len(received)
    rows = replicas * CAP
    return pl.pallas_call(
        functools.partial(down_kernel, replicas, len(after)),
        in_specs=[VMEM] * (replicas + 1) + [ANY] * len(after),
        out_specs=[VMEM, VMEM],
        out_shape=[
            jax.ShapeDtypeStruct((rows * slot_down_weight.shape[1] // LANES, LANES), jnp.bfloat16),
            jax.ShapeDtypeStruct((rows, LANES), jnp.bfloat16),
        ],
        compiler_params=PARAMS,
        name="down",
    )(*received, slot_down_weight, *after)


def up_kernel(parts, after, *refs):
    mids = refs[:parts]
    inside_ref, up_ref = refs[parts : parts + 2]
    out_refs = refs[parts + 2 + after :]
    slots, rank, width = up_ref.shape
    mid = mids[0][...].astype(jnp.float32)
    for m in mids[1:]:
        mid = mid + m[...].astype(jnp.float32)
    mid = mid.astype(jnp.bfloat16)
    wide = []
    for b in range(LANES // rank):
        lane = _iota((LANES, slots * rank), 0) - b * rank
        spread = _iota((LANES, slots * rank), 1) % rank == lane
        wide.append(_dot(mid, spread.astype(jnp.bfloat16)))
    wide = jnp.concatenate(wide, axis=0)
    mine = _iota(wide.shape, 1) // rank == inside_ref[:, 0:1].astype(jnp.int32)
    wide = jnp.where(mine, wide, 0.0).astype(jnp.bfloat16)
    delta = _dot(wide, up_ref[...].reshape(slots * rank, width)).astype(jnp.bfloat16)
    for r, out_ref in enumerate(out_refs):
        out_ref[...] = delta[r * CAP : (r + 1) * CAP, :]


def up(mids, inside, slot_up_weight, after=()):
    rows = inside.shape[0]
    replicas = rows // CAP
    width = slot_up_weight.shape[2]
    return pl.pallas_call(
        functools.partial(up_kernel, len(mids), len(after)),
        in_specs=[VMEM] * (len(mids) + 2) + [ANY] * len(after),
        out_specs=[VMEM] * replicas,
        out_shape=[jax.ShapeDtypeStruct((CAP, width), jnp.bfloat16)] * replicas,
        compiler_params=PARAMS,
        name="up",
    )(*mids, inside, slot_up_weight, *after)


def settle_kernel(step, replicas, after, *refs):
    returned = refs[:replicas]
    chosen_ref, a_ref, residual_ref, w_hbm = refs[replicas : replicas + 4]
    *out_refs, held, sems = refs[replicas + 4 + after :]
    width = residual_ref.shape[1]
    weights = Weights(w_hbm, held, sems, column_owner(step) * width, width)
    weights.start()
    rows = jnp.concatenate([r[...] for r in returned], axis=0)
    delta = _dot(chosen_ref[...], rows, 0, 0)
    total = residual_ref[...].astype(jnp.float32) + delta
    weights.wait()
    total = total + jnp.concatenate([p for _, p in weights.products(a_ref[...])], axis=1)
    for (start, chunk), out_ref in zip(chain_columns(width), out_refs):
        out_ref[...] = total[:, start : start + chunk]


def settle(step, returned, chosen, attended, residual, weight, after=()):
    replicas = len(returned)
    rows, width = residual.shape
    chains = chain_columns(width)
    return pl.pallas_call(
        functools.partial(settle_kernel, step, replicas, len(after)),
        in_specs=[VMEM] * (replicas + 3) + [ANY] * (1 + len(after)),
        out_specs=[VMEM] * len(chains),
        out_shape=[jax.ShapeDtypeStruct((rows, chunk), jnp.float32) for _, chunk in chains],
        scratch_shapes=Weights.scratch(weight.shape[0], width),
        compiler_params=PARAMS,
        cost_estimate=MEDIUM,
        name="settle",
    )(*returned, chosen, attended, residual, weight, *after)


def finish_kernel(start, arrived_ref, settled_ref, *refs):
    out_hbm, held, sems = refs[-3:]
    rows, chunk = arrived_ref.shape
    half = rows // 2
    copies = []
    for i in range(2):
        part = pl.ds(i * half, half)
        total = settled_ref[part, :] + arrived_ref[part, :].astype(jnp.float32)
        held[part, :] = total.astype(jnp.bfloat16)
        target = out_hbm.at[part, pl.ds(start, chunk)]
        copies.append(pltpu.make_async_copy(held.at[part, :], target, sems.at[i]))
        copies[-1].start()
    for copy in copies:
        copy.wait()


def finish(chain, arrived, settled, earlier, width):
    rows = arrived.shape[0]
    start, chunk = chain_columns(width)[chain]
    operands = [arrived, settled] + ([earlier] if earlier is not None else [])
    return pl.pallas_call(
        functools.partial(finish_kernel, start),
        in_specs=[VMEM, VMEM] + ([ANY] if earlier is not None else []),
        out_specs=ANY,
        out_shape=jax.ShapeDtypeStruct((rows, width), jnp.bfloat16),
        input_output_aliases={2: 0} if earlier is not None else {},
        scratch_shapes=[
            pltpu.VMEM((rows, chunk), jnp.bfloat16),
            pltpu.SemaphoreType.DMA((2,)),
        ],
        compiler_params=PARAMS,
        name="finish",
    )(*operands)


def hold_kernel(*refs):
    pass


def hold(x, after):
    return pl.pallas_call(
        hold_kernel,
        in_specs=[ANY] * (1 + len(after)),
        out_specs=ANY,
        out_shape=jax.ShapeDtypeStruct(x.shape, x.dtype),
        input_output_aliases={0: 0},
        compiler_params=PARAMS,
        name="hold",
    )(x, *after)


def per_device(
    residual,
    query,
    cached_key_rows,
    cached_value_rows,
    new_token_key,
    new_token_value,
    lengths,
    output_weight,
    slot_down_weight,
    slot_up_weight,
    placement,
    request_adapter,
):
    count = lax.axis_size("tensor")
    replicas = lax.axis_size("dp")
    block = residual.shape[1]
    order = ring_order(count)
    ring = [(order[p], order[(p + 1) % count]) for p in range(count)]

    def exchange(blocks):
        moved = [
            lax.ppermute(blocks[r], "dp", [(i, i ^ r) for i in range(replicas)])
            for r in range(1, replicas)
        ]
        return [blocks[0]] + moved

    def forward(x):
        return lax.ppermute(x, "tensor", ring)

    def pair_sums(x):
        found = []
        for away in range(1, count // 2):
            pairs = [(p, (p + away) % (count // 2)) for p in range(count // 2)]
            near, far = [], []
            for p, q in pairs:
                sender = 2 * p if p < q else 2 * p + 1
                straight = 2 * q + (sender % 2)
                near.append((sender, straight))
                far.append((sender, straight ^ 1))
            one = lax.ppermute(x, "tensor", near)
            other = lax.ppermute(x, "tensor", far)
            found += [one, other]
        return found

    def next_hop(step, chain, after, cost=None):
        arrived = forward(travelling[chain])
        travelling[chain] = hop(step, chain, arrived, attended, output_weight, block, after, cost)

    attended, first, chosen, *leaving = attend(
        query, cached_key_rows, cached_value_rows, new_token_key, new_token_value, lengths,
        output_weight, request_adapter, placement, block, replicas, slot_down_weight.shape[0],
    )
    second = hop(0, 1, None, attended, output_weight, block)
    rows_here = exchange(leaving)
    mid, inside = down(rows_here, slot_down_weight, after=[second])
    travelling = [first, hold(second, after=[mid])]

    def added(a, b):
        return (a.astype(jnp.float32) + b.astype(jnp.float32)).astype(a.dtype)

    rank_sum = added(mid, lax.ppermute(mid, "tensor", [(i, i ^ 1) for i in range(count)]))
    rank_sums = [rank_sum] + pair_sums(rank_sum)
    next_hop(1, 0, after=[rank_sum, travelling[1]], cost=LONG)
    next_hop(1, 1, after=[travelling[0]], cost=MEDIUM)
    for step in range(2, count - 1):
        for chain in range(2):
            if (step, chain) == (2, 0):
                next_hop(step, chain, after=(), cost=LONG)
                deltas = up(rank_sums, inside, slot_up_weight, after=[travelling[0]])
                returned = exchange(deltas)
            else:
                next_hop(step, chain, after=[deltas[0]])
    settled = settle(
        count - 1, returned, chosen, attended, residual, output_weight, after=[travelling[1]]
    )
    out = None
    for chain in range(2):
        arrived = forward(travelling[chain])
        out = finish(chain, arrived, settled[chain], out, block)
    return out


def solution(mesh):
    placed = (
        P(("parts", "dp"), "tensor"),
        P(("parts", "dp"), "tensor", None),
        P(("parts", "dp"), None, "tensor", None),
        P(("parts", "dp"), None, "tensor", None),
        P(("parts", "dp"), "tensor", None),
        P(("parts", "dp"), "tensor", None),
        P(("parts", "dp")),
        P("tensor", None),
        P("dp", None, "tensor"),
        P("dp", None, "tensor"),
        P("parts"),
        P(("parts", "dp")),
    )
    return jax.shard_map(
        per_device,
        mesh=mesh,
        in_specs=placed,
        out_specs=P(("parts", "dp"), "tensor"),
        check_vma=False,
    )
```

```python
import functools
import math

import jax
import jax.numpy as jnp
from jax import lax
from jax.experimental import pallas as pl
from jax.experimental.pallas import tpu as pltpu
from jax.sharding import PartitionSpec as P

GROUP = 4
CAP = 64
LANES = 128
SPAN = 64
MASKED = -1e30
VMEM_LIMIT = 50 * 1024 * 1024
FULL_VMEM = 61 * 1024 * 1024
SHARES = ((5, 3),)
PIECE = 512
SPLIT = 4

VMEM = pl.BlockSpec(memory_space=pltpu.VMEM)
ANY = pl.BlockSpec(memory_space=pl.ANY)
LONG = pl.CostEstimate(flops=20 * 10**9, transcendentals=0, bytes_accessed=40 * 10**6)
MEDIUM = pl.CostEstimate(flops=4 * 10**9, transcendentals=0, bytes_accessed=8 * 10**6)
PARAMS = pltpu.CompilerParams(vmem_limit_bytes=VMEM_LIMIT)


def _dot(a, b, left=1, right=0):
    return lax.dot_general(
        a, b, (((left,), (right,)), ((), ())), preferred_element_type=jnp.float32
    )


def _iota(shape, axis):
    return lax.broadcasted_iota(jnp.int32, shape, axis)


def ring_order(count):
    return list(range(0, count, 2)) + list(range(1, count, 2))[::-1]


def column_owner(step):
    count = lax.axis_size("tensor")
    here = lax.axis_index("tensor")
    half = here // 2
    spot = jnp.where(here % 2 == 0, half, count - 1 - half)
    spot = lax.rem(spot - 1 - step + 2 * count, count)
    return jnp.where(2 * spot < count, 2 * spot, 2 * (count - spot) - 1)


def chain_columns(width):
    shares = next(s for s in SHARES if width % (sum(s) * LANES) == 0)
    unit = width // sum(shares)
    return [(sum(shares[:c]) * unit, shares[c] * unit) for c in range(len(shares))]


class Weights:
    def __init__(self, w_ref, held, sems, first, width):
        depth = w_ref.shape[0] // SPLIT
        first = pl.multiple_of(first, LANES)
        self.held = held
        self.copies = [
            pltpu.make_async_copy(
                w_ref.at[pl.ds(s * depth, depth), pl.ds(first, width)],
                held.at[pl.ds(s * depth, depth), :],
                sems.at[s],
            )
            for s in range(SPLIT)
        ]

    def start(self):
        for copy in self.copies:
            copy.start()

    def wait(self):
        for copy in self.copies:
            copy.wait()

    def products(self, a):
        width = self.held.shape[1]
        for at in range(0, width, PIECE):
            columns = pl.ds(at, min(PIECE, width - at))
            yield columns, _dot(a, self.held[:, columns])

    @staticmethod
    def scratch(depth, width):
        return [
            pltpu.VMEM((depth, width), jnp.bfloat16),
            pltpu.SemaphoreType.DMA((SPLIT,)),
        ]


def row_max(arrays):
    full = None
    tops = []
    for x in arrays:
        width = x.shape[1]
        if width % LANES:
            tops.append(jnp.max(x, axis=1, keepdims=True))
            continue
        for at in range(0, width, LANES):
            tile = x[:, at : at + LANES]
            full = tile if full is None else jnp.maximum(full, tile)
    if full is not None:
        tops.append(jnp.max(full, axis=1, keepdims=True))
    return functools.reduce(jnp.maximum, tops)


def attend_kernel(
    heads, kv, cache, steps, block, replicas, slots,
    len_hbm, adapter_hbm, placement_hbm, q_hbm, k_hbm, v_hbm, nk_hbm, nv_hbm, w_hbm,
    *refs,
):
    a_hbm, out_hbm, chosen_hbm, *sent_hbm = refs[: 3 + replicas]
    (
        a_ref, out_ref, chosen_ref, sent_ref, out_sems,
        len_ref, adapter_ref, placement_ref, q_ref, k_ref, v_ref, nk_ref, nv_ref,
        scores_ref, mixed_ref, fresh_bias_ref, sems, small_sems, w_held, w_sems,
    ) = refs[3 + replicas :]
    requests = len_ref.shape[1]
    width = q_hbm.shape[1]
    per = requests // steps
    groups = per // GROUP
    group_rows = GROUP * heads
    group_cols = GROUP * cache * kv
    per_kv = heads // kv
    scale = math.log2(math.e) / math.sqrt(width)

    def part(kind, step):
        source, target, count = (
            (q_hbm, q_ref, heads),
            (k_hbm, k_ref, cache * kv),
            (v_hbm, v_ref, cache * kv),
        )[kind]
        rows = pl.ds(step * per * count, per * count)
        return pltpu.make_async_copy(source.at[rows, :], target.at[rows, :], sems.at[kind, step])

    small = [
        pltpu.make_async_copy(source, target, small_sems.at[i])
        for i, (source, target) in enumerate(
            (
                (nk_hbm, nk_ref),
                (len_hbm, len_ref),
                (nv_hbm, nv_ref),
                (adapter_hbm, adapter_ref),
                (placement_hbm, placement_ref),
            )
        )
    ]
    leaving = []

    def leave(source, target):
        copy = pltpu.make_async_copy(source, target, out_sems.at[len(leaving)])
        copy.start()
        leaving.append(copy)

    def multiply(first, count):
        rows = pl.ds(first, count)
        for columns, product in weights.products(a_ref[rows, :]):
            out_ref[rows, columns] = product.astype(jnp.bfloat16)
        leave(out_ref.at[rows, :], out_hbm.at[rows, :])

    chunk = out_ref.shape[1]
    weights = Weights(w_hbm, w_held, w_sems, column_owner(0) * block, chunk)
    part(0, 0).start()
    part(1, 0).start()
    for copy in small[:2]:
        copy.start()
    part(0, 1).start()
    part(1, 1).start()
    part(2, 0).start()
    for copy in small[2:]:
        copy.start()
    part(2, 1).start()
    for step in range(2, steps):
        for kind in range(3):
            part(kind, step).start()
    weights.start()

    row = _iota((group_rows, group_cols), 0)
    col = _iota((group_rows, group_cols), 1)
    same = (row // heads == col // (cache * kv)) & ((row % heads) // per_kv == col % kv)
    own_bias = jnp.where(same, 0.0, MASKED)
    row = _iota(fresh_bias_ref.shape, 0)
    col = _iota(fresh_bias_ref.shape, 1)
    same = (row // heads == col // kv) & ((row % heads) // per_kv == col % kv)
    fresh_bias_ref[...] = jnp.where(same, 0.0, MASKED)
    fresh_cols = SPAN * kv
    span_rows = SPAN * heads
    span_groups = SPAN // GROUP
    ones = jnp.ones((max(group_cols, fresh_cols), LANES), jnp.bfloat16)

    def arrive(step):
        part(0, step).wait()
        part(1, step).wait()

    def scores(step):
        side = step % 2
        q_at = step * per * heads
        k_at = step * per * cache * kv
        for g in range(groups):
            scores_ref[side, pl.ds(g * group_rows, group_rows), pl.ds(0, group_cols)] = _dot(
                q_ref[pl.ds(q_at + g * group_rows, group_rows), :],
                k_ref[pl.ds(k_at + g * group_cols, group_cols), :],
                1,
                1,
            )
        for span in range(per // SPAN):
            rows = pl.ds(span * span_rows, span_rows)
            scores_ref[side, rows, pl.ds(group_cols, fresh_cols)] = _dot(
                q_ref[pl.ds(q_at + span * span_rows, span_rows), :],
                nk_ref[pl.ds(step * per * kv + span * fresh_cols, fresh_cols), :],
                1,
                1,
            )

    for copy in small[:2]:
        copy.wait()
    counts = len_ref[...].astype(jnp.float32)
    all_groups = requests // GROUP
    of_group = _iota((all_groups, requests), 1) // GROUP == _iota((all_groups, requests), 0)
    counts = jnp.where(of_group, counts, 0.0).astype(jnp.bfloat16)
    spread = _iota((requests, group_cols), 0) % GROUP == _iota((requests, group_cols), 1) // (cache * kv)
    counts = _dot(counts, spread.astype(jnp.bfloat16))
    position = (_iota((all_groups, group_cols), 1) // kv) % cache
    length_bias = jnp.where(position.astype(jnp.float32) < counts, 0.0, MASKED)

    def soften(step):
        side = step % 2
        cached_weights = []
        fresh_weights = []
        for g in range(groups):
            rows = pl.ds(g * group_rows, group_rows)
            bias = own_bias + length_bias[step * groups + g : step * groups + g + 1, :]
            cached = scores_ref[side, rows, pl.ds(0, group_cols)] + bias
            inner = pl.ds((g % span_groups) * group_rows, group_rows)
            new = scores_ref[side, rows, pl.ds(group_cols, fresh_cols)]
            new = new + fresh_bias_ref[inner, :]
            top = row_max([cached, new])
            cached_weights.append(jnp.exp2((cached - top) * scale).astype(jnp.bfloat16))
            fresh_weights.append(jnp.exp2((new - top) * scale).astype(jnp.bfloat16))
        return cached_weights, fresh_weights

    def mix(step, cached_weights, fresh_weights):
        side = step % 2
        k_at = step * per * cache * kv
        f_at = step * per * kv
        for span in range(per // SPAN):
            inside = range(span * span_groups, (span + 1) * span_groups)
            mixed = [
                _dot(cached_weights[g], v_ref[pl.ds(k_at + g * group_cols, group_cols), :])
                for g in inside
            ]
            fresh = jnp.concatenate([fresh_weights[g] for g in inside], axis=0)
            values = nv_ref[pl.ds(f_at + span * fresh_cols, fresh_cols), :]
            mixed = jnp.concatenate(mixed, axis=0) + _dot(fresh, values)
            cached = jnp.concatenate([cached_weights[g] for g in inside], axis=0)
            total = _dot(cached, ones[:group_cols]) + _dot(fresh, ones[:fresh_cols])
            rows = pl.ds(span * span_rows, span_rows)
            inverse = pl.reciprocal(total, approx=True)
            mixed_ref[side, rows, :] = mixed * (inverse * (2.0 - total * inverse))
        for h in range(heads):
            a_ref[pl.ds(step * per, per), pl.ds(h * width, width)] = mixed_ref[
                side, pl.ds(h, per, stride=heads), :
            ].astype(jnp.bfloat16)

    arrive(0)
    scores(0)
    softened = soften(0)
    for step in range(steps):
        part(2, step).wait()
        if step == 0:
            for copy in small[2:]:
                copy.wait()
        if step + 1 < steps:
            arrive(step + 1)
            scores(step + 1)
        if step == 0:
            plan_routes(slots, adapter_ref, placement_ref, chosen_ref, sent_ref)
        if step == steps - 1:
            weights.wait()
            multiply(0, requests - per)
        mix(step, *softened)
        if step + 1 < steps:
            softened = soften(step + 1)
        rows = pl.ds(step * per, per)
        leave(a_ref.at[rows, :], a_hbm.at[rows, :])

    sent_ref[:, pl.ds(0, heads * width)] = _dot(chosen_ref[...], a_ref[...]).astype(jnp.bfloat16)
    leave(chosen_ref, chosen_hbm)
    for r in range(replicas):
        leave(sent_ref.at[pl.ds(r * CAP, CAP), :], sent_hbm[r])
    multiply(requests - per, per)
    for copy in leaving:
        copy.wait()


def plan_routes(slots, adapter_ref, placement_ref, chosen_ref, sent_ref):
    replicas = sent_ref.shape[0] // CAP
    requests = adapter_ref.shape[1]
    table = placement_ref.shape[1]
    matches = _iota((table, requests), 0) == adapter_ref[...]
    placed = jnp.broadcast_to(placement_ref[...].astype(jnp.float32), (8, table))
    slot = _dot(placed.astype(jnp.bfloat16), matches.astype(jnp.bfloat16)).astype(jnp.int32)
    slot = slot[0:1, :]
    holder = (slot // slots) ^ lax.axis_index("dp")
    inside = slot % slots
    of_holder = _iota((max(replicas, 8), requests), 0) == holder
    earlier = _iota((requests, requests), 0) < _iota((requests, requests), 1)
    before = _dot(of_holder.astype(jnp.bfloat16), earlier.astype(jnp.bfloat16))
    before = jnp.sum(jnp.where(of_holder, before, 0.0), axis=0, keepdims=True).astype(jnp.int32)
    target = holder * CAP + before
    here = _iota((replicas * CAP, requests), 0) == target
    chosen_ref[...] = here.astype(jnp.bfloat16)
    inner = jnp.sum(jnp.where(here, inside.astype(jnp.float32), 0.0), axis=1, keepdims=True)
    inner = jnp.broadcast_to(inner, (replicas * CAP, LANES)).astype(jnp.bfloat16)
    sent_ref[:, pl.ds(sent_ref.shape[1] - LANES, LANES)] = inner


def attend(
    query, keys, values, new_key, new_value, lengths, weight, request_adapter, placement,
    block, replicas, slots,
):
    requests, heads, width = query.shape
    cache, kv = keys.shape[1], keys.shape[2]
    steps = 2
    per = requests // steps
    columns = GROUP * cache * kv + SPAN * kv
    features = heads * width
    chunk = chain_columns(block)[0][1]
    small = [lengths.reshape(1, -1), request_adapter.reshape(1, -1), placement.reshape(1, -1)]
    operands = [
        query.reshape(requests * heads, width),
        keys.reshape(requests * cache * kv, width),
        values.reshape(requests * cache * kv, width),
        new_key.reshape(requests * kv, width),
        new_value.reshape(requests * kv, width),
    ]
    return pl.pallas_call(
        functools.partial(attend_kernel, heads, kv, cache, steps, block, replicas, slots),
        in_specs=[ANY] * 9,
        out_specs=[ANY] * (3 + replicas),
        out_shape=[
            jax.ShapeDtypeStruct((requests, features), jnp.bfloat16),
            jax.ShapeDtypeStruct((requests, chunk), jnp.bfloat16),
            jax.ShapeDtypeStruct((replicas * CAP, requests), jnp.bfloat16),
        ]
        + [jax.ShapeDtypeStruct((CAP, features + LANES), jnp.bfloat16)] * replicas,
        scratch_shapes=[
            pltpu.VMEM((requests, features), jnp.bfloat16),
            pltpu.VMEM((requests, chunk), jnp.bfloat16),
            pltpu.VMEM((replicas * CAP, requests), jnp.bfloat16),
            pltpu.VMEM((replicas * CAP, features + LANES), jnp.bfloat16),
            pltpu.SemaphoreType.DMA((1 + steps + 2 + replicas,)),
        ]
        + [pltpu.VMEM(x.shape, x.dtype) for x in small + operands]
        + [
            pltpu.VMEM((2, per * heads, columns), jnp.float32),
            pltpu.VMEM((2, per * heads, width), jnp.float32),
            pltpu.VMEM((SPAN * heads, SPAN * kv), jnp.float32),
            pltpu.SemaphoreType.DMA((3, steps)),
            pltpu.SemaphoreType.DMA((5,)),
        ]
        + Weights.scratch(weight.shape[0], chunk),
        compiler_params=pltpu.CompilerParams(vmem_limit_bytes=FULL_VMEM),
        name="attend",
    )(*small, *operands, weight)


def hop_kernel(step, block, start, arriving, after, *refs):
    if arriving:
        arrived_ref, *refs = refs
    a_ref, w_hbm, *refs = refs
    out_ref, held, sems = refs[after:]
    chunk = out_ref.shape[1]
    first = column_owner(step) * block + start
    weights = Weights(w_hbm, held, sems, first, chunk)
    weights.start()
    weights.wait()
    for columns, product in weights.products(a_ref[...]):
        if arriving:
            product = product + arrived_ref[:, columns].astype(jnp.float32)
        out_ref[:, columns] = product.astype(jnp.bfloat16)


def hop(step, chain, arrived, attended, weight, block, after=(), cost=None):
    arriving = arrived is not None
    start, chunk = chain_columns(block)[chain]
    operands = ([arrived] if arriving else []) + [attended, weight, *after]
    return pl.pallas_call(
        functools.partial(hop_kernel, step, block, start, arriving, len(after)),
        in_specs=[VMEM] * (1 + arriving) + [ANY] + [ANY] * len(after),
        out_specs=VMEM,
        out_shape=jax.ShapeDtypeStruct((attended.shape[0], chunk), jnp.bfloat16),
        scratch_shapes=Weights.scratch(weight.shape[0], chunk),
        compiler_params=PARAMS,
        cost_estimate=cost,
        name="hop",
    )(*operands)


def down_kernel(replicas, after, *refs):
    received = refs[:replicas]
    down_ref = refs[replicas]
    mid_ref, inside_ref = refs[replicas + 1 + after :]
    slots, rank, width = down_ref.shape
    rows = jnp.concatenate([r[:, pl.ds(0, width)] for r in received], axis=0)
    inside = jnp.concatenate([r[:, pl.ds(width, LANES)] for r in received], axis=0)
    inside_ref[...] = inside
    projected = _dot(rows, down_ref[...].reshape(slots * rank, width), 1, 1)
    lane_slot = _iota(projected.shape, 1) // rank
    mine = lane_slot == inside[:, 0:1].astype(jnp.int32)
    projected = jnp.where(mine, projected, 0.0).astype(jnp.bfloat16)
    beside = LANES // rank
    some = projected.shape[0] // beside
    packed = 0.0
    for b in range(beside):
        lane = _iota((slots * rank, LANES), 1) - b * rank
        fold = _iota((slots * rank, LANES), 0) % rank == lane
        packed = packed + _dot(projected[b * some : (b + 1) * some, :], fold.astype(jnp.bfloat16))
    mid_ref[...] = packed.astype(jnp.bfloat16)


def down(received, slot_down_weight, after=()):
    replicas = len(received)
    rows = replicas * CAP
    return pl.pallas_call(
        functools.partial(down_kernel, replicas, len(after)),
        in_specs=[VMEM] * (replicas + 1) + [ANY] * len(after),
        out_specs=[VMEM, VMEM],
        out_shape=[
            jax.ShapeDtypeStruct((rows * slot_down_weight.shape[1] // LANES, LANES), jnp.bfloat16),
            jax.ShapeDtypeStruct((rows, LANES), jnp.bfloat16),
        ],
        compiler_params=PARAMS,
        name="down",
    )(*received, slot_down_weight, *after)


def up_kernel(parts, after, *refs):
    mids = refs[:parts]
    inside_ref, up_ref = refs[parts : parts + 2]
    out_refs = refs[parts + 2 + after :]
    slots, rank, width = up_ref.shape
    mid = mids[0][...].astype(jnp.float32)
    for m in mids[1:]:
        mid = mid + m[...].astype(jnp.float32)
    mid = mid.astype(jnp.bfloat16)
    wide = []
    for b in range(LANES // rank):
        lane = _iota((LANES, slots * rank), 0) - b * rank
        spread = _iota((LANES, slots * rank), 1) % rank == lane
        wide.append(_dot(mid, spread.astype(jnp.bfloat16)))
    wide = jnp.concatenate(wide, axis=0)
    mine = _iota(wide.shape, 1) // rank == inside_ref[:, 0:1].astype(jnp.int32)
    wide = jnp.where(mine, wide, 0.0).astype(jnp.bfloat16)
    delta = _dot(wide, up_ref[...].reshape(slots * rank, width)).astype(jnp.bfloat16)
    for r, out_ref in enumerate(out_refs):
        out_ref[...] = delta[r * CAP : (r + 1) * CAP, :]


def up(mids, inside, slot_up_weight, after=()):
    rows = inside.shape[0]
    replicas = rows // CAP
    width = slot_up_weight.shape[2]
    return pl.pallas_call(
        functools.partial(up_kernel, len(mids), len(after)),
        in_specs=[VMEM] * (len(mids) + 2) + [ANY] * len(after),
        out_specs=[VMEM] * replicas,
        out_shape=[jax.ShapeDtypeStruct((CAP, width), jnp.bfloat16)] * replicas,
        compiler_params=PARAMS,
        name="up",
    )(*mids, inside, slot_up_weight, *after)


def settle_kernel(step, replicas, after, *refs):
    returned = refs[:replicas]
    chosen_ref, a_ref, residual_ref, w_hbm = refs[replicas : replicas + 4]
    *out_refs, held, sems = refs[replicas + 4 + after :]
    width = residual_ref.shape[1]
    weights = Weights(w_hbm, held, sems, column_owner(step) * width, width)
    weights.start()
    rows = jnp.concatenate([r[...] for r in returned], axis=0)
    delta = _dot(chosen_ref[...], rows, 0, 0)
    total = residual_ref[...].astype(jnp.float32) + delta
    weights.wait()
    total = total + jnp.concatenate([p for _, p in weights.products(a_ref[...])], axis=1)
    for (start, chunk), out_ref in zip(chain_columns(width), out_refs):
        out_ref[...] = total[:, start : start + chunk]


def settle(step, returned, chosen, attended, residual, weight, after=()):
    replicas = len(returned)
    rows, width = residual.shape
    chains = chain_columns(width)
    return pl.pallas_call(
        functools.partial(settle_kernel, step, replicas, len(after)),
        in_specs=[VMEM] * (replicas + 3) + [ANY] * (1 + len(after)),
        out_specs=[VMEM] * len(chains),
        out_shape=[jax.ShapeDtypeStruct((rows, chunk), jnp.float32) for _, chunk in chains],
        scratch_shapes=Weights.scratch(weight.shape[0], width),
        compiler_params=PARAMS,
        cost_estimate=MEDIUM,
        name="settle",
    )(*returned, chosen, attended, residual, weight, *after)


def finish_kernel(start, arrived_ref, settled_ref, *refs):
    out_hbm, held, sems = refs[-3:]
    rows, chunk = arrived_ref.shape
    half = rows // 2
    copies = []
    for i in range(2):
        part = pl.ds(i * half, half)
        total = settled_ref[part, :] + arrived_ref[part, :].astype(jnp.float32)
        held[part, :] = total.astype(jnp.bfloat16)
        target = out_hbm.at[part, pl.ds(start, chunk)]
        copies.append(pltpu.make_async_copy(held.at[part, :], target, sems.at[i]))
        copies[-1].start()
    for copy in copies:
        copy.wait()


def finish(chain, arrived, settled, earlier, width):
    rows = arrived.shape[0]
    start, chunk = chain_columns(width)[chain]
    operands = [arrived, settled] + ([earlier] if earlier is not None else [])
    return pl.pallas_call(
        functools.partial(finish_kernel, start),
        in_specs=[VMEM, VMEM] + ([ANY] if earlier is not None else []),
        out_specs=ANY,
        out_shape=jax.ShapeDtypeStruct((rows, width), jnp.bfloat16),
        input_output_aliases={2: 0} if earlier is not None else {},
        scratch_shapes=[
            pltpu.VMEM((rows, chunk), jnp.bfloat16),
            pltpu.SemaphoreType.DMA((2,)),
        ],
        compiler_params=PARAMS,
        name="finish",
    )(*operands)


def hold_kernel(*refs):
    pass


def hold(x, after):
    return pl.pallas_call(
        hold_kernel,
        in_specs=[ANY] * (1 + len(after)),
        out_specs=ANY,
        out_shape=jax.ShapeDtypeStruct(x.shape, x.dtype),
        input_output_aliases={0: 0},
        compiler_params=PARAMS,
        name="hold",
    )(x, *after)


def per_device(
    residual,
    query,
    cached_key_rows,
    cached_value_rows,
    new_token_key,
    new_token_value,
    lengths,
    output_weight,
    slot_down_weight,
    slot_up_weight,
    placement,
    request_adapter,
):
    count = lax.axis_size("tensor")
    replicas = lax.axis_size("dp")
    block = residual.shape[1]
    order = ring_order(count)
    ring = [(order[p], order[(p + 1) % count]) for p in range(count)]

    def exchange(blocks):
        moved = [
            lax.ppermute(blocks[r], "dp", [(i, i ^ r) for i in range(replicas)])
            for r in range(1, replicas)
        ]
        return [blocks[0]] + moved

    def forward(x):
        return lax.ppermute(x, "tensor", ring)

    def pair_sums(x):
        found = []
        for away in range(1, count // 2):
            pairs = [(p, (p + away) % (count // 2)) for p in range(count // 2)]
            near, far = [], []
            for p, q in pairs:
                sender = 2 * p if p < q else 2 * p + 1
                straight = 2 * q + (sender % 2)
                near.append((sender, straight))
                far.append((sender, straight ^ 1))
            one = lax.ppermute(x, "tensor", near)
            other = lax.ppermute(x, "tensor", far)
            found += [one, other]
        return found

    def next_hop(step, chain, after, cost=None):
        arrived = forward(travelling[chain])
        travelling[chain] = hop(step, chain, arrived, attended, output_weight, block, after, cost)

    attended, first, chosen, *leaving = attend(
        query, cached_key_rows, cached_value_rows, new_token_key, new_token_value, lengths,
        output_weight, request_adapter, placement, block, replicas, slot_down_weight.shape[0],
    )
    second = hop(0, 1, None, attended, output_weight, block)
    rows_here = exchange(leaving)
    mid, inside = down(rows_here, slot_down_weight, after=[second])
    travelling = [first, hold(second, after=[mid])]

    def added(a, b):
        return (a.astype(jnp.float32) + b.astype(jnp.float32)).astype(a.dtype)

    rank_sum = added(mid, lax.ppermute(mid, "tensor", [(i, i ^ 1) for i in range(count)]))
    rank_sums = [rank_sum] + pair_sums(rank_sum)
    next_hop(1, 0, after=[rank_sum, travelling[1]], cost=LONG)
    next_hop(1, 1, after=[travelling[0]], cost=MEDIUM)
    for step in range(2, count - 1):
        for chain in range(2):
            if (step, chain) == (2, 0):
                next_hop(step, chain, after=(), cost=LONG)
                deltas = up(rank_sums, inside, slot_up_weight, after=[travelling[0]])
                returned = exchange(deltas)
            else:
                next_hop(step, chain, after=[deltas[0]])
    settled = settle(
        count - 1, returned, chosen, attended, residual, output_weight, after=[travelling[1]]
    )
    out = None
    for chain in range(2):
        arrived = forward(travelling[chain])
        out = finish(chain, arrived, settled[chain], out, block)
    return out


def solution(mesh):
    placed = (
        P(("parts", "dp"), "tensor"),
        P(("parts", "dp"), "tensor", None),
        P(("parts", "dp"), None, "tensor", None),
        P(("parts", "dp"), None, "tensor", None),
        P(("parts", "dp"), "tensor", None),
        P(("parts", "dp"), "tensor", None),
        P(("parts", "dp")),
        P("tensor", None),
        P("dp", None, "tensor"),
        P("dp", None, "tensor"),
        P("parts"),
        P(("parts", "dp")),
    )
    return jax.shard_map(
        per_device,
        mesh=mesh,
        in_specs=placed,
        out_specs=P(("parts", "dp"), "tensor"),
        check_vma=False,
    )
```

```python
import functools
import math

import jax
import jax.numpy as jnp
from jax import lax
from jax.experimental import pallas as pl
from jax.experimental.pallas import tpu as pltpu
from jax.sharding import PartitionSpec as P

GROUP = 4
CAP = 64
LANES = 128
SPAN = 64
MASKED = -1e30
VMEM_LIMIT = 50 * 1024 * 1024
FULL_VMEM = 61 * 1024 * 1024
SHARES = ((5, 3),)
PIECE = 512
SPLIT = 4

VMEM = pl.BlockSpec(memory_space=pltpu.VMEM)
ANY = pl.BlockSpec(memory_space=pl.ANY)
LONG = pl.CostEstimate(flops=20 * 10**9, transcendentals=0, bytes_accessed=40 * 10**6)
MEDIUM = pl.CostEstimate(flops=4 * 10**9, transcendentals=0, bytes_accessed=8 * 10**6)
PARAMS = pltpu.CompilerParams(vmem_limit_bytes=VMEM_LIMIT)


def _dot(a, b, left=1, right=0):
    return lax.dot_general(
        a, b, (((left,), (right,)), ((), ())), preferred_element_type=jnp.float32
    )


def _iota(shape, axis):
    return lax.broadcasted_iota(jnp.int32, shape, axis)


def ring_order(count):
    return list(range(0, count, 2)) + list(range(1, count, 2))[::-1]


def column_owner(step):
    count = lax.axis_size("tensor")
    here = lax.axis_index("tensor")
    half = here // 2
    spot = jnp.where(here % 2 == 0, half, count - 1 - half)
    spot = lax.rem(spot - 1 - step + 2 * count, count)
    return jnp.where(2 * spot < count, 2 * spot, 2 * (count - spot) - 1)


def chain_columns(width):
    shares = next(s for s in SHARES if width % (sum(s) * LANES) == 0)
    unit = width // sum(shares)
    return [(sum(shares[:c]) * unit, shares[c] * unit) for c in range(len(shares))]


class Weights:
    def __init__(self, w_ref, held, sems, first, width):
        depth = w_ref.shape[0] // SPLIT
        first = pl.multiple_of(first, LANES)
        self.held = held
        self.copies = [
            pltpu.make_async_copy(
                w_ref.at[pl.ds(s * depth, depth), pl.ds(first, width)],
                held.at[pl.ds(s * depth, depth), :],
                sems.at[s],
            )
            for s in range(SPLIT)
        ]

    def start(self):
        for copy in self.copies:
            copy.start()

    def wait(self):
        for copy in self.copies:
            copy.wait()

    def products(self, a):
        width = self.held.shape[1]
        for at in range(0, width, PIECE):
            columns = pl.ds(at, min(PIECE, width - at))
            yield columns, _dot(a, self.held[:, columns])

    @staticmethod
    def scratch(depth, width):
        return [
            pltpu.VMEM((depth, width), jnp.bfloat16),
            pltpu.SemaphoreType.DMA((SPLIT,)),
        ]


def row_max(arrays):
    full = None
    tops = []
    for x in arrays:
        width = x.shape[1]
        if width % LANES:
            tops.append(jnp.max(x, axis=1, keepdims=True))
            continue
        for at in range(0, width, LANES):
            tile = x[:, at : at + LANES]
            full = tile if full is None else jnp.maximum(full, tile)
    if full is not None:
        tops.append(jnp.max(full, axis=1, keepdims=True))
    return functools.reduce(jnp.maximum, tops)


def attend_kernel(
    heads, kv, cache, steps, block, replicas, slots,
    len_hbm, adapter_hbm, placement_hbm, q_hbm, k_hbm, v_hbm, nk_hbm, nv_hbm, w_hbm,
    *refs,
):
    a_hbm, out_hbm, chosen_hbm, *sent_hbm = refs[: 3 + replicas]
    (
        a_ref, out_ref, chosen_ref, sent_ref, out_sems,
        len_ref, adapter_ref, placement_ref, q_ref, k_ref, v_ref, nk_ref, nv_ref,
        scores_ref, mixed_ref, fresh_bias_ref, sems, small_sems, w_held, w_sems,
    ) = refs[3 + replicas :]
    requests = len_ref.shape[1]
    width = q_hbm.shape[1]
    per = requests // steps
    groups = per // GROUP
    group_rows = GROUP * heads
    group_cols = GROUP * cache * kv
    per_kv = heads // kv
    scale = math.log2(math.e) / math.sqrt(width)

    def part(kind, step):
        source, target, count = (
            (q_hbm, q_ref, heads),
            (k_hbm, k_ref, cache * kv),
            (v_hbm, v_ref, cache * kv),
        )[kind]
        half = per * count // 2
        halves = []
        for i in range(2):
            rows = pl.ds(step * per * count + i * half, half)
            halves.append(
                pltpu.make_async_copy(
                    source.at[rows, :], target.at[rows, :], sems.at[kind, step, i]
                )
            )
        return halves

    def start(kind, step):
        for copy in part(kind, step):
            copy.start()

    def finished(kind, step):
        for copy in part(kind, step):
            copy.wait()

    small = [
        pltpu.make_async_copy(source, target, small_sems.at[i])
        for i, (source, target) in enumerate(
            (
                (nk_hbm, nk_ref),
                (len_hbm, len_ref),
                (nv_hbm, nv_ref),
                (adapter_hbm, adapter_ref),
                (placement_hbm, placement_ref),
            )
        )
    ]
    leaving = []

    def leave(source, target):
        copy = pltpu.make_async_copy(source, target, out_sems.at[len(leaving)])
        copy.start()
        leaving.append(copy)

    def multiply(first, count):
        rows = pl.ds(first, count)
        for columns, product in weights.products(a_ref[rows, :]):
            out_ref[rows, columns] = product.astype(jnp.bfloat16)
        leave(out_ref.at[rows, :], out_hbm.at[rows, :])

    chunk = out_ref.shape[1]
    weights = Weights(w_hbm, w_held, w_sems, column_owner(0) * block, chunk)
    start(0, 0)
    start(1, 0)
    for copy in small[:2]:
        copy.start()
    start(0, 1)
    start(1, 1)
    start(2, 0)
    for copy in small[2:]:
        copy.start()
    start(2, 1)
    for step in range(2, steps):
        for kind in range(3):
            start(kind, step)
    weights.start()

    row = _iota((group_rows, group_cols), 0)
    col = _iota((group_rows, group_cols), 1)
    same = (row // heads == col // (cache * kv)) & ((row % heads) // per_kv == col % kv)
    own_bias = jnp.where(same, 0.0, MASKED)
    row = _iota(fresh_bias_ref.shape, 0)
    col = _iota(fresh_bias_ref.shape, 1)
    same = (row // heads == col // kv) & ((row % heads) // per_kv == col % kv)
    fresh_bias_ref[...] = jnp.where(same, 0.0, MASKED)
    fresh_cols = SPAN * kv
    span_rows = SPAN * heads
    span_groups = SPAN // GROUP
    ones = jnp.ones((max(group_cols, fresh_cols), LANES), jnp.bfloat16)

    def arrive(step):
        finished(0, step)
        finished(1, step)

    def scores(step):
        side = step % 2
        q_at = step * per * heads
        k_at = step * per * cache * kv
        for g in range(groups):
            scores_ref[side, pl.ds(g * group_rows, group_rows), pl.ds(0, group_cols)] = _dot(
                q_ref[pl.ds(q_at + g * group_rows, group_rows), :],
                k_ref[pl.ds(k_at + g * group_cols, group_cols), :],
                1,
                1,
            )
        for span in range(per // SPAN):
            rows = pl.ds(span * span_rows, span_rows)
            scores_ref[side, rows, pl.ds(group_cols, fresh_cols)] = _dot(
                q_ref[pl.ds(q_at + span * span_rows, span_rows), :],
                nk_ref[pl.ds(step * per * kv + span * fresh_cols, fresh_cols), :],
                1,
                1,
            )

    for copy in small[:2]:
        copy.wait()
    counts = len_ref[...].astype(jnp.float32)
    all_groups = requests // GROUP
    of_group = _iota((all_groups, requests), 1) // GROUP == _iota((all_groups, requests), 0)
    counts = jnp.where(of_group, counts, 0.0).astype(jnp.bfloat16)
    spread = _iota((requests, group_cols), 0) % GROUP == _iota((requests, group_cols), 1) // (cache * kv)
    counts = _dot(counts, spread.astype(jnp.bfloat16))
    position = (_iota((all_groups, group_cols), 1) // kv) % cache
    length_bias = jnp.where(position.astype(jnp.float32) < counts, 0.0, MASKED)

    def soften(step):
        side = step % 2
        cached_weights = []
        fresh_weights = []
        for g in range(groups):
            rows = pl.ds(g * group_rows, group_rows)
            bias = own_bias + length_bias[step * groups + g : step * groups + g + 1, :]
            cached = scores_ref[side, rows, pl.ds(0, group_cols)] + bias
            inner = pl.ds((g % span_groups) * group_rows, group_rows)
            new = scores_ref[side, rows, pl.ds(group_cols, fresh_cols)]
            new = new + fresh_bias_ref[inner, :]
            top = row_max([cached, new])
            cached_weights.append(jnp.exp2((cached - top) * scale).astype(jnp.bfloat16))
            fresh_weights.append(jnp.exp2((new - top) * scale).astype(jnp.bfloat16))
        return cached_weights, fresh_weights

    def mix(step, cached_weights, fresh_weights):
        side = step % 2
        k_at = step * per * cache * kv
        f_at = step * per * kv
        for span in range(per // SPAN):
            inside = range(span * span_groups, (span + 1) * span_groups)
            mixed = [
                _dot(cached_weights[g], v_ref[pl.ds(k_at + g * group_cols, group_cols), :])
                for g in inside
            ]
            fresh = jnp.concatenate([fresh_weights[g] for g in inside], axis=0)
            values = nv_ref[pl.ds(f_at + span * fresh_cols, fresh_cols), :]
            mixed = jnp.concatenate(mixed, axis=0) + _dot(fresh, values)
            cached = jnp.concatenate([cached_weights[g] for g in inside], axis=0)
            total = _dot(cached, ones[:group_cols]) + _dot(fresh, ones[:fresh_cols])
            rows = pl.ds(span * span_rows, span_rows)
            inverse = pl.reciprocal(total, approx=True)
            mixed_ref[side, rows, :] = mixed * (inverse * (2.0 - total * inverse))
        for h in range(heads):
            a_ref[pl.ds(step * per, per), pl.ds(h * width, width)] = mixed_ref[
                side, pl.ds(h, per, stride=heads), :
            ].astype(jnp.bfloat16)

    arrive(0)
    scores(0)
    softened = soften(0)
    for step in range(steps):
        finished(2, step)
        if step == 0:
            for copy in small[2:]:
                copy.wait()
        if step + 1 < steps:
            arrive(step + 1)
            scores(step + 1)
        if step == 0:
            plan_routes(slots, adapter_ref, placement_ref, chosen_ref, sent_ref)
        if step == steps - 1:
            weights.wait()
            multiply(0, requests - per)
        mix(step, *softened)
        if step + 1 < steps:
            softened = soften(step + 1)
        rows = pl.ds(step * per, per)
        leave(a_ref.at[rows, :], a_hbm.at[rows, :])

    sent_ref[:, pl.ds(0, heads * width)] = _dot(chosen_ref[...], a_ref[...]).astype(jnp.bfloat16)
    leave(chosen_ref, chosen_hbm)
    for r in range(replicas):
        leave(sent_ref.at[pl.ds(r * CAP, CAP), :], sent_hbm[r])
    multiply(requests - per, per)
    for copy in leaving:
        copy.wait()


def plan_routes(slots, adapter_ref, placement_ref, chosen_ref, sent_ref):
    replicas = sent_ref.shape[0] // CAP
    requests = adapter_ref.shape[1]
    table = placement_ref.shape[1]
    matches = _iota((table, requests), 0) == adapter_ref[...]
    placed = jnp.broadcast_to(placement_ref[...].astype(jnp.float32), (8, table))
    slot = _dot(placed.astype(jnp.bfloat16), matches.astype(jnp.bfloat16)).astype(jnp.int32)
    slot = slot[0:1, :]
    holder = (slot // slots) ^ lax.axis_index("dp")
    inside = slot % slots
    of_holder = _iota((max(replicas, 8), requests), 0) == holder
    earlier = _iota((requests, requests), 0) < _iota((requests, requests), 1)
    before = _dot(of_holder.astype(jnp.bfloat16), earlier.astype(jnp.bfloat16))
    before = jnp.sum(jnp.where(of_holder, before, 0.0), axis=0, keepdims=True).astype(jnp.int32)
    target = holder * CAP + before
    here = _iota((replicas * CAP, requests), 0) == target
    chosen_ref[...] = here.astype(jnp.bfloat16)
    inner = jnp.sum(jnp.where(here, inside.astype(jnp.float32), 0.0), axis=1, keepdims=True)
    inner = jnp.broadcast_to(inner, (replicas * CAP, LANES)).astype(jnp.bfloat16)
    sent_ref[:, pl.ds(sent_ref.shape[1] - LANES, LANES)] = inner


def attend(
    query, keys, values, new_key, new_value, lengths, weight, request_adapter, placement,
    block, replicas, slots,
):
    requests, heads, width = query.shape
    cache, kv = keys.shape[1], keys.shape[2]
    steps = 2
    per = requests // steps
    columns = GROUP * cache * kv + SPAN * kv
    features = heads * width
    chunk = chain_columns(block)[0][1]
    small = [lengths.reshape(1, -1), request_adapter.reshape(1, -1), placement.reshape(1, -1)]
    operands = [
        query.reshape(requests * heads, width),
        keys.reshape(requests * cache * kv, width),
        values.reshape(requests * cache * kv, width),
        new_key.reshape(requests * kv, width),
        new_value.reshape(requests * kv, width),
    ]
    return pl.pallas_call(
        functools.partial(attend_kernel, heads, kv, cache, steps, block, replicas, slots),
        in_specs=[ANY] * 9,
        out_specs=[ANY] * (3 + replicas),
        out_shape=[
            jax.ShapeDtypeStruct((requests, features), jnp.bfloat16),
            jax.ShapeDtypeStruct((requests, chunk), jnp.bfloat16),
            jax.ShapeDtypeStruct((replicas * CAP, requests), jnp.bfloat16),
        ]
        + [jax.ShapeDtypeStruct((CAP, features + LANES), jnp.bfloat16)] * replicas,
        scratch_shapes=[
            pltpu.VMEM((requests, features), jnp.bfloat16),
            pltpu.VMEM((requests, chunk), jnp.bfloat16),
            pltpu.VMEM((replicas * CAP, requests), jnp.bfloat16),
            pltpu.VMEM((replicas * CAP, features + LANES), jnp.bfloat16),
            pltpu.SemaphoreType.DMA((1 + steps + 2 + replicas,)),
        ]
        + [pltpu.VMEM(x.shape, x.dtype) for x in small + operands]
        + [
            pltpu.VMEM((2, per * heads, columns), jnp.float32),
            pltpu.VMEM((2, per * heads, width), jnp.float32),
            pltpu.VMEM((SPAN * heads, SPAN * kv), jnp.float32),
            pltpu.SemaphoreType.DMA((3, steps, 2)),
            pltpu.SemaphoreType.DMA((5,)),
        ]
        + Weights.scratch(weight.shape[0], chunk),
        compiler_params=pltpu.CompilerParams(vmem_limit_bytes=FULL_VMEM),
        name="attend",
    )(*small, *operands, weight)


def hop_kernel(step, block, start, arriving, after, *refs):
    if arriving:
        arrived_ref, *refs = refs
    a_ref, w_hbm, *refs = refs
    out_ref, held, sems = refs[after:]
    chunk = out_ref.shape[1]
    first = column_owner(step) * block + start
    weights = Weights(w_hbm, held, sems, first, chunk)
    weights.start()
    weights.wait()
    for columns, product in weights.products(a_ref[...]):
        if arriving:
            product = product + arrived_ref[:, columns].astype(jnp.float32)
        out_ref[:, columns] = product.astype(jnp.bfloat16)


def hop(step, chain, arrived, attended, weight, block, after=(), cost=None):
    arriving = arrived is not None
    start, chunk = chain_columns(block)[chain]
    operands = ([arrived] if arriving else []) + [attended, weight, *after]
    return pl.pallas_call(
        functools.partial(hop_kernel, step, block, start, arriving, len(after)),
        in_specs=[VMEM] * (1 + arriving) + [ANY] + [ANY] * len(after),
        out_specs=VMEM,
        out_shape=jax.ShapeDtypeStruct((attended.shape[0], chunk), jnp.bfloat16),
        scratch_shapes=Weights.scratch(weight.shape[0], chunk),
        compiler_params=PARAMS,
        cost_estimate=cost,
        name="hop",
    )(*operands)


def down_kernel(replicas, after, *refs):
    received = refs[:replicas]
    down_ref = refs[replicas]
    mid_ref, inside_ref = refs[replicas + 1 + after :]
    slots, rank, width = down_ref.shape
    rows = jnp.concatenate([r[:, pl.ds(0, width)] for r in received], axis=0)
    inside = jnp.concatenate([r[:, pl.ds(width, LANES)] for r in received], axis=0)
    inside_ref[...] = inside
    projected = _dot(rows, down_ref[...].reshape(slots * rank, width), 1, 1)
    lane_slot = _iota(projected.shape, 1) // rank
    mine = lane_slot == inside[:, 0:1].astype(jnp.int32)
    projected = jnp.where(mine, projected, 0.0).astype(jnp.bfloat16)
    beside = LANES // rank
    some = projected.shape[0] // beside
    packed = 0.0
    for b in range(beside):
        lane = _iota((slots * rank, LANES), 1) - b * rank
        fold = _iota((slots * rank, LANES), 0) % rank == lane
        packed = packed + _dot(projected[b * some : (b + 1) * some, :], fold.astype(jnp.bfloat16))
    mid_ref[...] = packed.astype(jnp.bfloat16)


def down(received, slot_down_weight, after=()):
    replicas = len(received)
    rows = replicas * CAP
    return pl.pallas_call(
        functools.partial(down_kernel, replicas, len(after)),
        in_specs=[VMEM] * (replicas + 1) + [ANY] * len(after),
        out_specs=[VMEM, VMEM],
        out_shape=[
            jax.ShapeDtypeStruct((rows * slot_down_weight.shape[1] // LANES, LANES), jnp.bfloat16),
            jax.ShapeDtypeStruct((rows, LANES), jnp.bfloat16),
        ],
        compiler_params=PARAMS,
        name="down",
    )(*received, slot_down_weight, *after)


def up_kernel(parts, after, *refs):
    mids = refs[:parts]
    inside_ref, up_ref = refs[parts : parts + 2]
    out_refs = refs[parts + 2 + after :]
    slots, rank, width = up_ref.shape
    mid = mids[0][...].astype(jnp.float32)
    for m in mids[1:]:
        mid = mid + m[...].astype(jnp.float32)
    mid = mid.astype(jnp.bfloat16)
    wide = []
    for b in range(LANES // rank):
        lane = _iota((LANES, slots * rank), 0) - b * rank
        spread = _iota((LANES, slots * rank), 1) % rank == lane
        wide.append(_dot(mid, spread.astype(jnp.bfloat16)))
    wide = jnp.concatenate(wide, axis=0)
    mine = _iota(wide.shape, 1) // rank == inside_ref[:, 0:1].astype(jnp.int32)
    wide = jnp.where(mine, wide, 0.0).astype(jnp.bfloat16)
    delta = _dot(wide, up_ref[...].reshape(slots * rank, width)).astype(jnp.bfloat16)
    for r, out_ref in enumerate(out_refs):
        out_ref[...] = delta[r * CAP : (r + 1) * CAP, :]


def up(mids, inside, slot_up_weight, after=()):
    rows = inside.shape[0]
    replicas = rows // CAP
    width = slot_up_weight.shape[2]
    return pl.pallas_call(
        functools.partial(up_kernel, len(mids), len(after)),
        in_specs=[VMEM] * (len(mids) + 2) + [ANY] * len(after),
        out_specs=[VMEM] * replicas,
        out_shape=[jax.ShapeDtypeStruct((CAP, width), jnp.bfloat16)] * replicas,
        compiler_params=PARAMS,
        name="up",
    )(*mids, inside, slot_up_weight, *after)


def settle_kernel(step, replicas, after, *refs):
    returned = refs[:replicas]
    chosen_ref, a_ref, residual_ref, w_hbm = refs[replicas : replicas + 4]
    *out_refs, held, sems = refs[replicas + 4 + after :]
    width = residual_ref.shape[1]
    weights = Weights(w_hbm, held, sems, column_owner(step) * width, width)
    weights.start()
    rows = jnp.concatenate([r[...] for r in returned], axis=0)
    delta = _dot(chosen_ref[...], rows, 0, 0)
    total = residual_ref[...].astype(jnp.float32) + delta
    weights.wait()
    total = total + jnp.concatenate([p for _, p in weights.products(a_ref[...])], axis=1)
    for (start, chunk), out_ref in zip(chain_columns(width), out_refs):
        out_ref[...] = total[:, start : start + chunk]


def settle(step, returned, chosen, attended, residual, weight, after=()):
    replicas = len(returned)
    rows, width = residual.shape
    chains = chain_columns(width)
    return pl.pallas_call(
        functools.partial(settle_kernel, step, replicas, len(after)),
        in_specs=[VMEM] * (replicas + 3) + [ANY] * (1 + len(after)),
        out_specs=[VMEM] * len(chains),
        out_shape=[jax.ShapeDtypeStruct((rows, chunk), jnp.float32) for _, chunk in chains],
        scratch_shapes=Weights.scratch(weight.shape[0], width),
        compiler_params=PARAMS,
        cost_estimate=MEDIUM,
        name="settle",
    )(*returned, chosen, attended, residual, weight, *after)


def finish_kernel(start, arrived_ref, settled_ref, *refs):
    out_hbm, held, sems = refs[-3:]
    rows, chunk = arrived_ref.shape
    half = rows // 2
    copies = []
    for i in range(2):
        part = pl.ds(i * half, half)
        total = settled_ref[part, :] + arrived_ref[part, :].astype(jnp.float32)
        held[part, :] = total.astype(jnp.bfloat16)
        target = out_hbm.at[part, pl.ds(start, chunk)]
        copies.append(pltpu.make_async_copy(held.at[part, :], target, sems.at[i]))
        copies[-1].start()
    for copy in copies:
        copy.wait()


def finish(chain, arrived, settled, earlier, width):
    rows = arrived.shape[0]
    start, chunk = chain_columns(width)[chain]
    operands = [arrived, settled] + ([earlier] if earlier is not None else [])
    return pl.pallas_call(
        functools.partial(finish_kernel, start),
        in_specs=[VMEM, VMEM] + ([ANY] if earlier is not None else []),
        out_specs=ANY,
        out_shape=jax.ShapeDtypeStruct((rows, width), jnp.bfloat16),
        input_output_aliases={2: 0} if earlier is not None else {},
        scratch_shapes=[
            pltpu.VMEM((rows, chunk), jnp.bfloat16),
            pltpu.SemaphoreType.DMA((2,)),
        ],
        compiler_params=PARAMS,
        name="finish",
    )(*operands)


def hold_kernel(*refs):
    pass


def hold(x, after):
    return pl.pallas_call(
        hold_kernel,
        in_specs=[ANY] * (1 + len(after)),
        out_specs=ANY,
        out_shape=jax.ShapeDtypeStruct(x.shape, x.dtype),
        input_output_aliases={0: 0},
        compiler_params=PARAMS,
        name="hold",
    )(x, *after)


def per_device(
    residual,
    query,
    cached_key_rows,
    cached_value_rows,
    new_token_key,
    new_token_value,
    lengths,
    output_weight,
    slot_down_weight,
    slot_up_weight,
    placement,
    request_adapter,
):
    count = lax.axis_size("tensor")
    replicas = lax.axis_size("dp")
    block = residual.shape[1]
    order = ring_order(count)
    ring = [(order[p], order[(p + 1) % count]) for p in range(count)]

    def exchange(blocks):
        moved = [
            lax.ppermute(blocks[r], "dp", [(i, i ^ r) for i in range(replicas)])
            for r in range(1, replicas)
        ]
        return [blocks[0]] + moved

    def forward(x):
        return lax.ppermute(x, "tensor", ring)

    def pair_sums(x):
        found = []
        for away in range(1, count // 2):
            pairs = [(p, (p + away) % (count // 2)) for p in range(count // 2)]
            near, far = [], []
            for p, q in pairs:
                sender = 2 * p if p < q else 2 * p + 1
                straight = 2 * q + (sender % 2)
                near.append((sender, straight))
                far.append((sender, straight ^ 1))
            one = lax.ppermute(x, "tensor", near)
            other = lax.ppermute(x, "tensor", far)
            found += [one, other]
        return found

    def next_hop(step, chain, after, cost=None):
        arrived = forward(travelling[chain])
        travelling[chain] = hop(step, chain, arrived, attended, output_weight, block, after, cost)

    attended, first, chosen, *leaving = attend(
        query, cached_key_rows, cached_value_rows, new_token_key, new_token_value, lengths,
        output_weight, request_adapter, placement, block, replicas, slot_down_weight.shape[0],
    )
    second = hop(0, 1, None, attended, output_weight, block)
    rows_here = exchange(leaving)
    mid, inside = down(rows_here, slot_down_weight, after=[second])
    travelling = [first, hold(second, after=[mid])]

    def added(a, b):
        return (a.astype(jnp.float32) + b.astype(jnp.float32)).astype(a.dtype)

    rank_sum = added(mid, lax.ppermute(mid, "tensor", [(i, i ^ 1) for i in range(count)]))
    rank_sums = [rank_sum] + pair_sums(rank_sum)
    next_hop(1, 0, after=[rank_sum, travelling[1]], cost=LONG)
    next_hop(1, 1, after=[travelling[0]], cost=MEDIUM)
    for step in range(2, count - 1):
        for chain in range(2):
            if (step, chain) == (2, 0):
                next_hop(step, chain, after=(), cost=LONG)
                deltas = up(rank_sums, inside, slot_up_weight, after=[travelling[0]])
                returned = exchange(deltas)
            else:
                next_hop(step, chain, after=[deltas[0]])
    settled = settle(
        count - 1, returned, chosen, attended, residual, output_weight, after=[travelling[1]]
    )
    out = None
    for chain in range(2):
        arrived = forward(travelling[chain])
        out = finish(chain, arrived, settled[chain], out, block)
    return out


def solution(mesh):
    placed = (
        P(("parts", "dp"), "tensor"),
        P(("parts", "dp"), "tensor", None),
        P(("parts", "dp"), None, "tensor", None),
        P(("parts", "dp"), None, "tensor", None),
        P(("parts", "dp"), "tensor", None),
        P(("parts", "dp"), "tensor", None),
        P(("parts", "dp")),
        P("tensor", None),
        P("dp", None, "tensor"),
        P("dp", None, "tensor"),
        P("parts"),
        P(("parts", "dp")),
    )
    return jax.shard_map(
        per_device,
        mesh=mesh,
        in_specs=placed,
        out_specs=P(("parts", "dp"), "tensor"),
        check_vma=False,
    )
```

```python
import functools
import math

import jax
import jax.numpy as jnp
from jax import lax
from jax.experimental import pallas as pl
from jax.experimental.pallas import tpu as pltpu
from jax.sharding import PartitionSpec as P

GROUP = 4
CAP = 64
LANES = 128
SPAN = 64
MASKED = -1e30
VMEM_LIMIT = 50 * 1024 * 1024
FULL_VMEM = 61 * 1024 * 1024
SHARES = ((5, 3),)
PIECE = 512
SPLIT = 4

VMEM = pl.BlockSpec(memory_space=pltpu.VMEM)
ANY = pl.BlockSpec(memory_space=pl.ANY)
LONG = pl.CostEstimate(flops=20 * 10**9, transcendentals=0, bytes_accessed=40 * 10**6)
MEDIUM = pl.CostEstimate(flops=4 * 10**9, transcendentals=0, bytes_accessed=8 * 10**6)
PARAMS = pltpu.CompilerParams(vmem_limit_bytes=VMEM_LIMIT)


def _dot(a, b, left=1, right=0):
    return lax.dot_general(
        a, b, (((left,), (right,)), ((), ())), preferred_element_type=jnp.float32
    )


def _iota(shape, axis):
    return lax.broadcasted_iota(jnp.int32, shape, axis)


def ring_order(count):
    return list(range(0, count, 2)) + list(range(1, count, 2))[::-1]


def column_owner(step):
    count = lax.axis_size("tensor")
    here = lax.axis_index("tensor")
    half = here // 2
    spot = jnp.where(here % 2 == 0, half, count - 1 - half)
    spot = lax.rem(spot - 1 - step + 2 * count, count)
    return jnp.where(2 * spot < count, 2 * spot, 2 * (count - spot) - 1)


def chain_columns(width):
    shares = next(s for s in SHARES if width % (sum(s) * LANES) == 0)
    unit = width // sum(shares)
    return [(sum(shares[:c]) * unit, shares[c] * unit) for c in range(len(shares))]


class Weights:
    def __init__(self, w_ref, held, sems, first, width):
        depth = w_ref.shape[0] // SPLIT
        first = pl.multiple_of(first, LANES)
        self.held = held
        self.copies = [
            pltpu.make_async_copy(
                w_ref.at[pl.ds(s * depth, depth), pl.ds(first, width)],
                held.at[pl.ds(s * depth, depth), :],
                sems.at[s],
            )
            for s in range(SPLIT)
        ]

    def start(self):
        for copy in self.copies:
            copy.start()

    def wait(self):
        for copy in self.copies:
            copy.wait()

    def products(self, a):
        width = self.held.shape[1]
        for at in range(0, width, PIECE):
            columns = pl.ds(at, min(PIECE, width - at))
            yield columns, _dot(a, self.held[:, columns])

    @staticmethod
    def scratch(depth, width):
        return [
            pltpu.VMEM((depth, width), jnp.bfloat16),
            pltpu.SemaphoreType.DMA((SPLIT,)),
        ]


def row_max(arrays):
    full = None
    tops = []
    for x in arrays:
        width = x.shape[1]
        if width % LANES:
            tops.append(jnp.max(x, axis=1, keepdims=True))
            continue
        for at in range(0, width, LANES):
            tile = x[:, at : at + LANES]
            full = tile if full is None else jnp.maximum(full, tile)
    if full is not None:
        tops.append(jnp.max(full, axis=1, keepdims=True))
    return functools.reduce(jnp.maximum, tops)


def attend_kernel(
    heads, kv, cache, steps, block, replicas, slots,
    len_hbm, adapter_hbm, placement_hbm, q_hbm, k_hbm, v_hbm, nk_hbm, nv_hbm, w_hbm,
    *refs,
):
    a_hbm, out_hbm, chosen_hbm, *sent_hbm = refs[: 3 + replicas]
    (
        a_ref, out_ref, chosen_ref, sent_ref, out_sems,
        len_ref, adapter_ref, placement_ref, q_ref, k_ref, v_ref, nk_ref, nv_ref,
        scores_ref, mixed_ref, fresh_bias_ref, sems, small_sems, w_held, w_sems,
    ) = refs[3 + replicas :]
    requests = len_ref.shape[1]
    width = q_hbm.shape[1]
    per = requests // steps
    groups = per // GROUP
    group_rows = GROUP * heads
    group_cols = GROUP * cache * kv
    per_kv = heads // kv
    scale = math.log2(math.e) / math.sqrt(width)

    def part(kind, step):
        source, target, count = (
            (q_hbm, q_ref, heads),
            (k_hbm, k_ref, cache * kv),
            (v_hbm, v_ref, cache * kv),
        )[kind]
        rows = pl.ds(step * per * count, per * count)
        return pltpu.make_async_copy(source.at[rows, :], target.at[rows, :], sems.at[kind, step])

    small = [
        pltpu.make_async_copy(source, target, small_sems.at[i])
        for i, (source, target) in enumerate(
            (
                (nk_hbm, nk_ref),
                (len_hbm, len_ref),
                (nv_hbm, nv_ref),
                (adapter_hbm, adapter_ref),
                (placement_hbm, placement_ref),
            )
        )
    ]
    leaving = []

    def leave(source, target):
        copy = pltpu.make_async_copy(source, target, out_sems.at[len(leaving)])
        copy.start()
        leaving.append(copy)

    def multiply(first, count):
        rows = pl.ds(first, count)
        for columns, product in weights.products(a_ref[rows, :]):
            out_ref[rows, columns] = product.astype(jnp.bfloat16)
        leave(out_ref.at[rows, :], out_hbm.at[rows, :])

    chunk = out_ref.shape[1]
    weights = Weights(w_hbm, w_held, w_sems, column_owner(0) * block, chunk)
    part(0, 0).start()
    part(1, 0).start()
    for copy in small[:2]:
        copy.start()
    part(0, 1).start()
    part(1, 1).start()
    part(2, 0).start()
    for copy in small[2:]:
        copy.start()
    part(2, 1).start()
    for step in range(2, steps):
        for kind in range(3):
            part(kind, step).start()
    weights.start()

    row = _iota((group_rows, group_cols), 0)
    col = _iota((group_rows, group_cols), 1)
    same = (row // heads == col // (cache * kv)) & ((row % heads) // per_kv == col % kv)
    own_bias = jnp.where(same, 0.0, MASKED)
    row = _iota(fresh_bias_ref.shape, 0)
    col = _iota(fresh_bias_ref.shape, 1)
    same = (row // heads == col // kv) & ((row % heads) // per_kv == col % kv)
    fresh_bias_ref[...] = jnp.where(same, 0.0, MASKED)
    fresh_cols = SPAN * kv
    span_rows = SPAN * heads
    span_groups = SPAN // GROUP
    ones = jnp.ones((max(group_cols, fresh_cols), LANES), jnp.bfloat16)

    def arrive(step):
        part(0, step).wait()
        part(1, step).wait()

    def scores(step):
        side = step % 2
        q_at = step * per * heads
        k_at = step * per * cache * kv
        for g in range(groups):
            scores_ref[side, pl.ds(g * group_rows, group_rows), pl.ds(0, group_cols)] = _dot(
                q_ref[pl.ds(q_at + g * group_rows, group_rows), :],
                k_ref[pl.ds(k_at + g * group_cols, group_cols), :],
                1,
                1,
            )
        for span in range(per // SPAN):
            rows = pl.ds(span * span_rows, span_rows)
            scores_ref[side, rows, pl.ds(group_cols, fresh_cols)] = _dot(
                q_ref[pl.ds(q_at + span * span_rows, span_rows), :],
                nk_ref[pl.ds(step * per * kv + span * fresh_cols, fresh_cols), :],
                1,
                1,
            )

    for copy in small[:2]:
        copy.wait()
    counts = len_ref[...].astype(jnp.float32)
    all_groups = requests // GROUP
    of_group = _iota((all_groups, requests), 1) // GROUP == _iota((all_groups, requests), 0)
    counts = jnp.where(of_group, counts, 0.0).astype(jnp.bfloat16)
    spread = _iota((requests, group_cols), 0) % GROUP == _iota((requests, group_cols), 1) // (cache * kv)
    counts = _dot(counts, spread.astype(jnp.bfloat16))
    position = (_iota((all_groups, group_cols), 1) // kv) % cache
    length_bias = jnp.where(position.astype(jnp.float32) < counts, 0.0, MASKED)

    arrive(0)
    scores(0)
    for step in range(steps):
        side = step % 2
        k_at = step * per * cache * kv
        f_at = step * per * kv
        part(2, step).wait()
        if step == 0:
            for copy in small[2:]:
                copy.wait()
        if step + 1 < steps:
            arrive(step + 1)
            scores(step + 1)
        if step == 0:
            plan_routes(slots, adapter_ref, placement_ref, chosen_ref, sent_ref)
        if step == steps - 1:
            weights.wait()
            multiply(0, requests - per)
        for span in range(per // SPAN):
            cached_weights = []
            fresh_weights = []
            mixed = []
            for g in range(span * span_groups, (span + 1) * span_groups):
                rows = pl.ds(g * group_rows, group_rows)
                bias = own_bias + length_bias[step * groups + g : step * groups + g + 1, :]
                cached = scores_ref[side, rows, pl.ds(0, group_cols)] + bias
                inner = pl.ds((g % span_groups) * group_rows, group_rows)
                new = scores_ref[side, rows, pl.ds(group_cols, fresh_cols)]
                new = new + fresh_bias_ref[inner, :]
                top = row_max([cached, new])
                cached = jnp.exp2((cached - top) * scale).astype(jnp.bfloat16)
                cached_weights.append(cached)
                fresh_weights.append(jnp.exp2((new - top) * scale).astype(jnp.bfloat16))
                mixed.append(_dot(cached, v_ref[pl.ds(k_at + g * group_cols, group_cols), :]))
            fresh = jnp.concatenate(fresh_weights, axis=0)
            values = nv_ref[pl.ds(f_at + span * fresh_cols, fresh_cols), :]
            mixed = jnp.concatenate(mixed, axis=0) + _dot(fresh, values)
            total = _dot(jnp.concatenate(cached_weights, axis=0), ones[:group_cols])
            total = total + _dot(fresh, ones[:fresh_cols])
            rows = pl.ds(span * span_rows, span_rows)
            inverse = pl.reciprocal(total, approx=True)
            mixed_ref[side, rows, :] = mixed * (inverse * (2.0 - total * inverse))
        for h in range(heads):
            a_ref[pl.ds(step * per, per), pl.ds(h * width, width)] = mixed_ref[
                side, pl.ds(h, per, stride=heads), :
            ].astype(jnp.bfloat16)
        if step + 1 < steps:
            rows = pl.ds(step * per, per)
            leave(a_ref.at[rows, :], a_hbm.at[rows, :])

    sent_ref[:, pl.ds(0, heads * width)] = _dot(chosen_ref[...], a_ref[...]).astype(jnp.bfloat16)
    multiply(requests - per, per)
    for r in range(replicas):
        leave(sent_ref.at[pl.ds(r * CAP, CAP), :], sent_hbm[r])
    rows = pl.ds(requests - per, per)
    leave(a_ref.at[rows, :], a_hbm.at[rows, :])
    leave(chosen_ref, chosen_hbm)
    for copy in leaving:
        copy.wait()


def plan_routes(slots, adapter_ref, placement_ref, chosen_ref, sent_ref):
    replicas = sent_ref.shape[0] // CAP
    requests = adapter_ref.shape[1]
    table = placement_ref.shape[1]
    matches = _iota((table, requests), 0) == adapter_ref[...]
    placed = jnp.broadcast_to(placement_ref[...].astype(jnp.float32), (8, table))
    slot = _dot(placed.astype(jnp.bfloat16), matches.astype(jnp.bfloat16)).astype(jnp.int32)
    slot = slot[0:1, :]
    holder = (slot // slots) ^ lax.axis_index("dp")
    inside = slot % slots
    of_holder = _iota((max(replicas, 8), requests), 0) == holder
    earlier = _iota((requests, requests), 0) < _iota((requests, requests), 1)
    before = _dot(of_holder.astype(jnp.bfloat16), earlier.astype(jnp.bfloat16))
    before = jnp.sum(jnp.where(of_holder, before, 0.0), axis=0, keepdims=True).astype(jnp.int32)
    target = holder * CAP + before
    here = _iota((replicas * CAP, requests), 0) == target
    chosen_ref[...] = here.astype(jnp.bfloat16)
    inner = jnp.sum(jnp.where(here, inside.astype(jnp.float32), 0.0), axis=1, keepdims=True)
    inner = jnp.broadcast_to(inner, (replicas * CAP, LANES)).astype(jnp.bfloat16)
    sent_ref[:, pl.ds(sent_ref.shape[1] - LANES, LANES)] = inner


def attend(
    query, keys, values, new_key, new_value, lengths, weight, request_adapter, placement,
    block, replicas, slots,
):
    requests, heads, width = query.shape
    cache, kv = keys.shape[1], keys.shape[2]
    steps = 2
    per = requests // steps
    columns = GROUP * cache * kv + SPAN * kv
    features = heads * width
    chunk = chain_columns(block)[0][1]
    small = [lengths.reshape(1, -1), request_adapter.reshape(1, -1), placement.reshape(1, -1)]
    operands = [
        query.reshape(requests * heads, width),
        keys.reshape(requests * cache * kv, width),
        values.reshape(requests * cache * kv, width),
        new_key.reshape(requests * kv, width),
        new_value.reshape(requests * kv, width),
    ]
    return pl.pallas_call(
        functools.partial(attend_kernel, heads, kv, cache, steps, block, replicas, slots),
        in_specs=[ANY] * 9,
        out_specs=[ANY] * (3 + replicas),
        out_shape=[
            jax.ShapeDtypeStruct((requests, features), jnp.bfloat16),
            jax.ShapeDtypeStruct((requests, chunk), jnp.bfloat16),
            jax.ShapeDtypeStruct((replicas * CAP, requests), jnp.bfloat16),
        ]
        + [jax.ShapeDtypeStruct((CAP, features + LANES), jnp.bfloat16)] * replicas,
        scratch_shapes=[
            pltpu.VMEM((requests, features), jnp.bfloat16),
            pltpu.VMEM((requests, chunk), jnp.bfloat16),
            pltpu.VMEM((replicas * CAP, requests), jnp.bfloat16),
            pltpu.VMEM((replicas * CAP, features + LANES), jnp.bfloat16),
            pltpu.SemaphoreType.DMA((1 + steps + 2 + replicas,)),
        ]
        + [pltpu.VMEM(x.shape, x.dtype) for x in small + operands]
        + [
            pltpu.VMEM((2, per * heads, columns), jnp.float32),
            pltpu.VMEM((2, per * heads, width), jnp.float32),
            pltpu.VMEM((SPAN * heads, SPAN * kv), jnp.float32),
            pltpu.SemaphoreType.DMA((3, steps)),
            pltpu.SemaphoreType.DMA((5,)),
        ]
        + Weights.scratch(weight.shape[0], chunk),
        compiler_params=pltpu.CompilerParams(vmem_limit_bytes=FULL_VMEM),
        name="attend",
    )(*small, *operands, weight)


def hop_kernel(step, block, start, arriving, after, *refs):
    if arriving:
        arrived_ref, *refs = refs
    a_ref, w_hbm, *refs = refs
    out_ref, held, sems = refs[after:]
    chunk = out_ref.shape[1]
    first = column_owner(step) * block + start
    weights = Weights(w_hbm, held, sems, first, chunk)
    weights.start()
    weights.wait()
    for columns, product in weights.products(a_ref[...]):
        if arriving:
            product = product + arrived_ref[:, columns].astype(jnp.float32)
        out_ref[:, columns] = product.astype(jnp.bfloat16)


def hop(step, chain, arrived, attended, weight, block, after=(), cost=None):
    arriving = arrived is not None
    start, chunk = chain_columns(block)[chain]
    operands = ([arrived] if arriving else []) + [attended, weight, *after]
    return pl.pallas_call(
        functools.partial(hop_kernel, step, block, start, arriving, len(after)),
        in_specs=[VMEM] * (1 + arriving) + [ANY] + [ANY] * len(after),
        out_specs=VMEM,
        out_shape=jax.ShapeDtypeStruct((attended.shape[0], chunk), jnp.bfloat16),
        scratch_shapes=Weights.scratch(weight.shape[0], chunk),
        compiler_params=PARAMS,
        cost_estimate=cost,
        name="hop",
    )(*operands)


def down_kernel(replicas, after, *refs):
    received = refs[:replicas]
    down_ref = refs[replicas]
    mid_ref, inside_ref = refs[replicas + 1 + after :]
    slots, rank, width = down_ref.shape
    rows = jnp.concatenate([r[:, pl.ds(0, width)] for r in received], axis=0)
    inside = jnp.concatenate([r[:, pl.ds(width, LANES)] for r in received], axis=0)
    inside_ref[...] = inside
    projected = _dot(rows, down_ref[...].reshape(slots * rank, width), 1, 1)
    lane_slot = _iota(projected.shape, 1) // rank
    mine = lane_slot == inside[:, 0:1].astype(jnp.int32)
    projected = jnp.where(mine, projected, 0.0).astype(jnp.bfloat16)
    beside = LANES // rank
    some = projected.shape[0] // beside
    packed = 0.0
    for b in range(beside):
        lane = _iota((slots * rank, LANES), 1) - b * rank
        fold = _iota((slots * rank, LANES), 0) % rank == lane
        packed = packed + _dot(projected[b * some : (b + 1) * some, :], fold.astype(jnp.bfloat16))
    mid_ref[...] = packed.astype(jnp.bfloat16)


def down(received, slot_down_weight, after=()):
    replicas = len(received)
    rows = replicas * CAP
    return pl.pallas_call(
        functools.partial(down_kernel, replicas, len(after)),
        in_specs=[VMEM] * (replicas + 1) + [ANY] * len(after),
        out_specs=[VMEM, VMEM],
        out_shape=[
            jax.ShapeDtypeStruct((rows * slot_down_weight.shape[1] // LANES, LANES), jnp.bfloat16),
            jax.ShapeDtypeStruct((rows, LANES), jnp.bfloat16),
        ],
        compiler_params=PARAMS,
        name="down",
    )(*received, slot_down_weight, *after)


def up_kernel(parts, after, *refs):
    mids = refs[:parts]
    inside_ref, up_ref = refs[parts : parts + 2]
    out_refs = refs[parts + 2 + after :]
    slots, rank, width = up_ref.shape
    mid = mids[0][...].astype(jnp.float32)
    for m in mids[1:]:
        mid = mid + m[...].astype(jnp.float32)
    mid = mid.astype(jnp.bfloat16)
    wide = []
    for b in range(LANES // rank):
        lane = _iota((LANES, slots * rank), 0) - b * rank
        spread = _iota((LANES, slots * rank), 1) % rank == lane
        wide.append(_dot(mid, spread.astype(jnp.bfloat16)))
    wide = jnp.concatenate(wide, axis=0)
    mine = _iota(wide.shape, 1) // rank == inside_ref[:, 0:1].astype(jnp.int32)
    wide = jnp.where(mine, wide, 0.0).astype(jnp.bfloat16)
    delta = _dot(wide, up_ref[...].reshape(slots * rank, width)).astype(jnp.bfloat16)
    for r, out_ref in enumerate(out_refs):
        out_ref[...] = delta[r * CAP : (r + 1) * CAP, :]


def up(mids, inside, slot_up_weight, after=()):
    rows = inside.shape[0]
    replicas = rows // CAP
    width = slot_up_weight.shape[2]
    return pl.pallas_call(
        functools.partial(up_kernel, len(mids), len(after)),
        in_specs=[VMEM] * (len(mids) + 2) + [ANY] * len(after),
        out_specs=[VMEM] * replicas,
        out_shape=[jax.ShapeDtypeStruct((CAP, width), jnp.bfloat16)] * replicas,
        compiler_params=PARAMS,
        name="up",
    )(*mids, inside, slot_up_weight, *after)


def settle_kernel(step, replicas, after, *refs):
    returned = refs[:replicas]
    chosen_ref, a_ref, residual_ref, w_hbm = refs[replicas : replicas + 4]
    *out_refs, held, sems = refs[replicas + 4 + after :]
    width = residual_ref.shape[1]
    weights = Weights(w_hbm, held, sems, column_owner(step) * width, width)
    weights.start()
    rows = jnp.concatenate([r[...] for r in returned], axis=0)
    delta = _dot(chosen_ref[...], rows, 0, 0)
    total = residual_ref[...].astype(jnp.float32) + delta
    weights.wait()
    total = total + jnp.concatenate([p for _, p in weights.products(a_ref[...])], axis=1)
    for (start, chunk), out_ref in zip(chain_columns(width), out_refs):
        out_ref[...] = total[:, start : start + chunk]


def settle(step, returned, chosen, attended, residual, weight, after=()):
    replicas = len(returned)
    rows, width = residual.shape
    chains = chain_columns(width)
    return pl.pallas_call(
        functools.partial(settle_kernel, step, replicas, len(after)),
        in_specs=[VMEM] * (replicas + 3) + [ANY] * (1 + len(after)),
        out_specs=[VMEM] * len(chains),
        out_shape=[jax.ShapeDtypeStruct((rows, chunk), jnp.float32) for _, chunk in chains],
        scratch_shapes=Weights.scratch(weight.shape[0], width),
        compiler_params=PARAMS,
        cost_estimate=MEDIUM,
        name="settle",
    )(*returned, chosen, attended, residual, weight, *after)


def finish_kernel(start, arrived_ref, settled_ref, *refs):
    out_hbm, held, sems = refs[-3:]
    rows, chunk = arrived_ref.shape
    half = rows // 2
    copies = []
    for i in range(2):
        part = pl.ds(i * half, half)
        total = settled_ref[part, :] + arrived_ref[part, :].astype(jnp.float32)
        held[part, :] = total.astype(jnp.bfloat16)
        target = out_hbm.at[part, pl.ds(start, chunk)]
        copies.append(pltpu.make_async_copy(held.at[part, :], target, sems.at[i]))
        copies[-1].start()
    for copy in copies:
        copy.wait()


def finish(chain, arrived, settled, earlier, width):
    rows = arrived.shape[0]
    start, chunk = chain_columns(width)[chain]
    operands = [arrived, settled] + ([earlier] if earlier is not None else [])
    return pl.pallas_call(
        functools.partial(finish_kernel, start),
        in_specs=[VMEM, VMEM] + ([ANY] if earlier is not None else []),
        out_specs=ANY,
        out_shape=jax.ShapeDtypeStruct((rows, width), jnp.bfloat16),
        input_output_aliases={2: 0} if earlier is not None else {},
        scratch_shapes=[
            pltpu.VMEM((rows, chunk), jnp.bfloat16),
            pltpu.SemaphoreType.DMA((2,)),
        ],
        compiler_params=PARAMS,
        name="finish",
    )(*operands)


def hold_kernel(*refs):
    pass


def hold(x, after):
    return pl.pallas_call(
        hold_kernel,
        in_specs=[ANY] * (1 + len(after)),
        out_specs=ANY,
        out_shape=jax.ShapeDtypeStruct(x.shape, x.dtype),
        input_output_aliases={0: 0},
        compiler_params=PARAMS,
        name="hold",
    )(x, *after)


def per_device(
    residual,
    query,
    cached_key_rows,
    cached_value_rows,
    new_token_key,
    new_token_value,
    lengths,
    output_weight,
    slot_down_weight,
    slot_up_weight,
    placement,
    request_adapter,
):
    count = lax.axis_size("tensor")
    replicas = lax.axis_size("dp")
    block = residual.shape[1]
    order = ring_order(count)
    ring = [(order[p], order[(p + 1) % count]) for p in range(count)]

    def exchange(blocks):
        moved = [
            lax.ppermute(blocks[r], "dp", [(i, i ^ r) for i in range(replicas)])
            for r in range(1, replicas)
        ]
        return [blocks[0]] + moved

    def forward(x):
        return lax.ppermute(x, "tensor", ring)

    def pair_sums(x):
        found = []
        for away in range(1, count // 2):
            pairs = [(p, (p + away) % (count // 2)) for p in range(count // 2)]
            near, far = [], []
            for p, q in pairs:
                sender = 2 * p if p < q else 2 * p + 1
                straight = 2 * q + (sender % 2)
                near.append((sender, straight))
                far.append((sender, straight ^ 1))
            one = lax.ppermute(x, "tensor", near)
            other = lax.ppermute(x, "tensor", far)
            found += [one, other]
        return found

    def next_hop(step, chain, after, cost=None):
        arrived = forward(travelling[chain])
        travelling[chain] = hop(step, chain, arrived, attended, output_weight, block, after, cost)

    attended, first, chosen, *leaving = attend(
        query, cached_key_rows, cached_value_rows, new_token_key, new_token_value, lengths,
        output_weight, request_adapter, placement, block, replicas, slot_down_weight.shape[0],
    )
    second = hop(0, 1, None, attended, output_weight, block)
    rows_here = exchange(leaving)
    mid, inside = down(rows_here, slot_down_weight, after=[second])
    travelling = [first, hold(second, after=[mid])]

    def added(a, b):
        return (a.astype(jnp.float32) + b.astype(jnp.float32)).astype(a.dtype)

    rank_sum = added(mid, lax.ppermute(mid, "tensor", [(i, i ^ 1) for i in range(count)]))
    rank_sums = [rank_sum] + pair_sums(rank_sum)
    next_hop(1, 0, after=[rank_sum, travelling[1]], cost=LONG)
    next_hop(1, 1, after=[travelling[0]], cost=MEDIUM)
    for step in range(2, count - 1):
        for chain in range(2):
            if (step, chain) == (2, 0):
                next_hop(step, chain, after=(), cost=LONG)
                deltas = up(rank_sums, inside, slot_up_weight, after=[travelling[0]])
                returned = exchange(deltas)
            else:
                next_hop(step, chain, after=[deltas[0]])
    settled = settle(
        count - 1, returned, chosen, attended, residual, output_weight, after=[travelling[1]]
    )
    out = None
    for chain in range(2):
        arrived = forward(travelling[chain])
        out = finish(chain, arrived, settled[chain], out, block)
    return out


def solution(mesh):
    placed = (
        P(("parts", "dp"), "tensor"),
        P(("parts", "dp"), "tensor", None),
        P(("parts", "dp"), None, "tensor", None),
        P(("parts", "dp"), None, "tensor", None),
        P(("parts", "dp"), "tensor", None),
        P(("parts", "dp"), "tensor", None),
        P(("parts", "dp")),
        P("tensor", None),
        P("dp", None, "tensor"),
        P("dp", None, "tensor"),
        P("parts"),
        P(("parts", "dp")),
    )
    return jax.shard_map(
        per_device,
        mesh=mesh,
        in_specs=placed,
        out_specs=P(("parts", "dp"), "tensor"),
        check_vma=False,
    )
```

```python
import functools
import math

import jax
import jax.numpy as jnp
from jax import lax
from jax.experimental import pallas as pl
from jax.experimental.pallas import tpu as pltpu
from jax.sharding import PartitionSpec as P

GROUP = 4
CAP = 64
LANES = 128
SPAN = 64
MASKED = -1e30
VMEM_LIMIT = 50 * 1024 * 1024
FULL_VMEM = 61 * 1024 * 1024
SHARES = ((5, 3),)
PIECE = 512
SPLIT = 4

VMEM = pl.BlockSpec(memory_space=pltpu.VMEM)
ANY = pl.BlockSpec(memory_space=pl.ANY)
LONG = pl.CostEstimate(flops=20 * 10**9, transcendentals=0, bytes_accessed=40 * 10**6)
MEDIUM = pl.CostEstimate(flops=4 * 10**9, transcendentals=0, bytes_accessed=8 * 10**6)
PARAMS = pltpu.CompilerParams(vmem_limit_bytes=VMEM_LIMIT)


def _dot(a, b, left=1, right=0):
    return lax.dot_general(
        a, b, (((left,), (right,)), ((), ())), preferred_element_type=jnp.float32
    )


def _iota(shape, axis):
    return lax.broadcasted_iota(jnp.int32, shape, axis)


def ring_order(count):
    return list(range(0, count, 2)) + list(range(1, count, 2))[::-1]


def column_owner(step):
    count = lax.axis_size("tensor")
    here = lax.axis_index("tensor")
    half = here // 2
    spot = jnp.where(here % 2 == 0, half, count - 1 - half)
    spot = lax.rem(spot - 1 - step + 2 * count, count)
    return jnp.where(2 * spot < count, 2 * spot, 2 * (count - spot) - 1)


def chain_columns(width):
    shares = next(s for s in SHARES if width % (sum(s) * LANES) == 0)
    unit = width // sum(shares)
    return [(sum(shares[:c]) * unit, shares[c] * unit) for c in range(len(shares))]


class Weights:
    def __init__(self, w_ref, held, sems, first, width):
        depth = w_ref.shape[0] // SPLIT
        first = pl.multiple_of(first, LANES)
        self.held = held
        self.copies = [
            pltpu.make_async_copy(
                w_ref.at[pl.ds(s * depth, depth), pl.ds(first, width)],
                held.at[pl.ds(s * depth, depth), :],
                sems.at[s],
            )
            for s in range(SPLIT)
        ]

    def start(self):
        for copy in self.copies:
            copy.start()

    def wait(self):
        for copy in self.copies:
            copy.wait()

    def products(self, a):
        width = self.held.shape[1]
        for at in range(0, width, PIECE):
            columns = pl.ds(at, min(PIECE, width - at))
            yield columns, _dot(a, self.held[:, columns])

    @staticmethod
    def scratch(depth, width):
        return [
            pltpu.VMEM((depth, width), jnp.bfloat16),
            pltpu.SemaphoreType.DMA((SPLIT,)),
        ]


def row_max(arrays):
    full = None
    tops = []
    for x in arrays:
        width = x.shape[1]
        if width % LANES:
            tops.append(jnp.max(x, axis=1, keepdims=True))
            continue
        for at in range(0, width, LANES):
            tile = x[:, at : at + LANES]
            full = tile if full is None else jnp.maximum(full, tile)
    if full is not None:
        tops.append(jnp.max(full, axis=1, keepdims=True))
    return functools.reduce(jnp.maximum, tops)


def attend_kernel(
    heads, kv, cache, steps, block, replicas, slots,
    len_hbm, adapter_hbm, placement_hbm, q_hbm, k_hbm, v_hbm, nk_hbm, nv_hbm, w_hbm,
    *refs,
):
    a_hbm, out_hbm, chosen_hbm, *sent_hbm = refs[: 3 + replicas]
    (
        a_ref, out_ref, chosen_ref, sent_ref, out_sems,
        len_ref, adapter_ref, placement_ref, q_ref, k_ref, v_ref, nk_ref, nv_ref,
        scores_ref, mixed_ref, fresh_bias_ref, sems, small_sems, w_held, w_sems,
    ) = refs[3 + replicas :]
    requests = len_ref.shape[1]
    width = q_hbm.shape[1]
    per = requests // steps
    groups = per // GROUP
    group_rows = GROUP * heads
    group_cols = GROUP * cache * kv
    per_kv = heads // kv
    scale = math.log2(math.e) / math.sqrt(width)

    def part(kind, step):
        source, target, count = (
            (q_hbm, q_ref, heads),
            (k_hbm, k_ref, cache * kv),
            (v_hbm, v_ref, cache * kv),
        )[kind]
        rows = pl.ds(step * per * count, per * count)
        return pltpu.make_async_copy(source.at[rows, :], target.at[rows, :], sems.at[kind, step])

    small = [
        pltpu.make_async_copy(source, target, small_sems.at[i])
        for i, (source, target) in enumerate(
            (
                (nk_hbm, nk_ref),
                (len_hbm, len_ref),
                (nv_hbm, nv_ref),
                (adapter_hbm, adapter_ref),
                (placement_hbm, placement_ref),
            )
        )
    ]
    leaving = []

    def leave(source, target):
        copy = pltpu.make_async_copy(source, target, out_sems.at[len(leaving)])
        copy.start()
        leaving.append(copy)

    def multiply(first, count):
        rows = pl.ds(first, count)
        for columns, product in weights.products(a_ref[rows, :]):
            out_ref[rows, columns] = product.astype(jnp.bfloat16)
            leave(out_ref.at[rows, columns], out_hbm.at[rows, columns])

    chunk = out_ref.shape[1]
    weights = Weights(w_hbm, w_held, w_sems, column_owner(0) * block, chunk)
    part(0, 0).start()
    part(1, 0).start()
    for copy in small[:2]:
        copy.start()
    part(0, 1).start()
    part(1, 1).start()
    part(2, 0).start()
    for copy in small[2:]:
        copy.start()
    part(2, 1).start()
    for step in range(2, steps):
        for kind in range(3):
            part(kind, step).start()
    weights.start()

    row = _iota((group_rows, group_cols), 0)
    col = _iota((group_rows, group_cols), 1)
    same = (row // heads == col // (cache * kv)) & ((row % heads) // per_kv == col % kv)
    own_bias = jnp.where(same, 0.0, MASKED)
    row = _iota(fresh_bias_ref.shape, 0)
    col = _iota(fresh_bias_ref.shape, 1)
    same = (row // heads == col // kv) & ((row % heads) // per_kv == col % kv)
    fresh_bias_ref[...] = jnp.where(same, 0.0, MASKED)
    fresh_cols = SPAN * kv
    span_rows = SPAN * heads
    span_groups = SPAN // GROUP
    ones = jnp.ones((max(group_cols, fresh_cols), LANES), jnp.bfloat16)

    def arrive(step):
        part(0, step).wait()
        part(1, step).wait()

    def scores(step):
        side = step % 2
        q_at = step * per * heads
        k_at = step * per * cache * kv
        for g in range(groups):
            scores_ref[side, pl.ds(g * group_rows, group_rows), pl.ds(0, group_cols)] = _dot(
                q_ref[pl.ds(q_at + g * group_rows, group_rows), :],
                k_ref[pl.ds(k_at + g * group_cols, group_cols), :],
                1,
                1,
            )
        for span in range(per // SPAN):
            rows = pl.ds(span * span_rows, span_rows)
            scores_ref[side, rows, pl.ds(group_cols, fresh_cols)] = _dot(
                q_ref[pl.ds(q_at + span * span_rows, span_rows), :],
                nk_ref[pl.ds(step * per * kv + span * fresh_cols, fresh_cols), :],
                1,
                1,
            )

    for copy in small[:2]:
        copy.wait()
    counts = len_ref[...].astype(jnp.float32)
    all_groups = requests // GROUP
    of_group = _iota((all_groups, requests), 1) // GROUP == _iota((all_groups, requests), 0)
    counts = jnp.where(of_group, counts, 0.0).astype(jnp.bfloat16)
    spread = _iota((requests, group_cols), 0) % GROUP == _iota((requests, group_cols), 1) // (cache * kv)
    counts = _dot(counts, spread.astype(jnp.bfloat16))
    position = (_iota((all_groups, group_cols), 1) // kv) % cache
    length_bias = jnp.where(position.astype(jnp.float32) < counts, 0.0, MASKED)

    arrive(0)
    scores(0)
    for step in range(steps):
        side = step % 2
        k_at = step * per * cache * kv
        f_at = step * per * kv
        part(2, step).wait()
        if step == 0:
            for copy in small[2:]:
                copy.wait()
        if step + 1 < steps:
            arrive(step + 1)
            scores(step + 1)
        if step == 0:
            plan_routes(slots, adapter_ref, placement_ref, chosen_ref, sent_ref)
        if step == steps - 1:
            weights.wait()
            multiply(0, requests - per)
        for span in range(per // SPAN):
            cached_weights = []
            fresh_weights = []
            mixed = []
            for g in range(span * span_groups, (span + 1) * span_groups):
                rows = pl.ds(g * group_rows, group_rows)
                bias = own_bias + length_bias[step * groups + g : step * groups + g + 1, :]
                cached = scores_ref[side, rows, pl.ds(0, group_cols)] + bias
                inner = pl.ds((g % span_groups) * group_rows, group_rows)
                new = scores_ref[side, rows, pl.ds(group_cols, fresh_cols)]
                new = new + fresh_bias_ref[inner, :]
                top = row_max([cached, new])
                cached = jnp.exp2((cached - top) * scale).astype(jnp.bfloat16)
                cached_weights.append(cached)
                fresh_weights.append(jnp.exp2((new - top) * scale).astype(jnp.bfloat16))
                mixed.append(_dot(cached, v_ref[pl.ds(k_at + g * group_cols, group_cols), :]))
            fresh = jnp.concatenate(fresh_weights, axis=0)
            values = nv_ref[pl.ds(f_at + span * fresh_cols, fresh_cols), :]
            mixed = jnp.concatenate(mixed, axis=0) + _dot(fresh, values)
            total = _dot(jnp.concatenate(cached_weights, axis=0), ones[:group_cols])
            total = total + _dot(fresh, ones[:fresh_cols])
            rows = pl.ds(span * span_rows, span_rows)
            inverse = pl.reciprocal(total, approx=True)
            mixed_ref[side, rows, :] = mixed * (inverse * (2.0 - total * inverse))
        for h in range(heads):
            a_ref[pl.ds(step * per, per), pl.ds(h * width, width)] = mixed_ref[
                side, pl.ds(h, per, stride=heads), :
            ].astype(jnp.bfloat16)
        rows = pl.ds(step * per, per)
        leave(a_ref.at[rows, :], a_hbm.at[rows, :])

    sent_ref[:, pl.ds(0, heads * width)] = _dot(chosen_ref[...], a_ref[...]).astype(jnp.bfloat16)
    leave(chosen_ref, chosen_hbm)
    for r in range(replicas):
        leave(sent_ref.at[pl.ds(r * CAP, CAP), :], sent_hbm[r])
    multiply(requests - per, per)
    for copy in leaving:
        copy.wait()


def plan_routes(slots, adapter_ref, placement_ref, chosen_ref, sent_ref):
    replicas = sent_ref.shape[0] // CAP
    requests = adapter_ref.shape[1]
    table = placement_ref.shape[1]
    matches = _iota((table, requests), 0) == adapter_ref[...]
    placed = jnp.broadcast_to(placement_ref[...].astype(jnp.float32), (8, table))
    slot = _dot(placed.astype(jnp.bfloat16), matches.astype(jnp.bfloat16)).astype(jnp.int32)
    slot = slot[0:1, :]
    holder = (slot // slots) ^ lax.axis_index("dp")
    inside = slot % slots
    of_holder = _iota((max(replicas, 8), requests), 0) == holder
    earlier = _iota((requests, requests), 0) < _iota((requests, requests), 1)
    before = _dot(of_holder.astype(jnp.bfloat16), earlier.astype(jnp.bfloat16))
    before = jnp.sum(jnp.where(of_holder, before, 0.0), axis=0, keepdims=True).astype(jnp.int32)
    target = holder * CAP + before
    here = _iota((replicas * CAP, requests), 0) == target
    chosen_ref[...] = here.astype(jnp.bfloat16)
    inner = jnp.sum(jnp.where(here, inside.astype(jnp.float32), 0.0), axis=1, keepdims=True)
    inner = jnp.broadcast_to(inner, (replicas * CAP, LANES)).astype(jnp.bfloat16)
    sent_ref[:, pl.ds(sent_ref.shape[1] - LANES, LANES)] = inner


def attend(
    query, keys, values, new_key, new_value, lengths, weight, request_adapter, placement,
    block, replicas, slots,
):
    requests, heads, width = query.shape
    cache, kv = keys.shape[1], keys.shape[2]
    steps = 2
    per = requests // steps
    columns = GROUP * cache * kv + SPAN * kv
    features = heads * width
    chunk = chain_columns(block)[0][1]
    small = [lengths.reshape(1, -1), request_adapter.reshape(1, -1), placement.reshape(1, -1)]
    operands = [
        query.reshape(requests * heads, width),
        keys.reshape(requests * cache * kv, width),
        values.reshape(requests * cache * kv, width),
        new_key.reshape(requests * kv, width),
        new_value.reshape(requests * kv, width),
    ]
    return pl.pallas_call(
        functools.partial(attend_kernel, heads, kv, cache, steps, block, replicas, slots),
        in_specs=[ANY] * 9,
        out_specs=[ANY] * (3 + replicas),
        out_shape=[
            jax.ShapeDtypeStruct((requests, features), jnp.bfloat16),
            jax.ShapeDtypeStruct((requests, chunk), jnp.bfloat16),
            jax.ShapeDtypeStruct((replicas * CAP, requests), jnp.bfloat16),
        ]
        + [jax.ShapeDtypeStruct((CAP, features + LANES), jnp.bfloat16)] * replicas,
        scratch_shapes=[
            pltpu.VMEM((requests, features), jnp.bfloat16),
            pltpu.VMEM((requests, chunk), jnp.bfloat16),
            pltpu.VMEM((replicas * CAP, requests), jnp.bfloat16),
            pltpu.VMEM((replicas * CAP, features + LANES), jnp.bfloat16),
            pltpu.SemaphoreType.DMA((1 + steps + 2 * pl.cdiv(chunk, PIECE) + replicas,)),
        ]
        + [pltpu.VMEM(x.shape, x.dtype) for x in small + operands]
        + [
            pltpu.VMEM((2, per * heads, columns), jnp.float32),
            pltpu.VMEM((2, per * heads, width), jnp.float32),
            pltpu.VMEM((SPAN * heads, SPAN * kv), jnp.float32),
            pltpu.SemaphoreType.DMA((3, steps)),
            pltpu.SemaphoreType.DMA((5,)),
        ]
        + Weights.scratch(weight.shape[0], chunk),
        compiler_params=pltpu.CompilerParams(vmem_limit_bytes=FULL_VMEM),
        name="attend",
    )(*small, *operands, weight)


def hop_kernel(step, block, start, arriving, after, *refs):
    if arriving:
        arrived_ref, *refs = refs
    a_ref, w_hbm, *refs = refs
    out_ref, held, sems = refs[after:]
    chunk = out_ref.shape[1]
    first = column_owner(step) * block + start
    weights = Weights(w_hbm, held, sems, first, chunk)
    weights.start()
    weights.wait()
    for columns, product in weights.products(a_ref[...]):
        if arriving:
            product = product + arrived_ref[:, columns].astype(jnp.float32)
        out_ref[:, columns] = product.astype(jnp.bfloat16)


def hop(step, chain, arrived, attended, weight, block, after=(), cost=None):
    arriving = arrived is not None
    start, chunk = chain_columns(block)[chain]
    operands = ([arrived] if arriving else []) + [attended, weight, *after]
    return pl.pallas_call(
        functools.partial(hop_kernel, step, block, start, arriving, len(after)),
        in_specs=[VMEM] * (1 + arriving) + [ANY] + [ANY] * len(after),
        out_specs=VMEM,
        out_shape=jax.ShapeDtypeStruct((attended.shape[0], chunk), jnp.bfloat16),
        scratch_shapes=Weights.scratch(weight.shape[0], chunk),
        compiler_params=PARAMS,
        cost_estimate=cost,
        name="hop",
    )(*operands)


def down_kernel(replicas, after, *refs):
    received = refs[:replicas]
    down_ref = refs[replicas]
    mid_ref, inside_ref = refs[replicas + 1 + after :]
    slots, rank, width = down_ref.shape
    rows = jnp.concatenate([r[:, pl.ds(0, width)] for r in received], axis=0)
    inside = jnp.concatenate([r[:, pl.ds(width, LANES)] for r in received], axis=0)
    inside_ref[...] = inside
    projected = _dot(rows, down_ref[...].reshape(slots * rank, width), 1, 1)
    lane_slot = _iota(projected.shape, 1) // rank
    mine = lane_slot == inside[:, 0:1].astype(jnp.int32)
    projected = jnp.where(mine, projected, 0.0).astype(jnp.bfloat16)
    beside = LANES // rank
    some = projected.shape[0] // beside
    packed = 0.0
    for b in range(beside):
        lane = _iota((slots * rank, LANES), 1) - b * rank
        fold = _iota((slots * rank, LANES), 0) % rank == lane
        packed = packed + _dot(projected[b * some : (b + 1) * some, :], fold.astype(jnp.bfloat16))
    mid_ref[...] = packed.astype(jnp.bfloat16)


def down(received, slot_down_weight, after=()):
    replicas = len(received)
    rows = replicas * CAP
    return pl.pallas_call(
        functools.partial(down_kernel, replicas, len(after)),
        in_specs=[VMEM] * (replicas + 1) + [ANY] * len(after),
        out_specs=[VMEM, VMEM],
        out_shape=[
            jax.ShapeDtypeStruct((rows * slot_down_weight.shape[1] // LANES, LANES), jnp.bfloat16),
            jax.ShapeDtypeStruct((rows, LANES), jnp.bfloat16),
        ],
        compiler_params=PARAMS,
        name="down",
    )(*received, slot_down_weight, *after)


def up_kernel(parts, after, *refs):
    mids = refs[:parts]
    inside_ref, up_ref = refs[parts : parts + 2]
    out_refs = refs[parts + 2 + after :]
    slots, rank, width = up_ref.shape
    mid = mids[0][...].astype(jnp.float32)
    for m in mids[1:]:
        mid = mid + m[...].astype(jnp.float32)
    mid = mid.astype(jnp.bfloat16)
    wide = []
    for b in range(LANES // rank):
        lane = _iota((LANES, slots * rank), 0) - b * rank
        spread = _iota((LANES, slots * rank), 1) % rank == lane
        wide.append(_dot(mid, spread.astype(jnp.bfloat16)))
    wide = jnp.concatenate(wide, axis=0)
    mine = _iota(wide.shape, 1) // rank == inside_ref[:, 0:1].astype(jnp.int32)
    wide = jnp.where(mine, wide, 0.0).astype(jnp.bfloat16)
    delta = _dot(wide, up_ref[...].reshape(slots * rank, width)).astype(jnp.bfloat16)
    for r, out_ref in enumerate(out_refs):
        out_ref[...] = delta[r * CAP : (r + 1) * CAP, :]


def up(mids, inside, slot_up_weight, after=()):
    rows = inside.shape[0]
    replicas = rows // CAP
    width = slot_up_weight.shape[2]
    return pl.pallas_call(
        functools.partial(up_kernel, len(mids), len(after)),
        in_specs=[VMEM] * (len(mids) + 2) + [ANY] * len(after),
        out_specs=[VMEM] * replicas,
        out_shape=[jax.ShapeDtypeStruct((CAP, width), jnp.bfloat16)] * replicas,
        compiler_params=PARAMS,
        name="up",
    )(*mids, inside, slot_up_weight, *after)


def settle_kernel(step, replicas, after, *refs):
    returned = refs[:replicas]
    chosen_ref, a_ref, residual_ref, w_hbm = refs[replicas : replicas + 4]
    *out_refs, held, sems = refs[replicas + 4 + after :]
    width = residual_ref.shape[1]
    weights = Weights(w_hbm, held, sems, column_owner(step) * width, width)
    weights.start()
    rows = jnp.concatenate([r[...] for r in returned], axis=0)
    delta = _dot(chosen_ref[...], rows, 0, 0)
    total = residual_ref[...].astype(jnp.float32) + delta
    weights.wait()
    total = total + jnp.concatenate([p for _, p in weights.products(a_ref[...])], axis=1)
    for (start, chunk), out_ref in zip(chain_columns(width), out_refs):
        out_ref[...] = total[:, start : start + chunk]


def settle(step, returned, chosen, attended, residual, weight, after=()):
    replicas = len(returned)
    rows, width = residual.shape
    chains = chain_columns(width)
    return pl.pallas_call(
        functools.partial(settle_kernel, step, replicas, len(after)),
        in_specs=[VMEM] * (replicas + 3) + [ANY] * (1 + len(after)),
        out_specs=[VMEM] * len(chains),
        out_shape=[jax.ShapeDtypeStruct((rows, chunk), jnp.float32) for _, chunk in chains],
        scratch_shapes=Weights.scratch(weight.shape[0], width),
        compiler_params=PARAMS,
        cost_estimate=MEDIUM,
        name="settle",
    )(*returned, chosen, attended, residual, weight, *after)


def finish_kernel(start, arrived_ref, settled_ref, *refs):
    out_hbm, held, sems = refs[-3:]
    rows, chunk = arrived_ref.shape
    half = rows // 2
    copies = []
    for i in range(2):
        part = pl.ds(i * half, half)
        total = settled_ref[part, :] + arrived_ref[part, :].astype(jnp.float32)
        held[part, :] = total.astype(jnp.bfloat16)
        target = out_hbm.at[part, pl.ds(start, chunk)]
        copies.append(pltpu.make_async_copy(held.at[part, :], target, sems.at[i]))
        copies[-1].start()
    for copy in copies:
        copy.wait()


def finish(chain, arrived, settled, earlier, width):
    rows = arrived.shape[0]
    start, chunk = chain_columns(width)[chain]
    operands = [arrived, settled] + ([earlier] if earlier is not None else [])
    return pl.pallas_call(
        functools.partial(finish_kernel, start),
        in_specs=[VMEM, VMEM] + ([ANY] if earlier is not None else []),
        out_specs=ANY,
        out_shape=jax.ShapeDtypeStruct((rows, width), jnp.bfloat16),
        input_output_aliases={2: 0} if earlier is not None else {},
        scratch_shapes=[
            pltpu.VMEM((rows, chunk), jnp.bfloat16),
            pltpu.SemaphoreType.DMA((2,)),
        ],
        compiler_params=PARAMS,
        name="finish",
    )(*operands)


def hold_kernel(*refs):
    pass


def hold(x, after):
    return pl.pallas_call(
        hold_kernel,
        in_specs=[ANY] * (1 + len(after)),
        out_specs=ANY,
        out_shape=jax.ShapeDtypeStruct(x.shape, x.dtype),
        input_output_aliases={0: 0},
        compiler_params=PARAMS,
        name="hold",
    )(x, *after)


def per_device(
    residual,
    query,
    cached_key_rows,
    cached_value_rows,
    new_token_key,
    new_token_value,
    lengths,
    output_weight,
    slot_down_weight,
    slot_up_weight,
    placement,
    request_adapter,
):
    count = lax.axis_size("tensor")
    replicas = lax.axis_size("dp")
    block = residual.shape[1]
    order = ring_order(count)
    ring = [(order[p], order[(p + 1) % count]) for p in range(count)]

    def exchange(blocks):
        moved = [
            lax.ppermute(blocks[r], "dp", [(i, i ^ r) for i in range(replicas)])
            for r in range(1, replicas)
        ]
        return [blocks[0]] + moved

    def forward(x):
        return lax.ppermute(x, "tensor", ring)

    def pair_sums(x):
        found = []
        for away in range(1, count // 2):
            pairs = [(p, (p + away) % (count // 2)) for p in range(count // 2)]
            near, far = [], []
            for p, q in pairs:
                sender = 2 * p if p < q else 2 * p + 1
                straight = 2 * q + (sender % 2)
                near.append((sender, straight))
                far.append((sender, straight ^ 1))
            one = lax.ppermute(x, "tensor", near)
            other = lax.ppermute(x, "tensor", far)
            found += [one, other]
        return found

    def next_hop(step, chain, after, cost=None):
        arrived = forward(travelling[chain])
        travelling[chain] = hop(step, chain, arrived, attended, output_weight, block, after, cost)

    attended, first, chosen, *leaving = attend(
        query, cached_key_rows, cached_value_rows, new_token_key, new_token_value, lengths,
        output_weight, request_adapter, placement, block, replicas, slot_down_weight.shape[0],
    )
    second = hop(0, 1, None, attended, output_weight, block)
    rows_here = exchange(leaving)
    mid, inside = down(rows_here, slot_down_weight, after=[second])
    travelling = [first, hold(second, after=[mid])]

    def added(a, b):
        return (a.astype(jnp.float32) + b.astype(jnp.float32)).astype(a.dtype)

    rank_sum = added(mid, lax.ppermute(mid, "tensor", [(i, i ^ 1) for i in range(count)]))
    rank_sums = [rank_sum] + pair_sums(rank_sum)
    next_hop(1, 0, after=[rank_sum, travelling[1]], cost=LONG)
    next_hop(1, 1, after=[travelling[0]], cost=MEDIUM)
    for step in range(2, count - 1):
        for chain in range(2):
            if (step, chain) == (2, 0):
                next_hop(step, chain, after=(), cost=LONG)
                deltas = up(rank_sums, inside, slot_up_weight, after=[travelling[0]])
                returned = exchange(deltas)
            else:
                next_hop(step, chain, after=[deltas[0]])
    settled = settle(
        count - 1, returned, chosen, attended, residual, output_weight, after=[travelling[1]]
    )
    out = None
    for chain in range(2):
        arrived = forward(travelling[chain])
        out = finish(chain, arrived, settled[chain], out, block)
    return out


def solution(mesh):
    placed = (
        P(("parts", "dp"), "tensor"),
        P(("parts", "dp"), "tensor", None),
        P(("parts", "dp"), None, "tensor", None),
        P(("parts", "dp"), None, "tensor", None),
        P(("parts", "dp"), "tensor", None),
        P(("parts", "dp"), "tensor", None),
        P(("parts", "dp")),
        P("tensor", None),
        P("dp", None, "tensor"),
        P("dp", None, "tensor"),
        P("parts"),
        P(("parts", "dp")),
    )
    return jax.shard_map(
        per_device,
        mesh=mesh,
        in_specs=placed,
        out_specs=P(("parts", "dp"), "tensor"),
        check_vma=False,
    )
```
